32 devices in a mesh: gx: 4 (over z), gy: 8 (over y, x, core).
Axes of the slice: x: 2, y: 2, z: 4, core: 2. Of those that a mesh axis runs over, the one named last changes fastest.
Arguments:
- tokens: bfloat16 [8, 2560, 1536], P('gx', 'gy'), may hold values from -6 to 6
- cotangent: bfloat16 [8, 2560, 1536], P('gx', 'gy'), may hold values from -6 to 6
- segment: int32 [8, 2560], P('gx'), may hold values from -1 to 12, as said below
- parent: int32 [8, 13], P('gx'), may hold values from 0 to 12, as said below
- w_qkv: bfloat16 [1536, 2048], P(('gx', 'gy')), may hold values from -0.21875 to 0.21875
- qkv_bias: bfloat16 [2048], P(('gx', 'gy')), may hold values from -3 to 3
- w_out: bfloat16 [1536, 1536], P(None, ('gx', 'gy')), may hold values from -1.75 to 1.75
- gain_attn: bfloat16 [1536], P(('gx', 'gy')), may hold values from 0.5 to 1.5
- gain_ffn: bfloat16 [1536], P(('gx', 'gy')), may hold values from 0.5 to 1.5
- w_gate: bfloat16 [1536, 8960], P('gx', 'gy'), may hold values from -0.15625 to 0.15625
- w_up: bfloat16 [1536, 8960], P('gx', 'gy'), may hold values from -0.15625 to 0.15625
- w_down: bfloat16 [8960, 1536], P('gy', 'gx'), may hold values from -0.1875 to 0.1875
Outputs:
- layer_out: bfloat16 [8, 2560, 1536], P('gx', 'gy')
- grad_tokens: bfloat16 [8, 2560, 1536], P('gx', 'gy')
- grad_w_qkv: float32 [1536, 2048], P(('gx', 'gy'))
- grad_qkv_bias: float32 [2048], P(('gx', 'gy'))
- grad_w_out: float32 [1536, 1536], P(None, ('gx', 'gy'))
- grad_gain_attn: float32 [1536], P(('gx', 'gy'))
- grad_gain_ffn: float32 [1536], P(('gx', 'gy'))
- grad_w_gate: float32 [1536, 8960], P('gx', 'gy')
- grad_w_up: float32 [1536, 8960], P('gx', 'gy')
- grad_w_down: float32 [8960, 1536], P('gy', 'gx')
The draws below stay inside these ranges and needn't reach their ends.
Inputs may be any that keep to these rules, and one draw needn't show every extreme that they name: In each tree, the segment labels 0 to 12 each cover one run of slots, the runs in the order of a depth-first walk: a trunk of 1024 slots, then for each of four branches a run of 128 slots followed by its two leaves of 64 slots; -1 marks padding slots between runs; the trunk starts at slot 0 and the last leaf ends at slot 2559. Which label takes which run varies from tree to tree. The label of each segment's parent: the trunk is its own parent, each branch's parent is the trunk, each leaf's parent is a branch; consistent with segment of the same tree.
All inputs are finite; a program needn't handle non-finite values.
Results may differ from the reference program's by a relative error of at most 0.013.
Values may be sent and summed in bfloat16 or wider, within the bound.
A program may use at most 272 MiB of HBM per device.

```python
import math
import jax
import jax.numpy as jnp
import numpy as np
from jax import lax

D = 1536
HEADS = 12
KV_HEADS = 2
HEAD = 128
FF = 8960
TRUNK = 1024
BRANCH = 128
LEAF = 64
SLOT = 2560
SEGS = 13
TREES = 8
QKV = 2048


def tree_layout(key):
    order_len = np.array([TRUNK] + [BRANCH, LEAF, LEAF] * 4, dtype=np.int32)
    order_parent = np.array([0, 0, 1, 1, 0, 4, 4, 0, 7, 7, 0, 10, 10], dtype=np.int32)
    spare = SLOT - TRUNK - 4 * BRANCH - 8 * LEAF

    def one_tree(tree_key):
        label_key = jax.random.fold_in(tree_key, 1)
        gap_key = jax.random.fold_in(tree_key, 2)
        labels = jax.random.permutation(label_key, SEGS).astype(jnp.int32)
        cuts = jnp.sort(jax.random.randint(gap_key, (SEGS - 2,), 0, spare + 1).astype(jnp.int32))
        edges = jnp.concatenate([jnp.zeros((1,), jnp.int32), cuts, jnp.full((1,), spare, jnp.int32)])
        gaps = jnp.concatenate([jnp.zeros((1,), jnp.int32), edges[1:] - edges[:-1]])
        lengths = jnp.asarray(order_len)
        starts = (jnp.cumsum(lengths + gaps) - lengths).astype(jnp.int32)
        places = jnp.arange(SLOT, dtype=jnp.int32)
        inside = (places[:, None] >= starts[None, :]) & (places[:, None] < (starts + lengths)[None, :])
        labelled = jnp.sum(jnp.where(inside, labels[None, :], 0), axis=1).astype(jnp.int32)
        segment = jnp.where(jnp.any(inside, axis=1), labelled, -1).astype(jnp.int32)
        parent = jnp.zeros((SEGS,), jnp.int32).at[labels].set(labels[jnp.asarray(order_parent)])
        return (segment, parent)
    tree_keys = jax.random.split(key, TREES)
    return jax.vmap(one_tree)(tree_keys)


def draw_segment(key, part):
    shared = tree_layout(key)
    return shared[0]


def draw_parent(key, part):
    shared = tree_layout(key)
    return shared[1]


def strengthened(entries, key, source, target, shards_of, factor):
    def block_of(position):
        return (jnp.arange(entries.shape[position]) // (entries.shape[position] // shards_of)).reshape((-1,) + (1,) * (entries.ndim - 1 - position))

    near = jax.random.permutation(key, shards_of)[block_of(target)]
    other_side = (block_of(target) + shards_of // 2) % shards_of
    return jnp.where((block_of(source) == near) | (block_of(source) == other_side), factor * entries, entries)


def shard_levels(stream_key, extent, shards, least, top_value):
    def one(dim, shards_of):
        steps = jax.random.uniform(jax.random.fold_in(jax.random.fold_in(stream_key, 6), dim), (shards_of,), jnp.float32, least / len(shards), top_value / len(shards))
        return jnp.repeat(jnp.exp(steps), extent[dim] // shards_of).reshape((-1,) + (1,) * (len(extent) - dim - 1))

    gain = one(*shards[0])
    for cut in shards[1:]:
        gain = gain * one(*cut)
    return gain


def gaussian(own_key, extent, scale, most, cuts=(), held_as=jnp.bfloat16):
    entries = jax.random.normal(own_key, extent, jnp.float32) * scale
    if len(cuts) > 0:
        entries = shard_levels(own_key, extent, cuts, -0.22, 0.18) * entries
    return jnp.clip(entries, min=-most, max=most).astype(held_as)


def gaussian_with(own_key, extent, scale, reach, cuts, heavy, kind=jnp.bfloat16):
    values = scale * jax.random.normal(own_key, extent, jnp.float32)
    if cuts:
        values = values * shard_levels(own_key, extent, cuts, -0.22, 0.18)
    return jnp.clip(strengthened(values, jax.random.fold_in(own_key, 3), *heavy), -reach, reach).astype(kind)


def setup_inputs(seed: int = 0) -> dict:
    arg_keys = jax.random.split(jax.random.key(seed), 13)
    return {
        "tokens": gaussian(arg_keys[0], (TREES, SLOT, D), 1.0, 6.0, ((0, 4), (1, 8))),
        "cotangent": gaussian(arg_keys[1], (TREES, SLOT, D), 1.0, 6.0, ((0, 4), (1, 8))),
        "segment": draw_segment(jax.random.fold_in(arg_keys[12], 71), 0),
        "parent": draw_parent(jax.random.fold_in(arg_keys[12], 71), 0),
        "w_qkv": gaussian(arg_keys[4], (D, QKV), (D // 2) ** -0.5, 0.21875, ((0, 32),)),
        "qkv_bias": gaussian(arg_keys[5], (QKV,), 0.5, 3.0, ((0, 32),)),
        "w_out": gaussian(arg_keys[6], (HEADS * HEAD, D), (max(1, HEADS * HEAD // 128)) ** -0.5, 1.75, ((1, 32),)),
        "gain_attn": jnp.clip(1.0 + 0.1 * jax.random.normal(arg_keys[7], (D,), jnp.float32), 0.5, 1.5).astype(jnp.bfloat16),
        "gain_ffn": jnp.clip(1.0 + 0.1 * jax.random.normal(arg_keys[8], (D,), jnp.float32), 0.5, 1.5).astype(jnp.bfloat16),
        "w_gate": gaussian(arg_keys[9], (D, FF), D ** -0.5, 0.15625, ((0, 4), (1, 8))),
        "w_up": gaussian(arg_keys[10], (D, FF), D ** -0.5, 0.15625, ((0, 4), (1, 8))),
        "w_down": gaussian_with(arg_keys[11], (FF, D), (FF // 4) ** -0.5, 0.1875, ((0, 8), (1, 4)), (0, 1, 8, 2.0)),
    }


EPS = 1e-06
THETA = 1000000.0
NEGATIVE = -1e+30

@jax.custom_vjp
def low(v):
    return lax.optimization_barrier(v.astype(jnp.bfloat16)).astype(jnp.float32)

@jax.custom_vjp
def low_back(v):
    return v

def low_keep(v):
    return (low(v), None)

def low_pass(kept, grad):
    return (grad,)

def back_keep(v):
    return (v, None)

def back_low(kept, grad):
    return (low(grad),)
low.defvjp(low_keep, low_pass)
low_back.defvjp(back_keep, back_low)

def tree_tables(segment, parent):
    slot_len = segment.shape[0]
    seg_count = parent.shape[0]
    places = jnp.arange(slot_len, dtype=jnp.int32)
    labels = jnp.arange(seg_count, dtype=jnp.int32)
    member = segment[:, None] == labels[None, :]
    valid = segment >= 0
    first = lax.optimization_barrier(jnp.min(jnp.where(member, places[:, None], slot_len), axis=0)).astype(jnp.int32)
    length = lax.optimization_barrier(jnp.sum(member.astype(jnp.int32), axis=0)).astype(jnp.int32)
    parent_hit = parent[:, None] == labels[None, :]
    grand = lax.optimization_barrier(jnp.sum(jnp.where(parent_hit, parent[None, :], 0), axis=1)).astype(jnp.int32)
    grand_hit = grand[:, None] == labels[None, :]
    parent_len = lax.optimization_barrier(jnp.sum(jnp.where(parent_hit, length[None, :], 0), axis=1)).astype(jnp.int32)
    grand_len = lax.optimization_barrier(jnp.sum(jnp.where(grand_hit, length[None, :], 0), axis=1)).astype(jnp.int32)
    base = jnp.where(parent != labels, parent_len, 0) + jnp.where(grand != parent, grand_len, 0)

    def lookup(table):
        return lax.optimization_barrier(jnp.sum(jnp.where(member, table[None, :], 0), axis=1)).astype(jnp.int32)
    upper_one = jnp.where(valid, lookup(parent), -2).astype(jnp.int32)
    upper_two = jnp.where(valid, lookup(grand), -2).astype(jnp.int32)
    depth_pos = jnp.where(valid, places - lookup(first) + lookup(base), 0).astype(jnp.int32)
    return (valid, upper_one, upper_two, depth_pos)

def allowed(seg_query, upper_one, upper_two, place_query, seg_keys, valid_keys, place_keys):
    related = (seg_keys[None, :] == seg_query[:, None]) | (seg_keys[None, :] == upper_one[:, None])
    related = related | (seg_keys[None, :] == upper_two[:, None])
    earlier = place_keys[None, :] <= place_query[:, None]
    return related & earlier & valid_keys[None, :] | (place_keys[None, :] == place_query[:, None])

def rotation(depth_pos, width):
    half = width // 2
    freqs = jnp.exp(jnp.arange(half, dtype=jnp.float32) * (-2.0 * math.log(THETA) / width))
    angle = depth_pos.astype(jnp.float32)[:, None] * freqs[None, :]
    cosine = jnp.concatenate([jnp.cos(angle), jnp.cos(angle)], axis=1)
    sine = jnp.concatenate([jnp.sin(angle), jnp.sin(angle)], axis=1)
    return (cosine, sine)

def turn(heads, cosine, sine):
    half = heads.shape[-1] // 2
    swapped = jnp.concatenate([-heads[..., half:], heads[..., :half]], axis=-1)
    return heads * cosine[:, None, :] + swapped * sine[:, None, :]

def rms_unit(values):
    return values * lax.rsqrt(lax.optimization_barrier(jnp.mean(values * values, axis=-1, keepdims=True)) + EPS)

def matmul(left, right):
    return jnp.dot(left, right, precision=lax.Precision.HIGHEST)

def attention(query, keys, values, segment, tables):
    valid, upper_one, upper_two, depth_pos = tables
    block = math.gcd(SLOT, 512)
    group = HEADS // KV_HEADS
    scale = 1.0 / math.sqrt(HEAD)
    places = jnp.arange(SLOT, dtype=jnp.int32)

    def one_block(index):
        start = (index * block).astype(jnp.int32)

        def take_rows(array):
            return lax.dynamic_slice_in_dim(array, start, block, 0)
        mask = allowed(take_rows(segment), take_rows(upper_one), take_rows(upper_two), take_rows(places), segment, valid, places)
        block_query = take_rows(query)
        pieces = []
        for head_group in range(KV_HEADS):
            group_query = block_query[:, head_group * group:(head_group + 1) * group, :]
            scores = jnp.einsum('rhd,kd->hrk', group_query, keys[:, head_group, :], precision=lax.Precision.HIGHEST) * scale
            scores = low_back(scores)
            scores = jnp.where(mask[None], scores, NEGATIVE)
            probs = low(jax.nn.softmax(scores, axis=-1))
            pieces.append(jnp.einsum('hrk,kd->rhd', probs, values[:, head_group, :], precision=lax.Precision.HIGHEST))
        return jnp.concatenate(pieces, axis=1).reshape(block, HEADS * HEAD)
    blocks = lax.map(jax.checkpoint(one_block), jnp.arange(SLOT // block, dtype=jnp.int32))
    return blocks.reshape(SLOT, HEADS * HEAD)

def layer(params, inputs, segment, tables):
    w_qkv, qkv_bias, w_out, gain_attn, gain_ffn, w_gate, w_up, w_down = params
    depth_pos = tables[3]
    qwidth = HEADS * HEAD
    kwidth = KV_HEADS * HEAD
    normed_one = low(rms_unit(inputs) * gain_attn)
    linear = low_back(matmul(normed_one, w_qkv) + qkv_bias)
    cosine, sine = rotation(depth_pos, HEAD)
    query = low(turn(linear[:, :qwidth].reshape(SLOT, HEADS, HEAD), cosine, sine))
    keys = low(turn(linear[:, qwidth:qwidth + kwidth].reshape(SLOT, KV_HEADS, HEAD), cosine, sine))
    values = low(linear[:, qwidth + kwidth:].reshape(SLOT, KV_HEADS, HEAD))
    heads_out = low(low_back(attention(query, keys, values, segment, tables)))
    resid = inputs + low_back(matmul(heads_out, w_out))
    normed_two = low(rms_unit(resid) * gain_ffn)
    gate = low_back(matmul(normed_two, w_gate))
    upward = low_back(matmul(normed_two, w_up))
    hidden = low(jax.nn.silu(gate) * upward)
    return resid + low_back(matmul(hidden, w_down))

def reference(tokens, cotangent, segment, parent, w_qkv, qkv_bias, w_out, gain_attn, gain_ffn, w_gate, w_up, w_down):
    params = tuple((weight.astype(jnp.float32) for weight in (w_qkv, qkv_bias, w_out, gain_attn, gain_ffn, w_gate, w_up, w_down)))

    def one_tree(totals, item):
        tree_tokens, tree_grad, tree_segment, tree_parent = item
        tables = tree_tables(tree_segment, tree_parent)

        def forward(weights, inputs):
            return layer(weights, inputs, tree_segment, tables)
        result, pullback = jax.vjp(forward, params, tree_tokens.astype(jnp.float32))
        weight_grads, input_grad = pullback(tree_grad.astype(jnp.float32))
        totals = tuple((total + grad for total, grad in zip(totals, weight_grads)))
        return (totals, (result.astype(jnp.bfloat16), input_grad.astype(jnp.bfloat16)))
    zeros = tuple((jnp.zeros_like(weight) for weight in params))
    totals, (layer_out, grad_tokens) = lax.scan(one_tree, zeros, (tokens, cotangent, segment, parent))
    return (layer_out, grad_tokens, totals[0], totals[1], totals[2], totals[3], totals[4], totals[5], totals[6], totals[7])
```

```python
from functools import reduce
import math

import jax
import jax.numpy as jnp
from jax import lax
from jax.experimental import pallas as pl
from jax.experimental.pallas import tpu as pltpu
from jax.sharding import PartitionSpec as P

HEADS = 12
KV_HEADS = 2
HEAD = 128

QUERY_TILE = 128
KEY_TILE = 256
ROW_TILE = 128
FFN_CHUNK = 768
FFN_PARTS = 2
WG_TILE = 384
LOG2E = 1.0 / math.log(2.0)


EPS = 1e-06
THETA = 1000000.0
NEGATIVE = -1e30


def tree_tables(segment, parent):
    slot_len = segment.shape[0]
    seg_count = parent.shape[0]
    places = jnp.arange(slot_len, dtype=jnp.int32)
    labels = jnp.arange(seg_count, dtype=jnp.int32)
    member = segment[:, None] == labels[None, :]
    valid = segment >= 0
    first = jnp.min(jnp.where(member, places[:, None], slot_len), axis=0)
    length = jnp.sum(member.astype(jnp.int32), axis=0)
    parent_hit = parent[:, None] == labels[None, :]
    grand = jnp.sum(jnp.where(parent_hit, parent[None, :], 0), axis=1)
    grand_hit = grand[:, None] == labels[None, :]
    parent_len = jnp.sum(jnp.where(parent_hit, length[None, :], 0), axis=1)
    grand_len = jnp.sum(jnp.where(grand_hit, length[None, :], 0), axis=1)
    base = jnp.where(parent != labels, parent_len, 0) + jnp.where(grand != parent, grand_len, 0)

    def lookup(table):
        return jnp.sum(jnp.where(member, table[None, :], 0), axis=1)

    upper_one = jnp.where(valid, lookup(parent), -2)
    upper_two = jnp.where(valid, lookup(grand), -2)
    depth_pos = jnp.where(valid, places - lookup(first) + lookup(base), 0)
    return (valid, upper_one, upper_two, depth_pos)


def allowed(seg_query, upper_one, upper_two, place_query, seg_keys, valid_keys, place_keys):
    related = (seg_keys[None, :] == seg_query[:, None]) | (seg_keys[None, :] == upper_one[:, None])
    related = related | (seg_keys[None, :] == upper_two[:, None])
    earlier = place_keys[None, :] <= place_query[:, None]
    return related & earlier & valid_keys[None, :] | (place_keys[None, :] == place_query[:, None])


def rotation(depth_pos, width):
    half = width // 2
    freqs = jnp.exp(jnp.arange(half, dtype=jnp.float32) * (-2.0 * math.log(THETA) / width))
    angle = depth_pos.astype(jnp.float32)[:, None] * freqs[None, :]
    cosine = jnp.concatenate([jnp.cos(angle), jnp.cos(angle)], axis=1)
    sine = jnp.concatenate([jnp.sin(angle), jnp.sin(angle)], axis=1)
    return (cosine, sine)


def turn(heads, cosine, sine):
    half = heads.shape[-1] // 2
    swapped = jnp.concatenate([-heads[..., half:], heads[..., :half]], axis=-1)
    return heads * cosine[:, None, :] + swapped * sine[:, None, :]


def norm_parts(values, gain):
    inverse = lax.rsqrt(jnp.mean(values * values, axis=-1, keepdims=True) + EPS)
    unit = values * inverse
    return (unit, inverse, (unit * gain).astype(jnp.bfloat16))


def norm_back(grad_normed, unit, inverse, gain):
    scaled = grad_normed * gain
    back = inverse * (scaled - unit * jnp.mean(scaled * unit, axis=-1, keepdims=True))
    return (back, jnp.sum(grad_normed * unit, axis=0))


def masked_scores(group_query, group_keys, mask, scale):
    scores = (
        jnp.einsum("rhd,kd->hrk", group_query, group_keys, preferred_element_type=jnp.float32)
        * scale
    )
    return jnp.where(mask[None], scores, NEGATIVE)


def attend(query_low, keys_all, values_all, mask, scale):
    group = HEADS // KV_HEADS
    pieces = []
    totals = []
    for head_group in range(KV_HEADS):
        group_query = query_low[:, head_group * group : (head_group + 1) * group, :]
        columns = slice(head_group * HEAD, (head_group + 1) * HEAD)
        scores = masked_scores(group_query, keys_all[:, columns], mask, scale)
        top_score = jnp.max(scores, axis=-1, keepdims=True)
        expo = jnp.exp(scores - top_score)
        denom = jnp.sum(expo, axis=-1, keepdims=True)
        probs_low = (expo / denom).astype(jnp.bfloat16)
        pieces.append(
            jnp.einsum(
                "hrk,kd->rhd", probs_low, values_all[:, columns], preferred_element_type=jnp.float32
            )
        )
        totals.append(top_score + jnp.log(denom))
    return (jnp.concatenate(pieces, axis=1), totals)


def attend_back(query_low, keys_all, values_all, mask, totals, grad_heads, scale):
    group = HEADS // KV_HEADS
    grad_query, grad_keys, grad_values = ([], [], [])
    for head_group in range(KV_HEADS):
        heads_sel = slice(head_group * group, (head_group + 1) * group)
        columns = slice(head_group * HEAD, (head_group + 1) * HEAD)
        group_query = query_low[:, heads_sel, :]
        group_keys = keys_all[:, columns]
        group_grad = grad_heads[:, heads_sel, :]
        scores = masked_scores(group_query, group_keys, mask, scale)
        probs = jnp.exp(scores - totals[head_group])
        probs_low = probs.astype(jnp.bfloat16)
        grad_values.append(
            jnp.einsum("hrk,rhd->kd", probs_low, group_grad, preferred_element_type=jnp.float32)
        )
        grad_probs = jnp.einsum(
            "rhd,kd->hrk", group_grad, values_all[:, columns], preferred_element_type=jnp.float32
        )
        grad_scores = (
            probs * (grad_probs - jnp.sum(probs * grad_probs, axis=-1, keepdims=True))
        ).astype(jnp.bfloat16)
        grad_query.append(
            jnp.einsum("hrk,kd->rhd", grad_scores, group_keys, preferred_element_type=jnp.float32)
            * scale
        )
        grad_keys.append(
            jnp.einsum("hrk,rhd->kd", grad_scores, group_query, preferred_element_type=jnp.float32)
            * scale
        )
    return (
        jnp.concatenate(grad_query, axis=1),
        jnp.concatenate(grad_keys, axis=1),
        jnp.concatenate(grad_values, axis=1),
    )


def add_trees(left, right):
    return jax.tree.map(jnp.add, left, right)


def on_device(
    tokens,
    cotangent,
    segment,
    parent,
    w_qkv,
    qkv_bias,
    w_out,
    gain_attn,
    gain_ffn,
    w_gate,
    w_up,
    w_down,
):
    micro = tokens.shape[0]
    row_count = tokens.shape[1]
    slot_len = segment.shape[1]
    qwidth = HEADS * HEAD
    kwidth = KV_HEADS * HEAD
    scale = 1.0 / math.sqrt(HEAD)
    offset = lax.axis_index("gy") * row_count
    place_all = jnp.arange(slot_len, dtype=jnp.int32)
    place_own = offset + jnp.arange(row_count, dtype=jnp.int32)
    outputs, input_grads, attn_list, ffn_list = ([], [], [], [])
    for micro_index in range(micro):
        attn_full = (
            lax.all_gather(w_qkv, ("gx", "gy"), axis=0, tiled=True),
            lax.all_gather(qkv_bias, ("gx", "gy"), axis=0, tiled=True),
            lax.all_gather(w_out, ("gx", "gy"), axis=1, tiled=True),
            lax.all_gather(gain_attn, ("gx", "gy"), axis=0, tiled=True),
            lax.all_gather(gain_ffn, ("gx", "gy"), axis=0, tiled=True),
        )
        ffn_full = (
            lax.all_gather(w_gate, "gx", axis=0, tiled=True),
            lax.all_gather(w_up, "gx", axis=0, tiled=True),
            lax.all_gather(w_down, "gx", axis=1, tiled=True),
        )
        qkv_full, bias_full, out_full, gain_one_full, gain_two_full = attn_full
        gate_full, up_full, down_full = ffn_full
        gain_one = gain_one_full.astype(jnp.float32)
        gain_two = gain_two_full.astype(jnp.float32)
        seg_tree = segment[micro_index]
        valid, upper_one, upper_two, depth_pos = tree_tables(seg_tree, parent[micro_index])

        def take_own(array):
            return lax.dynamic_slice_in_dim(array, offset, row_count, 0)

        mask = allowed(
            take_own(seg_tree),
            take_own(upper_one),
            take_own(upper_two),
            place_own,
            seg_tree,
            valid,
            place_all,
        )
        cosine, sine = rotation(take_own(depth_pos), HEAD)
        inputs = tokens[micro_index].astype(jnp.float32)
        unit_one, inverse_one, normed_one = norm_parts(inputs, gain_one)
        linear = jnp.dot(
            normed_one, qkv_full, preferred_element_type=jnp.float32
        ) + bias_full.astype(jnp.float32)
        query_low = turn(linear[:, :qwidth].reshape(row_count, HEADS, HEAD), cosine, sine).astype(
            jnp.bfloat16
        )
        keys_low = turn(
            linear[:, qwidth : qwidth + kwidth].reshape(row_count, KV_HEADS, HEAD), cosine, sine
        )
        keys_low = keys_low.reshape(row_count, kwidth).astype(jnp.bfloat16)
        values_low = linear[:, qwidth + kwidth :].astype(jnp.bfloat16)
        keys_all, values_all = (
            lax.all_gather(keys_low, "gy", axis=0, tiled=True),
            lax.all_gather(values_low, "gy", axis=0, tiled=True),
        )
        heads_raw, totals = attend(query_low, keys_all, values_all, mask, scale)
        heads_out = heads_raw.reshape(row_count, qwidth).astype(jnp.bfloat16)
        resid = inputs + jnp.dot(heads_out, out_full, preferred_element_type=jnp.float32)
        unit_two, inverse_two, normed_two = norm_parts(resid, gain_two)
        normed_all = lax.all_gather(normed_two, "gy", axis=0, tiled=True)
        gate = jnp.dot(normed_all, gate_full, preferred_element_type=jnp.float32)
        upward = jnp.dot(normed_all, up_full, preferred_element_type=jnp.float32)
        sigma = jax.nn.sigmoid(gate)
        swish = gate * sigma
        hidden = (swish * upward).astype(jnp.bfloat16)
        ffn_own = lax.psum_scatter(
            jnp.dot(hidden, down_full, preferred_element_type=jnp.float32),
            "gy",
            scatter_dimension=0,
            tiled=True,
        )
        outputs.append((resid + ffn_own).astype(jnp.bfloat16))
        grad_low = cotangent[micro_index]
        grad_all = lax.all_gather(grad_low, "gy", axis=0, tiled=True)
        grad_hidden = jnp.dot(grad_all, down_full.T, preferred_element_type=jnp.float32)
        grad_down = jnp.dot(hidden.T, grad_all, preferred_element_type=jnp.float32)
        grad_gate = (grad_hidden * upward * sigma * (1.0 + gate * (1.0 - sigma))).astype(
            jnp.bfloat16
        )
        grad_up = (grad_hidden * swish).astype(jnp.bfloat16)
        grad_wgate = jnp.dot(normed_all.T, grad_gate, preferred_element_type=jnp.float32)
        grad_wup = jnp.dot(normed_all.T, grad_up, preferred_element_type=jnp.float32)
        grad_normed_two = lax.psum_scatter(
            jnp.dot(grad_gate, gate_full.T, preferred_element_type=jnp.float32)
            + jnp.dot(grad_up, up_full.T, preferred_element_type=jnp.float32),
            "gy",
            scatter_dimension=0,
            tiled=True,
        )
        back_two, grad_gain_two = norm_back(grad_normed_two, unit_two, inverse_two, gain_two)
        grad_resid = grad_low.astype(jnp.float32) + back_two
        grad_branch = grad_resid.astype(jnp.bfloat16)
        grad_wout = jnp.dot(heads_out.T, grad_branch, preferred_element_type=jnp.float32)
        grad_heads = jnp.dot(grad_branch, out_full.T, preferred_element_type=jnp.float32).astype(
            jnp.bfloat16
        )
        grad_heads = grad_heads.reshape(row_count, HEADS, HEAD)
        grad_query, keys_part, values_part = attend_back(
            query_low, keys_all, values_all, mask, totals, grad_heads, scale
        )
        grad_keys, grad_values = (
            lax.psum_scatter(keys_part, "gy", scatter_dimension=0, tiled=True),
            lax.psum_scatter(values_part, "gy", scatter_dimension=0, tiled=True),
        )
        query_lin = turn(grad_query, cosine, -sine).reshape(row_count, qwidth)
        keys_lin = turn(grad_keys.reshape(row_count, KV_HEADS, HEAD), cosine, -sine).reshape(
            row_count, kwidth
        )
        grad_linear = jnp.concatenate([query_lin, keys_lin, grad_values], axis=1).astype(
            jnp.bfloat16
        )
        grad_wqkv = jnp.dot(normed_one.T, grad_linear, preferred_element_type=jnp.float32)
        grad_bias = jnp.sum(grad_linear.astype(jnp.float32), axis=0)
        grad_normed_one = jnp.dot(grad_linear, qkv_full.T, preferred_element_type=jnp.float32)
        back_one, grad_gain_one = norm_back(grad_normed_one, unit_one, inverse_one, gain_one)
        input_grads.append((grad_resid + back_one).astype(jnp.bfloat16))
        attn_list.append((grad_wqkv, grad_bias, grad_wout, grad_gain_one, grad_gain_two))
        ffn_list.append((grad_wgate, grad_wup, grad_down))
    attn_total = reduce(add_trees, attn_list)
    ffn_total = reduce(add_trees, ffn_list)
    attn_total = (
        lax.psum_scatter(attn_total[0], ("gx", "gy"), scatter_dimension=0, tiled=True),
        lax.psum_scatter(attn_total[1], ("gx", "gy"), scatter_dimension=0, tiled=True),
        lax.psum_scatter(attn_total[2], ("gx", "gy"), scatter_dimension=1, tiled=True),
        lax.psum_scatter(attn_total[3], ("gx", "gy"), scatter_dimension=0, tiled=True),
        lax.psum_scatter(attn_total[4], ("gx", "gy"), scatter_dimension=0, tiled=True),
    )
    ffn_total = (
        lax.psum_scatter(ffn_total[0], "gx", scatter_dimension=0, tiled=True),
        lax.psum_scatter(ffn_total[1], "gx", scatter_dimension=0, tiled=True),
        lax.psum_scatter(ffn_total[2], "gx", scatter_dimension=1, tiled=True),
    )
    layer_out = jnp.stack(outputs, axis=0)
    grad_tokens = jnp.stack(input_grads, axis=0)
    return (
        layer_out,
        grad_tokens,
        attn_total[0],
        attn_total[1],
        attn_total[2],
        attn_total[3],
        attn_total[4],
        ffn_total[0],
        ffn_total[1],
        ffn_total[2],
    )


def dot_nn(left, right):
    return lax.dot_general(left, right, (((1,), (0,)), ((), ())), preferred_element_type=jnp.float32)


def dot_nt(left, right):
    return lax.dot_general(left, right, (((1,), (1,)), ((), ())), preferred_element_type=jnp.float32)


def dot_tn(left, right):
    return lax.dot_general(left, right, (((0,), (0,)), ((), ())), preferred_element_type=jnp.float32)


def cost(flops, moved, trans=0):
    return pl.CostEstimate(flops=int(flops), bytes_accessed=int(moved), transcendentals=int(trans))


def params(mib):
    return pltpu.CompilerParams(vmem_limit_bytes=mib * 1024 * 1024)


def sigmoid(v):
    return 0.5 * jnp.tanh(0.5 * v) + 0.5


def ffn_body(n_ref, c_ref, wg_ref, wu_ref, wd_ref, hid_ref, dg_ref, du_ref, f_ref, dn_ref, f_acc, dn_acc):
    step = pl.program_id(0)

    @pl.when(step == 0)
    def _():
        f_acc[...] = jnp.zeros_like(f_acc)
        dn_acc[...] = jnp.zeros_like(dn_acc)

    rows = n_ref.shape[0]
    part = rows // FFN_PARTS
    for index in range(FFN_PARTS):
        take = pl.ds(index * part, part)
        gate = dot_nn(n_ref[take, :], wg_ref[...])
        upward = dot_nn(n_ref[take, :], wu_ref[...])
        sigma = sigmoid(gate)
        swish = gate * sigma
        hidden = (swish * upward).astype(jnp.bfloat16)
        hid_ref[take, :] = hidden
        grad_hidden = dot_nt(c_ref[take, :], wd_ref[...])
        grad_gate = (grad_hidden * upward * sigma * (1.0 + gate * (1.0 - sigma))).astype(jnp.bfloat16)
        grad_up = (grad_hidden * swish).astype(jnp.bfloat16)
        dg_ref[take, :] = grad_gate
        du_ref[take, :] = grad_up
        f_acc[take, :] += dot_nn(hidden, wd_ref[...])
        dn_acc[take, :] += dot_nt(grad_gate, wg_ref[...]) + dot_nt(grad_up, wu_ref[...])

    @pl.when(step == pl.num_programs(0) - 1)
    def _():
        f_ref[...] = f_acc[...].astype(f_ref.dtype)
        dn_ref[...] = dn_acc[...].astype(dn_ref.dtype)


def ffn_block(normed, cotan, w_gate, w_up, w_down):
    rows, width = normed.shape
    units = w_gate.shape[1]
    chunk = FFN_CHUNK
    steps = units // chunk
    whole = pl.BlockSpec((rows, width), lambda j: (0, 0))
    tall = pl.BlockSpec((rows, chunk), lambda j: (0, j))
    low = jnp.bfloat16
    return pl.pallas_call(
        ffn_body,
        grid=(steps,),
        in_specs=[
            whole,
            whole,
            pl.BlockSpec((width, chunk), lambda j: (0, j)),
            pl.BlockSpec((width, chunk), lambda j: (0, j)),
            pl.BlockSpec((chunk, width), lambda j: (j, 0)),
        ],
        out_specs=[tall, tall, tall, whole, whole],
        out_shape=[jax.ShapeDtypeStruct((rows, units), low)] * 3
        + [jax.ShapeDtypeStruct((rows, width), low)] * 2,
        scratch_shapes=[pltpu.VMEM((rows, width), jnp.float32)] * 2,
        compiler_params=params(60),
        cost_estimate=cost(12 * rows * width * units, 6 * width * units + 6 * rows * (width + units)),
        name="ffn_block",
    )(normed, cotan, w_gate, w_up, w_down)


def wgrad_body(*refs):
    count = (len(refs) - 1) // 2
    out_ref = refs[-1]
    slots, wide = out_ref.shape[1], out_ref.shape[3]
    total = dot_tn(refs[0][...], refs[count][...])
    for index in range(1, count):
        total = total + dot_tn(refs[index][...], refs[count + index][...])
    for slot in range(slots):
        out_ref[0, slot] = total[:, slot * wide : (slot + 1) * wide].astype(out_ref.dtype)


def wgrad(lefts, rights, slots):
    rows, units = lefts[0].shape
    width = rights[0].shape[1]
    tile = WG_TILE
    per_half = units // 2 // tile
    wide = width // slots
    count = len(lefts)
    return pl.pallas_call(
        wgrad_body,
        grid=(units // tile,),
        in_specs=[pl.BlockSpec((rows, tile), lambda j: (0, j))] * count
        + [pl.BlockSpec((rows, width), lambda j: (0, 0))] * count,
        out_specs=pl.BlockSpec((1, slots, tile, wide), lambda j: (j // per_half, 0, j % per_half, 0)),
        out_shape=jax.ShapeDtypeStruct((2, slots, units // 2, wide), jnp.bfloat16),
        compiler_params=params(60),
        cost_estimate=cost(2 * count * rows * width * units, 2 * count * rows * (width + units)),
        name="ffn_wgrad",
    )(*lefts, *rights)


def group_rows(source_ref, group, per_group):
    return jnp.concatenate(
        [source_ref[:, (group * per_group + h) * HEAD : (group * per_group + h + 1) * HEAD] for h in range(per_group)],
        axis=0,
    )


def attend_body(list_ref, count_ref, q_ref, kv_ref, bias_ref, o_ref, lse_ref, qs, acc, top, den):
    block = pl.program_id(0)
    per_group = HEADS // KV_HEADS
    for group in range(KV_HEADS):
        qs[group] = group_rows(q_ref, group, per_group)
    acc[...] = jnp.zeros_like(acc)
    den[...] = jnp.zeros_like(den)
    top[...] = jnp.full_like(top, 2 * NEGATIVE)
    factor = LOG2E / math.sqrt(HEAD)

    def body(n, carry):
        rows = pl.ds(pl.multiple_of(list_ref[block, n] * KEY_TILE, KEY_TILE), KEY_TILE)
        bias = jnp.concatenate([bias_ref[rows, :].astype(jnp.float32)] * per_group, axis=1)
        for group in range(KV_HEADS):
            keys = kv_ref[rows, group * HEAD : (group + 1) * HEAD]
            values = kv_ref[rows, (KV_HEADS + group) * HEAD : (KV_HEADS + group + 1) * HEAD]
            scores = dot_nt(keys, qs[group]) * factor + bias
            old = top[group]
            new = jnp.maximum(old, jnp.max(scores, axis=0, keepdims=True))
            probs = jnp.exp2(scores - new)
            shrink = jnp.exp2(old - new)
            den[group] = den[group] * shrink + jnp.sum(probs, axis=0, keepdims=True)
            acc[group] = acc[group] * shrink + dot_tn(values, probs.astype(jnp.bfloat16))
            top[group] = new
        return carry

    lax.fori_loop(0, count_ref[block], body, 0)
    for group in range(KV_HEADS):
        out = acc[group] / den[group]
        lse_ref[0, group] = top[group] + jnp.log(den[group]) * LOG2E
        for h in range(per_group):
            head = group * per_group + h
            o_ref[:, head * HEAD : (head + 1) * HEAD] = out[:, h * HEAD : (h + 1) * HEAD].T.astype(o_ref.dtype)


def attend_fast(block_list, block_count, query, keyval, bias):
    rows, qwidth = query.shape
    slots = keyval.shape[0]
    blocks = rows // QUERY_TILE
    per_group = HEADS // KV_HEADS
    lanes = per_group * QUERY_TILE
    whole = pl.BlockSpec(keyval.shape, lambda i, a, b: (0, 0))
    tile = pl.BlockSpec((QUERY_TILE, qwidth), lambda i, a, b: (i, 0))
    return pl.pallas_call(
        attend_body,
        grid_spec=pltpu.PrefetchScalarGridSpec(
            num_scalar_prefetch=2,
            grid=(blocks,),
            in_specs=[tile, whole, pl.BlockSpec((slots, QUERY_TILE), lambda i, a, b: (0, i))],
            out_specs=[tile, pl.BlockSpec((1, KV_HEADS, 1, lanes), lambda i, a, b: (i, 0, 0, 0))],
            scratch_shapes=[
                pltpu.VMEM((KV_HEADS, lanes, HEAD), jnp.bfloat16),
                pltpu.VMEM((KV_HEADS, HEAD, lanes), jnp.float32),
                pltpu.VMEM((KV_HEADS, 1, lanes), jnp.float32),
                pltpu.VMEM((KV_HEADS, 1, lanes), jnp.float32),
            ],
        ),
        out_shape=[
            jax.ShapeDtypeStruct((rows, qwidth), jnp.bfloat16),
            jax.ShapeDtypeStruct((blocks, KV_HEADS, 1, lanes), jnp.float32),
        ],
        compiler_params=params(48),
        cost_estimate=cost(2 * rows * slots * qwidth * 2, 4 * slots * rows, HEADS * rows * slots // 2),
        name="tree_attention",
    )(block_list, block_count, query, keyval, bias)


def attend_back_body(
    list_ref, count_ref, q_ref, kv_ref, bias_ref, lse_ref, o_ref, do_ref, cos_ref, sin_ref,
    dq_ref, dkv_ref, qs, dos, delta, dqt, dkv,
):
    block = pl.program_id(0)
    per_group = HEADS // KV_HEADS
    scale = 1.0 / math.sqrt(HEAD)
    factor = LOG2E * scale
    lanes = qs.shape[1]

    @pl.when(block == 0)
    def _():
        dkv[...] = jnp.zeros_like(dkv)

    for group in range(KV_HEADS):
        qs[group] = group_rows(q_ref, group, per_group)
        grads = group_rows(do_ref, group, per_group)
        dos[group] = grads
        both = grads.astype(jnp.float32) * group_rows(o_ref, group, per_group).astype(jnp.float32)
        delta[group] = lax.dot_general(
            jnp.ones((8, HEAD), jnp.float32), both, (((1,), (1,)), ((), ())),
            precision=lax.Precision.HIGHEST, preferred_element_type=jnp.float32,
        )[0:1]
    dqt[...] = jnp.zeros_like(dqt)

    def body(n, carry):
        rows = pl.ds(pl.multiple_of(list_ref[block, n] * KEY_TILE, KEY_TILE), KEY_TILE)
        bias = jnp.concatenate([bias_ref[rows, :].astype(jnp.float32)] * per_group, axis=1)
        for group in range(KV_HEADS):
            kcols = slice(group * HEAD, (group + 1) * HEAD)
            vcols = slice((KV_HEADS + group) * HEAD, (KV_HEADS + group + 1) * HEAD)
            keys = kv_ref[rows, kcols]
            values = kv_ref[rows, vcols]
            scores = dot_nt(keys, qs[group]) * factor + bias
            probs = jnp.exp2(scores - lse_ref[0, group])
            grad_probs = dot_nt(values, dos[group])
            grad_scores = (probs * (grad_probs - delta[group])).astype(jnp.bfloat16)
            dkv[rows, vcols] += dot_nn(probs.astype(jnp.bfloat16), dos[group])
            dkv[rows, kcols] += dot_nn(grad_scores, qs[group])
            dqt[group] += dot_tn(keys, grad_scores)
        return carry

    lax.fori_loop(0, count_ref[block], body, 0)
    cosine, sine = cos_ref[...], sin_ref[...]
    for group in range(KV_HEADS):
        for h in range(per_group):
            head = group * per_group + h
            grad = dqt[group, :, h * HEAD : (h + 1) * HEAD].T * scale
            grad = grad * cosine - pltpu.roll(grad, HEAD // 2, 1) * sine
            dq_ref[:, head * HEAD : (head + 1) * HEAD] = grad.astype(dq_ref.dtype)

    @pl.when(block == pl.num_programs(0) - 1)
    def _():
        kwidth = KV_HEADS * HEAD
        dkv_ref[:, :kwidth] = (dkv[:, :kwidth] * scale).astype(dkv_ref.dtype)
        dkv_ref[:, kwidth:] = dkv[:, kwidth:].astype(dkv_ref.dtype)


def attend_back_fast(block_list, block_count, query, keyval, bias, lse, heads_out, grad_heads, cosine, sine):
    rows, qwidth = query.shape
    slots = keyval.shape[0]
    blocks = rows // QUERY_TILE
    per_group = HEADS // KV_HEADS
    lanes = per_group * QUERY_TILE
    whole = pl.BlockSpec(keyval.shape, lambda i, a, b: (0, 0))
    tile = pl.BlockSpec((QUERY_TILE, qwidth), lambda i, a, b: (i, 0))
    turned = pl.BlockSpec((QUERY_TILE, HEAD), lambda i, a, b: (i, 0))
    return pl.pallas_call(
        attend_back_body,
        grid_spec=pltpu.PrefetchScalarGridSpec(
            num_scalar_prefetch=2,
            grid=(blocks,),
            in_specs=[
                tile,
                whole,
                pl.BlockSpec((slots, QUERY_TILE), lambda i, a, b: (0, i)),
                pl.BlockSpec((1, KV_HEADS, 1, lanes), lambda i, a, b: (i, 0, 0, 0)),
                tile,
                tile,
                turned,
                turned,
            ],
            out_specs=[tile, whole],
            scratch_shapes=[
                pltpu.VMEM((KV_HEADS, lanes, HEAD), jnp.bfloat16),
                pltpu.VMEM((KV_HEADS, lanes, HEAD), jnp.bfloat16),
                pltpu.VMEM((KV_HEADS, 1, lanes), jnp.float32),
                pltpu.VMEM((KV_HEADS, HEAD, lanes), jnp.float32),
                pltpu.VMEM(keyval.shape, jnp.float32),
            ],
        ),
        out_shape=[
            jax.ShapeDtypeStruct((rows, qwidth), jnp.bfloat16),
            jax.ShapeDtypeStruct(keyval.shape, jnp.bfloat16),
        ],
        compiler_params=params(56),
        cost_estimate=cost(5 * rows * slots * qwidth * 2, 8 * slots * rows, HEADS * rows * slots // 2),
        name="tree_attention_back",
    )(block_list, block_count, query, keyval, bias, lse, heads_out, grad_heads, cosine, sine)


def project_body(x_ref, gain_ref, w_ref, b_ref, cos_ref, sin_ref, n_ref, q_ref, kv_ref):
    values = x_ref[...].astype(jnp.float32)
    inverse = lax.rsqrt(jnp.mean(values * values, axis=-1, keepdims=True) + EPS)
    normed = (values * inverse * gain_ref[...]).astype(jnp.bfloat16)
    n_ref[...] = normed
    linear = dot_nn(normed, w_ref[...]) + b_ref[...]
    cosine, sine = cos_ref[...], sin_ref[...]
    for head in range(HEADS + KV_HEADS):
        lane = linear[:, head * HEAD : (head + 1) * HEAD]
        lane = (lane * cosine + pltpu.roll(lane, HEAD // 2, 1) * sine).astype(jnp.bfloat16)
        if head < HEADS:
            q_ref[:, head * HEAD : (head + 1) * HEAD] = lane
        else:
            kv_ref[:, (head - HEADS) * HEAD : (head - HEADS + 1) * HEAD] = lane
    kv_ref[:, KV_HEADS * HEAD :] = linear[:, (HEADS + KV_HEADS) * HEAD :].astype(jnp.bfloat16)


def project(inputs, gain, w_qkv, bias, cosine, sine):
    rows, width = inputs.shape
    qwidth, kwidth = HEADS * HEAD, 2 * KV_HEADS * HEAD
    tile = ROW_TILE
    fixed = lambda i: (0, 0)
    moving = lambda i: (i, 0)
    return pl.pallas_call(
        project_body,
        grid=(rows // tile,),
        in_specs=[
            pl.BlockSpec((tile, width), moving),
            pl.BlockSpec((1, width), fixed),
            pl.BlockSpec(w_qkv.shape, fixed),
            pl.BlockSpec((1, qwidth + kwidth), fixed),
            pl.BlockSpec((tile, HEAD), moving),
            pl.BlockSpec((tile, HEAD), moving),
        ],
        out_specs=[
            pl.BlockSpec((tile, width), moving),
            pl.BlockSpec((tile, qwidth), moving),
            pl.BlockSpec((tile, kwidth), moving),
        ],
        out_shape=[
            jax.ShapeDtypeStruct((rows, width), jnp.bfloat16),
            jax.ShapeDtypeStruct((rows, qwidth), jnp.bfloat16),
            jax.ShapeDtypeStruct((rows, kwidth), jnp.bfloat16),
        ],
        compiler_params=params(48),
        cost_estimate=cost(2 * rows * width * (qwidth + kwidth), 2 * width * (qwidth + kwidth) + 8 * rows * width),
        name="project",
    )(inputs, gain, w_qkv, bias, cosine, sine)


CORE, ALONG_X, ALONG_Y, ACROSS = 1, 2, 4, 6
OTHERS = (ALONG_X, ALONG_Y, ACROSS)


def swap(array, bits):
    return lax.ppermute(array, "gy", [(i, i ^ bits) for i in range(8)])


def ring(array):
    return lax.ppermute(array, "gx", [(i, (i + 1) % 4) for i in range(4)])


def pick(array, index):
    return lax.dynamic_index_in_dim(array, index, 0, keepdims=False)


def after(array, *earlier):
    return lax.optimization_barrier((array, *earlier))[0]


def slot_columns(array, plane):
    wide = array.shape[-1] // 4
    return jnp.concatenate(
        [lax.dynamic_slice_in_dim(array, lax.rem(plane + 4 - s, 4) * wide, wide, array.ndim - 1) for s in range(4)],
        axis=array.ndim - 1,
    )


def pair_rows(pair, core):
    kept, got = pick(pair, core), swap(pick(pair, 1 - core), CORE)
    return jnp.where(core == 0, jnp.concatenate([kept, got]), jnp.concatenate([got, kept]))


def unpair_rows(rows, core):
    half = rows.shape[0] // 2
    kept = lax.dynamic_slice_in_dim(rows, core * half, half, 0)
    got = swap(lax.dynamic_slice_in_dim(rows, (1 - core) * half, half, 0), CORE)
    return jnp.where(core == 0, jnp.stack([kept, got]), jnp.stack([got, kept]))


def ring_slots(own):
    slots = [own]
    for _ in range(3):
        slots.append(ring(slots[-1]))
    return slots


def ring_sums(slots):
    moving = ring(slots[1])
    for s in (2, 3):
        moving = ring((slots[s].astype(jnp.float32) + moving.astype(jnp.float32)).astype(jnp.bfloat16))
    return slots[0].astype(jnp.float32) + moving.astype(jnp.float32)


def plane_order(blocks, chip):
    rows = blocks[0].shape[0]
    whole = jnp.zeros((4 * rows,) + blocks[0].shape[1:], blocks[0].dtype)
    for index, block in enumerate(blocks):
        whole = lax.dynamic_update_slice_in_dim(whole, block, (chip ^ index) * rows, 0)
    return whole


def gather_small(row, plane, me):
    slots = ring_slots(row)
    rows = jnp.concatenate(slots)
    rows = jnp.concatenate([pick(rows, lax.rem(plane + 4 - s, 4))[None] for s in range(4)])[:, None]
    for level, bits in enumerate((CORE, ALONG_X, ALONG_Y)):
        other = swap(rows, bits)
        rows = jnp.where(
            (me >> level) % 2 == 0,
            jnp.concatenate([rows, other], axis=1),
            jnp.concatenate([other, rows], axis=1),
        )
    return rows.reshape(32, row.shape[1])


def sum_small(rows, plane, me):
    rows = rows.reshape(4, 8, rows.shape[1])
    for level, bits in ((2, ALONG_Y), (1, ALONG_X), (0, CORE)):
        half = rows.shape[1] // 2
        bit = (me >> level) % 2
        kept = lax.dynamic_slice_in_dim(rows, bit * half, half, 1)
        rows = kept + swap(lax.dynamic_slice_in_dim(rows, (1 - bit) * half, half, 1), bits)
    slots = [pick(rows, lax.rem(plane + 4 - s, 4)) for s in range(4)]
    moving = ring(slots[1])
    for s in (2, 3):
        moving = ring(slots[s] + moving)
    return (slots[0] + moving)[0]


def on_core(
    tokens,
    cotangent,
    segment,
    parent,
    w_qkv,
    qkv_bias,
    w_out,
    gain_attn,
    gain_ffn,
    w_gate,
    w_up,
    w_down,
):
    low, full = jnp.bfloat16, jnp.float32
    me = lax.axis_index("gy")
    plane = lax.axis_index("gx")
    core, chip = me % 2, me // 2
    rows, width = 2 * tokens.shape[1], tokens.shape[2]
    slot_len = segment.shape[1]
    own_units = w_gate.shape[1]
    pad_units = -(-own_units // 384) * 384
    qwidth, kwidth = HEADS * HEAD, KV_HEADS * HEAD
    offset = chip * rows

    nb, ng = qkv_bias.shape[0], gain_attn.shape[0]
    packed = jnp.zeros((1, 256), low)
    packed = packed.at[0, :nb].set(qkv_bias).at[0, nb : nb + ng].set(gain_attn)
    packed = packed.at[0, nb + ng : nb + 2 * ng].set(gain_ffn)
    small = gather_small(packed, plane, me).astype(full)
    bias_full = small[:, :nb].reshape(1, -1)
    gain_one = small[:, nb : nb + ng].reshape(1, -1)
    gain_two = small[:, nb + ng : nb + 2 * ng].reshape(1, -1)
    qkv_full = lax.all_gather(w_qkv, ("gx", "gy"), axis=0, tiled=True)
    out_full = lax.all_gather(after(w_out, qkv_full), ("gx", "gy"), axis=1, tiled=True)

    inputs_low = pair_rows(tokens, core)
    grad_low = pair_rows(cotangent, core)

    more = pad_units - own_units
    gate_slots = ring_slots(jnp.pad(w_gate, ((0, 0), (0, more))))
    up_slots = ring_slots(jnp.pad(w_up, ((0, 0), (0, more))))
    down_slots = ring_slots(jnp.pad(w_down, ((0, more), (0, 0))))

    def both_cores(slots, axis):
        mine = jnp.concatenate(slots, axis=axis)
        return jnp.concatenate([mine] + [jnp.concatenate([swap(s, CORE) for s in slots], axis=axis)], axis=1 - axis)

    gate_full, up_full = both_cores(gate_slots, 0), both_cores(up_slots, 0)
    down_full = both_cores(down_slots, 1)

    seg_tree = pick(segment, core)
    valid, upper_one, upper_two, depth_pos = tree_tables(seg_tree, pick(parent, core))
    places = jnp.arange(slot_len, dtype=jnp.int32)

    def take_own(array):
        return lax.dynamic_slice_in_dim(array, offset, rows, 0)

    mask = allowed(
        take_own(seg_tree), take_own(upper_one), take_own(upper_two), take_own(places), seg_tree, valid, places
    )
    qblocks, kblocks = rows // QUERY_TILE, slot_len // KEY_TILE
    active = mask.reshape(qblocks, QUERY_TILE, kblocks, KEY_TILE).any(axis=(1, 3))
    block_count = active.sum(axis=1).astype(jnp.int32)
    rank = jnp.cumsum(active.astype(jnp.int32), axis=1) - 1
    numbers = jnp.arange(kblocks, dtype=jnp.int32)
    hit = active[:, :, None] & (rank[:, :, None] == numbers[None, None, :])
    block_list = jnp.sum(jnp.where(hit, numbers[None, :, None], 0), axis=1).astype(jnp.int32)
    mask_bias = jnp.where(mask.T, 0.0, NEGATIVE).astype(low)
    cosine, sine = rotation(take_own(depth_pos), HEAD)
    sine = sine * jnp.where(jnp.arange(HEAD) < HEAD // 2, -1.0, 1.0)

    normed_one, query, keyval_own = project(inputs_low, gain_one, qkv_full, bias_full, cosine, sine)
    keyval = plane_order([keyval_own] + [swap(keyval_own, bits) for bits in OTHERS], chip)
    heads_out, lse = attend_fast(block_list, block_count, query, keyval, mask_bias)
    inputs = inputs_low.astype(full)
    resid = inputs + jnp.dot(heads_out, out_full, preferred_element_type=full)
    unit_two, inverse_two, normed_two = norm_parts(resid, gain_two)

    normed_slots = slot_columns(normed_two, plane)
    cotan_slots = slot_columns(grad_low, plane)
    normed_blocks = [normed_slots] + [swap(normed_slots, bits) for bits in OTHERS]
    cotan_blocks = [cotan_slots] + [swap(cotan_slots, bits) for bits in OTHERS]
    results = []
    for normed, cotan in zip(normed_blocks, cotan_blocks):
        if results:
            normed = after(normed, results[-1][4])
        results.append(ffn_block(normed, cotan, gate_full, up_full, down_full))
    hidden_b, gate_b, up_b, out_b, back_b = zip(*results)
    grad_normed = [back_b[0]] + [swap(b, bits) for b, bits in zip(back_b[1:], OTHERS)]
    ffn_out = [out_b[0]] + [swap(after(b, back_b[3]), bits) for b, bits in zip(out_b[1:], OTHERS)]
    ffn_grads = []
    for left, right in ((hidden_b, cotan_blocks), (gate_b, normed_blocks), (up_b, normed_blocks)):
        if ffn_grads:
            left = (after(left[0], parts),) + left[1:]
        else:
            left = (after(left[0], back_b[3]),) + left[1:]
        parts = wgrad(left, right, 4)
        mine = parts[0].astype(full) + swap(parts[1], CORE).astype(full)
        ffn_grads.append(ring_sums(mine.astype(low)))
    grad_down = ffn_grads[0][:own_units]
    grad_wgate = ffn_grads[1].T[:, :own_units]
    grad_wup = ffn_grads[2].T[:, :own_units]

    grad_normed_two = slot_columns(sum(b.astype(full) for b in grad_normed), plane)
    back_two, grad_gain_two = norm_back(grad_normed_two, unit_two, inverse_two, gain_two)
    grad_resid = grad_low.astype(full) + back_two
    grad_branch = grad_resid.astype(low)
    grad_heads = jnp.dot(grad_branch, out_full.T, preferred_element_type=full).astype(low)
    query_lin, keyval_part = attend_back_fast(
        block_list, block_count, query, keyval, mask_bias, lse, heads_out, grad_heads, cosine, sine
    )
    grad_wout = jnp.dot(heads_out.T, grad_branch, preferred_element_type=full).astype(low)
    grad_wout = lax.psum_scatter(grad_wout, ("gx", "gy"), scatter_dimension=1, tiled=True).astype(full)

    def part_of(index):
        return lax.dynamic_slice_in_dim(keyval_part, (chip ^ index) * rows, rows, 0)

    keyval_grad = part_of(0).astype(full) + sum(
        swap(part_of(index + 1), bits).astype(full) for index, bits in enumerate(OTHERS)
    )
    keys_grad = keyval_grad[:, :kwidth].reshape(rows, KV_HEADS, HEAD)
    keys_lin = keys_grad * cosine[:, None, :] - jnp.roll(keys_grad, HEAD // 2, axis=-1) * sine[:, None, :]
    keyval_lin = jnp.concatenate([keys_lin.reshape(rows, kwidth), keyval_grad[:, kwidth:]], axis=1).astype(low)
    grad_linear = jnp.concatenate([query_lin, keyval_lin], axis=1)
    grad_wqkv = jnp.dot(normed_one.T, grad_linear, preferred_element_type=full).astype(low)
    grad_wqkv = lax.psum_scatter(grad_wqkv, ("gx", "gy"), scatter_dimension=0, tiled=True).astype(full)
    grad_bias = jnp.sum(grad_linear.astype(full), axis=0)
    grad_normed_one = jnp.dot(grad_linear, qkv_full.T, preferred_element_type=full)
    unit_one, inverse_one, _ = norm_parts(inputs, gain_one)
    back_one, grad_gain_one = norm_back(grad_normed_one, unit_one, inverse_one, gain_one)
    grad_tokens = unpair_rows((grad_resid + back_one).astype(low), core)
    layer_out = unpair_rows((resid + slot_columns(sum(b.astype(full) for b in ffn_out), plane)).astype(low), core)

    packed = jnp.concatenate(
        [grad_bias.reshape(32, nb), grad_gain_one.reshape(32, ng), grad_gain_two.reshape(32, ng)], axis=1
    )
    small = sum_small(packed, plane, me)
    return (
        layer_out,
        grad_tokens,
        grad_wqkv,
        small[:nb],
        grad_wout,
        small[nb : nb + ng],
        small[nb + ng :],
        grad_wgate,
        grad_wup,
        grad_down,
    )


def solution(mesh):
    in_specs = (
        P("gx", "gy", None),
        P("gx", "gy", None),
        P("gx", None),
        P("gx", None),
        P(("gx", "gy"), None),
        P(("gx", "gy")),
        P(None, ("gx", "gy")),
        P(("gx", "gy")),
        P(("gx", "gy")),
        P("gx", "gy"),
        P("gx", "gy"),
        P("gy", "gx"),
    )
    out_specs = (
        P("gx", "gy", None),
        P("gx", "gy", None),
        P(("gx", "gy"), None),
        P(("gx", "gy")),
        P(None, ("gx", "gy")),
        P(("gx", "gy")),
        P(("gx", "gy")),
        P("gx", "gy"),
        P("gx", "gy"),
        P("gy", "gx"),
    )
    return jax.shard_map(
        on_core if tuple(mesh.shape.values()) == (4, 8) else on_device,
        mesh=mesh,
        in_specs=in_specs,
        out_specs=out_specs,
        check_vma=False,
    )
```

```python
from functools import reduce
import math

import jax
import jax.numpy as jnp
from jax import lax
from jax.experimental import pallas as pl
from jax.experimental.pallas import tpu as pltpu
from jax.sharding import PartitionSpec as P

HEADS = 12
KV_HEADS = 2
HEAD = 128

QUERY_TILE = 128
KEY_TILE = 256
ROW_TILE = 128
FFN_CHUNK = 768
FFN_PARTS = 2
WG_TILE = 384
PACE = 0.15
LOG2E = 1.0 / math.log(2.0)


EPS = 1e-06
THETA = 1000000.0
NEGATIVE = -1e30


def tree_tables(segment, parent):
    slot_len = segment.shape[0]
    seg_count = parent.shape[0]
    places = jnp.arange(slot_len, dtype=jnp.int32)
    labels = jnp.arange(seg_count, dtype=jnp.int32)
    member = segment[:, None] == labels[None, :]
    valid = segment >= 0
    first = jnp.min(jnp.where(member, places[:, None], slot_len), axis=0)
    length = jnp.sum(member.astype(jnp.int32), axis=0)
    parent_hit = parent[:, None] == labels[None, :]
    grand = jnp.sum(jnp.where(parent_hit, parent[None, :], 0), axis=1)
    grand_hit = grand[:, None] == labels[None, :]
    parent_len = jnp.sum(jnp.where(parent_hit, length[None, :], 0), axis=1)
    grand_len = jnp.sum(jnp.where(grand_hit, length[None, :], 0), axis=1)
    base = jnp.where(parent != labels, parent_len, 0) + jnp.where(grand != parent, grand_len, 0)

    def lookup(table):
        return jnp.sum(jnp.where(member, table[None, :], 0), axis=1)

    upper_one = jnp.where(valid, lookup(parent), -2)
    upper_two = jnp.where(valid, lookup(grand), -2)
    depth_pos = jnp.where(valid, places - lookup(first) + lookup(base), 0)
    return (valid, upper_one, upper_two, depth_pos)


def allowed(seg_query, upper_one, upper_two, place_query, seg_keys, valid_keys, place_keys):
    related = (seg_keys[None, :] == seg_query[:, None]) | (seg_keys[None, :] == upper_one[:, None])
    related = related | (seg_keys[None, :] == upper_two[:, None])
    earlier = place_keys[None, :] <= place_query[:, None]
    return related & earlier & valid_keys[None, :] | (place_keys[None, :] == place_query[:, None])


def rotation(depth_pos, width):
    half = width // 2
    freqs = jnp.exp(jnp.arange(half, dtype=jnp.float32) * (-2.0 * math.log(THETA) / width))
    angle = depth_pos.astype(jnp.float32)[:, None] * freqs[None, :]
    cosine = jnp.concatenate([jnp.cos(angle), jnp.cos(angle)], axis=1)
    sine = jnp.concatenate([jnp.sin(angle), jnp.sin(angle)], axis=1)
    return (cosine, sine)


def turn(heads, cosine, sine):
    half = heads.shape[-1] // 2
    swapped = jnp.concatenate([-heads[..., half:], heads[..., :half]], axis=-1)
    return heads * cosine[:, None, :] + swapped * sine[:, None, :]


def norm_parts(values, gain):
    inverse = lax.rsqrt(jnp.mean(values * values, axis=-1, keepdims=True) + EPS)
    unit = values * inverse
    return (unit, inverse, (unit * gain).astype(jnp.bfloat16))


def norm_back(grad_normed, unit, inverse, gain):
    scaled = grad_normed * gain
    back = inverse * (scaled - unit * jnp.mean(scaled * unit, axis=-1, keepdims=True))
    return (back, jnp.sum(grad_normed * unit, axis=0))


def masked_scores(group_query, group_keys, mask, scale):
    scores = (
        jnp.einsum("rhd,kd->hrk", group_query, group_keys, preferred_element_type=jnp.float32)
        * scale
    )
    return jnp.where(mask[None], scores, NEGATIVE)


def attend(query_low, keys_all, values_all, mask, scale):
    group = HEADS // KV_HEADS
    pieces = []
    totals = []
    for head_group in range(KV_HEADS):
        group_query = query_low[:, head_group * group : (head_group + 1) * group, :]
        columns = slice(head_group * HEAD, (head_group + 1) * HEAD)
        scores = masked_scores(group_query, keys_all[:, columns], mask, scale)
        top_score = jnp.max(scores, axis=-1, keepdims=True)
        expo = jnp.exp(scores - top_score)
        denom = jnp.sum(expo, axis=-1, keepdims=True)
        probs_low = (expo / denom).astype(jnp.bfloat16)
        pieces.append(
            jnp.einsum(
                "hrk,kd->rhd", probs_low, values_all[:, columns], preferred_element_type=jnp.float32
            )
        )
        totals.append(top_score + jnp.log(denom))
    return (jnp.concatenate(pieces, axis=1), totals)


def attend_back(query_low, keys_all, values_all, mask, totals, grad_heads, scale):
    group = HEADS // KV_HEADS
    grad_query, grad_keys, grad_values = ([], [], [])
    for head_group in range(KV_HEADS):
        heads_sel = slice(head_group * group, (head_group + 1) * group)
        columns = slice(head_group * HEAD, (head_group + 1) * HEAD)
        group_query = query_low[:, heads_sel, :]
        group_keys = keys_all[:, columns]
        group_grad = grad_heads[:, heads_sel, :]
        scores = masked_scores(group_query, group_keys, mask, scale)
        probs = jnp.exp(scores - totals[head_group])
        probs_low = probs.astype(jnp.bfloat16)
        grad_values.append(
            jnp.einsum("hrk,rhd->kd", probs_low, group_grad, preferred_element_type=jnp.float32)
        )
        grad_probs = jnp.einsum(
            "rhd,kd->hrk", group_grad, values_all[:, columns], preferred_element_type=jnp.float32
        )
        grad_scores = (
            probs * (grad_probs - jnp.sum(probs * grad_probs, axis=-1, keepdims=True))
        ).astype(jnp.bfloat16)
        grad_query.append(
            jnp.einsum("hrk,kd->rhd", grad_scores, group_keys, preferred_element_type=jnp.float32)
            * scale
        )
        grad_keys.append(
            jnp.einsum("hrk,rhd->kd", grad_scores, group_query, preferred_element_type=jnp.float32)
            * scale
        )
    return (
        jnp.concatenate(grad_query, axis=1),
        jnp.concatenate(grad_keys, axis=1),
        jnp.concatenate(grad_values, axis=1),
    )


def add_trees(left, right):
    return jax.tree.map(jnp.add, left, right)


def on_device(
    tokens,
    cotangent,
    segment,
    parent,
    w_qkv,
    qkv_bias,
    w_out,
    gain_attn,
    gain_ffn,
    w_gate,
    w_up,
    w_down,
):
    micro = tokens.shape[0]
    row_count = tokens.shape[1]
    slot_len = segment.shape[1]
    qwidth = HEADS * HEAD
    kwidth = KV_HEADS * HEAD
    scale = 1.0 / math.sqrt(HEAD)
    offset = lax.axis_index("gy") * row_count
    place_all = jnp.arange(slot_len, dtype=jnp.int32)
    place_own = offset + jnp.arange(row_count, dtype=jnp.int32)
    outputs, input_grads, attn_list, ffn_list = ([], [], [], [])
    for micro_index in range(micro):
        attn_full = (
            lax.all_gather(w_qkv, ("gx", "gy"), axis=0, tiled=True),
            lax.all_gather(qkv_bias, ("gx", "gy"), axis=0, tiled=True),
            lax.all_gather(w_out, ("gx", "gy"), axis=1, tiled=True),
            lax.all_gather(gain_attn, ("gx", "gy"), axis=0, tiled=True),
            lax.all_gather(gain_ffn, ("gx", "gy"), axis=0, tiled=True),
        )
        ffn_full = (
            lax.all_gather(w_gate, "gx", axis=0, tiled=True),
            lax.all_gather(w_up, "gx", axis=0, tiled=True),
            lax.all_gather(w_down, "gx", axis=1, tiled=True),
        )
        qkv_full, bias_full, out_full, gain_one_full, gain_two_full = attn_full
        gate_full, up_full, down_full = ffn_full
        gain_one = gain_one_full.astype(jnp.float32)
        gain_two = gain_two_full.astype(jnp.float32)
        seg_tree = segment[micro_index]
        valid, upper_one, upper_two, depth_pos = tree_tables(seg_tree, parent[micro_index])

        def take_own(array):
            return lax.dynamic_slice_in_dim(array, offset, row_count, 0)

        mask = allowed(
            take_own(seg_tree),
            take_own(upper_one),
            take_own(upper_two),
            place_own,
            seg_tree,
            valid,
            place_all,
        )
        cosine, sine = rotation(take_own(depth_pos), HEAD)
        inputs = tokens[micro_index].astype(jnp.float32)
        unit_one, inverse_one, normed_one = norm_parts(inputs, gain_one)
        linear = jnp.dot(
            normed_one, qkv_full, preferred_element_type=jnp.float32
        ) + bias_full.astype(jnp.float32)
        query_low = turn(linear[:, :qwidth].reshape(row_count, HEADS, HEAD), cosine, sine).astype(
            jnp.bfloat16
        )
        keys_low = turn(
            linear[:, qwidth : qwidth + kwidth].reshape(row_count, KV_HEADS, HEAD), cosine, sine
        )
        keys_low = keys_low.reshape(row_count, kwidth).astype(jnp.bfloat16)
        values_low = linear[:, qwidth + kwidth :].astype(jnp.bfloat16)
        keys_all, values_all = (
            lax.all_gather(keys_low, "gy", axis=0, tiled=True),
            lax.all_gather(values_low, "gy", axis=0, tiled=True),
        )
        heads_raw, totals = attend(query_low, keys_all, values_all, mask, scale)
        heads_out = heads_raw.reshape(row_count, qwidth).astype(jnp.bfloat16)
        resid = inputs + jnp.dot(heads_out, out_full, preferred_element_type=jnp.float32)
        unit_two, inverse_two, normed_two = norm_parts(resid, gain_two)
        normed_all = lax.all_gather(normed_two, "gy", axis=0, tiled=True)
        gate = jnp.dot(normed_all, gate_full, preferred_element_type=jnp.float32)
        upward = jnp.dot(normed_all, up_full, preferred_element_type=jnp.float32)
        sigma = jax.nn.sigmoid(gate)
        swish = gate * sigma
        hidden = (swish * upward).astype(jnp.bfloat16)
        ffn_own = lax.psum_scatter(
            jnp.dot(hidden, down_full, preferred_element_type=jnp.float32),
            "gy",
            scatter_dimension=0,
            tiled=True,
        )
        outputs.append((resid + ffn_own).astype(jnp.bfloat16))
        grad_low = cotangent[micro_index]
        grad_all = lax.all_gather(grad_low, "gy", axis=0, tiled=True)
        grad_hidden = jnp.dot(grad_all, down_full.T, preferred_element_type=jnp.float32)
        grad_down = jnp.dot(hidden.T, grad_all, preferred_element_type=jnp.float32)
        grad_gate = (grad_hidden * upward * sigma * (1.0 + gate * (1.0 - sigma))).astype(
            jnp.bfloat16
        )
        grad_up = (grad_hidden * swish).astype(jnp.bfloat16)
        grad_wgate = jnp.dot(normed_all.T, grad_gate, preferred_element_type=jnp.float32)
        grad_wup = jnp.dot(normed_all.T, grad_up, preferred_element_type=jnp.float32)
        grad_normed_two = lax.psum_scatter(
            jnp.dot(grad_gate, gate_full.T, preferred_element_type=jnp.float32)
            + jnp.dot(grad_up, up_full.T, preferred_element_type=jnp.float32),
            "gy",
            scatter_dimension=0,
            tiled=True,
        )
        back_two, grad_gain_two = norm_back(grad_normed_two, unit_two, inverse_two, gain_two)
        grad_resid = grad_low.astype(jnp.float32) + back_two
        grad_branch = grad_resid.astype(jnp.bfloat16)
        grad_wout = jnp.dot(heads_out.T, grad_branch, preferred_element_type=jnp.float32)
        grad_heads = jnp.dot(grad_branch, out_full.T, preferred_element_type=jnp.float32).astype(
            jnp.bfloat16
        )
        grad_heads = grad_heads.reshape(row_count, HEADS, HEAD)
        grad_query, keys_part, values_part = attend_back(
            query_low, keys_all, values_all, mask, totals, grad_heads, scale
        )
        grad_keys, grad_values = (
            lax.psum_scatter(keys_part, "gy", scatter_dimension=0, tiled=True),
            lax.psum_scatter(values_part, "gy", scatter_dimension=0, tiled=True),
        )
        query_lin = turn(grad_query, cosine, -sine).reshape(row_count, qwidth)
        keys_lin = turn(grad_keys.reshape(row_count, KV_HEADS, HEAD), cosine, -sine).reshape(
            row_count, kwidth
        )
        grad_linear = jnp.concatenate([query_lin, keys_lin, grad_values], axis=1).astype(
            jnp.bfloat16
        )
        grad_wqkv = jnp.dot(normed_one.T, grad_linear, preferred_element_type=jnp.float32)
        grad_bias = jnp.sum(grad_linear.astype(jnp.float32), axis=0)
        grad_normed_one = jnp.dot(grad_linear, qkv_full.T, preferred_element_type=jnp.float32)
        back_one, grad_gain_one = norm_back(grad_normed_one, unit_one, inverse_one, gain_one)
        input_grads.append((grad_resid + back_one).astype(jnp.bfloat16))
        attn_list.append((grad_wqkv, grad_bias, grad_wout, grad_gain_one, grad_gain_two))
        ffn_list.append((grad_wgate, grad_wup, grad_down))
    attn_total = reduce(add_trees, attn_list)
    ffn_total = reduce(add_trees, ffn_list)
    attn_total = (
        lax.psum_scatter(attn_total[0], ("gx", "gy"), scatter_dimension=0, tiled=True),
        lax.psum_scatter(attn_total[1], ("gx", "gy"), scatter_dimension=0, tiled=True),
        lax.psum_scatter(attn_total[2], ("gx", "gy"), scatter_dimension=1, tiled=True),
        lax.psum_scatter(attn_total[3], ("gx", "gy"), scatter_dimension=0, tiled=True),
        lax.psum_scatter(attn_total[4], ("gx", "gy"), scatter_dimension=0, tiled=True),
    )
    ffn_total = (
        lax.psum_scatter(ffn_total[0], "gx", scatter_dimension=0, tiled=True),
        lax.psum_scatter(ffn_total[1], "gx", scatter_dimension=0, tiled=True),
        lax.psum_scatter(ffn_total[2], "gx", scatter_dimension=1, tiled=True),
    )
    layer_out = jnp.stack(outputs, axis=0)
    grad_tokens = jnp.stack(input_grads, axis=0)
    return (
        layer_out,
        grad_tokens,
        attn_total[0],
        attn_total[1],
        attn_total[2],
        attn_total[3],
        attn_total[4],
        ffn_total[0],
        ffn_total[1],
        ffn_total[2],
    )


def dot_nn(left, right):
    return lax.dot_general(left, right, (((1,), (0,)), ((), ())), preferred_element_type=jnp.float32)


def dot_nt(left, right):
    return lax.dot_general(left, right, (((1,), (1,)), ((), ())), preferred_element_type=jnp.float32)


def dot_tn(left, right):
    return lax.dot_general(left, right, (((0,), (0,)), ((), ())), preferred_element_type=jnp.float32)


def cost(flops, moved, trans=0):
    return pl.CostEstimate(flops=int(flops * PACE), bytes_accessed=int(moved * PACE), transcendentals=int(trans * PACE))


def params(mib):
    return pltpu.CompilerParams(vmem_limit_bytes=mib * 1024 * 1024)


def sigmoid(v):
    return 0.5 * jnp.tanh(0.5 * v) + 0.5


def ffn_copies(chunk, pieces, held, sems):
    units = pieces[0].shape[1]
    tile = FFN_CHUNK // 2
    slot = chunk % 2
    copies = []
    for part in range(2):
        column = chunk * FFN_CHUNK + part * tile
        owner, inside = column // units, column % units
        for kind in range(3):
            copies.append(
                pltpu.make_async_copy(
                    pieces[3 * owner + kind].at[:, pl.ds(inside, tile)],
                    held.at[slot, kind, :, pl.ds(part * tile, tile)],
                    sems.at[slot, part * 3 + kind],
                )
            )
    return copies


def ffn_body(n_ref, c_ref, *refs):
    pieces = refs[:6]
    hid_ref, dg_ref, du_ref, f_ref, dn_ref, f_acc, dn_acc, held, sems = refs[6:]
    step = pl.program_id(0)
    chunks = 2 * pieces[0].shape[1] // FFN_CHUNK

    @pl.when(step == 0)
    def _():
        for copy in ffn_copies(0, pieces, held, sems):
            copy.start()
        f_acc[...] = jnp.zeros_like(f_acc)
        dn_acc[...] = jnp.zeros_like(dn_acc)

    for chunk in range(chunks):

        @pl.when(step == chunk)
        def _():
            if chunk + 1 < chunks:
                for copy in ffn_copies(chunk + 1, pieces, held, sems):
                    copy.start()
            for copy in ffn_copies(chunk, pieces, held, sems):
                copy.wait()

    slot = step % 2
    rows = n_ref.shape[0]
    part = rows // FFN_PARTS
    for index in range(FFN_PARTS):
        take = pl.ds(index * part, part)
        gate = dot_nn(n_ref[take, :], held[slot, 0])
        upward = dot_nn(n_ref[take, :], held[slot, 1])
        sigma = sigmoid(gate)
        swish = gate * sigma
        hidden = (swish * upward).astype(jnp.bfloat16)
        hid_ref[take, :] = hidden
        grad_hidden = dot_nn(c_ref[take, :], held[slot, 2])
        grad_gate = (grad_hidden * upward * sigma * (1.0 + gate * (1.0 - sigma))).astype(jnp.bfloat16)
        grad_up = (grad_hidden * swish).astype(jnp.bfloat16)
        dg_ref[take, :] = grad_gate
        du_ref[take, :] = grad_up
        f_acc[take, :] += dot_nt(hidden, held[slot, 2])
        dn_acc[take, :] += dot_nt(grad_gate, held[slot, 0]) + dot_nt(grad_up, held[slot, 1])

    @pl.when(step == pl.num_programs(0) - 1)
    def _():
        f_ref[...] = f_acc[...].astype(f_ref.dtype)
        dn_ref[...] = dn_acc[...].astype(dn_ref.dtype)


def ffn_block(normed, cotan, pieces):
    rows, width = normed.shape
    units = 2 * pieces[0].shape[1]
    chunk = FFN_CHUNK
    whole = pl.BlockSpec((rows, width), lambda j: (0, 0))
    tall = pl.BlockSpec((rows, chunk), lambda j: (0, j))
    low = jnp.bfloat16
    return pl.pallas_call(
        ffn_body,
        grid=(units // chunk,),
        in_specs=[whole, whole] + [pl.BlockSpec(memory_space=pl.ANY)] * len(pieces),
        out_specs=[tall, tall, tall, whole, whole],
        out_shape=[jax.ShapeDtypeStruct((rows, units), low)] * 3
        + [jax.ShapeDtypeStruct((rows, width), low)] * 2,
        scratch_shapes=[pltpu.VMEM((rows, width), jnp.float32)] * 2
        + [pltpu.VMEM((2, 3, width, chunk), low), pltpu.SemaphoreType.DMA((2, len(pieces)))],
        compiler_params=params(60),
        cost_estimate=cost(12 * rows * width * units, 6 * width * units + 6 * rows * (width + units)),
        name="ffn_block",
    )(normed, cotan, *pieces)


def wgrad_body(per_half, *refs):
    count = (len(refs) - 2) // 2
    total = dot_tn(refs[0][...], refs[count][...])
    for index in range(1, count):
        total = total + dot_tn(refs[index][...], refs[count + index][...])

    def store(out_ref):
        slots, _, wide = out_ref.shape
        for slot in range(slots):
            out_ref[slot] = total[:, slot * wide : (slot + 1) * wide].astype(out_ref.dtype)

    first = pl.program_id(0) < per_half
    pl.when(first)(lambda: store(refs[-2]))
    pl.when(jnp.logical_not(first))(lambda: store(refs[-1]))


def wgrad(lefts, rights, slots):
    rows, units = lefts[0].shape
    width = rights[0].shape[1]
    tile = WG_TILE
    per_half = units // 2 // tile
    wide = width // slots
    count = len(lefts)
    return pl.pallas_call(
        lambda *refs: wgrad_body(per_half, *refs),
        grid=(units // tile,),
        in_specs=[pl.BlockSpec((rows, tile), lambda j: (0, j))] * count
        + [pl.BlockSpec((rows, width), lambda j: (0, 0))] * count,
        out_specs=[
            pl.BlockSpec((slots, tile, wide), lambda j: (0, jnp.minimum(j, per_half - 1), 0)),
            pl.BlockSpec((slots, tile, wide), lambda j: (0, jnp.maximum(j - per_half, 0), 0)),
        ],
        out_shape=[jax.ShapeDtypeStruct((slots, units // 2, wide), jnp.bfloat16)] * 2,
        compiler_params=params(60),
        cost_estimate=cost(2 * count * rows * width * units, 2 * count * rows * (width + units)),
        name="ffn_wgrad",
    )(*lefts, *rights)


def group_rows(source_ref, group, per_group):
    return jnp.concatenate(
        [source_ref[:, (group * per_group + h) * HEAD : (group * per_group + h + 1) * HEAD] for h in range(per_group)],
        axis=0,
    )


def attend_body(list_ref, count_ref, q_ref, kv_ref, bias_ref, o_ref, lse_ref, qs, acc, top, den):
    block = pl.program_id(0)
    per_group = HEADS // KV_HEADS
    for group in range(KV_HEADS):
        qs[group] = group_rows(q_ref, group, per_group)
    acc[...] = jnp.zeros_like(acc)
    den[...] = jnp.zeros_like(den)
    top[...] = jnp.full_like(top, 2 * NEGATIVE)
    factor = LOG2E / math.sqrt(HEAD)

    def body(n, carry):
        rows = pl.ds(pl.multiple_of(list_ref[block, n] * KEY_TILE, KEY_TILE), KEY_TILE)
        bias = jnp.concatenate([bias_ref[rows, :].astype(jnp.float32)] * per_group, axis=1)
        for group in range(KV_HEADS):
            keys = kv_ref[rows, group * HEAD : (group + 1) * HEAD]
            values = kv_ref[rows, (KV_HEADS + group) * HEAD : (KV_HEADS + group + 1) * HEAD]
            scores = dot_nt(keys, qs[group]) * factor + bias
            old = top[group]
            new = jnp.maximum(old, jnp.max(scores, axis=0, keepdims=True))
            probs = jnp.exp2(scores - new)
            shrink = jnp.exp2(old - new)
            den[group] = den[group] * shrink + jnp.sum(probs, axis=0, keepdims=True)
            acc[group] = acc[group] * shrink + dot_tn(values, probs.astype(jnp.bfloat16))
            top[group] = new
        return carry

    lax.fori_loop(0, count_ref[block], body, 0)
    for group in range(KV_HEADS):
        out = acc[group] / den[group]
        lse_ref[0, group] = top[group] + jnp.log(den[group]) * LOG2E
        for h in range(per_group):
            head = group * per_group + h
            o_ref[:, head * HEAD : (head + 1) * HEAD] = out[:, h * HEAD : (h + 1) * HEAD].T.astype(o_ref.dtype)


def attend_fast(block_list, block_count, query, keyval, bias):
    rows, qwidth = query.shape
    slots = keyval.shape[0]
    blocks = rows // QUERY_TILE
    per_group = HEADS // KV_HEADS
    lanes = per_group * QUERY_TILE
    whole = pl.BlockSpec(keyval.shape, lambda i, a, b: (0, 0))
    tile = pl.BlockSpec((QUERY_TILE, qwidth), lambda i, a, b: (i, 0))
    return pl.pallas_call(
        attend_body,
        grid_spec=pltpu.PrefetchScalarGridSpec(
            num_scalar_prefetch=2,
            grid=(blocks,),
            in_specs=[tile, whole, pl.BlockSpec((slots, QUERY_TILE), lambda i, a, b: (0, i))],
            out_specs=[tile, pl.BlockSpec((1, KV_HEADS, 1, lanes), lambda i, a, b: (i, 0, 0, 0))],
            scratch_shapes=[
                pltpu.VMEM((KV_HEADS, lanes, HEAD), jnp.bfloat16),
                pltpu.VMEM((KV_HEADS, HEAD, lanes), jnp.float32),
                pltpu.VMEM((KV_HEADS, 1, lanes), jnp.float32),
                pltpu.VMEM((KV_HEADS, 1, lanes), jnp.float32),
            ],
        ),
        out_shape=[
            jax.ShapeDtypeStruct((rows, qwidth), jnp.bfloat16),
            jax.ShapeDtypeStruct((blocks, KV_HEADS, 1, lanes), jnp.float32),
        ],
        compiler_params=params(48),
        cost_estimate=cost(2 * rows * slots * qwidth * 2, 4 * slots * rows, HEADS * rows * slots // 2),
        name="tree_attention",
    )(block_list, block_count, query, keyval, bias)


def attend_back_body(
    list_ref, count_ref, q_ref, kv_ref, bias_ref, lse_ref, o_ref, do_ref, cos_ref, sin_ref,
    dq_ref, dkv_ref, qs, dos, delta, dqt, dkv,
):
    block = pl.program_id(0)
    per_group = HEADS // KV_HEADS
    scale = 1.0 / math.sqrt(HEAD)
    factor = LOG2E * scale
    lanes = qs.shape[1]

    @pl.when(block == 0)
    def _():
        dkv[...] = jnp.zeros_like(dkv)

    for group in range(KV_HEADS):
        qs[group] = group_rows(q_ref, group, per_group)
        grads = group_rows(do_ref, group, per_group)
        dos[group] = grads
        both = grads.astype(jnp.float32) * group_rows(o_ref, group, per_group).astype(jnp.float32)
        delta[group] = lax.dot_general(
            jnp.ones((8, HEAD), jnp.float32), both, (((1,), (1,)), ((), ())),
            precision=lax.Precision.HIGHEST, preferred_element_type=jnp.float32,
        )[0:1]
    dqt[...] = jnp.zeros_like(dqt)

    def body(n, carry):
        rows = pl.ds(pl.multiple_of(list_ref[block, n] * KEY_TILE, KEY_TILE), KEY_TILE)
        bias = jnp.concatenate([bias_ref[rows, :].astype(jnp.float32)] * per_group, axis=1)
        for group in range(KV_HEADS):
            kcols = slice(group * HEAD, (group + 1) * HEAD)
            vcols = slice((KV_HEADS + group) * HEAD, (KV_HEADS + group + 1) * HEAD)
            keys = kv_ref[rows, kcols]
            values = kv_ref[rows, vcols]
            scores = dot_nt(keys, qs[group]) * factor + bias
            probs = jnp.exp2(scores - lse_ref[0, group])
            grad_probs = dot_nt(values, dos[group])
            grad_scores = (probs * (grad_probs - delta[group])).astype(jnp.bfloat16)
            dkv[rows, vcols] += dot_nn(probs.astype(jnp.bfloat16), dos[group])
            dkv[rows, kcols] += dot_nn(grad_scores, qs[group])
            dqt[group] += dot_tn(keys, grad_scores)
        return carry

    lax.fori_loop(0, count_ref[block], body, 0)
    cosine, sine = cos_ref[...], sin_ref[...]
    for group in range(KV_HEADS):
        for h in range(per_group):
            head = group * per_group + h
            grad = dqt[group, :, h * HEAD : (h + 1) * HEAD].T * scale
            grad = grad * cosine - pltpu.roll(grad, HEAD // 2, 1) * sine
            dq_ref[:, head * HEAD : (head + 1) * HEAD] = grad.astype(dq_ref.dtype)

    @pl.when(block == pl.num_programs(0) - 1)
    def _():
        kwidth = KV_HEADS * HEAD
        dkv_ref[:, :kwidth] = (dkv[:, :kwidth] * scale).astype(dkv_ref.dtype)
        dkv_ref[:, kwidth:] = dkv[:, kwidth:].astype(dkv_ref.dtype)


def attend_back_fast(block_list, block_count, query, keyval, bias, lse, heads_out, grad_heads, cosine, sine):
    rows, qwidth = query.shape
    slots = keyval.shape[0]
    blocks = rows // QUERY_TILE
    per_group = HEADS // KV_HEADS
    lanes = per_group * QUERY_TILE
    whole = pl.BlockSpec(keyval.shape, lambda i, a, b: (0, 0))
    tile = pl.BlockSpec((QUERY_TILE, qwidth), lambda i, a, b: (i, 0))
    turned = pl.BlockSpec((QUERY_TILE, HEAD), lambda i, a, b: (i, 0))
    return pl.pallas_call(
        attend_back_body,
        grid_spec=pltpu.PrefetchScalarGridSpec(
            num_scalar_prefetch=2,
            grid=(blocks,),
            in_specs=[
                tile,
                whole,
                pl.BlockSpec((slots, QUERY_TILE), lambda i, a, b: (0, i)),
                pl.BlockSpec((1, KV_HEADS, 1, lanes), lambda i, a, b: (i, 0, 0, 0)),
                tile,
                tile,
                turned,
                turned,
            ],
            out_specs=[tile, whole],
            scratch_shapes=[
                pltpu.VMEM((KV_HEADS, lanes, HEAD), jnp.bfloat16),
                pltpu.VMEM((KV_HEADS, lanes, HEAD), jnp.bfloat16),
                pltpu.VMEM((KV_HEADS, 1, lanes), jnp.float32),
                pltpu.VMEM((KV_HEADS, HEAD, lanes), jnp.float32),
                pltpu.VMEM(keyval.shape, jnp.float32),
            ],
        ),
        out_shape=[
            jax.ShapeDtypeStruct((rows, qwidth), jnp.bfloat16),
            jax.ShapeDtypeStruct(keyval.shape, jnp.bfloat16),
        ],
        compiler_params=params(56),
        cost_estimate=cost(5 * rows * slots * qwidth * 2, 8 * slots * rows, HEADS * rows * slots // 2),
        name="tree_attention_back",
    )(block_list, block_count, query, keyval, bias, lse, heads_out, grad_heads, cosine, sine)


def project_body(x_ref, gain_ref, w_ref, b_ref, cos_ref, sin_ref, n_ref, q_ref, kv_ref):
    values = x_ref[...].astype(jnp.float32)
    inverse = lax.rsqrt(jnp.mean(values * values, axis=-1, keepdims=True) + EPS)
    normed = (values * inverse * gain_ref[...]).astype(jnp.bfloat16)
    n_ref[...] = normed
    linear = dot_nn(normed, w_ref[...]) + b_ref[...]
    cosine, sine = cos_ref[...], sin_ref[...]
    for head in range(HEADS + KV_HEADS):
        lane = linear[:, head * HEAD : (head + 1) * HEAD]
        lane = (lane * cosine + pltpu.roll(lane, HEAD // 2, 1) * sine).astype(jnp.bfloat16)
        if head < HEADS:
            q_ref[:, head * HEAD : (head + 1) * HEAD] = lane
        else:
            kv_ref[:, (head - HEADS) * HEAD : (head - HEADS + 1) * HEAD] = lane
    kv_ref[:, KV_HEADS * HEAD :] = linear[:, (HEADS + KV_HEADS) * HEAD :].astype(jnp.bfloat16)


def project(inputs, gain, w_qkv, bias, cosine, sine):
    rows, width = inputs.shape
    qwidth, kwidth = HEADS * HEAD, 2 * KV_HEADS * HEAD
    tile = ROW_TILE
    fixed = lambda i: (0, 0)
    moving = lambda i: (i, 0)
    return pl.pallas_call(
        project_body,
        grid=(rows // tile,),
        in_specs=[
            pl.BlockSpec((tile, width), moving),
            pl.BlockSpec((1, width), fixed),
            pl.BlockSpec((width, qwidth + kwidth), fixed),
            pl.BlockSpec((1, qwidth + kwidth), fixed),
            pl.BlockSpec((tile, HEAD), moving),
            pl.BlockSpec((tile, HEAD), moving),
        ],
        out_specs=[
            pl.BlockSpec((tile, width), moving),
            pl.BlockSpec((tile, qwidth), moving),
            pl.BlockSpec((tile, kwidth), moving),
        ],
        out_shape=[
            jax.ShapeDtypeStruct((rows, width), jnp.bfloat16),
            jax.ShapeDtypeStruct((rows, qwidth), jnp.bfloat16),
            jax.ShapeDtypeStruct((rows, kwidth), jnp.bfloat16),
        ],
        compiler_params=params(48),
        cost_estimate=cost(2 * rows * width * (qwidth + kwidth), 2 * width * (qwidth + kwidth) + 8 * rows * width),
        name="project",
    )(inputs, gain, w_qkv, bias, cosine, sine)


def spread_body(own, rows, whole, rows_x, rows_y, rows_d, sent, landed, kept):
    me, plane = lax.axis_index("gy"), lax.axis_index("gx")
    core = me + 1 - 2 * lax.rem(me, 2)
    along_x = me + 2 - 4 * lax.rem(me // 2, 2)
    along_y = me + 4 - 8 * (me // 4)
    across = along_x + 4 - 8 * (along_x // 4)
    places = [lax.rem(plane + 4 - k, 4) for k in range(4)]
    ahead = [lax.rem(plane + k, 4) for k in range(4)]
    barrier = pltpu.get_barrier_semaphore()
    peers = [{"gy": core}, {"gy": along_x}, {"gy": along_y}] + [{"gx": ahead[k]} for k in (1, 2, 3)]
    for peer in peers:
        pl.semaphore_signal(barrier, inc=1, device_id=peer, device_id_type=pl.DeviceIdType.MESH)
    pl.semaphore_wait(barrier, len(peers))
    copies = []

    def send(source, target, peer):
        copy = pltpu.make_async_remote_copy(
            source,
            target,
            sent.at[len(copies)],
            landed.at[len(copies)],
            device_id=peer,
            device_id_type=pl.DeviceIdType.MESH,
        )
        copies.append(copy)
        copy.start()
        return copy

    to_core, to_x, to_y = peers[:3]
    from_z = [send(own, whole.at[plane, me], peers[2 + k]) for k in (1, 2, 3)]
    local = pltpu.make_async_copy(own, whole.at[plane, me], kept)
    local.start()
    from_x, from_y, from_d, from_core = [], [], [], []
    for k in range(4):
        block = whole.at[places[k], me]
        source = own if k == 0 else block
        if k > 0:
            from_z[k - 1].wait_recv()
        from_x.append(send(source, block, to_x))
        from_y.append(send(source, block, to_y))
        from_core.append(send(source, block, to_core))
    moved_x, moved_y = send(rows, rows_x, to_x), send(rows, rows_y, to_y)
    for k in range(4):
        block_x, block_y = whole.at[places[k], along_x], whole.at[places[k], along_y]
        from_x[k].wait_recv()
        if k < 2:
            from_d.append(send(block_x, block_x, to_y))
        from_core.append(send(block_x, block_x, to_core))
        from_y[k].wait_recv()
        if k >= 2:
            from_d.append(send(block_y, block_y, to_x))
        from_core.append(send(block_y, block_y, to_core))
    for k in range(4):
        block = whole.at[places[k], across]
        from_d[k].wait_recv()
        from_core.append(send(block, block, to_core))
    half = rows.shape[0] // 2
    first, second = pl.ds(0, half), pl.ds(half, half)
    moved_x.wait_recv()
    moved_d = [send(rows_x.at[first], rows_d.at[first], to_y)]
    moved_y.wait_recv()
    moved_d.append(send(rows_y.at[second], rows_d.at[second], to_x))
    for copy in from_core + moved_d:
        copy.wait_recv()
    for copy in copies:
        copy.wait_send()
    local.wait()


def spread(own, rows):
    deep, wide = own.shape
    anywhere = pl.BlockSpec(memory_space=pl.ANY)
    whole, *others = pl.pallas_call(
        spread_body,
        in_specs=[anywhere] * 2,
        out_specs=[anywhere] * 4,
        out_shape=[jax.ShapeDtypeStruct((4, 8, deep, wide), own.dtype)]
        + [jax.ShapeDtypeStruct(rows.shape, rows.dtype)] * 3,
        scratch_shapes=[
            pltpu.SemaphoreType.DMA((35,)),
            pltpu.SemaphoreType.DMA((35,)),
            pltpu.SemaphoreType.DMA,
        ],
        compiler_params=pltpu.CompilerParams(collective_id=0, has_side_effects=True),
        cost_estimate=cost(0, 300 * 1024 * 1024),
        name="spread",
    )(own, rows)
    return whole.reshape(32 * deep, wide), others


CORE, ALONG_X, ALONG_Y, ACROSS = 1, 2, 4, 6
OTHERS = (ALONG_X, ALONG_Y, ACROSS)


def swap(array, bits):
    return lax.ppermute(array, "gy", [(i, i ^ bits) for i in range(8)])


def ring(array):
    return lax.ppermute(array, "gx", [(i, (i + 1) % 4) for i in range(4)])


def pick(array, index):
    return lax.dynamic_index_in_dim(array, index, 0, keepdims=False)


def after(array, *earlier):
    return lax.optimization_barrier((array, *earlier))[0]


def pair_rows(pair, core):
    kept, got = pick(pair, core), swap(pick(pair, 1 - core), CORE)
    return jnp.where(core == 0, jnp.concatenate([kept, got]), jnp.concatenate([got, kept]))


def unpair_rows(rows, core):
    half = rows.shape[0] // 2
    kept = lax.dynamic_slice_in_dim(rows, core * half, half, 0)
    got = swap(lax.dynamic_slice_in_dim(rows, (1 - core) * half, half, 0), CORE)
    return jnp.where(core == 0, jnp.stack([kept, got]), jnp.stack([got, kept]))


def ring_sums(slots):
    moving = ring(slots[1])
    for s in (2, 3):
        moving = ring((slots[s].astype(jnp.float32) + moving.astype(jnp.float32)).astype(jnp.bfloat16))
    return slots[0].astype(jnp.float32) + moving.astype(jnp.float32)


def plane_order(blocks, chip):
    rows = blocks[0].shape[0]
    whole = jnp.zeros((4 * rows,) + blocks[0].shape[1:], blocks[0].dtype)
    for index, block in enumerate(blocks):
        whole = lax.dynamic_update_slice_in_dim(whole, block, (chip ^ index) * rows, 0)
    return whole


def sum_rows(rows, plane, me, order):
    width = rows.shape[1]
    rows = rows.reshape(4, 2, 2, 2, rows.shape[0] // 32, width)
    axis = {ALONG_Y: 1, ALONG_X: 2, CORE: 3}
    for bits in order:
        bit = (me // bits) % 2
        kept = lax.dynamic_slice_in_dim(rows, bit, 1, axis[bits])
        sent = lax.dynamic_slice_in_dim(rows, 1 - bit, 1, axis[bits])
        rows = (kept.astype(jnp.float32) + swap(sent, bits).astype(jnp.float32)).astype(rows.dtype)
    rows = rows.reshape(4, -1, width)
    return ring_sums([pick(rows, lax.rem(plane + 4 - s, 4)) for s in range(4)])


def sum_small(rows, plane, me):
    rows = rows.reshape(4, 8, rows.shape[1])
    for level, bits in ((2, ALONG_Y), (1, ALONG_X), (0, CORE)):
        half = rows.shape[1] // 2
        bit = (me >> level) % 2
        kept = lax.dynamic_slice_in_dim(rows, bit * half, half, 1)
        rows = kept + swap(lax.dynamic_slice_in_dim(rows, (1 - bit) * half, half, 1), bits)
    slots = [pick(rows, lax.rem(plane + 4 - s, 4)) for s in range(4)]
    moving = ring(slots[1])
    for s in (2, 3):
        moving = ring(slots[s] + moving)
    return (slots[0] + moving)[0]


def on_core(
    tokens,
    cotangent,
    segment,
    parent,
    w_qkv,
    qkv_bias,
    w_out,
    gain_attn,
    gain_ffn,
    w_gate,
    w_up,
    w_down,
):
    low, full = jnp.bfloat16, jnp.float32
    me = lax.axis_index("gy")
    plane = lax.axis_index("gx")
    core, chip = me % 2, me // 2
    rows, width = 2 * tokens.shape[1], tokens.shape[2]
    slot_len = segment.shape[1]
    own_units = w_gate.shape[1]
    pad_units = -(-own_units // 384) * 384
    qwidth, kwidth = HEADS * HEAD, KV_HEADS * HEAD
    offset = chip * rows

    nb, ng = qkv_bias.shape[0], gain_attn.shape[0]
    packed = jnp.concatenate([qkv_bias, gain_attn, gain_ffn]).reshape(-1, 1)
    packed = jnp.pad(packed, ((0, 4 * ng - packed.shape[0]), (0, 0))).reshape(4, ng).T
    packed = jnp.pad(packed, ((0, 0), (0, HEAD - 4)))
    attn_own = jnp.concatenate([w_qkv, w_out.T, packed], axis=1)

    inputs_low = pair_rows(tokens, core)
    grad_low = pair_rows(cotangent, core)

    seg_tree = pick(segment, core)
    valid, upper_one, upper_two, depth_pos = tree_tables(seg_tree, pick(parent, core))
    places = jnp.arange(slot_len, dtype=jnp.int32)

    def take_own(array):
        return lax.dynamic_slice_in_dim(array, offset, rows, 0)

    cosine, sine = rotation(take_own(depth_pos), HEAD)
    sine = sine * jnp.where(jnp.arange(HEAD) < HEAD // 2, -1.0, 1.0)

    more = pad_units - own_units
    shards = [jnp.pad(w, ((0, 0), (0, more))) for w in (w_gate, w_up, w_down.T)]
    weights = [lax.all_gather(w, "gx", axis=0, tiled=True) for w in shards]
    attn_all, cotan_others = spread(after(attn_own, inputs_low, cosine, sine), grad_low)
    cotan_blocks = [grad_low] + cotan_others
    qwide = qwidth + 2 * kwidth
    small = attn_all[:, qwide + width :].reshape(32, ng, HEAD)[:, :, :4].transpose(0, 2, 1).reshape(32, 4 * ng)
    small = small.astype(full)
    bias_full = small[:, :nb].reshape(1, -1)
    gain_one = small[:, nb : nb + ng].reshape(1, -1)
    gain_two = small[:, nb + ng : nb + 2 * ng].reshape(1, -1)
    out_turned = attn_all[:, qwide : qwide + width]

    normed_one, query, keyval_own = project(inputs_low, gain_one, attn_all, bias_full, cosine, sine)
    mask = allowed(
        after(take_own(seg_tree), keyval_own), take_own(upper_one), take_own(upper_two), take_own(places), seg_tree, valid, places
    )
    qblocks, kblocks = rows // QUERY_TILE, slot_len // KEY_TILE
    active = mask.reshape(qblocks, QUERY_TILE, kblocks, KEY_TILE).any(axis=(1, 3))
    block_count = active.sum(axis=1).astype(jnp.int32)
    rank = jnp.cumsum(active.astype(jnp.int32), axis=1) - 1
    numbers = jnp.arange(kblocks, dtype=jnp.int32)
    hit = active[:, :, None] & (rank[:, :, None] == numbers[None, None, :])
    block_list = jnp.sum(jnp.where(hit, numbers[None, :, None], 0), axis=1).astype(jnp.int32)
    mask_bias = jnp.where(mask.T, 0.0, NEGATIVE).astype(low)

    keyval = plane_order([keyval_own] + [swap(keyval_own, bits) for bits in OTHERS], chip)
    other_weights = [swap(after(w, keyval), CORE) for w in weights[:2]]
    heads_out, lse = attend_fast(block_list, block_count, query, keyval, mask_bias)
    inputs = inputs_low.astype(full)
    resid = inputs + lax.dot_general(heads_out, out_turned, (((1,), (1,)), ((), ())), preferred_element_type=full)
    unit_two, inverse_two, normed_two = norm_parts(resid, gain_two)

    other_weights.append(swap(after(weights[2], heads_out), CORE))
    pieces = weights + other_weights
    normed_x, normed_y = swap(normed_two, ALONG_X), swap(normed_two, ALONG_Y)
    results = [ffn_block(normed_two, cotan_blocks[0], pieces)]
    normed_d = swap(after(normed_two, results[0][4]), ACROSS)
    normed_blocks = [normed_two, normed_x, normed_y, normed_d]
    for normed, cotan in zip(normed_blocks[1:], cotan_blocks[1:]):
        results.append(ffn_block(after(normed, results[-1][4]), cotan, pieces))
    hidden_b, gate_b, up_b, out_b, back_b = zip(*results)
    back_got = [swap(b, bits) for b, bits in zip(back_b[1:], OTHERS)]

    def both_halves(mine, other):
        mine = (mine.astype(full) + other.astype(full)).astype(low)
        mine = mine.reshape(-1, mine.shape[-1])
        return mine, lax.psum_scatter(mine, "gx", scatter_dimension=0, tiled=True).astype(full)

    down_mine, down_sent = wgrad((after(hidden_b[0], back_b[3]),) + hidden_b[1:], cotan_blocks, 4)
    down_got = swap(down_sent, CORE)
    gate_mine, gate_sent = wgrad((after(gate_b[0], down_sent, back_got[0]),) + gate_b[1:], normed_blocks, 4)
    gate_got = swap(gate_sent, CORE)
    down_sum, grad_down = both_halves(after(down_mine, gate_sent), down_got)

    grad_normed_two = sum(after(b, gate_sent).astype(full) for b in [back_b[0]] + back_got)
    back_two, grad_gain_two = norm_back(grad_normed_two, unit_two, inverse_two, gain_two)
    grad_resid = grad_low.astype(full) + back_two
    grad_branch = grad_resid.astype(low)
    grad_heads = jnp.dot(grad_branch, out_turned, preferred_element_type=full).astype(low)
    grad_wout = jnp.dot(grad_branch.T, heads_out, preferred_element_type=full).astype(low)
    out_got = [swap(after(b, grad_normed_two), bits) for b, bits in zip(out_b[1:], OTHERS)]
    gate_sum, grad_wgate = both_halves(gate_mine, gate_got)
    grad_heads = after(grad_heads, grad_wout, gate_sum, down_sum)
    query_lin, keyval_part = attend_back_fast(
        block_list, block_count, query, keyval, mask_bias, lse, heads_out, grad_heads, cosine, sine
    )

    grad_wout = sum_rows(grad_wout, plane, me, (CORE, ALONG_X, ALONG_Y)).T
    up_mine, up_sent = wgrad((after(up_b[0], query_lin),) + up_b[1:], normed_blocks, 4)
    up_sum, grad_wup = both_halves(up_mine, swap(up_sent, CORE))
    grad_down = grad_down[:own_units]
    grad_wgate, grad_wup = grad_wgate.T[:, :own_units], grad_wup.T[:, :own_units]

    def part_of(index):
        return lax.dynamic_slice_in_dim(keyval_part, (chip ^ index) * rows, rows, 0)

    keyval_grad = after(part_of(0), up_sent).astype(full) + sum(
        swap(part_of(index + 1), bits).astype(full) for index, bits in enumerate(OTHERS)
    )
    keys_grad = keyval_grad[:, :kwidth].reshape(rows, KV_HEADS, HEAD)
    keys_lin = keys_grad * cosine[:, None, :] - jnp.roll(keys_grad, HEAD // 2, axis=-1) * sine[:, None, :]
    keyval_lin = jnp.concatenate([keys_lin.reshape(rows, kwidth), keyval_grad[:, kwidth:]], axis=1).astype(low)
    grad_linear = jnp.concatenate([query_lin, keyval_lin], axis=1)
    grad_wqkv = jnp.dot(normed_one.T, grad_linear, preferred_element_type=full).astype(low)
    middle = grad_wqkv.shape[1] // 2
    grad_wqkv = jnp.concatenate(
        [
            sum_rows(grad_wqkv[:, :middle], plane, me, (CORE, ALONG_X, ALONG_Y)),
            sum_rows(grad_wqkv[:, middle:], plane, me, (CORE, ALONG_Y, ALONG_X)),
        ],
        axis=1,
    )
    grad_bias = jnp.sum(grad_linear.astype(full), axis=0)
    grad_normed_one = jnp.dot(grad_linear, attn_all[:, :qwide].T, preferred_element_type=full)
    unit_one, inverse_one, _ = norm_parts(inputs, gain_one)
    back_one, grad_gain_one = norm_back(grad_normed_one, unit_one, inverse_one, gain_one)
    grad_tokens = unpair_rows((grad_resid + back_one).astype(low), core)
    ffn_out = sum(after(b, query_lin).astype(full) for b in [out_b[0]] + out_got)
    layer_out = unpair_rows((resid + ffn_out).astype(low), core)

    packed = jnp.concatenate(
        [grad_bias.reshape(32, nb), grad_gain_one.reshape(32, ng), grad_gain_two.reshape(32, ng)], axis=1
    )
    small = sum_small(packed, plane, me)
    return (
        layer_out,
        grad_tokens,
        grad_wqkv,
        small[:nb],
        grad_wout,
        small[nb : nb + ng],
        small[nb + ng :],
        grad_wgate,
        grad_wup,
        grad_down,
    )


def solution(mesh):
    in_specs = (
        P("gx", "gy", None),
        P("gx", "gy", None),
        P("gx", None),
        P("gx", None),
        P(("gx", "gy"), None),
        P(("gx", "gy")),
        P(None, ("gx", "gy")),
        P(("gx", "gy")),
        P(("gx", "gy")),
        P("gx", "gy"),
        P("gx", "gy"),
        P("gy", "gx"),
    )
    out_specs = (
        P("gx", "gy", None),
        P("gx", "gy", None),
        P(("gx", "gy"), None),
        P(("gx", "gy")),
        P(None, ("gx", "gy")),
        P(("gx", "gy")),
        P(("gx", "gy")),
        P("gx", "gy"),
        P("gx", "gy"),
        P("gy", "gx"),
    )
    return jax.shard_map(
        on_core if tuple(mesh.shape.values()) == (4, 8) else on_device,
        mesh=mesh,
        in_specs=in_specs,
        out_specs=out_specs,
        check_vma=False,
    )
```

```python
from functools import reduce
import math

import jax
import jax.numpy as jnp
from jax import lax
from jax.experimental import pallas as pl
from jax.experimental.pallas import tpu as pltpu
from jax.sharding import PartitionSpec as P

HEADS = 12
KV_HEADS = 2
HEAD = 128

QUERY_TILE = 128
KEY_TILE = 256
ROW_TILE = 128
FFN_CHUNK = 768
FFN_PARTS = 2
WG_TILE = 384
PACE = 1.0
LOG2E = 1.0 / math.log(2.0)

CORE, ALONG_X, ALONG_Y, ACROSS = 1, 2, 4, 6
OTHERS = (ALONG_X, ALONG_Y, ACROSS)
RING = 8


EPS = 1e-06
THETA = 1000000.0
NEGATIVE = -1e30


def tree_tables(segment, parent):
    slot_len = segment.shape[0]
    seg_count = parent.shape[0]
    places = jnp.arange(slot_len, dtype=jnp.int32)
    labels = jnp.arange(seg_count, dtype=jnp.int32)
    member = segment[:, None] == labels[None, :]
    valid = segment >= 0
    first = jnp.min(jnp.where(member, places[:, None], slot_len), axis=0)
    length = jnp.sum(member.astype(jnp.int32), axis=0)
    parent_hit = parent[:, None] == labels[None, :]
    grand = jnp.sum(jnp.where(parent_hit, parent[None, :], 0), axis=1)
    grand_hit = grand[:, None] == labels[None, :]
    parent_len = jnp.sum(jnp.where(parent_hit, length[None, :], 0), axis=1)
    grand_len = jnp.sum(jnp.where(grand_hit, length[None, :], 0), axis=1)
    base = jnp.where(parent != labels, parent_len, 0) + jnp.where(grand != parent, grand_len, 0)

    def lookup(table):
        return jnp.sum(jnp.where(member, table[None, :], 0), axis=1)

    upper_one = jnp.where(valid, lookup(parent), -2)
    upper_two = jnp.where(valid, lookup(grand), -2)
    depth_pos = jnp.where(valid, places - lookup(first) + lookup(base), 0)
    return (valid, upper_one, upper_two, depth_pos)


def allowed(seg_query, upper_one, upper_two, place_query, seg_keys, valid_keys, place_keys):
    related = (seg_keys[None, :] == seg_query[:, None]) | (seg_keys[None, :] == upper_one[:, None])
    related = related | (seg_keys[None, :] == upper_two[:, None])
    earlier = place_keys[None, :] <= place_query[:, None]
    return related & earlier & valid_keys[None, :] | (place_keys[None, :] == place_query[:, None])


def rotation(depth_pos, width):
    half = width // 2
    freqs = jnp.exp(jnp.arange(half, dtype=jnp.float32) * (-2.0 * math.log(THETA) / width))
    angle = depth_pos.astype(jnp.float32)[:, None] * freqs[None, :]
    cosine = jnp.concatenate([jnp.cos(angle), jnp.cos(angle)], axis=1)
    sine = jnp.concatenate([jnp.sin(angle), jnp.sin(angle)], axis=1)
    return (cosine, sine)


def turn(heads, cosine, sine):
    half = heads.shape[-1] // 2
    swapped = jnp.concatenate([-heads[..., half:], heads[..., :half]], axis=-1)
    return heads * cosine[:, None, :] + swapped * sine[:, None, :]


def norm_parts(values, gain):
    inverse = lax.rsqrt(jnp.mean(values * values, axis=-1, keepdims=True) + EPS)
    unit = values * inverse
    return (unit, inverse, (unit * gain).astype(jnp.bfloat16))


def norm_back(grad_normed, unit, inverse, gain):
    scaled = grad_normed * gain
    back = inverse * (scaled - unit * jnp.mean(scaled * unit, axis=-1, keepdims=True))
    return (back, jnp.sum(grad_normed * unit, axis=0))


def masked_scores(group_query, group_keys, mask, scale):
    scores = (
        jnp.einsum("rhd,kd->hrk", group_query, group_keys, preferred_element_type=jnp.float32)
        * scale
    )
    return jnp.where(mask[None], scores, NEGATIVE)


def attend(query_low, keys_all, values_all, mask, scale):
    group = HEADS // KV_HEADS
    pieces = []
    totals = []
    for head_group in range(KV_HEADS):
        group_query = query_low[:, head_group * group : (head_group + 1) * group, :]
        columns = slice(head_group * HEAD, (head_group + 1) * HEAD)
        scores = masked_scores(group_query, keys_all[:, columns], mask, scale)
        top_score = jnp.max(scores, axis=-1, keepdims=True)
        expo = jnp.exp(scores - top_score)
        denom = jnp.sum(expo, axis=-1, keepdims=True)
        probs_low = (expo / denom).astype(jnp.bfloat16)
        pieces.append(
            jnp.einsum(
                "hrk,kd->rhd", probs_low, values_all[:, columns], preferred_element_type=jnp.float32
            )
        )
        totals.append(top_score + jnp.log(denom))
    return (jnp.concatenate(pieces, axis=1), totals)


def attend_back(query_low, keys_all, values_all, mask, totals, grad_heads, scale):
    group = HEADS // KV_HEADS
    grad_query, grad_keys, grad_values = ([], [], [])
    for head_group in range(KV_HEADS):
        heads_sel = slice(head_group * group, (head_group + 1) * group)
        columns = slice(head_group * HEAD, (head_group + 1) * HEAD)
        group_query = query_low[:, heads_sel, :]
        group_keys = keys_all[:, columns]
        group_grad = grad_heads[:, heads_sel, :]
        scores = masked_scores(group_query, group_keys, mask, scale)
        probs = jnp.exp(scores - totals[head_group])
        probs_low = probs.astype(jnp.bfloat16)
        grad_values.append(
            jnp.einsum("hrk,rhd->kd", probs_low, group_grad, preferred_element_type=jnp.float32)
        )
        grad_probs = jnp.einsum(
            "rhd,kd->hrk", group_grad, values_all[:, columns], preferred_element_type=jnp.float32
        )
        grad_scores = (
            probs * (grad_probs - jnp.sum(probs * grad_probs, axis=-1, keepdims=True))
        ).astype(jnp.bfloat16)
        grad_query.append(
            jnp.einsum("hrk,kd->rhd", grad_scores, group_keys, preferred_element_type=jnp.float32)
            * scale
        )
        grad_keys.append(
            jnp.einsum("hrk,rhd->kd", grad_scores, group_query, preferred_element_type=jnp.float32)
            * scale
        )
    return (
        jnp.concatenate(grad_query, axis=1),
        jnp.concatenate(grad_keys, axis=1),
        jnp.concatenate(grad_values, axis=1),
    )


def add_trees(left, right):
    return jax.tree.map(jnp.add, left, right)


def on_device(
    tokens,
    cotangent,
    segment,
    parent,
    w_qkv,
    qkv_bias,
    w_out,
    gain_attn,
    gain_ffn,
    w_gate,
    w_up,
    w_down,
):
    micro = tokens.shape[0]
    row_count = tokens.shape[1]
    slot_len = segment.shape[1]
    qwidth = HEADS * HEAD
    kwidth = KV_HEADS * HEAD
    scale = 1.0 / math.sqrt(HEAD)
    offset = lax.axis_index("gy") * row_count
    place_all = jnp.arange(slot_len, dtype=jnp.int32)
    place_own = offset + jnp.arange(row_count, dtype=jnp.int32)
    outputs, input_grads, attn_list, ffn_list = ([], [], [], [])
    for micro_index in range(micro):
        attn_full = (
            lax.all_gather(w_qkv, ("gx", "gy"), axis=0, tiled=True),
            lax.all_gather(qkv_bias, ("gx", "gy"), axis=0, tiled=True),
            lax.all_gather(w_out, ("gx", "gy"), axis=1, tiled=True),
            lax.all_gather(gain_attn, ("gx", "gy"), axis=0, tiled=True),
            lax.all_gather(gain_ffn, ("gx", "gy"), axis=0, tiled=True),
        )
        ffn_full = (
            lax.all_gather(w_gate, "gx", axis=0, tiled=True),
            lax.all_gather(w_up, "gx", axis=0, tiled=True),
            lax.all_gather(w_down, "gx", axis=1, tiled=True),
        )
        qkv_full, bias_full, out_full, gain_one_full, gain_two_full = attn_full
        gate_full, up_full, down_full = ffn_full
        gain_one = gain_one_full.astype(jnp.float32)
        gain_two = gain_two_full.astype(jnp.float32)
        seg_tree = segment[micro_index]
        valid, upper_one, upper_two, depth_pos = tree_tables(seg_tree, parent[micro_index])

        def take_own(array):
            return lax.dynamic_slice_in_dim(array, offset, row_count, 0)

        mask = allowed(
            take_own(seg_tree),
            take_own(upper_one),
            take_own(upper_two),
            place_own,
            seg_tree,
            valid,
            place_all,
        )
        cosine, sine = rotation(take_own(depth_pos), HEAD)
        inputs = tokens[micro_index].astype(jnp.float32)
        unit_one, inverse_one, normed_one = norm_parts(inputs, gain_one)
        linear = jnp.dot(
            normed_one, qkv_full, preferred_element_type=jnp.float32
        ) + bias_full.astype(jnp.float32)
        query_low = turn(linear[:, :qwidth].reshape(row_count, HEADS, HEAD), cosine, sine).astype(
            jnp.bfloat16
        )
        keys_low = turn(
            linear[:, qwidth : qwidth + kwidth].reshape(row_count, KV_HEADS, HEAD), cosine, sine
        )
        keys_low = keys_low.reshape(row_count, kwidth).astype(jnp.bfloat16)
        values_low = linear[:, qwidth + kwidth :].astype(jnp.bfloat16)
        keys_all, values_all = (
            lax.all_gather(keys_low, "gy", axis=0, tiled=True),
            lax.all_gather(values_low, "gy", axis=0, tiled=True),
        )
        heads_raw, totals = attend(query_low, keys_all, values_all, mask, scale)
        heads_out = heads_raw.reshape(row_count, qwidth).astype(jnp.bfloat16)
        resid = inputs + jnp.dot(heads_out, out_full, preferred_element_type=jnp.float32)
        unit_two, inverse_two, normed_two = norm_parts(resid, gain_two)
        normed_all = lax.all_gather(normed_two, "gy", axis=0, tiled=True)
        gate = jnp.dot(normed_all, gate_full, preferred_element_type=jnp.float32)
        upward = jnp.dot(normed_all, up_full, preferred_element_type=jnp.float32)
        sigma = jax.nn.sigmoid(gate)
        swish = gate * sigma
        hidden = (swish * upward).astype(jnp.bfloat16)
        ffn_own = lax.psum_scatter(
            jnp.dot(hidden, down_full, preferred_element_type=jnp.float32),
            "gy",
            scatter_dimension=0,
            tiled=True,
        )
        outputs.append((resid + ffn_own).astype(jnp.bfloat16))
        grad_low = cotangent[micro_index]
        grad_all = lax.all_gather(grad_low, "gy", axis=0, tiled=True)
        grad_hidden = jnp.dot(grad_all, down_full.T, preferred_element_type=jnp.float32)
        grad_down = jnp.dot(hidden.T, grad_all, preferred_element_type=jnp.float32)
        grad_gate = (grad_hidden * upward * sigma * (1.0 + gate * (1.0 - sigma))).astype(
            jnp.bfloat16
        )
        grad_up = (grad_hidden * swish).astype(jnp.bfloat16)
        grad_wgate = jnp.dot(normed_all.T, grad_gate, preferred_element_type=jnp.float32)
        grad_wup = jnp.dot(normed_all.T, grad_up, preferred_element_type=jnp.float32)
        grad_normed_two = lax.psum_scatter(
            jnp.dot(grad_gate, gate_full.T, preferred_element_type=jnp.float32)
            + jnp.dot(grad_up, up_full.T, preferred_element_type=jnp.float32),
            "gy",
            scatter_dimension=0,
            tiled=True,
        )
        back_two, grad_gain_two = norm_back(grad_normed_two, unit_two, inverse_two, gain_two)
        grad_resid = grad_low.astype(jnp.float32) + back_two
        grad_branch = grad_resid.astype(jnp.bfloat16)
        grad_wout = jnp.dot(heads_out.T, grad_branch, preferred_element_type=jnp.float32)
        grad_heads = jnp.dot(grad_branch, out_full.T, preferred_element_type=jnp.float32).astype(
            jnp.bfloat16
        )
        grad_heads = grad_heads.reshape(row_count, HEADS, HEAD)
        grad_query, keys_part, values_part = attend_back(
            query_low, keys_all, values_all, mask, totals, grad_heads, scale
        )
        grad_keys, grad_values = (
            lax.psum_scatter(keys_part, "gy", scatter_dimension=0, tiled=True),
            lax.psum_scatter(values_part, "gy", scatter_dimension=0, tiled=True),
        )
        query_lin = turn(grad_query, cosine, -sine).reshape(row_count, qwidth)
        keys_lin = turn(grad_keys.reshape(row_count, KV_HEADS, HEAD), cosine, -sine).reshape(
            row_count, kwidth
        )
        grad_linear = jnp.concatenate([query_lin, keys_lin, grad_values], axis=1).astype(
            jnp.bfloat16
        )
        grad_wqkv = jnp.dot(normed_one.T, grad_linear, preferred_element_type=jnp.float32)
        grad_bias = jnp.sum(grad_linear.astype(jnp.float32), axis=0)
        grad_normed_one = jnp.dot(grad_linear, qkv_full.T, preferred_element_type=jnp.float32)
        back_one, grad_gain_one = norm_back(grad_normed_one, unit_one, inverse_one, gain_one)
        input_grads.append((grad_resid + back_one).astype(jnp.bfloat16))
        attn_list.append((grad_wqkv, grad_bias, grad_wout, grad_gain_one, grad_gain_two))
        ffn_list.append((grad_wgate, grad_wup, grad_down))
    attn_total = reduce(add_trees, attn_list)
    ffn_total = reduce(add_trees, ffn_list)
    attn_total = (
        lax.psum_scatter(attn_total[0], ("gx", "gy"), scatter_dimension=0, tiled=True),
        lax.psum_scatter(attn_total[1], ("gx", "gy"), scatter_dimension=0, tiled=True),
        lax.psum_scatter(attn_total[2], ("gx", "gy"), scatter_dimension=1, tiled=True),
        lax.psum_scatter(attn_total[3], ("gx", "gy"), scatter_dimension=0, tiled=True),
        lax.psum_scatter(attn_total[4], ("gx", "gy"), scatter_dimension=0, tiled=True),
    )
    ffn_total = (
        lax.psum_scatter(ffn_total[0], "gx", scatter_dimension=0, tiled=True),
        lax.psum_scatter(ffn_total[1], "gx", scatter_dimension=0, tiled=True),
        lax.psum_scatter(ffn_total[2], "gx", scatter_dimension=1, tiled=True),
    )
    layer_out = jnp.stack(outputs, axis=0)
    grad_tokens = jnp.stack(input_grads, axis=0)
    return (
        layer_out,
        grad_tokens,
        attn_total[0],
        attn_total[1],
        attn_total[2],
        attn_total[3],
        attn_total[4],
        ffn_total[0],
        ffn_total[1],
        ffn_total[2],
    )


def dot_nn(left, right):
    return lax.dot_general(left, right, (((1,), (0,)), ((), ())), preferred_element_type=jnp.float32)


def dot_nt(left, right):
    return lax.dot_general(left, right, (((1,), (1,)), ((), ())), preferred_element_type=jnp.float32)


def dot_tn(left, right):
    return lax.dot_general(left, right, (((0,), (0,)), ((), ())), preferred_element_type=jnp.float32)


def cost(flops, moved, trans=0):
    return pl.CostEstimate(flops=int(flops * PACE), bytes_accessed=int(moved * PACE), transcendentals=int(trans * PACE))


def params(mib):
    return pltpu.CompilerParams(vmem_limit_bytes=mib * 1024 * 1024)


def sigmoid(v):
    return 0.5 * jnp.tanh(0.5 * v) + 0.5


def peers_of():
    me, plane = lax.axis_index("gy"), lax.axis_index("gx")
    along_x = me + 2 - 4 * lax.rem(me // 2, 2)
    return {
        CORE: {"gy": me + 1 - 2 * lax.rem(me, 2)},
        ALONG_X: {"gy": along_x},
        ALONG_Y: {"gy": me + 4 - 8 * (me // 4)},
        ACROSS: {"gy": along_x + 4 - 8 * (along_x // 4)},
        RING: {"gx": lax.rem(plane + 1, 4)},
        RING + 1: {"gx": lax.rem(plane + 2, 4)},
        -RING: {"gx": lax.rem(plane + 3, 4)},
    }


def greet(bits_used):
    peers = peers_of()
    barrier = pltpu.get_barrier_semaphore()
    greeted = [bits for bits in bits_used] + [-RING] * (RING in bits_used)
    for bits in greeted:
        pl.semaphore_signal(barrier, inc=1, device_id=peers[bits], device_id_type=pl.DeviceIdType.MESH)
    pl.semaphore_wait(barrier, len(greeted))


def side_copies(sides, sources, targets, sent, landed):
    peers = peers_of()
    copies = []
    for parts, target in zip(sides, targets):
        for _, take, fill, bits in parts:
            copies.append(
                pltpu.make_async_remote_copy(
                    sources[len(copies)].at[pl.ds(*take)],
                    target.at[pl.ds(*fill)],
                    sent.at[len(copies)],
                    landed.at[len(copies)],
                    device_id=peers[bits],
                    device_id_type=pl.DeviceIdType.MESH,
                )
            )
    return copies


def whole_side(array, bits):
    return [(array, (0, array.shape[0]), (0, array.shape[0]), bits)]


def rows_side(array, start, count, bits):
    return [(array, (start, count), (0, count), bits)]


def call_beside(body, sides, collective, operands, grid, in_specs, out_specs, out_shape, scratch_shapes, mib, estimate, name):
    n_in, n_out, n_scratch = len(in_specs), len(out_specs), len(scratch_shapes)
    flat = [part for parts in sides for part in parts]
    bits_used = sorted({part[3] for part in flat})

    def whole_body(*refs):
        ins, refs = refs[:n_in], refs[n_in:]
        sources, refs = refs[: len(flat)], refs[len(flat) :]
        outs, refs = refs[:n_out], refs[n_out:]
        targets, refs = refs[: len(sides)], refs[len(sides) :]
        scratch, refs = refs[:n_scratch], refs[n_scratch:]
        step, last = pl.program_id(0), pl.num_programs(0) - 1
        if flat:

            @pl.when(step == 0)
            def _():
                greet(bits_used)
                for copy in side_copies(sides, sources, targets, *refs):
                    copy.start()

        body(*ins, *outs, *scratch)
        if flat:

            @pl.when(step == last)
            def _():
                for copy in side_copies(sides, sources, targets, *refs):
                    copy.wait()

    anywhere = pl.BlockSpec(memory_space=pl.ANY)
    extra = {"collective_id": collective, "has_side_effects": True} if flat else {}
    results = pl.pallas_call(
        whole_body,
        grid=grid,
        in_specs=list(in_specs) + [anywhere] * len(flat),
        out_specs=list(out_specs) + [anywhere] * len(sides),
        out_shape=list(out_shape)
        + [jax.ShapeDtypeStruct((sum(p[2][1] for p in parts),) + parts[0][0].shape[1:], parts[0][0].dtype) for parts in sides],
        scratch_shapes=list(scratch_shapes) + ([pltpu.SemaphoreType.DMA((len(flat),))] * 2 if flat else []),
        compiler_params=pltpu.CompilerParams(vmem_limit_bytes=mib * 1024 * 1024, **extra),
        cost_estimate=estimate,
        name=name,
    )(*operands, *[part[0] for part in flat])
    return results[:n_out], results[n_out:]


def ffn_copies(chunk, pieces, held, sems):
    units = pieces[0].shape[1]
    tile = FFN_CHUNK // 2
    slot = chunk % 2
    copies = []
    for part in range(2):
        column = chunk * FFN_CHUNK + part * tile
        owner, inside = column // units, column % units
        for kind in range(3):
            copies.append(
                pltpu.make_async_copy(
                    pieces[3 * owner + kind].at[:, pl.ds(inside, tile)],
                    held.at[slot, kind, :, pl.ds(part * tile, tile)],
                    sems.at[slot, part * 3 + kind],
                )
            )
    return copies


def ffn_body(n_ref, c_ref, *refs):
    pieces = refs[:6]
    hid_ref, dg_ref, du_ref, f_ref, dn_ref, f_acc, dn_acc, held, sems = refs[6:]
    step = pl.program_id(0)
    chunks = 2 * pieces[0].shape[1] // FFN_CHUNK

    @pl.when(step == 0)
    def _():
        for copy in ffn_copies(0, pieces, held, sems):
            copy.start()
        f_acc[...] = jnp.zeros_like(f_acc)
        dn_acc[...] = jnp.zeros_like(dn_acc)

    for chunk in range(chunks):

        @pl.when(step == chunk)
        def _():
            if chunk + 1 < chunks:
                for copy in ffn_copies(chunk + 1, pieces, held, sems):
                    copy.start()
            for copy in ffn_copies(chunk, pieces, held, sems):
                copy.wait()

    slot = step % 2
    rows = n_ref.shape[0]
    part = rows // FFN_PARTS
    for index in range(FFN_PARTS):
        take = pl.ds(index * part, part)
        gate = dot_nn(n_ref[take, :], held[slot, 0])
        upward = dot_nn(n_ref[take, :], held[slot, 1])
        sigma = sigmoid(gate)
        swish = gate * sigma
        hidden = (swish * upward).astype(jnp.bfloat16)
        hid_ref[take, :] = hidden
        grad_hidden = dot_nn(c_ref[take, :], held[slot, 2])
        grad_gate = (grad_hidden * upward * sigma * (1.0 + gate * (1.0 - sigma))).astype(jnp.bfloat16)
        grad_up = (grad_hidden * swish).astype(jnp.bfloat16)
        dg_ref[take, :] = grad_gate
        du_ref[take, :] = grad_up
        f_acc[take, :] += dot_nt(hidden, held[slot, 2])
        dn_acc[take, :] += dot_nt(grad_gate, held[slot, 0]) + dot_nt(grad_up, held[slot, 1])

    @pl.when(step == pl.num_programs(0) - 1)
    def _():
        f_ref[...] = f_acc[...].astype(f_ref.dtype)
        dn_ref[...] = dn_acc[...].astype(dn_ref.dtype)


def ffn_block(normed, cotan, pieces, collective, sides=()):
    rows, width = normed.shape
    units = 2 * pieces[0].shape[1]
    chunk = FFN_CHUNK
    whole = pl.BlockSpec((rows, width), lambda j: (0, 0))
    tall = pl.BlockSpec((rows, chunk), lambda j: (0, j))
    low = jnp.bfloat16
    return call_beside(
        ffn_body,
        sides,
        collective,
        (normed, cotan, *pieces),
        (units // chunk,),
        [whole, whole] + [pl.BlockSpec(memory_space=pl.ANY)] * len(pieces),
        [tall, tall, tall, whole, whole],
        [jax.ShapeDtypeStruct((rows, units), low)] * 3 + [jax.ShapeDtypeStruct((rows, width), low)] * 2,
        [pltpu.VMEM((rows, width), jnp.float32)] * 2
        + [pltpu.VMEM((2, 3, width, chunk), low), pltpu.SemaphoreType.DMA((2, len(pieces)))],
        60,
        cost(12 * rows * width * units, 6 * width * units + 6 * rows * (width + units)),
        "ffn_block",
    )


def wgrad_body(per_half, *refs):
    count = (len(refs) - 2) // 2
    total = dot_tn(refs[0][...], refs[count][...])
    for index in range(1, count):
        total = total + dot_tn(refs[index][...], refs[count + index][...])

    def store(out_ref):
        slots, _, wide = out_ref.shape
        for slot in range(slots):
            out_ref[slot] = total[:, slot * wide : (slot + 1) * wide].astype(out_ref.dtype)

    first = pl.program_id(0) < per_half
    pl.when(first)(lambda: store(refs[-2]))
    pl.when(jnp.logical_not(first))(lambda: store(refs[-1]))


def wgrad(lefts, rights, slots, collective, sides=()):
    rows, units = lefts[0].shape
    width = rights[0].shape[1]
    tile = WG_TILE
    per_half = units // 2 // tile
    wide = width // slots
    count = len(lefts)
    return call_beside(
        lambda *refs: wgrad_body(per_half, *refs),
        sides,
        collective,
        (*lefts, *rights),
        (units // tile,),
        [pl.BlockSpec((rows, tile), lambda j: (0, j))] * count
        + [pl.BlockSpec((rows, width), lambda j: (0, 0))] * count,
        [
            pl.BlockSpec((slots, tile, wide), lambda j: (0, jnp.minimum(j, per_half - 1), 0)),
            pl.BlockSpec((slots, tile, wide), lambda j: (0, jnp.maximum(j - per_half, 0), 0)),
        ],
        [jax.ShapeDtypeStruct((slots, units // 2, wide), jnp.bfloat16)] * 2,
        [],
        60,
        cost(2 * count * rows * width * units, 2 * count * rows * (width + units)),
        "ffn_wgrad",
    )


def group_rows(source_ref, group, per_group):
    return jnp.concatenate(
        [source_ref[:, (group * per_group + h) * HEAD : (group * per_group + h + 1) * HEAD] for h in range(per_group)],
        axis=0,
    )


def attend_body(list_ref, count_ref, q_ref, kv_ref, bias_ref, o_ref, lse_ref, qs, acc, top, den):
    block = pl.program_id(0)
    per_group = HEADS // KV_HEADS
    for group in range(KV_HEADS):
        qs[group] = group_rows(q_ref, group, per_group)
    acc[...] = jnp.zeros_like(acc)
    den[...] = jnp.zeros_like(den)
    top[...] = jnp.full_like(top, 2 * NEGATIVE)
    factor = LOG2E / math.sqrt(HEAD)

    def body(n, carry):
        rows = pl.ds(pl.multiple_of(list_ref[block, n] * KEY_TILE, KEY_TILE), KEY_TILE)
        bias = jnp.concatenate([bias_ref[rows, :].astype(jnp.float32)] * per_group, axis=1)
        for group in range(KV_HEADS):
            keys = kv_ref[rows, group * HEAD : (group + 1) * HEAD]
            values = kv_ref[rows, (KV_HEADS + group) * HEAD : (KV_HEADS + group + 1) * HEAD]
            scores = dot_nt(keys, qs[group]) * factor + bias
            old = top[group]
            new = jnp.maximum(old, jnp.max(scores, axis=0, keepdims=True))
            probs = jnp.exp2(scores - new)
            shrink = jnp.exp2(old - new)
            den[group] = den[group] * shrink + jnp.sum(probs, axis=0, keepdims=True)
            acc[group] = acc[group] * shrink + dot_tn(values, probs.astype(jnp.bfloat16))
            top[group] = new
        return carry

    lax.fori_loop(0, count_ref[block], body, 0)
    for group in range(KV_HEADS):
        out = acc[group] / den[group]
        lse_ref[0, group] = top[group] + jnp.log(den[group]) * LOG2E
        for h in range(per_group):
            head = group * per_group + h
            o_ref[:, head * HEAD : (head + 1) * HEAD] = out[:, h * HEAD : (h + 1) * HEAD].T.astype(o_ref.dtype)


def attend_fast(block_list, block_count, query, keyval, bias):
    rows, qwidth = query.shape
    slots = keyval.shape[0]
    blocks = rows // QUERY_TILE
    per_group = HEADS // KV_HEADS
    lanes = per_group * QUERY_TILE
    whole = pl.BlockSpec(keyval.shape, lambda i, a, b: (0, 0))
    tile = pl.BlockSpec((QUERY_TILE, qwidth), lambda i, a, b: (i, 0))
    return pl.pallas_call(
        attend_body,
        grid_spec=pltpu.PrefetchScalarGridSpec(
            num_scalar_prefetch=2,
            grid=(blocks,),
            in_specs=[tile, whole, pl.BlockSpec((slots, QUERY_TILE), lambda i, a, b: (0, i))],
            out_specs=[tile, pl.BlockSpec((1, KV_HEADS, 1, lanes), lambda i, a, b: (i, 0, 0, 0))],
            scratch_shapes=[
                pltpu.VMEM((KV_HEADS, lanes, HEAD), jnp.bfloat16),
                pltpu.VMEM((KV_HEADS, HEAD, lanes), jnp.float32),
                pltpu.VMEM((KV_HEADS, 1, lanes), jnp.float32),
                pltpu.VMEM((KV_HEADS, 1, lanes), jnp.float32),
            ],
        ),
        out_shape=[
            jax.ShapeDtypeStruct((rows, qwidth), jnp.bfloat16),
            jax.ShapeDtypeStruct((blocks, KV_HEADS, 1, lanes), jnp.float32),
        ],
        compiler_params=params(48),
        cost_estimate=cost(2 * rows * slots * qwidth * 2, 4 * slots * rows, HEADS * rows * slots // 2),
        name="tree_attention",
    )(block_list, block_count, query, keyval, bias)


def attend_back_body(
    list_ref, count_ref, q_ref, kv_ref, bias_ref, lse_ref, o_ref, do_ref, cos_ref, sin_ref,
    dq_ref, dkv_ref, qs, dos, delta, dqt, dkv,
):
    block = pl.program_id(0)
    per_group = HEADS // KV_HEADS
    scale = 1.0 / math.sqrt(HEAD)
    factor = LOG2E * scale
    lanes = qs.shape[1]

    @pl.when(block == 0)
    def _():
        dkv[...] = jnp.zeros_like(dkv)

    for group in range(KV_HEADS):
        qs[group] = group_rows(q_ref, group, per_group)
        grads = group_rows(do_ref, group, per_group)
        dos[group] = grads
        both = grads.astype(jnp.float32) * group_rows(o_ref, group, per_group).astype(jnp.float32)
        delta[group] = lax.dot_general(
            jnp.ones((8, HEAD), jnp.float32), both, (((1,), (1,)), ((), ())),
            precision=lax.Precision.HIGHEST, preferred_element_type=jnp.float32,
        )[0:1]
    dqt[...] = jnp.zeros_like(dqt)

    def body(n, carry):
        rows = pl.ds(pl.multiple_of(list_ref[block, n] * KEY_TILE, KEY_TILE), KEY_TILE)
        bias = jnp.concatenate([bias_ref[rows, :].astype(jnp.float32)] * per_group, axis=1)
        for group in range(KV_HEADS):
            kcols = slice(group * HEAD, (group + 1) * HEAD)
            vcols = slice((KV_HEADS + group) * HEAD, (KV_HEADS + group + 1) * HEAD)
            keys = kv_ref[rows, kcols]
            values = kv_ref[rows, vcols]
            scores = dot_nt(keys, qs[group]) * factor + bias
            probs = jnp.exp2(scores - lse_ref[0, group])
            grad_probs = dot_nt(values, dos[group])
            grad_scores = (probs * (grad_probs - delta[group])).astype(jnp.bfloat16)
            dkv[rows, vcols] += dot_nn(probs.astype(jnp.bfloat16), dos[group])
            dkv[rows, kcols] += dot_nn(grad_scores, qs[group])
            dqt[group] += dot_tn(keys, grad_scores)
        return carry

    lax.fori_loop(0, count_ref[block], body, 0)
    cosine, sine = cos_ref[...], sin_ref[...]
    for group in range(KV_HEADS):
        for h in range(per_group):
            head = group * per_group + h
            grad = dqt[group, :, h * HEAD : (h + 1) * HEAD].T * scale
            grad = grad * cosine - pltpu.roll(grad, HEAD // 2, 1) * sine
            dq_ref[:, head * HEAD : (head + 1) * HEAD] = grad.astype(dq_ref.dtype)

    @pl.when(block == pl.num_programs(0) - 1)
    def _():
        kwidth = KV_HEADS * HEAD
        dkv_ref[:, :kwidth] = (dkv[:, :kwidth] * scale).astype(dkv_ref.dtype)
        dkv_ref[:, kwidth:] = dkv[:, kwidth:].astype(dkv_ref.dtype)


def attend_back_fast(block_list, block_count, query, keyval, bias, lse, heads_out, grad_heads, cosine, sine):
    rows, qwidth = query.shape
    slots = keyval.shape[0]
    blocks = rows // QUERY_TILE
    per_group = HEADS // KV_HEADS
    lanes = per_group * QUERY_TILE
    whole = pl.BlockSpec(keyval.shape, lambda i, a, b: (0, 0))
    tile = pl.BlockSpec((QUERY_TILE, qwidth), lambda i, a, b: (i, 0))
    turned = pl.BlockSpec((QUERY_TILE, HEAD), lambda i, a, b: (i, 0))
    return pl.pallas_call(
        attend_back_body,
        grid_spec=pltpu.PrefetchScalarGridSpec(
            num_scalar_prefetch=2,
            grid=(blocks,),
            in_specs=[
                tile,
                whole,
                pl.BlockSpec((slots, QUERY_TILE), lambda i, a, b: (0, i)),
                pl.BlockSpec((1, KV_HEADS, 1, lanes), lambda i, a, b: (i, 0, 0, 0)),
                tile,
                tile,
                turned,
                turned,
            ],
            out_specs=[tile, whole],
            scratch_shapes=[
                pltpu.VMEM((KV_HEADS, lanes, HEAD), jnp.bfloat16),
                pltpu.VMEM((KV_HEADS, lanes, HEAD), jnp.bfloat16),
                pltpu.VMEM((KV_HEADS, 1, lanes), jnp.float32),
                pltpu.VMEM((KV_HEADS, HEAD, lanes), jnp.float32),
                pltpu.VMEM(keyval.shape, jnp.float32),
            ],
        ),
        out_shape=[
            jax.ShapeDtypeStruct((rows, qwidth), jnp.bfloat16),
            jax.ShapeDtypeStruct(keyval.shape, jnp.bfloat16),
        ],
        compiler_params=params(56),
        cost_estimate=cost(5 * rows * slots * qwidth * 2, 8 * slots * rows, HEADS * rows * slots // 2),
        name="tree_attention_back",
    )(block_list, block_count, query, keyval, bias, lse, heads_out, grad_heads, cosine, sine)


def project_body(x_ref, gain_ref, w_ref, b_ref, cos_ref, sin_ref, n_ref, q_ref, kv_ref):
    values = x_ref[...].astype(jnp.float32)
    inverse = lax.rsqrt(jnp.mean(values * values, axis=-1, keepdims=True) + EPS)
    normed = (values * inverse * gain_ref[...]).astype(jnp.bfloat16)
    n_ref[...] = normed
    linear = dot_nn(normed, w_ref[...]) + b_ref[...]
    cosine, sine = cos_ref[...], sin_ref[...]
    for head in range(HEADS + KV_HEADS):
        lane = linear[:, head * HEAD : (head + 1) * HEAD]
        lane = (lane * cosine + pltpu.roll(lane, HEAD // 2, 1) * sine).astype(jnp.bfloat16)
        if head < HEADS:
            q_ref[:, head * HEAD : (head + 1) * HEAD] = lane
        else:
            kv_ref[:, (head - HEADS) * HEAD : (head - HEADS + 1) * HEAD] = lane
    kv_ref[:, KV_HEADS * HEAD :] = linear[:, (HEADS + KV_HEADS) * HEAD :].astype(jnp.bfloat16)


def project(inputs, gain, w_qkv, bias, cosine, sine):
    rows, width = inputs.shape
    qwidth, kwidth = HEADS * HEAD, 2 * KV_HEADS * HEAD
    tile = ROW_TILE
    fixed = lambda i: (0, 0)
    moving = lambda i: (i, 0)
    return pl.pallas_call(
        project_body,
        grid=(rows // tile,),
        in_specs=[
            pl.BlockSpec((tile, width), moving),
            pl.BlockSpec((1, width), fixed),
            pl.BlockSpec((width, qwidth + kwidth), fixed),
            pl.BlockSpec((1, qwidth + kwidth), fixed),
            pl.BlockSpec((tile, HEAD), moving),
            pl.BlockSpec((tile, HEAD), moving),
        ],
        out_specs=[
            pl.BlockSpec((tile, width), moving),
            pl.BlockSpec((tile, qwidth), moving),
            pl.BlockSpec((tile, kwidth), moving),
        ],
        out_shape=[
            jax.ShapeDtypeStruct((rows, width), jnp.bfloat16),
            jax.ShapeDtypeStruct((rows, qwidth), jnp.bfloat16),
            jax.ShapeDtypeStruct((rows, kwidth), jnp.bfloat16),
        ],
        compiler_params=params(48),
        cost_estimate=cost(2 * rows * width * (qwidth + kwidth), 2 * width * (qwidth + kwidth) + 8 * rows * width),
        name="project",
    )(inputs, gain, w_qkv, bias, cosine, sine)


def spread_body(own, rows, whole, rows_x, rows_y, rows_d, sent, landed, kept):
    me, plane = lax.axis_index("gy"), lax.axis_index("gx")
    core = me + 1 - 2 * lax.rem(me, 2)
    along_x = me + 2 - 4 * lax.rem(me // 2, 2)
    along_y = me + 4 - 8 * (me // 4)
    across = along_x + 4 - 8 * (along_x // 4)
    places = [lax.rem(plane + 4 - k, 4) for k in range(4)]
    ahead = [lax.rem(plane + k, 4) for k in range(4)]
    barrier = pltpu.get_barrier_semaphore()
    peers = [{"gy": core}, {"gy": along_x}, {"gy": along_y}] + [{"gx": ahead[k]} for k in (1, 2, 3)]
    for peer in peers:
        pl.semaphore_signal(barrier, inc=1, device_id=peer, device_id_type=pl.DeviceIdType.MESH)
    pl.semaphore_wait(barrier, len(peers))
    copies = []

    def send(source, target, peer):
        copy = pltpu.make_async_remote_copy(
            source,
            target,
            sent.at[len(copies)],
            landed.at[len(copies)],
            device_id=peer,
            device_id_type=pl.DeviceIdType.MESH,
        )
        copies.append(copy)
        copy.start()
        return copy

    to_core, to_x, to_y = peers[:3]
    from_z = [send(own, whole.at[plane, me], peers[2 + k]) for k in (1, 2, 3)]
    local = pltpu.make_async_copy(own, whole.at[plane, me], kept)
    local.start()
    from_x, from_y, from_d, from_core = [], [], [], []
    for k in range(4):
        block = whole.at[places[k], me]
        source = own if k == 0 else block
        if k > 0:
            from_z[k - 1].wait_recv()
        from_x.append(send(source, block, to_x))
        from_y.append(send(source, block, to_y))
        from_core.append(send(source, block, to_core))
    moved_x, moved_y = send(rows, rows_x, to_x), send(rows, rows_y, to_y)
    for k in range(4):
        block_x, block_y = whole.at[places[k], along_x], whole.at[places[k], along_y]
        from_x[k].wait_recv()
        if k < 2:
            from_d.append(send(block_x, block_x, to_y))
        from_core.append(send(block_x, block_x, to_core))
        from_y[k].wait_recv()
        if k >= 2:
            from_d.append(send(block_y, block_y, to_x))
        from_core.append(send(block_y, block_y, to_core))
    for k in range(4):
        block = whole.at[places[k], across]
        from_d[k].wait_recv()
        from_core.append(send(block, block, to_core))
    half = rows.shape[0] // 2
    first, second = pl.ds(0, half), pl.ds(half, half)
    moved_x.wait_recv()
    moved_d = [send(rows_x.at[first], rows_d.at[first], to_y)]
    moved_y.wait_recv()
    moved_d.append(send(rows_y.at[second], rows_d.at[second], to_x))
    for copy in from_core + moved_d:
        copy.wait_recv()
    for copy in copies:
        copy.wait_send()
    local.wait()


def spread(own, rows):
    deep, wide = own.shape
    anywhere = pl.BlockSpec(memory_space=pl.ANY)
    whole, *others = pl.pallas_call(
        spread_body,
        in_specs=[anywhere] * 2,
        out_specs=[anywhere] * 4,
        out_shape=[jax.ShapeDtypeStruct((4, 8, deep, wide), own.dtype)]
        + [jax.ShapeDtypeStruct(rows.shape, rows.dtype)] * 3,
        scratch_shapes=[
            pltpu.SemaphoreType.DMA((35,)),
            pltpu.SemaphoreType.DMA((35,)),
            pltpu.SemaphoreType.DMA,
        ],
        compiler_params=pltpu.CompilerParams(collective_id=0, has_side_effects=True),
        cost_estimate=cost(0, 300 * 1024 * 1024),
        name="spread",
    )(own, rows)
    return whole.reshape(32 * deep, wide), others


def finish_body(wide_ref, out_ref, mine_ref, sent_ref, *refs):
    results, scratch = refs[:3], refs[3:]
    kept, got_core, got_first, got_second, got_ring = [scratch[i : i + 2] for i in range(0, 10, 2)]
    units, got_units, units_ring, units_moving, sent, landed, local = scratch[10:]
    me, plane = lax.axis_index("gy"), lax.axis_index("gx")
    core, x, y = lax.rem(me, 2), lax.rem(me // 2, 2), me // 4
    places = [lax.rem(plane + 4 - s, 4) for s in range(4)]
    peers = peers_of()
    full = jnp.float32
    greet((CORE, ALONG_X, ALONG_Y, RING, RING + 1))
    copies, loads = [], []

    def send(source, target, bits):
        copy = pltpu.make_async_remote_copy(
            source,
            target,
            sent.at[len(copies)],
            landed.at[len(copies)],
            device_id=peers[bits],
            device_id_type=pl.DeviceIdType.MESH,
        )
        copies.append(copy)
        copy.start()
        return copy

    def load(source, target):
        copy = pltpu.make_async_copy(source, target, local.at[len(loads)])
        loads.append(copy)
        copy.start()
        return copy

    inputs = (wide_ref, out_ref)
    core_copies = [send(sent_ref, got_units, CORE)]
    core_copies += [send(inputs[i].at[:, :, :, 1 - core], got_core[i], CORE) for i in range(2)]
    held = [load(mine_ref, units)]
    held += [load(inputs[i].at[:, :, :, core], kept[i]) for i in range(2)]

    core_copies[0].wait_recv()
    held[0].wait()

    @pl.loop(0, 4)
    def _(p):
        units[p] += got_units[p]

    units_copy = send(units.at[places[1]], units_ring.at[0], RING)
    steps = []
    for i in range(2):
        core_copies[1 + i].wait_recv()
        held[1 + i].wait()

        @pl.loop(0, 4)
        def _(p):
            for a in range(2):
                for b in range(2):
                    kept[i][p, a, b] += got_core[i][p, a, b]

        middle = kept[i].shape[-1] // 256 * 128
        first, second = pl.ds(0, middle), pl.ds(middle, kept[i].shape[-1] - middle)
        steps.append((
            send(kept[i].at[:, :, 1 - x, :, first], got_first[i].at[:, :, :, first], ALONG_X),
            send(kept[i].at[:, 1 - y, :, :, second], got_first[i].at[:, :, :, second], ALONG_Y),
            first,
            second,
        ))
    units_copy.wait_recv()
    units_moving[0] = units[places[2]] + units_ring[0]
    units_copy = send(units_moving.at[0], units_ring.at[1], RING)
    nexts = []
    for i in range(2):
        first_copy, second_copy, first, second = steps[i]
        first_copy.wait_recv()

        @pl.loop(0, 4)
        def _(p):
            for a in range(2):
                kept[i][p, a, x, :, first] += got_first[i][p, a, :, first]

        third_copy = send(kept[i].at[:, 1 - y, x, :, first], got_second[i].at[:, :, first], ALONG_Y)
        second_copy.wait_recv()

        @pl.loop(0, 4)
        def _(p):
            for b in range(2):
                kept[i][p, y, b, :, second] += got_first[i][p, b, :, second]

        nexts.append((third_copy, send(kept[i].at[:, y, 1 - x, :, second], got_second[i].at[:, :, second], ALONG_X)))
    units_copy.wait_recv()
    units_moving[1] = units[places[3]] + units_ring[1]
    units_copy = send(units_moving.at[1], units_ring.at[2], RING)
    ring_copies = []
    for i in range(2):
        for copy in nexts[i]:
            copy.wait_recv()

        @pl.loop(0, 4)
        def _(p):
            kept[i][p, y, x] += got_second[i][p]

        for k, bits in ((1, RING), (2, RING + 1), (3, -RING)):
            there = lax.rem(plane + k, 4)
            ring_copies.append(send(kept[i].at[there, y, x], got_ring[i].at[k - 1], bits))
    for i in range(2):
        total = kept[i][plane, y, x].astype(full)
        for k in range(3):
            ring_copies[3 * i + k].wait_recv()
            total = total + got_ring[i][k].astype(full)
        results[i][...] = total
    units_copy.wait_recv()
    results[2][...] = units[places[0]].astype(full) + units_ring[2].astype(full)
    for copy in copies:
        copy.wait_send()


def finish(wide, out, mine, sent, collective):
    low, full = jnp.bfloat16, jnp.float32
    deep = wide.shape[0] // 32
    wide, out = (a.reshape(4, 2, 2, 2, deep, a.shape[1]) for a in (wide, out))
    columns = (wide.shape[-1], out.shape[-1])
    block = mine.shape[1:]
    anywhere = pl.BlockSpec(memory_space=pl.ANY)
    inside = pl.BlockSpec(memory_space=pltpu.VMEM)

    def pairs(*lead):
        return [pltpu.VMEM((*lead, deep, c), low) for c in columns]

    return pl.pallas_call(
        finish_body,
        in_specs=[anywhere] * 4,
        out_specs=[inside] * 3,
        out_shape=[jax.ShapeDtypeStruct((deep, c), full) for c in columns] + [jax.ShapeDtypeStruct(block, full)],
        scratch_shapes=[
            *pairs(4, 2, 2),
            *pairs(4, 2, 2),
            *pairs(4, 2),
            *pairs(4),
            *pairs(3),
            pltpu.VMEM((4, *block), low),
            pltpu.VMEM((4, *block), low),
            pltpu.VMEM((3, *block), low),
            pltpu.VMEM((2, *block), low),
            pltpu.SemaphoreType.DMA((20,)),
            pltpu.SemaphoreType.DMA((20,)),
            pltpu.SemaphoreType.DMA((3,)),
        ],
        compiler_params=pltpu.CompilerParams(
            vmem_limit_bytes=56 * 1024 * 1024, collective_id=collective, has_side_effects=True
        ),
        cost_estimate=cost(0, 200 * 1024 * 1024),
        name="finish",
    )(wide, out, mine, sent)


def swap(array, bits):
    return lax.ppermute(array, "gy", [(i, i ^ bits) for i in range(8)])


def pick(array, index):
    return lax.dynamic_index_in_dim(array, index, 0, keepdims=False)


def after(array, *earlier):
    return lax.optimization_barrier((array, *earlier))[0]


def pair_rows(pair, core):
    kept, got = pick(pair, core), swap(pick(pair, 1 - core), CORE)
    return jnp.where(core == 0, jnp.concatenate([kept, got]), jnp.concatenate([got, kept]))


def unpair_rows(rows, core):
    half = rows.shape[0] // 2
    kept = lax.dynamic_slice_in_dim(rows, core * half, half, 0)
    got = swap(lax.dynamic_slice_in_dim(rows, (1 - core) * half, half, 0), CORE)
    return jnp.where(core == 0, jnp.stack([kept, got]), jnp.stack([got, kept]))


def plane_order(blocks, chip):
    rows = blocks[0].shape[0]
    whole = jnp.zeros((4 * rows,) + blocks[0].shape[1:], blocks[0].dtype)
    for index, block in enumerate(blocks):
        whole = lax.dynamic_update_slice_in_dim(whole, block, (chip ^ index) * rows, 0)
    return whole


def on_core(
    tokens,
    cotangent,
    segment,
    parent,
    w_qkv,
    qkv_bias,
    w_out,
    gain_attn,
    gain_ffn,
    w_gate,
    w_up,
    w_down,
):
    low, full = jnp.bfloat16, jnp.float32
    me = lax.axis_index("gy")
    plane = lax.axis_index("gx")
    core, chip = me % 2, me // 2
    rows, width = 2 * tokens.shape[1], tokens.shape[2]
    slot_len = segment.shape[1]
    own_units = w_gate.shape[1]
    pad_units = -(-own_units // 384) * 384
    qwidth, kwidth = HEADS * HEAD, KV_HEADS * HEAD
    offset = chip * rows

    nb, ng = qkv_bias.shape[0], gain_attn.shape[0]
    packed = jnp.concatenate([qkv_bias, gain_attn, gain_ffn]).reshape(-1, 1)
    packed = jnp.pad(packed, ((0, 4 * ng - packed.shape[0]), (0, 0))).reshape(4, ng).T
    packed = jnp.pad(packed, ((0, 0), (0, HEAD - 4)))
    attn_own = jnp.concatenate([w_qkv, w_out.T, packed], axis=1)

    inputs_low = pair_rows(tokens, core)
    grad_low = pair_rows(cotangent, core)

    seg_tree = pick(segment, core)
    valid, upper_one, upper_two, depth_pos = tree_tables(seg_tree, pick(parent, core))
    places = jnp.arange(slot_len, dtype=jnp.int32)

    def take_own(array):
        return lax.dynamic_slice_in_dim(array, offset, rows, 0)

    cosine, sine = rotation(take_own(depth_pos), HEAD)
    sine = sine * jnp.where(jnp.arange(HEAD) < HEAD // 2, -1.0, 1.0)

    more = pad_units - own_units
    shards = [jnp.pad(w, ((0, 0), (0, more))) for w in (w_gate, w_up, w_down.T)]
    weights = [lax.all_gather(w, "gx", axis=0, tiled=True) for w in shards]
    attn_all, cotan_others = spread(after(attn_own, inputs_low, cosine, sine), grad_low)
    cotan_blocks = [grad_low] + cotan_others
    qwide = qwidth + 2 * kwidth
    small = attn_all[:, qwide + width :].reshape(32, ng, HEAD)[:, :, :4].transpose(0, 2, 1).reshape(32, 4 * ng)
    small = small.astype(full)
    bias_full = small[:, :nb].reshape(1, -1)
    gain_one = small[:, nb : nb + ng].reshape(1, -1)
    gain_two = small[:, nb + ng : nb + 2 * ng].reshape(1, -1)
    out_turned = attn_all[:, qwide : qwide + width]

    normed_one, query, keyval_own = project(inputs_low, gain_one, attn_all, bias_full, cosine, sine)
    mask = allowed(
        after(take_own(seg_tree), keyval_own), take_own(upper_one), take_own(upper_two), take_own(places), seg_tree, valid, places
    )
    qblocks, kblocks = rows // QUERY_TILE, slot_len // KEY_TILE
    active = mask.reshape(qblocks, QUERY_TILE, kblocks, KEY_TILE).any(axis=(1, 3))
    block_count = active.sum(axis=1).astype(jnp.int32)
    rank = jnp.cumsum(active.astype(jnp.int32), axis=1) - 1
    numbers = jnp.arange(kblocks, dtype=jnp.int32)
    hit = active[:, :, None] & (rank[:, :, None] == numbers[None, None, :])
    block_list = jnp.sum(jnp.where(hit, numbers[None, :, None], 0), axis=1).astype(jnp.int32)
    mask_bias = jnp.where(mask.T, 0.0, NEGATIVE).astype(low)

    keyval = plane_order([keyval_own] + [swap(keyval_own, bits) for bits in OTHERS], chip)
    other_weights = [swap(after(w, keyval), CORE) for w in weights[:2]]
    heads_out, lse = attend_fast(block_list, block_count, query, keyval, mask_bias)
    inputs = inputs_low.astype(full)
    resid = inputs + lax.dot_general(heads_out, out_turned, (((1,), (1,)), ((), ())), preferred_element_type=full)
    unit_two, inverse_two, normed_two = norm_parts(resid, gain_two)

    other_weights.append(swap(after(weights[2], heads_out), CORE))
    pieces = weights + other_weights
    half = rows // 2
    first, second = (0, half), (half, half)
    own, (normed_x, normed_y) = ffn_block(
        normed_two, cotan_blocks[0], pieces, 1, [whole_side(normed_two, ALONG_X), whole_side(normed_two, ALONG_Y)]
    )
    passed_on = [(normed_x, first, first, ALONG_Y), (normed_y, second, second, ALONG_X)]
    near_x, (normed_d,) = ffn_block(normed_x, cotan_blocks[1], pieces, 2, [passed_on])
    near_y, (back_x,) = ffn_block(
        after(normed_y, near_x[4]), cotan_blocks[2], pieces, 3, [rows_side(near_x[4], 0, 512, ALONG_X)]
    )
    far, (back_y, back_x_end) = ffn_block(
        normed_d,
        cotan_blocks[3],
        pieces,
        4,
        [rows_side(near_y[4], 0, 512, ALONG_Y), rows_side(near_x[4], 512, rows - 512, ALONG_X)],
    )
    normed_blocks = [normed_two, normed_x, normed_y, normed_d]
    hidden_b, gate_b, up_b, out_b, back_b = zip(own, near_x, near_y, far)

    (down_mine, down_sent), (back_d,) = wgrad(hidden_b, cotan_blocks, 4, 5, [rows_side(back_b[3], 0, 384, ACROSS)])
    (gate_mine, gate_sent), (down_got, back_d_end, back_y_end) = wgrad(
        gate_b,
        normed_blocks,
        4,
        6,
        [
            whole_side(down_sent, CORE),
            rows_side(after(back_b[3], back_d), 384, rows - 384, ACROSS),
            rows_side(after(back_b[2], back_d), 512, rows - 512, ALONG_Y),
        ],
    )
    gate_got = swap(gate_sent, CORE)
    down_sum = down_mine.astype(full) + down_got.astype(full)
    back_x, back_y, back_d = (
        jnp.concatenate(pair)
        for pair in ((back_x, back_x_end), (back_y, back_y_end), (back_d, back_d_end))
    )

    grad_normed_two = sum(after(b, gate_sent).astype(full) for b in (back_b[0], back_x, back_y, back_d))
    back_two, grad_gain_two = norm_back(grad_normed_two, unit_two, inverse_two, gain_two)
    grad_resid = grad_low.astype(full) + back_two
    grad_branch = grad_resid.astype(low)
    grad_heads = jnp.dot(grad_branch, out_turned, preferred_element_type=full).astype(low)
    grad_wout = jnp.dot(grad_branch.T, heads_out, preferred_element_type=full).astype(low)
    out_got = [swap(after(b, grad_normed_two), bits) for b, bits in zip(out_b[1:], OTHERS)]
    gate_sum = gate_mine.astype(full) + gate_got.astype(full)
    both = jnp.concatenate([down_sum, gate_sum], axis=1).astype(low)
    grad_heads = after(grad_heads, grad_wout, both)
    both = lax.psum_scatter(both, "gx", scatter_dimension=0, tiled=True)[0].astype(full)
    grad_down, grad_wgate = both[:own_units], both[pad_units : pad_units + own_units].T
    query_lin, keyval_part = attend_back_fast(
        block_list, block_count, query, keyval, mask_bias, lse, heads_out, grad_heads, cosine, sine
    )

    parts = [lax.dynamic_slice_in_dim(keyval_part, (chip ^ i) * rows, rows, 0) for i in range(4)]
    (up_mine, up_sent), others = wgrad(
        up_b, normed_blocks, 4, 7, [whole_side(part, bits) for part, bits in zip(parts[1:], OTHERS)]
    )

    keyval_grad = sum(part.astype(full) for part in (parts[0], *others))
    keys_grad = keyval_grad[:, :kwidth].reshape(rows, KV_HEADS, HEAD)
    keys_lin = keys_grad * cosine[:, None, :] - jnp.roll(keys_grad, HEAD // 2, axis=-1) * sine[:, None, :]
    keyval_lin = jnp.concatenate([keys_lin.reshape(rows, kwidth), keyval_grad[:, kwidth:]], axis=1).astype(low)
    grad_linear = jnp.concatenate([query_lin, keyval_lin], axis=1)
    grad_wqkv = jnp.dot(normed_one.T, grad_linear, preferred_element_type=full).astype(low)
    grad_bias = jnp.sum(grad_linear.astype(full), axis=0)
    grad_normed_one = jnp.dot(grad_linear, attn_all[:, :qwide].T, preferred_element_type=full)
    unit_one, inverse_one, _ = norm_parts(inputs, gain_one)
    back_one, grad_gain_one = norm_back(grad_normed_one, unit_one, inverse_one, gain_one)
    grad_tokens = unpair_rows((grad_resid + back_one).astype(low), core)
    ffn_out = sum(after(b, query_lin).astype(full) for b in [out_b[0]] + out_got)
    layer_out = unpair_rows((resid + ffn_out).astype(low), core)

    packed = jnp.concatenate(
        [grad_bias.reshape(32, nb), grad_gain_one.reshape(32, ng), grad_gain_two.reshape(32, ng)], axis=1
    )
    packed = jnp.pad(packed, ((0, 0), (0, 4 * ng - packed.shape[1]))).reshape(32, 4, ng).transpose(0, 2, 1)
    packed = jnp.pad(packed.reshape(32 * ng, 4), ((0, 0), (0, HEAD - 4))).astype(low)
    wide, grad_wout, grad_wup = finish(
        jnp.concatenate([grad_wqkv, packed], axis=1), grad_wout, up_mine, up_sent, 8
    )
    grad_wqkv, grad_wout = wide[:, :qwide], grad_wout.T
    small = wide[:, qwide : qwide + 4].T.reshape(-1)
    grad_wup = grad_wup.T[:, :own_units]
    return (
        layer_out,
        grad_tokens,
        grad_wqkv,
        small[:nb],
        grad_wout,
        small[nb : nb + ng],
        small[nb + ng : nb + 2 * ng],
        grad_wgate,
        grad_wup,
        grad_down,
    )


def solution(mesh):
    in_specs = (
        P("gx", "gy", None),
        P("gx", "gy", None),
        P("gx", None),
        P("gx", None),
        P(("gx", "gy"), None),
        P(("gx", "gy")),
        P(None, ("gx", "gy")),
        P(("gx", "gy")),
        P(("gx", "gy")),
        P("gx", "gy"),
        P("gx", "gy"),
        P("gy", "gx"),
    )
    out_specs = (
        P("gx", "gy", None),
        P("gx", "gy", None),
        P(("gx", "gy"), None),
        P(("gx", "gy")),
        P(None, ("gx", "gy")),
        P(("gx", "gy")),
        P(("gx", "gy")),
        P("gx", "gy"),
        P("gx", "gy"),
        P("gy", "gx"),
    )
    return jax.shard_map(
        on_core if tuple(mesh.shape.values()) == (4, 8) else on_device,
        mesh=mesh,
        in_specs=in_specs,
        out_specs=out_specs,
        check_vma=False,
    )
```

```python
from functools import reduce
import math

import jax
import jax.numpy as jnp
from jax import lax
from jax.experimental import pallas as pl
from jax.experimental.pallas import tpu as pltpu
from jax.sharding import PartitionSpec as P

HEADS = 12
KV_HEADS = 2
HEAD = 128

QUERY_TILE = 128
KEY_TILE = 256
ROW_TILE = 128
BRANCH_CUTS = (4, 3)
FFN_CHUNK = 768
FFN_PARTS = 2
WG_TILE = 384
PACE = 1.0
LOG2E = 1.0 / math.log(2.0)

CORE, ALONG_X, ALONG_Y, ACROSS = 1, 2, 4, 6
OTHERS = (ALONG_X, ALONG_Y, ACROSS)
RING = 8


EPS = 1e-06
THETA = 1000000.0
NEGATIVE = -1e30


def tree_tables(segment, parent):
    slot_len = segment.shape[0]
    seg_count = parent.shape[0]
    places = jnp.arange(slot_len, dtype=jnp.int32)
    labels = jnp.arange(seg_count, dtype=jnp.int32)
    member = segment[:, None] == labels[None, :]
    valid = segment >= 0
    first = jnp.min(jnp.where(member, places[:, None], slot_len), axis=0)
    length = jnp.sum(member.astype(jnp.int32), axis=0)
    parent_hit = parent[:, None] == labels[None, :]
    grand = jnp.sum(jnp.where(parent_hit, parent[None, :], 0), axis=1)
    grand_hit = grand[:, None] == labels[None, :]
    parent_len = jnp.sum(jnp.where(parent_hit, length[None, :], 0), axis=1)
    grand_len = jnp.sum(jnp.where(grand_hit, length[None, :], 0), axis=1)
    base = jnp.where(parent != labels, parent_len, 0) + jnp.where(grand != parent, grand_len, 0)

    def lookup(table):
        return jnp.sum(jnp.where(member, table[None, :], 0), axis=1)

    upper_one = jnp.where(valid, lookup(parent), -2)
    upper_two = jnp.where(valid, lookup(grand), -2)
    depth_pos = jnp.where(valid, places - lookup(first) + lookup(base), 0)
    return (valid, upper_one, upper_two, depth_pos)


def allowed(seg_query, upper_one, upper_two, place_query, seg_keys, valid_keys, place_keys):
    related = (seg_keys[None, :] == seg_query[:, None]) | (seg_keys[None, :] == upper_one[:, None])
    related = related | (seg_keys[None, :] == upper_two[:, None])
    earlier = place_keys[None, :] <= place_query[:, None]
    return related & earlier & valid_keys[None, :] | (place_keys[None, :] == place_query[:, None])


def rotation(depth_pos, width):
    half = width // 2
    freqs = jnp.exp(jnp.arange(half, dtype=jnp.float32) * (-2.0 * math.log(THETA) / width))
    angle = depth_pos.astype(jnp.float32)[:, None] * freqs[None, :]
    cosine = jnp.concatenate([jnp.cos(angle), jnp.cos(angle)], axis=1)
    sine = jnp.concatenate([jnp.sin(angle), jnp.sin(angle)], axis=1)
    return (cosine, sine)


def turn(heads, cosine, sine):
    half = heads.shape[-1] // 2
    swapped = jnp.concatenate([-heads[..., half:], heads[..., :half]], axis=-1)
    return heads * cosine[:, None, :] + swapped * sine[:, None, :]


def norm_parts(values, gain):
    inverse = lax.rsqrt(jnp.mean(values * values, axis=-1, keepdims=True) + EPS)
    unit = values * inverse
    return (unit, inverse, (unit * gain).astype(jnp.bfloat16))


def norm_back(grad_normed, unit, inverse, gain):
    scaled = grad_normed * gain
    back = inverse * (scaled - unit * jnp.mean(scaled * unit, axis=-1, keepdims=True))
    return (back, jnp.sum(grad_normed * unit, axis=0))


def masked_scores(group_query, group_keys, mask, scale):
    scores = (
        jnp.einsum("rhd,kd->hrk", group_query, group_keys, preferred_element_type=jnp.float32)
        * scale
    )
    return jnp.where(mask[None], scores, NEGATIVE)


def attend(query_low, keys_all, values_all, mask, scale):
    group = HEADS // KV_HEADS
    pieces = []
    totals = []
    for head_group in range(KV_HEADS):
        group_query = query_low[:, head_group * group : (head_group + 1) * group, :]
        columns = slice(head_group * HEAD, (head_group + 1) * HEAD)
        scores = masked_scores(group_query, keys_all[:, columns], mask, scale)
        top_score = jnp.max(scores, axis=-1, keepdims=True)
        expo = jnp.exp(scores - top_score)
        denom = jnp.sum(expo, axis=-1, keepdims=True)
        probs_low = (expo / denom).astype(jnp.bfloat16)
        pieces.append(
            jnp.einsum(
                "hrk,kd->rhd", probs_low, values_all[:, columns], preferred_element_type=jnp.float32
            )
        )
        totals.append(top_score + jnp.log(denom))
    return (jnp.concatenate(pieces, axis=1), totals)


def attend_back(query_low, keys_all, values_all, mask, totals, grad_heads, scale):
    group = HEADS // KV_HEADS
    grad_query, grad_keys, grad_values = ([], [], [])
    for head_group in range(KV_HEADS):
        heads_sel = slice(head_group * group, (head_group + 1) * group)
        columns = slice(head_group * HEAD, (head_group + 1) * HEAD)
        group_query = query_low[:, heads_sel, :]
        group_keys = keys_all[:, columns]
        group_grad = grad_heads[:, heads_sel, :]
        scores = masked_scores(group_query, group_keys, mask, scale)
        probs = jnp.exp(scores - totals[head_group])
        probs_low = probs.astype(jnp.bfloat16)
        grad_values.append(
            jnp.einsum("hrk,rhd->kd", probs_low, group_grad, preferred_element_type=jnp.float32)
        )
        grad_probs = jnp.einsum(
            "rhd,kd->hrk", group_grad, values_all[:, columns], preferred_element_type=jnp.float32
        )
        grad_scores = (
            probs * (grad_probs - jnp.sum(probs * grad_probs, axis=-1, keepdims=True))
        ).astype(jnp.bfloat16)
        grad_query.append(
            jnp.einsum("hrk,kd->rhd", grad_scores, group_keys, preferred_element_type=jnp.float32)
            * scale
        )
        grad_keys.append(
            jnp.einsum("hrk,rhd->kd", grad_scores, group_query, preferred_element_type=jnp.float32)
            * scale
        )
    return (
        jnp.concatenate(grad_query, axis=1),
        jnp.concatenate(grad_keys, axis=1),
        jnp.concatenate(grad_values, axis=1),
    )


def add_trees(left, right):
    return jax.tree.map(jnp.add, left, right)


def on_device(
    tokens,
    cotangent,
    segment,
    parent,
    w_qkv,
    qkv_bias,
    w_out,
    gain_attn,
    gain_ffn,
    w_gate,
    w_up,
    w_down,
):
    micro = tokens.shape[0]
    row_count = tokens.shape[1]
    slot_len = segment.shape[1]
    qwidth = HEADS * HEAD
    kwidth = KV_HEADS * HEAD
    scale = 1.0 / math.sqrt(HEAD)
    offset = lax.axis_index("gy") * row_count
    place_all = jnp.arange(slot_len, dtype=jnp.int32)
    place_own = offset + jnp.arange(row_count, dtype=jnp.int32)
    outputs, input_grads, attn_list, ffn_list = ([], [], [], [])
    for micro_index in range(micro):
        attn_full = (
            lax.all_gather(w_qkv, ("gx", "gy"), axis=0, tiled=True),
            lax.all_gather(qkv_bias, ("gx", "gy"), axis=0, tiled=True),
            lax.all_gather(w_out, ("gx", "gy"), axis=1, tiled=True),
            lax.all_gather(gain_attn, ("gx", "gy"), axis=0, tiled=True),
            lax.all_gather(gain_ffn, ("gx", "gy"), axis=0, tiled=True),
        )
        ffn_full = (
            lax.all_gather(w_gate, "gx", axis=0, tiled=True),
            lax.all_gather(w_up, "gx", axis=0, tiled=True),
            lax.all_gather(w_down, "gx", axis=1, tiled=True),
        )
        qkv_full, bias_full, out_full, gain_one_full, gain_two_full = attn_full
        gate_full, up_full, down_full = ffn_full
        gain_one = gain_one_full.astype(jnp.float32)
        gain_two = gain_two_full.astype(jnp.float32)
        seg_tree = segment[micro_index]
        valid, upper_one, upper_two, depth_pos = tree_tables(seg_tree, parent[micro_index])

        def take_own(array):
            return lax.dynamic_slice_in_dim(array, offset, row_count, 0)

        mask = allowed(
            take_own(seg_tree),
            take_own(upper_one),
            take_own(upper_two),
            place_own,
            seg_tree,
            valid,
            place_all,
        )
        cosine, sine = rotation(take_own(depth_pos), HEAD)
        inputs = tokens[micro_index].astype(jnp.float32)
        unit_one, inverse_one, normed_one = norm_parts(inputs, gain_one)
        linear = jnp.dot(
            normed_one, qkv_full, preferred_element_type=jnp.float32
        ) + bias_full.astype(jnp.float32)
        query_low = turn(linear[:, :qwidth].reshape(row_count, HEADS, HEAD), cosine, sine).astype(
            jnp.bfloat16
        )
        keys_low = turn(
            linear[:, qwidth : qwidth + kwidth].reshape(row_count, KV_HEADS, HEAD), cosine, sine
        )
        keys_low = keys_low.reshape(row_count, kwidth).astype(jnp.bfloat16)
        values_low = linear[:, qwidth + kwidth :].astype(jnp.bfloat16)
        keys_all, values_all = (
            lax.all_gather(keys_low, "gy", axis=0, tiled=True),
            lax.all_gather(values_low, "gy", axis=0, tiled=True),
        )
        heads_raw, totals = attend(query_low, keys_all, values_all, mask, scale)
        heads_out = heads_raw.reshape(row_count, qwidth).astype(jnp.bfloat16)
        resid = inputs + jnp.dot(heads_out, out_full, preferred_element_type=jnp.float32)
        unit_two, inverse_two, normed_two = norm_parts(resid, gain_two)
        normed_all = lax.all_gather(normed_two, "gy", axis=0, tiled=True)
        gate = jnp.dot(normed_all, gate_full, preferred_element_type=jnp.float32)
        upward = jnp.dot(normed_all, up_full, preferred_element_type=jnp.float32)
        sigma = jax.nn.sigmoid(gate)
        swish = gate * sigma
        hidden = (swish * upward).astype(jnp.bfloat16)
        ffn_own = lax.psum_scatter(
            jnp.dot(hidden, down_full, preferred_element_type=jnp.float32),
            "gy",
            scatter_dimension=0,
            tiled=True,
        )
        outputs.append((resid + ffn_own).astype(jnp.bfloat16))
        grad_low = cotangent[micro_index]
        grad_all = lax.all_gather(grad_low, "gy", axis=0, tiled=True)
        grad_hidden = jnp.dot(grad_all, down_full.T, preferred_element_type=jnp.float32)
        grad_down = jnp.dot(hidden.T, grad_all, preferred_element_type=jnp.float32)
        grad_gate = (grad_hidden * upward * sigma * (1.0 + gate * (1.0 - sigma))).astype(
            jnp.bfloat16
        )
        grad_up = (grad_hidden * swish).astype(jnp.bfloat16)
        grad_wgate = jnp.dot(normed_all.T, grad_gate, preferred_element_type=jnp.float32)
        grad_wup = jnp.dot(normed_all.T, grad_up, preferred_element_type=jnp.float32)
        grad_normed_two = lax.psum_scatter(
            jnp.dot(grad_gate, gate_full.T, preferred_element_type=jnp.float32)
            + jnp.dot(grad_up, up_full.T, preferred_element_type=jnp.float32),
            "gy",
            scatter_dimension=0,
            tiled=True,
        )
        back_two, grad_gain_two = norm_back(grad_normed_two, unit_two, inverse_two, gain_two)
        grad_resid = grad_low.astype(jnp.float32) + back_two
        grad_branch = grad_resid.astype(jnp.bfloat16)
        grad_wout = jnp.dot(heads_out.T, grad_branch, preferred_element_type=jnp.float32)
        grad_heads = jnp.dot(grad_branch, out_full.T, preferred_element_type=jnp.float32).astype(
            jnp.bfloat16
        )
        grad_heads = grad_heads.reshape(row_count, HEADS, HEAD)
        grad_query, keys_part, values_part = attend_back(
            query_low, keys_all, values_all, mask, totals, grad_heads, scale
        )
        grad_keys, grad_values = (
            lax.psum_scatter(keys_part, "gy", scatter_dimension=0, tiled=True),
            lax.psum_scatter(values_part, "gy", scatter_dimension=0, tiled=True),
        )
        query_lin = turn(grad_query, cosine, -sine).reshape(row_count, qwidth)
        keys_lin = turn(grad_keys.reshape(row_count, KV_HEADS, HEAD), cosine, -sine).reshape(
            row_count, kwidth
        )
        grad_linear = jnp.concatenate([query_lin, keys_lin, grad_values], axis=1).astype(
            jnp.bfloat16
        )
        grad_wqkv = jnp.dot(normed_one.T, grad_linear, preferred_element_type=jnp.float32)
        grad_bias = jnp.sum(grad_linear.astype(jnp.float32), axis=0)
        grad_normed_one = jnp.dot(grad_linear, qkv_full.T, preferred_element_type=jnp.float32)
        back_one, grad_gain_one = norm_back(grad_normed_one, unit_one, inverse_one, gain_one)
        input_grads.append((grad_resid + back_one).astype(jnp.bfloat16))
        attn_list.append((grad_wqkv, grad_bias, grad_wout, grad_gain_one, grad_gain_two))
        ffn_list.append((grad_wgate, grad_wup, grad_down))
    attn_total = reduce(add_trees, attn_list)
    ffn_total = reduce(add_trees, ffn_list)
    attn_total = (
        lax.psum_scatter(attn_total[0], ("gx", "gy"), scatter_dimension=0, tiled=True),
        lax.psum_scatter(attn_total[1], ("gx", "gy"), scatter_dimension=0, tiled=True),
        lax.psum_scatter(attn_total[2], ("gx", "gy"), scatter_dimension=1, tiled=True),
        lax.psum_scatter(attn_total[3], ("gx", "gy"), scatter_dimension=0, tiled=True),
        lax.psum_scatter(attn_total[4], ("gx", "gy"), scatter_dimension=0, tiled=True),
    )
    ffn_total = (
        lax.psum_scatter(ffn_total[0], "gx", scatter_dimension=0, tiled=True),
        lax.psum_scatter(ffn_total[1], "gx", scatter_dimension=0, tiled=True),
        lax.psum_scatter(ffn_total[2], "gx", scatter_dimension=1, tiled=True),
    )
    layer_out = jnp.stack(outputs, axis=0)
    grad_tokens = jnp.stack(input_grads, axis=0)
    return (
        layer_out,
        grad_tokens,
        attn_total[0],
        attn_total[1],
        attn_total[2],
        attn_total[3],
        attn_total[4],
        ffn_total[0],
        ffn_total[1],
        ffn_total[2],
    )


def dot_nn(left, right):
    return lax.dot_general(left, right, (((1,), (0,)), ((), ())), preferred_element_type=jnp.float32)


def dot_nt(left, right):
    return lax.dot_general(left, right, (((1,), (1,)), ((), ())), preferred_element_type=jnp.float32)


def dot_tn(left, right):
    return lax.dot_general(left, right, (((0,), (0,)), ((), ())), preferred_element_type=jnp.float32)


def cost(flops, moved, trans=0):
    return pl.CostEstimate(flops=int(flops * PACE), bytes_accessed=int(moved * PACE), transcendentals=int(trans * PACE))


def params(mib):
    return pltpu.CompilerParams(vmem_limit_bytes=mib * 1024 * 1024)


def sigmoid(v):
    return 0.5 * jnp.tanh(0.5 * v) + 0.5


def peers_of():
    me, plane = lax.axis_index("gy"), lax.axis_index("gx")
    along_x = me + 2 - 4 * lax.rem(me // 2, 2)
    return {
        CORE: {"gy": me + 1 - 2 * lax.rem(me, 2)},
        ALONG_X: {"gy": along_x},
        ALONG_Y: {"gy": me + 4 - 8 * (me // 4)},
        ACROSS: {"gy": along_x + 4 - 8 * (along_x // 4)},
        RING: {"gx": lax.rem(plane + 1, 4)},
        RING + 1: {"gx": lax.rem(plane + 2, 4)},
        -RING: {"gx": lax.rem(plane + 3, 4)},
    }


def greet(bits_used):
    peers = peers_of()
    barrier = pltpu.get_barrier_semaphore()
    greeted = [bits for bits in bits_used] + [-RING] * (RING in bits_used)
    for bits in greeted:
        pl.semaphore_signal(barrier, inc=1, device_id=peers[bits], device_id_type=pl.DeviceIdType.MESH)
    pl.semaphore_wait(barrier, len(greeted))


def side_copies(sides, sources, targets, sent, landed):
    peers = peers_of()
    copies = []
    for parts, target in zip(sides, targets):
        for _, take, fill, bits in parts:
            copies.append(
                pltpu.make_async_remote_copy(
                    sources[len(copies)].at[pl.ds(*take)],
                    target.at[pl.ds(*fill)],
                    sent.at[len(copies)],
                    landed.at[len(copies)],
                    device_id=peers[bits],
                    device_id_type=pl.DeviceIdType.MESH,
                )
            )
    return copies


def whole_side(array, bits):
    return [(array, (0, array.shape[0]), (0, array.shape[0]), bits)]


def rows_side(array, start, count, bits):
    return [(array, (start, count), (0, count), bits)]


def call_beside(body, sides, collective, operands, grid, in_specs, out_specs, out_shape, scratch_shapes, mib, estimate, name):
    n_in, n_out, n_scratch = len(in_specs), len(out_specs), len(scratch_shapes)
    flat = [part for parts in sides for part in parts]
    bits_used = sorted({part[3] for part in flat})

    def whole_body(*refs):
        ins, refs = refs[:n_in], refs[n_in:]
        sources, refs = refs[: len(flat)], refs[len(flat) :]
        outs, refs = refs[:n_out], refs[n_out:]
        targets, refs = refs[: len(sides)], refs[len(sides) :]
        scratch, refs = refs[:n_scratch], refs[n_scratch:]
        step, last = pl.program_id(0), pl.num_programs(0) - 1
        if flat:

            @pl.when(step == 0)
            def _():
                greet(bits_used)
                for copy in side_copies(sides, sources, targets, *refs):
                    copy.start()

        body(*ins, *outs, *scratch)
        if flat:

            @pl.when(step == last)
            def _():
                for copy in side_copies(sides, sources, targets, *refs):
                    copy.wait()

    anywhere = pl.BlockSpec(memory_space=pl.ANY)
    extra = {"collective_id": collective, "has_side_effects": True} if flat else {}
    results = pl.pallas_call(
        whole_body,
        grid=grid,
        in_specs=list(in_specs) + [anywhere] * len(flat),
        out_specs=list(out_specs) + [anywhere] * len(sides),
        out_shape=list(out_shape)
        + [jax.ShapeDtypeStruct((sum(p[2][1] for p in parts),) + parts[0][0].shape[1:], parts[0][0].dtype) for parts in sides],
        scratch_shapes=list(scratch_shapes) + ([pltpu.SemaphoreType.DMA((len(flat),))] * 2 if flat else []),
        compiler_params=pltpu.CompilerParams(vmem_limit_bytes=mib * 1024 * 1024, **extra),
        cost_estimate=estimate,
        name=name,
    )(*operands, *[part[0] for part in flat])
    return results[:n_out], results[n_out:]


def ffn_copies(chunk, pieces, held, sems):
    units = pieces[0].shape[1]
    tile = FFN_CHUNK // 2
    slot = chunk % 2
    copies = []
    for part in range(2):
        column = chunk * FFN_CHUNK + part * tile
        owner, inside = column // units, column % units
        for kind in range(3):
            copies.append(
                pltpu.make_async_copy(
                    pieces[3 * owner + kind].at[:, pl.ds(inside, tile)],
                    held.at[slot, kind, :, pl.ds(part * tile, tile)],
                    sems.at[slot, part * 3 + kind],
                )
            )
    return copies


def ffn_body(n_ref, c_ref, *refs):
    pieces = refs[:6]
    hid_ref, dg_ref, du_ref, f_ref, dn_ref, f_acc, dn_acc, held, sems = refs[6:]
    step = pl.program_id(0)
    chunks = 2 * pieces[0].shape[1] // FFN_CHUNK

    @pl.when(step == 0)
    def _():
        for copy in ffn_copies(0, pieces, held, sems):
            copy.start()
        f_acc[...] = jnp.zeros_like(f_acc)
        dn_acc[...] = jnp.zeros_like(dn_acc)

    for chunk in range(chunks):

        @pl.when(step == chunk)
        def _():
            if chunk + 1 < chunks:
                for copy in ffn_copies(chunk + 1, pieces, held, sems):
                    copy.start()
            for copy in ffn_copies(chunk, pieces, held, sems):
                copy.wait()

    slot = step % 2
    rows = n_ref.shape[0]
    part = rows // FFN_PARTS
    for index in range(FFN_PARTS):
        take = pl.ds(index * part, part)
        gate = dot_nn(n_ref[take, :], held[slot, 0])
        upward = dot_nn(n_ref[take, :], held[slot, 1])
        sigma = sigmoid(gate)
        swish = gate * sigma
        hidden = (swish * upward).astype(jnp.bfloat16)
        hid_ref[take, :] = hidden
        grad_hidden = dot_nn(c_ref[take, :], held[slot, 2])
        grad_gate = (grad_hidden * upward * sigma * (1.0 + gate * (1.0 - sigma))).astype(jnp.bfloat16)
        grad_up = (grad_hidden * swish).astype(jnp.bfloat16)
        dg_ref[take, :] = grad_gate
        du_ref[take, :] = grad_up
        f_acc[take, :] += dot_nt(hidden, held[slot, 2])
        dn_acc[take, :] += dot_nt(grad_gate, held[slot, 0]) + dot_nt(grad_up, held[slot, 1])

    @pl.when(step == pl.num_programs(0) - 1)
    def _():
        f_ref[...] = f_acc[...].astype(f_ref.dtype)
        dn_ref[...] = dn_acc[...].astype(dn_ref.dtype)


def ffn_block(normed, cotan, pieces, collective, sides=()):
    rows, width = normed.shape
    units = 2 * pieces[0].shape[1]
    chunk = FFN_CHUNK
    whole = pl.BlockSpec((rows, width), lambda j: (0, 0))
    tall = pl.BlockSpec((rows, chunk), lambda j: (0, j))
    low = jnp.bfloat16
    return call_beside(
        ffn_body,
        sides,
        collective,
        (normed, cotan, *pieces),
        (units // chunk,),
        [whole, whole] + [pl.BlockSpec(memory_space=pl.ANY)] * len(pieces),
        [tall, tall, tall, whole, whole],
        [jax.ShapeDtypeStruct((rows, units), low)] * 3 + [jax.ShapeDtypeStruct((rows, width), low)] * 2,
        [pltpu.VMEM((rows, width), jnp.float32)] * 2
        + [pltpu.VMEM((2, 3, width, chunk), low), pltpu.SemaphoreType.DMA((2, len(pieces)))],
        60,
        cost(12 * rows * width * units, 6 * width * units + 6 * rows * (width + units)),
        "ffn_block",
    )


def wgrad_body(per_half, *refs):
    count = (len(refs) - 2) // 2
    total = dot_tn(refs[0][...], refs[count][...])
    for index in range(1, count):
        total = total + dot_tn(refs[index][...], refs[count + index][...])

    def store(out_ref):
        slots, _, wide = out_ref.shape
        for slot in range(slots):
            out_ref[slot] = total[:, slot * wide : (slot + 1) * wide].astype(out_ref.dtype)

    first = pl.program_id(0) < per_half
    pl.when(first)(lambda: store(refs[-2]))
    pl.when(jnp.logical_not(first))(lambda: store(refs[-1]))


def wgrad(lefts, rights, slots, collective, sides=()):
    rows, units = lefts[0].shape
    width = rights[0].shape[1]
    tile = WG_TILE
    per_half = units // 2 // tile
    wide = width // slots
    count = len(lefts)
    return call_beside(
        lambda *refs: wgrad_body(per_half, *refs),
        sides,
        collective,
        (*lefts, *rights),
        (units // tile,),
        [pl.BlockSpec((rows, tile), lambda j: (0, j))] * count
        + [pl.BlockSpec((rows, width), lambda j: (0, 0))] * count,
        [
            pl.BlockSpec((slots, tile, wide), lambda j: (0, jnp.minimum(j, per_half - 1), 0)),
            pl.BlockSpec((slots, tile, wide), lambda j: (0, jnp.maximum(j - per_half, 0), 0)),
        ],
        [jax.ShapeDtypeStruct((slots, units // 2, wide), jnp.bfloat16)] * 2,
        [],
        60,
        cost(2 * count * rows * width * units, 2 * count * rows * (width + units)),
        "ffn_wgrad",
    )


def group_rows(source_ref, group, per_group):
    return jnp.concatenate(
        [source_ref[:, (group * per_group + h) * HEAD : (group * per_group + h + 1) * HEAD] for h in range(per_group)],
        axis=0,
    )


def attend_body(list_ref, count_ref, q_ref, kv_ref, bias_ref, o_ref, lse_ref, qs, acc, top, den):
    block = pl.program_id(0)
    per_group = HEADS // KV_HEADS
    for group in range(KV_HEADS):
        qs[group] = group_rows(q_ref, group, per_group)
    acc[...] = jnp.zeros_like(acc)
    den[...] = jnp.zeros_like(den)
    top[...] = jnp.full_like(top, 2 * NEGATIVE)
    factor = LOG2E / math.sqrt(HEAD)

    def body(n, carry):
        rows = pl.ds(pl.multiple_of(list_ref[block, n] * KEY_TILE, KEY_TILE), KEY_TILE)
        bias = jnp.concatenate([bias_ref[rows, :].astype(jnp.float32)] * per_group, axis=1)
        products = [dot_nt(kv_ref[rows, g * HEAD : (g + 1) * HEAD], qs[g]) for g in range(KV_HEADS)]
        for group in range(KV_HEADS):
            values = kv_ref[rows, (KV_HEADS + group) * HEAD : (KV_HEADS + group + 1) * HEAD]
            scores = products[group] * factor + bias
            old = top[group]
            new = jnp.maximum(old, jnp.max(scores, axis=0, keepdims=True))
            probs = jnp.exp2(scores - new)
            shrink = jnp.exp2(old - new)
            den[group] = den[group] * shrink + jnp.sum(probs, axis=0, keepdims=True)
            acc[group] = acc[group] * shrink + dot_tn(values, probs.astype(jnp.bfloat16))
            top[group] = new
        return carry

    lax.fori_loop(0, count_ref[block], body, 0)
    for group in range(KV_HEADS):
        out = acc[group] / den[group]
        lse_ref[0, group] = top[group] + jnp.log(den[group]) * LOG2E
        for h in range(per_group):
            head = group * per_group + h
            o_ref[:, head * HEAD : (head + 1) * HEAD] = out[:, h * HEAD : (h + 1) * HEAD].T.astype(o_ref.dtype)


def attend_fast(block_list, block_count, query, keyval, bias):
    rows, qwidth = query.shape
    slots = keyval.shape[0]
    blocks = rows // QUERY_TILE
    per_group = HEADS // KV_HEADS
    lanes = per_group * QUERY_TILE
    whole = pl.BlockSpec(keyval.shape, lambda i, a, b: (0, 0))
    tile = pl.BlockSpec((QUERY_TILE, qwidth), lambda i, a, b: (i, 0))
    return pl.pallas_call(
        attend_body,
        grid_spec=pltpu.PrefetchScalarGridSpec(
            num_scalar_prefetch=2,
            grid=(blocks,),
            in_specs=[tile, whole, pl.BlockSpec((slots, QUERY_TILE), lambda i, a, b: (0, i))],
            out_specs=[tile, pl.BlockSpec((1, KV_HEADS, 1, lanes), lambda i, a, b: (i, 0, 0, 0))],
            scratch_shapes=[
                pltpu.VMEM((KV_HEADS, lanes, HEAD), jnp.bfloat16),
                pltpu.VMEM((KV_HEADS, HEAD, lanes), jnp.float32),
                pltpu.VMEM((KV_HEADS, 1, lanes), jnp.float32),
                pltpu.VMEM((KV_HEADS, 1, lanes), jnp.float32),
            ],
        ),
        out_shape=[
            jax.ShapeDtypeStruct((rows, qwidth), jnp.bfloat16),
            jax.ShapeDtypeStruct((blocks, KV_HEADS, 1, lanes), jnp.float32),
        ],
        compiler_params=params(48),
        cost_estimate=cost(2 * rows * slots * qwidth * 2, 4 * slots * rows, HEADS * rows * slots // 2),
        name="tree_attention",
    )(block_list, block_count, query, keyval, bias)


def attend_back_body(
    list_ref, count_ref, q_ref, kv_ref, bias_ref, lse_ref, o_ref, do_ref, cos_ref, sin_ref,
    dq_ref, dkv_ref, qs, dos, delta, dqt, dkv,
):
    block = pl.program_id(0)
    per_group = HEADS // KV_HEADS
    scale = 1.0 / math.sqrt(HEAD)
    factor = LOG2E * scale
    lanes = qs.shape[1]

    @pl.when(block == 0)
    def _():
        dkv[...] = jnp.zeros_like(dkv)

    for group in range(KV_HEADS):
        qs[group] = group_rows(q_ref, group, per_group)
        grads = group_rows(do_ref, group, per_group)
        dos[group] = grads
        both = grads.astype(jnp.float32) * group_rows(o_ref, group, per_group).astype(jnp.float32)
        delta[group] = lax.dot_general(
            jnp.ones((8, HEAD), jnp.float32), both, (((1,), (1,)), ((), ())),
            precision=lax.Precision.HIGHEST, preferred_element_type=jnp.float32,
        )[0:1]
    dqt[...] = jnp.zeros_like(dqt)

    def body(n, carry):
        rows = pl.ds(pl.multiple_of(list_ref[block, n] * KEY_TILE, KEY_TILE), KEY_TILE)
        bias = jnp.concatenate([bias_ref[rows, :].astype(jnp.float32)] * per_group, axis=1)
        for group in range(KV_HEADS):
            kcols = slice(group * HEAD, (group + 1) * HEAD)
            vcols = slice((KV_HEADS + group) * HEAD, (KV_HEADS + group + 1) * HEAD)
            keys = kv_ref[rows, kcols]
            values = kv_ref[rows, vcols]
            scores = dot_nt(keys, qs[group]) * factor + bias
            probs = jnp.exp2(scores - lse_ref[0, group])
            grad_probs = dot_nt(values, dos[group])
            grad_scores = (probs * (grad_probs - delta[group])).astype(jnp.bfloat16)
            dkv[rows, vcols] += dot_nn(probs.astype(jnp.bfloat16), dos[group])
            dkv[rows, kcols] += dot_nn(grad_scores, qs[group])
            dqt[group] += dot_tn(keys, grad_scores)
        return carry

    lax.fori_loop(0, count_ref[block], body, 0)
    cosine, sine = cos_ref[...], sin_ref[...]
    for group in range(KV_HEADS):
        for h in range(per_group):
            head = group * per_group + h
            grad = dqt[group, :, h * HEAD : (h + 1) * HEAD].T * scale
            grad = grad * cosine - pltpu.roll(grad, HEAD // 2, 1) * sine
            dq_ref[:, head * HEAD : (head + 1) * HEAD] = grad.astype(dq_ref.dtype)

    @pl.when(block == pl.num_programs(0) - 1)
    def _():
        kwidth = KV_HEADS * HEAD
        dkv_ref[:, :kwidth] = (dkv[:, :kwidth] * scale).astype(dkv_ref.dtype)
        dkv_ref[:, kwidth:] = dkv[:, kwidth:].astype(dkv_ref.dtype)


def attend_back_fast(block_list, block_count, query, keyval, bias, lse, heads_out, grad_heads, cosine, sine):
    rows, qwidth = query.shape
    slots = keyval.shape[0]
    blocks = rows // QUERY_TILE
    per_group = HEADS // KV_HEADS
    lanes = per_group * QUERY_TILE
    whole = pl.BlockSpec(keyval.shape, lambda i, a, b: (0, 0))
    tile = pl.BlockSpec((QUERY_TILE, qwidth), lambda i, a, b: (i, 0))
    turned = pl.BlockSpec((QUERY_TILE, HEAD), lambda i, a, b: (i, 0))
    return pl.pallas_call(
        attend_back_body,
        grid_spec=pltpu.PrefetchScalarGridSpec(
            num_scalar_prefetch=2,
            grid=(blocks,),
            in_specs=[
                tile,
                whole,
                pl.BlockSpec((slots, QUERY_TILE), lambda i, a, b: (0, i)),
                pl.BlockSpec((1, KV_HEADS, 1, lanes), lambda i, a, b: (i, 0, 0, 0)),
                tile,
                tile,
                turned,
                turned,
            ],
            out_specs=[tile, whole],
            scratch_shapes=[
                pltpu.VMEM((KV_HEADS, lanes, HEAD), jnp.bfloat16),
                pltpu.VMEM((KV_HEADS, lanes, HEAD), jnp.bfloat16),
                pltpu.VMEM((KV_HEADS, 1, lanes), jnp.float32),
                pltpu.VMEM((KV_HEADS, HEAD, lanes), jnp.float32),
                pltpu.VMEM(keyval.shape, jnp.float32),
            ],
        ),
        out_shape=[
            jax.ShapeDtypeStruct((rows, qwidth), jnp.bfloat16),
            jax.ShapeDtypeStruct(keyval.shape, jnp.bfloat16),
        ],
        compiler_params=params(56),
        cost_estimate=cost(5 * rows * slots * qwidth * 2, 8 * slots * rows, HEADS * rows * slots // 2),
        name="tree_attention_back",
    )(block_list, block_count, query, keyval, bias, lse, heads_out, grad_heads, cosine, sine)


def project_body(x_ref, gain_ref, w_ref, b_ref, cos_ref, sin_ref, n_ref, q_ref, kv_ref):
    values = x_ref[...].astype(jnp.float32)
    inverse = lax.rsqrt(jnp.mean(values * values, axis=-1, keepdims=True) + EPS)
    normed = (values * inverse * gain_ref[...]).astype(jnp.bfloat16)
    n_ref[...] = normed
    linear = dot_nn(normed, w_ref[...]) + b_ref[...]
    cosine, sine = cos_ref[...], sin_ref[...]
    for head in range(HEADS + KV_HEADS):
        lane = linear[:, head * HEAD : (head + 1) * HEAD]
        lane = (lane * cosine + pltpu.roll(lane, HEAD // 2, 1) * sine).astype(jnp.bfloat16)
        if head < HEADS:
            q_ref[:, head * HEAD : (head + 1) * HEAD] = lane
        else:
            kv_ref[:, (head - HEADS) * HEAD : (head - HEADS + 1) * HEAD] = lane
    kv_ref[:, KV_HEADS * HEAD :] = linear[:, (HEADS + KV_HEADS) * HEAD :].astype(jnp.bfloat16)


def project(inputs, gain, w_qkv, bias, cosine, sine):
    rows, width = inputs.shape
    qwidth, kwidth = HEADS * HEAD, 2 * KV_HEADS * HEAD
    tile = ROW_TILE
    fixed = lambda i: (0, 0)
    moving = lambda i: (i, 0)
    return pl.pallas_call(
        project_body,
        grid=(rows // tile,),
        in_specs=[
            pl.BlockSpec((tile, width), moving),
            pl.BlockSpec((1, width), fixed),
            pl.BlockSpec((width, qwidth + kwidth), fixed),
            pl.BlockSpec((1, qwidth + kwidth), fixed),
            pl.BlockSpec((tile, HEAD), moving),
            pl.BlockSpec((tile, HEAD), moving),
        ],
        out_specs=[
            pl.BlockSpec((tile, width), moving),
            pl.BlockSpec((tile, qwidth), moving),
            pl.BlockSpec((tile, kwidth), moving),
        ],
        out_shape=[
            jax.ShapeDtypeStruct((rows, width), jnp.bfloat16),
            jax.ShapeDtypeStruct((rows, qwidth), jnp.bfloat16),
            jax.ShapeDtypeStruct((rows, kwidth), jnp.bfloat16),
        ],
        compiler_params=params(48),
        cost_estimate=cost(2 * rows * width * (qwidth + kwidth), 2 * width * (qwidth + kwidth) + 8 * rows * width),
        name="project",
    )(inputs, gain, w_qkv, bias, cosine, sine)


def spread_body(*refs):
    owns, rows, whole, rows_x, rows_y, rows_d, sent, landed, kept = refs[:4], *refs[4:]
    me, plane = lax.axis_index("gy"), lax.axis_index("gx")
    peers = peers_of()
    along_x, along_y, across = (peers[bits]["gy"] for bits in OTHERS)
    places = [lax.rem(plane + 4 - k, 4) for k in range(4)]
    greet((CORE, ALONG_X, ALONG_Y))
    copies = []

    def send(source, target, bits):
        copy = pltpu.make_async_remote_copy(
            source,
            target,
            sent.at[len(copies)],
            landed.at[len(copies)],
            device_id=peers[bits],
            device_id_type=pl.DeviceIdType.MESH,
        )
        copies.append(copy)
        copy.start()
        return copy

    from_x, from_y, from_d, from_core, local = [], [], [], [], []
    for k in range(4):
        block = whole.at[places[k], me]
        from_x.append(send(owns[k], block, ALONG_X))
        from_y.append(send(owns[k], block, ALONG_Y))
        from_core.append(send(owns[k], block, CORE))
        local.append(pltpu.make_async_copy(owns[k], block, kept.at[k]))
        local[k].start()
    moved_x, moved_y = send(rows, rows_x, ALONG_X), send(rows, rows_y, ALONG_Y)
    for k in range(4):
        block_x, block_y = whole.at[places[k], along_x], whole.at[places[k], along_y]
        from_x[k].wait_recv()
        if k < 2:
            from_d.append(send(block_x, block_x, ALONG_Y))
        from_core.append(send(block_x, block_x, CORE))
        from_y[k].wait_recv()
        if k >= 2:
            from_d.append(send(block_y, block_y, ALONG_X))
        from_core.append(send(block_y, block_y, CORE))
    for k in range(4):
        block = whole.at[places[k], across]
        from_d[k].wait_recv()
        from_core.append(send(block, block, CORE))
    half = rows.shape[0] // 2
    first, second = pl.ds(0, half), pl.ds(half, half)
    moved_x.wait_recv()
    moved_d = [send(rows_x.at[first], rows_d.at[first], ALONG_Y)]
    moved_y.wait_recv()
    moved_d.append(send(rows_y.at[second], rows_d.at[second], ALONG_X))
    for copy in from_core + moved_d:
        copy.wait_recv()
    for copy in copies:
        copy.wait_send()
    for copy in local:
        copy.wait()


def spread(owns, rows):
    deep, wide = owns[0].shape
    anywhere = pl.BlockSpec(memory_space=pl.ANY)
    whole, *others = pl.pallas_call(
        spread_body,
        in_specs=[anywhere] * 5,
        out_specs=[anywhere] * 4,
        out_shape=[jax.ShapeDtypeStruct((4, 8, deep, wide), rows.dtype)]
        + [jax.ShapeDtypeStruct(rows.shape, rows.dtype)] * 3,
        scratch_shapes=[
            pltpu.SemaphoreType.DMA((32,)),
            pltpu.SemaphoreType.DMA((32,)),
            pltpu.SemaphoreType.DMA((4,)),
        ],
        compiler_params=pltpu.CompilerParams(collective_id=0, has_side_effects=True),
        cost_estimate=cost(0, 300 * 1024 * 1024),
        name="spread",
    )(*owns, rows)
    return whole.reshape(32 * deep, wide), others


def unit_back(grad_normed, values, gain):
    inverse = lax.rsqrt(jnp.mean(values * values, axis=-1, keepdims=True) + EPS)
    unit = values * inverse
    scaled = grad_normed * gain
    back = inverse * (scaled - unit * jnp.mean(scaled * unit, axis=-1, keepdims=True))
    return back, jnp.sum(grad_normed * unit, axis=0, keepdims=True)


def branch_back_body(own_ref, xa_ref, xb_ref, ya_ref, yb_ref, resid_ref, cot_ref, gain_ref, heads_ref, *refs):
    turned, (resid_out, heads_out, gain_out, weight_out, branch) = refs[:-5], refs[-5:]
    step, full = pl.program_id(0), jnp.float32
    tile = own_ref.shape[0]
    from_x = jnp.where(step < BRANCH_CUTS[0], xa_ref[...].astype(full), xb_ref[...].astype(full))
    from_y = jnp.where(step < BRANCH_CUTS[1], ya_ref[...].astype(full), yb_ref[...].astype(full))
    grad_normed = own_ref[...].astype(full) + from_x + from_y
    back, gain_part = unit_back(grad_normed, resid_ref[...], gain_ref[...])
    grad_resid = cot_ref[...].astype(full) + back
    resid_out[...] = grad_resid
    low = grad_resid.astype(jnp.bfloat16)
    branch[pl.ds(pl.multiple_of(step * tile, tile), tile), :] = low
    gain_out[...] = jnp.where(step == 0, 0.0, gain_out[...]) + gain_part
    wide = turned[0].shape[1]
    for index, piece in enumerate(turned):
        heads_out[:, index * wide : (index + 1) * wide] = dot_nn(low, piece[...]).astype(jnp.bfloat16)

    @pl.when(step == pl.num_programs(0) - 1)
    def _():
        weight_out[...] = dot_tn(branch[...], heads_ref[...]).astype(jnp.bfloat16)


def branch_back(own, from_x, from_y, resid, cotan, gain, heads, weights, first_column):
    rows, width = own.shape
    tile, wide = ROW_TILE, 512
    steps = rows // tile
    low, full = jnp.bfloat16, jnp.float32
    moving = pl.BlockSpec((tile, width), lambda i: (i, 0))
    fixed = pl.BlockSpec((1, width), lambda i: (0, 0))
    first, then = [], []
    for count in BRANCH_CUTS:
        first.append(pl.BlockSpec((tile, width), lambda i, n=count: (jnp.minimum(i, n - 1), 0)))
        then.append(pl.BlockSpec((tile, width), lambda i, n=count: (jnp.maximum(i - n, 0), 0)))
    return pl.pallas_call(
        branch_back_body,
        grid=(steps,),
        in_specs=[moving, first[0], then[0], first[1], then[1], moving, moving, fixed]
        + [pl.BlockSpec((rows, width), lambda i: (0, 0))]
        + [pl.BlockSpec((width, wide), lambda i, j=j: (0, first_column // wide + j)) for j in range(width // wide)],
        out_specs=[moving, moving, fixed, pl.BlockSpec((width, width), lambda i: (0, 0))],
        out_shape=[
            jax.ShapeDtypeStruct((rows, width), full),
            jax.ShapeDtypeStruct((rows, width), low),
            jax.ShapeDtypeStruct((1, width), full),
            jax.ShapeDtypeStruct((width, width), low),
        ],
        scratch_shapes=[pltpu.VMEM((rows, width), low)],
        compiler_params=params(56),
        cost_estimate=cost(4 * rows * width * width, 20 * rows * width + 4 * width * width),
        name="branch_back",
    )(own, *from_x, *from_y, resid, cotan, gain, heads, *[weights] * (width // wide))


def project_back_body(q_ref, own_ref, x_ref, y_ref, d_ref, cos_ref, sin_ref, w_ref, in_ref, gain_ref, resid_ref, normed_ref,
                      tokens_out, bias_out, gain_out, weight_out, linear):
    step, full = pl.program_id(0), jnp.float32
    tile, qwidth = q_ref.shape
    total = own_ref[...].astype(full) + x_ref[...].astype(full) + y_ref[...].astype(full) + d_ref[...].astype(full)
    pieces = [q_ref[...]]
    for head in range(2 * KV_HEADS):
        lane = total[:, head * HEAD : (head + 1) * HEAD]
        if head < KV_HEADS:
            lane = lane * cos_ref[...] - pltpu.roll(lane, HEAD // 2, 1) * sin_ref[...]
        pieces.append(lane.astype(jnp.bfloat16))
    lin = jnp.concatenate(pieces, axis=1)
    linear[pl.ds(pl.multiple_of(step * tile, tile), tile), :] = lin
    bias_part = jnp.sum(lin.astype(full), axis=0, keepdims=True)
    bias_out[...] = jnp.where(step == 0, 0.0, bias_out[...]) + bias_part
    back, gain_part = unit_back(dot_nt(lin, w_ref[...]), in_ref[...].astype(full), gain_ref[...])
    gain_out[...] = jnp.where(step == 0, 0.0, gain_out[...]) + gain_part
    tokens_out[...] = (resid_ref[...] + back).astype(jnp.bfloat16)

    @pl.when(step == pl.num_programs(0) - 1)
    def _():
        weight_out[...] = dot_tn(normed_ref[...], linear[...]).astype(jnp.bfloat16)


def project_back(query_lin, parts, cosine, sine, weights, inputs, gain, grad_resid, normed):
    rows, width = inputs.shape
    qwidth, kwidth = query_lin.shape[1], parts[0].shape[1]
    qwide, tile = qwidth + kwidth, ROW_TILE
    low, full = jnp.bfloat16, jnp.float32

    def moving(columns):
        return pl.BlockSpec((tile, columns), lambda i: (i, 0))

    def fixed(high, columns):
        return pl.BlockSpec((high, columns), lambda i: (0, 0))

    return pl.pallas_call(
        project_back_body,
        grid=(rows // tile,),
        in_specs=[moving(qwidth)] + [moving(kwidth)] * 4 + [moving(HEAD)] * 2
        + [fixed(width, qwide), moving(width), fixed(1, width), moving(width), fixed(rows, width)],
        out_specs=[moving(width), fixed(1, qwide), fixed(1, width), fixed(width, qwide)],
        out_shape=[
            jax.ShapeDtypeStruct((rows, width), low),
            jax.ShapeDtypeStruct((1, qwide), full),
            jax.ShapeDtypeStruct((1, width), full),
            jax.ShapeDtypeStruct((width, qwide), low),
        ],
        scratch_shapes=[pltpu.VMEM((rows, qwide), low)],
        compiler_params=params(56),
        cost_estimate=cost(4 * rows * width * qwide, 20 * rows * width + 4 * width * qwide),
        name="project_back",
    )(query_lin, *parts, cosine, sine, weights, inputs, gain, grad_resid, normed)


def finish_body(wide_ref, out_ref, mine_ref, sent_ref, *refs):
    results, scratch = refs[:3], refs[3:]
    kept, got_core, got_first, got_second, got_ring = [scratch[i : i + 2] for i in range(0, 10, 2)]
    units, got_units, units_ring, units_moving, sent, landed, local = scratch[10:]
    me, plane = lax.axis_index("gy"), lax.axis_index("gx")
    core, x, y = lax.rem(me, 2), lax.rem(me // 2, 2), me // 4
    places = [lax.rem(plane + 4 - s, 4) for s in range(4)]
    peers = peers_of()
    full = jnp.float32
    greet((CORE, ALONG_X, ALONG_Y, RING, RING + 1))
    copies, loads = [], []

    def send(source, target, bits):
        copy = pltpu.make_async_remote_copy(
            source,
            target,
            sent.at[len(copies)],
            landed.at[len(copies)],
            device_id=peers[bits],
            device_id_type=pl.DeviceIdType.MESH,
        )
        copies.append(copy)
        copy.start()
        return copy

    def load(source, target):
        copy = pltpu.make_async_copy(source, target, local.at[len(loads)])
        loads.append(copy)
        copy.start()
        return copy

    inputs = (wide_ref, out_ref)
    core_copies = [send(sent_ref, got_units, CORE)]
    core_copies += [send(inputs[i].at[:, :, :, 1 - core], got_core[i], CORE) for i in range(2)]
    held = [load(mine_ref, units)]
    held += [load(inputs[i].at[:, :, :, core], kept[i]) for i in range(2)]

    core_copies[0].wait_recv()
    held[0].wait()

    @pl.loop(0, 4)
    def _(p):
        units[p] += got_units[p]

    units_copy = send(units.at[places[1]], units_ring.at[0], RING)
    steps = []
    for i in range(2):
        core_copies[1 + i].wait_recv()
        held[1 + i].wait()

        @pl.loop(0, 4)
        def _(p):
            for a in range(2):
                for b in range(2):
                    kept[i][p, a, b] += got_core[i][p, a, b]

        middle = kept[i].shape[-1] // 256 * 128
        first, second = pl.ds(0, middle), pl.ds(middle, kept[i].shape[-1] - middle)
        steps.append((
            send(kept[i].at[:, :, 1 - x, :, first], got_first[i].at[:, :, :, first], ALONG_X),
            send(kept[i].at[:, 1 - y, :, :, second], got_first[i].at[:, :, :, second], ALONG_Y),
            first,
            second,
        ))
    units_copy.wait_recv()
    units_moving[0] = units[places[2]] + units_ring[0]
    units_copy = send(units_moving.at[0], units_ring.at[1], RING)
    nexts = []
    for i in range(2):
        first_copy, second_copy, first, second = steps[i]
        first_copy.wait_recv()

        @pl.loop(0, 4)
        def _(p):
            for a in range(2):
                kept[i][p, a, x, :, first] += got_first[i][p, a, :, first]

        third_copy = send(kept[i].at[:, 1 - y, x, :, first], got_second[i].at[:, :, first], ALONG_Y)
        second_copy.wait_recv()

        @pl.loop(0, 4)
        def _(p):
            for b in range(2):
                kept[i][p, y, b, :, second] += got_first[i][p, b, :, second]

        nexts.append((third_copy, send(kept[i].at[:, y, 1 - x, :, second], got_second[i].at[:, :, second], ALONG_X)))
    units_copy.wait_recv()
    units_moving[1] = units[places[3]] + units_ring[1]
    units_copy = send(units_moving.at[1], units_ring.at[2], RING)
    ring_copies = []
    for i in range(2):
        for copy in nexts[i]:
            copy.wait_recv()

        @pl.loop(0, 4)
        def _(p):
            kept[i][p, y, x] += got_second[i][p]

        for k, bits in ((1, RING), (2, RING + 1), (3, -RING)):
            there = lax.rem(plane + k, 4)
            ring_copies.append(send(kept[i].at[there, y, x], got_ring[i].at[k - 1], bits))
    for i in range(2):
        total = kept[i][plane, y, x].astype(full)
        for k in range(3):
            ring_copies[3 * i + k].wait_recv()
            total = total + got_ring[i][k].astype(full)
        results[i][...] = total
    units_copy.wait_recv()
    results[2][...] = units[places[0]].astype(full) + units_ring[2].astype(full)
    for copy in copies:
        copy.wait_send()


def finish(wide, out, mine, sent, collective):
    low, full = jnp.bfloat16, jnp.float32
    deep = wide.shape[0] // 32
    wide, out = (a.reshape(4, 2, 2, 2, deep, a.shape[1]) for a in (wide, out))
    columns = (wide.shape[-1], out.shape[-1])
    block = mine.shape[1:]
    anywhere = pl.BlockSpec(memory_space=pl.ANY)
    inside = pl.BlockSpec(memory_space=pltpu.VMEM)

    def pairs(*lead):
        return [pltpu.VMEM((*lead, deep, c), low) for c in columns]

    return pl.pallas_call(
        finish_body,
        in_specs=[anywhere] * 4,
        out_specs=[inside] * 3,
        out_shape=[jax.ShapeDtypeStruct((deep, c), full) for c in columns] + [jax.ShapeDtypeStruct(block, full)],
        scratch_shapes=[
            *pairs(4, 2, 2),
            *pairs(4, 2, 2),
            *pairs(4, 2),
            *pairs(4),
            *pairs(3),
            pltpu.VMEM((4, *block), low),
            pltpu.VMEM((4, *block), low),
            pltpu.VMEM((3, *block), low),
            pltpu.VMEM((2, *block), low),
            pltpu.SemaphoreType.DMA((20,)),
            pltpu.SemaphoreType.DMA((20,)),
            pltpu.SemaphoreType.DMA((3,)),
        ],
        compiler_params=pltpu.CompilerParams(
            vmem_limit_bytes=56 * 1024 * 1024, collective_id=collective, has_side_effects=True
        ),
        cost_estimate=cost(0, 200 * 1024 * 1024),
        name="finish",
    )(wide, out, mine, sent)


def swap(array, bits):
    return lax.ppermute(array, "gy", [(i, i ^ bits) for i in range(8)])


def pick(array, index):
    return lax.dynamic_index_in_dim(array, index, 0, keepdims=False)


def after(array, *earlier):
    return lax.optimization_barrier((array, *earlier))[0]


def pair_rows(pair, core):
    kept, got = pick(pair, core), swap(pick(pair, 1 - core), CORE)
    return jnp.where(core == 0, jnp.concatenate([kept, got]), jnp.concatenate([got, kept]))


def unpair_rows(rows, core):
    half = rows.shape[0] // 2
    kept = lax.dynamic_slice_in_dim(rows, core * half, half, 0)
    got = swap(lax.dynamic_slice_in_dim(rows, (1 - core) * half, half, 0), CORE)
    return jnp.where(core == 0, jnp.stack([kept, got]), jnp.stack([got, kept]))


def plane_order(blocks, chip):
    rows = blocks[0].shape[0]
    whole = jnp.zeros((4 * rows,) + blocks[0].shape[1:], blocks[0].dtype)
    for index, block in enumerate(blocks):
        whole = lax.dynamic_update_slice_in_dim(whole, block, (chip ^ index) * rows, 0)
    return whole


def on_core(
    tokens,
    cotangent,
    segment,
    parent,
    w_qkv,
    qkv_bias,
    w_out,
    gain_attn,
    gain_ffn,
    w_gate,
    w_up,
    w_down,
):
    low, full = jnp.bfloat16, jnp.float32
    me = lax.axis_index("gy")
    plane = lax.axis_index("gx")
    core, chip = me % 2, me // 2
    rows, width = 2 * tokens.shape[1], tokens.shape[2]
    slot_len = segment.shape[1]
    own_units = w_gate.shape[1]
    pad_units = -(-own_units // 384) * 384
    qwidth, kwidth = HEADS * HEAD, KV_HEADS * HEAD
    offset = chip * rows

    nb, ng = qkv_bias.shape[0], gain_attn.shape[0]
    packed = jnp.concatenate([qkv_bias, gain_attn, gain_ffn]).reshape(-1, 1)
    packed = jnp.pad(packed, ((0, 4 * ng - packed.shape[0]), (0, 0))).reshape(4, ng).T
    packed = jnp.pad(packed, ((0, 0), (0, HEAD - 4)))
    attn_own = jnp.concatenate([w_qkv, w_out.T, packed], axis=1)
    attn_slots = [attn_own] + [
        lax.ppermute(attn_own, "gx", [(i, (i + k) % 4) for i in range(4)]) for k in (1, 2, 3)
    ]

    inputs_low = pair_rows(tokens, core)
    grad_low = pair_rows(cotangent, core)

    seg_tree = pick(segment, core)
    valid, upper_one, upper_two, depth_pos = tree_tables(seg_tree, pick(parent, core))
    places = jnp.arange(slot_len, dtype=jnp.int32)

    def take_own(array):
        return lax.dynamic_slice_in_dim(array, offset, rows, 0)

    cosine, sine = rotation(take_own(depth_pos), HEAD)
    sine = sine * jnp.where(jnp.arange(HEAD) < HEAD // 2, -1.0, 1.0)

    more = pad_units - own_units
    shards = [jnp.pad(w, ((0, 0), (0, more))) for w in (w_gate, w_up, w_down.T)]
    weights = [lax.all_gather(after(w, *attn_slots, inputs_low, grad_low), "gx", axis=0, tiled=True) for w in shards]
    attn_all, cotan_others = spread([after(s, inputs_low, cosine, sine, *shards) for s in attn_slots], grad_low)
    cotan_blocks = [grad_low] + cotan_others
    qwide = qwidth + 2 * kwidth
    small = attn_all[:, qwide + width :].reshape(32, ng, HEAD)[:, :, :4].transpose(0, 2, 1).reshape(32, 4 * ng)
    small = small.astype(full)
    bias_full = small[:, :nb].reshape(1, -1)
    gain_one = small[:, nb : nb + ng].reshape(1, -1)
    gain_two = small[:, nb + ng : nb + 2 * ng].reshape(1, -1)
    out_turned = attn_all[:, qwide : qwide + width]

    normed_one, query, keyval_own = project(inputs_low, gain_one, attn_all, bias_full, cosine, sine)
    mask = allowed(
        after(take_own(seg_tree), keyval_own), take_own(upper_one), take_own(upper_two), take_own(places), seg_tree, valid, places
    )
    qblocks, kblocks = rows // QUERY_TILE, slot_len // KEY_TILE
    active = mask.reshape(qblocks, QUERY_TILE, kblocks, KEY_TILE).any(axis=(1, 3))
    block_count = active.sum(axis=1).astype(jnp.int32)
    rank = jnp.cumsum(active.astype(jnp.int32), axis=1) - 1
    numbers = jnp.arange(kblocks, dtype=jnp.int32)
    hit = active[:, :, None] & (rank[:, :, None] == numbers[None, None, :])
    block_list = jnp.sum(jnp.where(hit, numbers[None, :, None], 0), axis=1).astype(jnp.int32)
    mask_bias = jnp.where(mask.T, 0.0, NEGATIVE).astype(low)

    keyval = plane_order([keyval_own] + [swap(keyval_own, bits) for bits in OTHERS], chip)
    other_weights = [swap(after(w, keyval), CORE) for w in weights[:2]]
    heads_out, lse = attend_fast(block_list, block_count, query, keyval, mask_bias)
    inputs = inputs_low.astype(full)
    resid = inputs + lax.dot_general(heads_out, out_turned, (((1,), (1,)), ((), ())), preferred_element_type=full)
    normed_two = norm_parts(resid, gain_two)[2]

    other_weights.append(swap(after(weights[2], heads_out), CORE))
    pieces = weights + other_weights
    half = rows // 2
    first, second = (0, half), (half, half)
    own, (normed_x, normed_y) = ffn_block(
        normed_two, cotan_blocks[0], pieces, 1, [whole_side(normed_two, ALONG_X), whole_side(normed_two, ALONG_Y)]
    )
    passed_on = [(normed_x, first, first, ALONG_Y), (normed_y, second, second, ALONG_X)]
    near_x, (normed_d,) = ffn_block(normed_x, cotan_blocks[1], pieces, 2, [passed_on])
    cut, early = (count * ROW_TILE for count in BRANCH_CUTS)
    rest, few = rows - cut, rows // 10 * 3
    far, (back_x,) = ffn_block(normed_d, cotan_blocks[3], pieces, 3, [rows_side(near_x[4], 0, cut, ALONG_X)])
    near_y, (back_d,) = ffn_block(
        after(normed_y, far[4]), cotan_blocks[2], pieces, 4, [rows_side(far[4], 0, cut, ALONG_X)]
    )
    normed_blocks = [normed_two, normed_x, normed_y, normed_d]
    hidden_b, gate_b, up_b, out_b, back_b = zip(own, near_x, near_y, far)

    def join(mine, passed):
        return (mine.astype(full) + passed.astype(full)).astype(low)

    (down_mine, down_sent), (back_x_end, back_d_end, out_d_end, back_y) = wgrad(
        hidden_b,
        cotan_blocks,
        4,
        5,
        [
            rows_side(back_b[1], cut, rest, ALONG_X),
            rows_side(back_b[3], cut, rest, ALONG_X),
            rows_side(out_b[3], 0, few, ALONG_X),
            rows_side(join(back_b[2][:early], back_d[:early]), 0, early, ALONG_Y),
        ],
    )
    late = join(back_b[2][early:], jnp.concatenate([back_d[early:], back_d_end]))
    (gate_mine, gate_sent), (down_got, out_d, back_y_end) = wgrad(
        gate_b,
        normed_blocks,
        4,
        6,
        [
            whole_side(down_sent, CORE),
            rows_side(out_b[3], few, rows - few, ALONG_X),
            rows_side(late, 0, rows - early, ALONG_Y),
        ],
    )
    gate_got = swap(gate_sent, CORE)
    down_sum = down_mine.astype(full) + down_got.astype(full)
    out_d = jnp.concatenate([out_d_end, out_d])

    grad_resid, grad_heads, grad_gain_two, grad_wout = branch_back(
        back_b[0],
        (back_x, back_x_end),
        (back_y, back_y_end),
        resid,
        grad_low,
        gain_two,
        heads_out,
        attn_all,
        qwide,
    )
    out_got = [swap(after(out_b[1], gate_sent), ALONG_X), swap(join(out_b[2], out_d), ALONG_Y)]
    gate_sum = gate_mine.astype(full) + gate_got.astype(full)
    both = jnp.concatenate([down_sum, gate_sum], axis=1).astype(low)
    grad_heads = after(grad_heads, grad_wout, both)
    both = lax.psum_scatter(both, "gx", scatter_dimension=0, tiled=True)[0].astype(full)
    grad_down, grad_wgate = both[:own_units], both[pad_units : pad_units + own_units].T
    query_lin, keyval_part = attend_back_fast(
        block_list, block_count, query, keyval, mask_bias, lse, heads_out, grad_heads, cosine, sine
    )

    parts = [lax.dynamic_slice_in_dim(keyval_part, (chip ^ i) * rows, rows, 0) for i in range(4)]
    (up_mine, up_sent), others = wgrad(
        up_b, normed_blocks, 4, 7, [whole_side(part, bits) for part, bits in zip(parts[1:], OTHERS)]
    )

    grad_rows, grad_bias, grad_gain_one, grad_wqkv = project_back(
        query_lin, (parts[0], *others), cosine, sine, attn_all, inputs_low, gain_one, grad_resid, normed_one
    )
    grad_tokens = unpair_rows(grad_rows, core)
    ffn_out = sum(after(b, query_lin).astype(full) for b in [out_b[0]] + out_got)
    layer_out = unpair_rows((resid + ffn_out).astype(low), core)

    packed = jnp.concatenate(
        [grad_bias.reshape(32, nb), grad_gain_one.reshape(32, ng), grad_gain_two.reshape(32, ng)], axis=1
    )
    packed = jnp.pad(packed, ((0, 0), (0, 4 * ng - packed.shape[1]))).reshape(32, 4, ng).transpose(0, 2, 1)
    packed = jnp.pad(packed.reshape(32 * ng, 4), ((0, 0), (0, HEAD - 4))).astype(low)
    wide, grad_wout, grad_wup = finish(
        jnp.concatenate([grad_wqkv, packed], axis=1), grad_wout, up_mine, up_sent, 8
    )
    grad_wqkv, grad_wout = wide[:, :qwide], grad_wout.T
    small = wide[:, qwide : qwide + 4].T.reshape(-1)
    grad_wup = grad_wup.T[:, :own_units]
    return (
        layer_out,
        grad_tokens,
        grad_wqkv,
        small[:nb],
        grad_wout,
        small[nb : nb + ng],
        small[nb + ng : nb + 2 * ng],
        grad_wgate,
        grad_wup,
        grad_down,
    )


def solution(mesh):
    in_specs = (
        P("gx", "gy", None),
        P("gx", "gy", None),
        P("gx", None),
        P("gx", None),
        P(("gx", "gy"), None),
        P(("gx", "gy")),
        P(None, ("gx", "gy")),
        P(("gx", "gy")),
        P(("gx", "gy")),
        P("gx", "gy"),
        P("gx", "gy"),
        P("gy", "gx"),
    )
    out_specs = (
        P("gx", "gy", None),
        P("gx", "gy", None),
        P(("gx", "gy"), None),
        P(("gx", "gy")),
        P(None, ("gx", "gy")),
        P(("gx", "gy")),
        P(("gx", "gy")),
        P("gx", "gy"),
        P("gx", "gy"),
        P("gy", "gx"),
    )
    return jax.shard_map(
        on_core if tuple(mesh.shape.values()) == (4, 8) else on_device,
        mesh=mesh,
        in_specs=in_specs,
        out_specs=out_specs,
        check_vma=False,
    )
```

```python
from functools import reduce
import math

import jax
import jax.numpy as jnp
from jax import lax
from jax.experimental import pallas as pl
from jax.experimental.pallas import tpu as pltpu
from jax.sharding import PartitionSpec as P

HEADS = 12
KV_HEADS = 2
HEAD = 128

QUERY_TILE = 128
KEY_TILE = 256
ROW_TILE = 128
BRANCH_CUTS = (4, 3)
FFN_CHUNK = 768
FFN_PARTS = 2
WG_TILE = 384
PACE = 1.0
LOG2E = 1.0 / math.log(2.0)

CORE, ALONG_X, ALONG_Y, ACROSS = 1, 2, 4, 6
OTHERS = (ALONG_X, ALONG_Y, ACROSS)
RING = 8


EPS = 1e-06
THETA = 1000000.0
NEGATIVE = -1e30


def tree_tables(segment, parent):
    slot_len = segment.shape[0]
    seg_count = parent.shape[0]
    places = jnp.arange(slot_len, dtype=jnp.int32)
    labels = jnp.arange(seg_count, dtype=jnp.int32)
    member = segment[:, None] == labels[None, :]
    valid = segment >= 0
    first = jnp.min(jnp.where(member, places[:, None], slot_len), axis=0)
    length = jnp.sum(member.astype(jnp.int32), axis=0)
    parent_hit = parent[:, None] == labels[None, :]
    grand = jnp.sum(jnp.where(parent_hit, parent[None, :], 0), axis=1)
    grand_hit = grand[:, None] == labels[None, :]
    parent_len = jnp.sum(jnp.where(parent_hit, length[None, :], 0), axis=1)
    grand_len = jnp.sum(jnp.where(grand_hit, length[None, :], 0), axis=1)
    base = jnp.where(parent != labels, parent_len, 0) + jnp.where(grand != parent, grand_len, 0)

    def lookup(table):
        return jnp.sum(jnp.where(member, table[None, :], 0), axis=1)

    upper_one = jnp.where(valid, lookup(parent), -2)
    upper_two = jnp.where(valid, lookup(grand), -2)
    depth_pos = jnp.where(valid, places - lookup(first) + lookup(base), 0)
    return (valid, upper_one, upper_two, depth_pos)


def allowed(seg_query, upper_one, upper_two, place_query, seg_keys, valid_keys, place_keys):
    related = (seg_keys[None, :] == seg_query[:, None]) | (seg_keys[None, :] == upper_one[:, None])
    related = related | (seg_keys[None, :] == upper_two[:, None])
    earlier = place_keys[None, :] <= place_query[:, None]
    return related & earlier & valid_keys[None, :] | (place_keys[None, :] == place_query[:, None])


def rotation(depth_pos, width):
    half = width // 2
    freqs = jnp.exp(jnp.arange(half, dtype=jnp.float32) * (-2.0 * math.log(THETA) / width))
    angle = depth_pos.astype(jnp.float32)[:, None] * freqs[None, :]
    cosine = jnp.concatenate([jnp.cos(angle), jnp.cos(angle)], axis=1)
    sine = jnp.concatenate([jnp.sin(angle), jnp.sin(angle)], axis=1)
    return (cosine, sine)


def turn(heads, cosine, sine):
    half = heads.shape[-1] // 2
    swapped = jnp.concatenate([-heads[..., half:], heads[..., :half]], axis=-1)
    return heads * cosine[:, None, :] + swapped * sine[:, None, :]


def norm_parts(values, gain):
    inverse = lax.rsqrt(jnp.mean(values * values, axis=-1, keepdims=True) + EPS)
    unit = values * inverse
    return (unit, inverse, (unit * gain).astype(jnp.bfloat16))


def norm_back(grad_normed, unit, inverse, gain):
    scaled = grad_normed * gain
    back = inverse * (scaled - unit * jnp.mean(scaled * unit, axis=-1, keepdims=True))
    return (back, jnp.sum(grad_normed * unit, axis=0))


def masked_scores(group_query, group_keys, mask, scale):
    scores = (
        jnp.einsum("rhd,kd->hrk", group_query, group_keys, preferred_element_type=jnp.float32)
        * scale
    )
    return jnp.where(mask[None], scores, NEGATIVE)


def attend(query_low, keys_all, values_all, mask, scale):
    group = HEADS // KV_HEADS
    pieces = []
    totals = []
    for head_group in range(KV_HEADS):
        group_query = query_low[:, head_group * group : (head_group + 1) * group, :]
        columns = slice(head_group * HEAD, (head_group + 1) * HEAD)
        scores = masked_scores(group_query, keys_all[:, columns], mask, scale)
        top_score = jnp.max(scores, axis=-1, keepdims=True)
        expo = jnp.exp(scores - top_score)
        denom = jnp.sum(expo, axis=-1, keepdims=True)
        probs_low = (expo / denom).astype(jnp.bfloat16)
        pieces.append(
            jnp.einsum(
                "hrk,kd->rhd", probs_low, values_all[:, columns], preferred_element_type=jnp.float32
            )
        )
        totals.append(top_score + jnp.log(denom))
    return (jnp.concatenate(pieces, axis=1), totals)


def attend_back(query_low, keys_all, values_all, mask, totals, grad_heads, scale):
    group = HEADS // KV_HEADS
    grad_query, grad_keys, grad_values = ([], [], [])
    for head_group in range(KV_HEADS):
        heads_sel = slice(head_group * group, (head_group + 1) * group)
        columns = slice(head_group * HEAD, (head_group + 1) * HEAD)
        group_query = query_low[:, heads_sel, :]
        group_keys = keys_all[:, columns]
        group_grad = grad_heads[:, heads_sel, :]
        scores = masked_scores(group_query, group_keys, mask, scale)
        probs = jnp.exp(scores - totals[head_group])
        probs_low = probs.astype(jnp.bfloat16)
        grad_values.append(
            jnp.einsum("hrk,rhd->kd", probs_low, group_grad, preferred_element_type=jnp.float32)
        )
        grad_probs = jnp.einsum(
            "rhd,kd->hrk", group_grad, values_all[:, columns], preferred_element_type=jnp.float32
        )
        grad_scores = (
            probs * (grad_probs - jnp.sum(probs * grad_probs, axis=-1, keepdims=True))
        ).astype(jnp.bfloat16)
        grad_query.append(
            jnp.einsum("hrk,kd->rhd", grad_scores, group_keys, preferred_element_type=jnp.float32)
            * scale
        )
        grad_keys.append(
            jnp.einsum("hrk,rhd->kd", grad_scores, group_query, preferred_element_type=jnp.float32)
            * scale
        )
    return (
        jnp.concatenate(grad_query, axis=1),
        jnp.concatenate(grad_keys, axis=1),
        jnp.concatenate(grad_values, axis=1),
    )


def add_trees(left, right):
    return jax.tree.map(jnp.add, left, right)


def on_device(
    tokens,
    cotangent,
    segment,
    parent,
    w_qkv,
    qkv_bias,
    w_out,
    gain_attn,
    gain_ffn,
    w_gate,
    w_up,
    w_down,
):
    micro = tokens.shape[0]
    row_count = tokens.shape[1]
    slot_len = segment.shape[1]
    qwidth = HEADS * HEAD
    kwidth = KV_HEADS * HEAD
    scale = 1.0 / math.sqrt(HEAD)
    offset = lax.axis_index("gy") * row_count
    place_all = jnp.arange(slot_len, dtype=jnp.int32)
    place_own = offset + jnp.arange(row_count, dtype=jnp.int32)
    outputs, input_grads, attn_list, ffn_list = ([], [], [], [])
    for micro_index in range(micro):
        attn_full = (
            lax.all_gather(w_qkv, ("gx", "gy"), axis=0, tiled=True),
            lax.all_gather(qkv_bias, ("gx", "gy"), axis=0, tiled=True),
            lax.all_gather(w_out, ("gx", "gy"), axis=1, tiled=True),
            lax.all_gather(gain_attn, ("gx", "gy"), axis=0, tiled=True),
            lax.all_gather(gain_ffn, ("gx", "gy"), axis=0, tiled=True),
        )
        ffn_full = (
            lax.all_gather(w_gate, "gx", axis=0, tiled=True),
            lax.all_gather(w_up, "gx", axis=0, tiled=True),
            lax.all_gather(w_down, "gx", axis=1, tiled=True),
        )
        qkv_full, bias_full, out_full, gain_one_full, gain_two_full = attn_full
        gate_full, up_full, down_full = ffn_full
        gain_one = gain_one_full.astype(jnp.float32)
        gain_two = gain_two_full.astype(jnp.float32)
        seg_tree = segment[micro_index]
        valid, upper_one, upper_two, depth_pos = tree_tables(seg_tree, parent[micro_index])

        def take_own(array):
            return lax.dynamic_slice_in_dim(array, offset, row_count, 0)

        mask = allowed(
            take_own(seg_tree),
            take_own(upper_one),
            take_own(upper_two),
            place_own,
            seg_tree,
            valid,
            place_all,
        )
        cosine, sine = rotation(take_own(depth_pos), HEAD)
        inputs = tokens[micro_index].astype(jnp.float32)
        unit_one, inverse_one, normed_one = norm_parts(inputs, gain_one)
        linear = jnp.dot(
            normed_one, qkv_full, preferred_element_type=jnp.float32
        ) + bias_full.astype(jnp.float32)
        query_low = turn(linear[:, :qwidth].reshape(row_count, HEADS, HEAD), cosine, sine).astype(
            jnp.bfloat16
        )
        keys_low = turn(
            linear[:, qwidth : qwidth + kwidth].reshape(row_count, KV_HEADS, HEAD), cosine, sine
        )
        keys_low = keys_low.reshape(row_count, kwidth).astype(jnp.bfloat16)
        values_low = linear[:, qwidth + kwidth :].astype(jnp.bfloat16)
        keys_all, values_all = (
            lax.all_gather(keys_low, "gy", axis=0, tiled=True),
            lax.all_gather(values_low, "gy", axis=0, tiled=True),
        )
        heads_raw, totals = attend(query_low, keys_all, values_all, mask, scale)
        heads_out = heads_raw.reshape(row_count, qwidth).astype(jnp.bfloat16)
        resid = inputs + jnp.dot(heads_out, out_full, preferred_element_type=jnp.float32)
        unit_two, inverse_two, normed_two = norm_parts(resid, gain_two)
        normed_all = lax.all_gather(normed_two, "gy", axis=0, tiled=True)
        gate = jnp.dot(normed_all, gate_full, preferred_element_type=jnp.float32)
        upward = jnp.dot(normed_all, up_full, preferred_element_type=jnp.float32)
        sigma = jax.nn.sigmoid(gate)
        swish = gate * sigma
        hidden = (swish * upward).astype(jnp.bfloat16)
        ffn_own = lax.psum_scatter(
            jnp.dot(hidden, down_full, preferred_element_type=jnp.float32),
            "gy",
            scatter_dimension=0,
            tiled=True,
        )
        outputs.append((resid + ffn_own).astype(jnp.bfloat16))
        grad_low = cotangent[micro_index]
        grad_all = lax.all_gather(grad_low, "gy", axis=0, tiled=True)
        grad_hidden = jnp.dot(grad_all, down_full.T, preferred_element_type=jnp.float32)
        grad_down = jnp.dot(hidden.T, grad_all, preferred_element_type=jnp.float32)
        grad_gate = (grad_hidden * upward * sigma * (1.0 + gate * (1.0 - sigma))).astype(
            jnp.bfloat16
        )
        grad_up = (grad_hidden * swish).astype(jnp.bfloat16)
        grad_wgate = jnp.dot(normed_all.T, grad_gate, preferred_element_type=jnp.float32)
        grad_wup = jnp.dot(normed_all.T, grad_up, preferred_element_type=jnp.float32)
        grad_normed_two = lax.psum_scatter(
            jnp.dot(grad_gate, gate_full.T, preferred_element_type=jnp.float32)
            + jnp.dot(grad_up, up_full.T, preferred_element_type=jnp.float32),
            "gy",
            scatter_dimension=0,
            tiled=True,
        )
        back_two, grad_gain_two = norm_back(grad_normed_two, unit_two, inverse_two, gain_two)
        grad_resid = grad_low.astype(jnp.float32) + back_two
        grad_branch = grad_resid.astype(jnp.bfloat16)
        grad_wout = jnp.dot(heads_out.T, grad_branch, preferred_element_type=jnp.float32)
        grad_heads = jnp.dot(grad_branch, out_full.T, preferred_element_type=jnp.float32).astype(
            jnp.bfloat16
        )
        grad_heads = grad_heads.reshape(row_count, HEADS, HEAD)
        grad_query, keys_part, values_part = attend_back(
            query_low, keys_all, values_all, mask, totals, grad_heads, scale
        )
        grad_keys, grad_values = (
            lax.psum_scatter(keys_part, "gy", scatter_dimension=0, tiled=True),
            lax.psum_scatter(values_part, "gy", scatter_dimension=0, tiled=True),
        )
        query_lin = turn(grad_query, cosine, -sine).reshape(row_count, qwidth)
        keys_lin = turn(grad_keys.reshape(row_count, KV_HEADS, HEAD), cosine, -sine).reshape(
            row_count, kwidth
        )
        grad_linear = jnp.concatenate([query_lin, keys_lin, grad_values], axis=1).astype(
            jnp.bfloat16
        )
        grad_wqkv = jnp.dot(normed_one.T, grad_linear, preferred_element_type=jnp.float32)
        grad_bias = jnp.sum(grad_linear.astype(jnp.float32), axis=0)
        grad_normed_one = jnp.dot(grad_linear, qkv_full.T, preferred_element_type=jnp.float32)
        back_one, grad_gain_one = norm_back(grad_normed_one, unit_one, inverse_one, gain_one)
        input_grads.append((grad_resid + back_one).astype(jnp.bfloat16))
        attn_list.append((grad_wqkv, grad_bias, grad_wout, grad_gain_one, grad_gain_two))
        ffn_list.append((grad_wgate, grad_wup, grad_down))
    attn_total = reduce(add_trees, attn_list)
    ffn_total = reduce(add_trees, ffn_list)
    attn_total = (
        lax.psum_scatter(attn_total[0], ("gx", "gy"), scatter_dimension=0, tiled=True),
        lax.psum_scatter(attn_total[1], ("gx", "gy"), scatter_dimension=0, tiled=True),
        lax.psum_scatter(attn_total[2], ("gx", "gy"), scatter_dimension=1, tiled=True),
        lax.psum_scatter(attn_total[3], ("gx", "gy"), scatter_dimension=0, tiled=True),
        lax.psum_scatter(attn_total[4], ("gx", "gy"), scatter_dimension=0, tiled=True),
    )
    ffn_total = (
        lax.psum_scatter(ffn_total[0], "gx", scatter_dimension=0, tiled=True),
        lax.psum_scatter(ffn_total[1], "gx", scatter_dimension=0, tiled=True),
        lax.psum_scatter(ffn_total[2], "gx", scatter_dimension=1, tiled=True),
    )
    layer_out = jnp.stack(outputs, axis=0)
    grad_tokens = jnp.stack(input_grads, axis=0)
    return (
        layer_out,
        grad_tokens,
        attn_total[0],
        attn_total[1],
        attn_total[2],
        attn_total[3],
        attn_total[4],
        ffn_total[0],
        ffn_total[1],
        ffn_total[2],
    )


def dot_nn(left, right):
    return lax.dot_general(left, right, (((1,), (0,)), ((), ())), preferred_element_type=jnp.float32)


def dot_nt(left, right):
    return lax.dot_general(left, right, (((1,), (1,)), ((), ())), preferred_element_type=jnp.float32)


def dot_tn(left, right):
    return lax.dot_general(left, right, (((0,), (0,)), ((), ())), preferred_element_type=jnp.float32)


def cost(flops, moved, trans=0):
    return pl.CostEstimate(flops=int(flops * PACE), bytes_accessed=int(moved * PACE), transcendentals=int(trans * PACE))


def params(mib):
    return pltpu.CompilerParams(vmem_limit_bytes=mib * 1024 * 1024)


def sigmoid(v):
    return 0.5 * jnp.tanh(0.5 * v) + 0.5


def peers_of():
    me, plane = lax.axis_index("gy"), lax.axis_index("gx")
    along_x = me + 2 - 4 * lax.rem(me // 2, 2)
    return {
        CORE: {"gy": me + 1 - 2 * lax.rem(me, 2)},
        ALONG_X: {"gy": along_x},
        ALONG_Y: {"gy": me + 4 - 8 * (me // 4)},
        ACROSS: {"gy": along_x + 4 - 8 * (along_x // 4)},
        RING: {"gx": lax.rem(plane + 1, 4)},
        RING + 1: {"gx": lax.rem(plane + 2, 4)},
        -RING: {"gx": lax.rem(plane + 3, 4)},
    }


def greet(bits_used):
    peers = peers_of()
    barrier = pltpu.get_barrier_semaphore()
    greeted = [bits for bits in bits_used] + [-RING] * (RING in bits_used)
    for bits in greeted:
        pl.semaphore_signal(barrier, inc=1, device_id=peers[bits], device_id_type=pl.DeviceIdType.MESH)
    pl.semaphore_wait(barrier, len(greeted))


def side_copies(sides, sources, targets, sent, landed):
    peers = peers_of()
    copies = []
    for parts, target in zip(sides, targets):
        for _, take, fill, bits in parts:
            if take is None:
                take = (pl.multiple_of(peers[bits]["gy"] // 2 * fill[1], fill[1]), fill[1])
            copies.append(
                pltpu.make_async_remote_copy(
                    sources[len(copies)].at[pl.ds(*take)],
                    target.at[pl.ds(*fill)],
                    sent.at[len(copies)],
                    landed.at[len(copies)],
                    device_id=peers[bits],
                    device_id_type=pl.DeviceIdType.MESH,
                )
            )
    return copies


def whole_side(array, bits):
    return [(array, (0, array.shape[0]), (0, array.shape[0]), bits)]


def rows_side(array, start, count, bits):
    return [(array, (start, count), (0, count), bits)]


def chip_side(array, bits):
    return [(array, None, (0, array.shape[0] // 4), bits)]


def call_beside(body, sides, collective, operands, grid, in_specs, out_specs, out_shape, scratch_shapes, mib, estimate, name):
    n_in, n_out, n_scratch = len(in_specs), len(out_specs), len(scratch_shapes)
    flat = [part for parts in sides for part in parts]
    bits_used = sorted({part[3] for part in flat})

    def whole_body(*refs):
        ins, refs = refs[:n_in], refs[n_in:]
        sources, refs = refs[: len(flat)], refs[len(flat) :]
        outs, refs = refs[:n_out], refs[n_out:]
        targets, refs = refs[: len(sides)], refs[len(sides) :]
        scratch, refs = refs[:n_scratch], refs[n_scratch:]
        step, last = pl.program_id(0), pl.num_programs(0) - 1
        if flat:

            @pl.when(step == 0)
            def _():
                greet(bits_used)
                for copy in side_copies(sides, sources, targets, *refs):
                    copy.start()

        body(*ins, *outs, *scratch)
        if flat:

            @pl.when(step == last)
            def _():
                for copy in side_copies(sides, sources, targets, *refs):
                    copy.wait()

    anywhere = pl.BlockSpec(memory_space=pl.ANY)
    extra = {"collective_id": collective, "has_side_effects": True} if flat else {}
    results = pl.pallas_call(
        whole_body,
        grid=grid,
        in_specs=list(in_specs) + [anywhere] * len(flat),
        out_specs=list(out_specs) + [anywhere] * len(sides),
        out_shape=list(out_shape)
        + [jax.ShapeDtypeStruct((sum(p[2][1] for p in parts),) + parts[0][0].shape[1:], parts[0][0].dtype) for parts in sides],
        scratch_shapes=list(scratch_shapes) + ([pltpu.SemaphoreType.DMA((len(flat),))] * 2 if flat else []),
        compiler_params=pltpu.CompilerParams(vmem_limit_bytes=mib * 1024 * 1024, **extra),
        cost_estimate=estimate,
        name=name,
    )(*operands, *[part[0] for part in flat])
    return results[:n_out], results[n_out:]


def ffn_copies(chunk, pieces, held, sems):
    units = pieces[0].shape[1]
    tile = FFN_CHUNK // 2
    slot = chunk % 2
    copies = []
    for part in range(2):
        column = chunk * FFN_CHUNK + part * tile
        owner, inside = column // units, column % units
        for kind in range(3):
            copies.append(
                pltpu.make_async_copy(
                    pieces[3 * owner + kind].at[:, pl.ds(inside, tile)],
                    held.at[slot, kind, :, pl.ds(part * tile, tile)],
                    sems.at[slot, part * 3 + kind],
                )
            )
    return copies


def ffn_body(n_ref, c_ref, *refs):
    pieces = refs[:6]
    hid_ref, dg_ref, du_ref, f_ref, dn_ref, f_acc, dn_acc, held, sems = refs[6:]
    step = pl.program_id(0)
    chunks = 2 * pieces[0].shape[1] // FFN_CHUNK

    @pl.when(step == 0)
    def _():
        for copy in ffn_copies(0, pieces, held, sems):
            copy.start()
        f_acc[...] = jnp.zeros_like(f_acc)
        dn_acc[...] = jnp.zeros_like(dn_acc)

    for chunk in range(chunks):

        @pl.when(step == chunk)
        def _():
            if chunk + 1 < chunks:
                for copy in ffn_copies(chunk + 1, pieces, held, sems):
                    copy.start()
            for copy in ffn_copies(chunk, pieces, held, sems):
                copy.wait()

    slot = step % 2
    rows = n_ref.shape[0]
    part = rows // FFN_PARTS
    takes = [pl.ds(index * part, part) for index in range(FFN_PARTS)]

    def products(take):
        return (
            dot_nn(n_ref[take, :], held[slot, 0]),
            dot_nn(n_ref[take, :], held[slot, 1]),
            dot_nn(c_ref[take, :], held[slot, 2]),
        )

    later = products(takes[0])
    for index, take in enumerate(takes):
        gate, upward, grad_hidden = later
        if index + 1 < FFN_PARTS:
            later = products(takes[index + 1])
        sigma = sigmoid(gate)
        swish = gate * sigma
        hidden = (swish * upward).astype(jnp.bfloat16)
        hid_ref[take, :] = hidden
        grad_gate = (grad_hidden * upward * sigma * (1.0 + gate * (1.0 - sigma))).astype(jnp.bfloat16)
        grad_up = (grad_hidden * swish).astype(jnp.bfloat16)
        dg_ref[take, :] = grad_gate
        du_ref[take, :] = grad_up
        f_acc[take, :] += dot_nt(hidden, held[slot, 2])
        dn_acc[take, :] += dot_nt(grad_gate, held[slot, 0]) + dot_nt(grad_up, held[slot, 1])

    @pl.when(step == pl.num_programs(0) - 1)
    def _():
        f_ref[...] = f_acc[...].astype(f_ref.dtype)
        dn_ref[...] = dn_acc[...].astype(dn_ref.dtype)


def ffn_block(normed, cotan, pieces, collective, sides=()):
    rows, width = normed.shape
    units = 2 * pieces[0].shape[1]
    chunk = FFN_CHUNK
    whole = pl.BlockSpec((rows, width), lambda j: (0, 0))
    tall = pl.BlockSpec((rows, chunk), lambda j: (0, j))
    low = jnp.bfloat16
    return call_beside(
        ffn_body,
        sides,
        collective,
        (normed, cotan, *pieces),
        (units // chunk,),
        [whole, whole] + [pl.BlockSpec(memory_space=pl.ANY)] * len(pieces),
        [tall, tall, tall, whole, whole],
        [jax.ShapeDtypeStruct((rows, units), low)] * 3 + [jax.ShapeDtypeStruct((rows, width), low)] * 2,
        [pltpu.VMEM((rows, width), jnp.float32)] * 2
        + [pltpu.VMEM((2, 3, width, chunk), low), pltpu.SemaphoreType.DMA((2, len(pieces)))],
        60,
        cost(12 * rows * width * units, 6 * width * units + 6 * rows * (width + units)),
        "ffn_block",
    )


def wgrad_body(per_half, *refs):
    count = (len(refs) - 2) // 2
    total = dot_tn(refs[0][...], refs[count][...])
    for index in range(1, count):
        total = total + dot_tn(refs[index][...], refs[count + index][...])

    def store(out_ref):
        slots, _, wide = out_ref.shape
        for slot in range(slots):
            out_ref[slot] = total[:, slot * wide : (slot + 1) * wide].astype(out_ref.dtype)

    first = pl.program_id(0) < per_half
    pl.when(first)(lambda: store(refs[-2]))
    pl.when(jnp.logical_not(first))(lambda: store(refs[-1]))


def wgrad(lefts, rights, slots, collective, sides=()):
    rows, units = lefts[0].shape
    width = rights[0].shape[1]
    tile = WG_TILE
    per_half = units // 2 // tile
    wide = width // slots
    count = len(lefts)
    return call_beside(
        lambda *refs: wgrad_body(per_half, *refs),
        sides,
        collective,
        (*lefts, *rights),
        (units // tile,),
        [pl.BlockSpec((rows, tile), lambda j: (0, j))] * count
        + [pl.BlockSpec((rows, width), lambda j: (0, 0))] * count,
        [
            pl.BlockSpec((slots, tile, wide), lambda j: (0, jnp.minimum(j, per_half - 1), 0)),
            pl.BlockSpec((slots, tile, wide), lambda j: (0, jnp.maximum(j - per_half, 0), 0)),
        ],
        [jax.ShapeDtypeStruct((slots, units // 2, wide), jnp.bfloat16)] * 2,
        [],
        60,
        cost(2 * count * rows * width * units, 2 * count * rows * (width + units)),
        "ffn_wgrad",
    )


def group_rows(source_ref, group, per_group):
    return jnp.concatenate(
        [source_ref[:, (group * per_group + h) * HEAD : (group * per_group + h + 1) * HEAD] for h in range(per_group)],
        axis=0,
    )


def attend_body(list_ref, count_ref, q_ref, kv_ref, bias_ref, o_ref, lse_ref, qs, acc, top, den):
    block = pl.program_id(0)
    per_group = HEADS // KV_HEADS
    for group in range(KV_HEADS):
        qs[group] = group_rows(q_ref, group, per_group)
    acc[...] = jnp.zeros_like(acc)
    den[...] = jnp.zeros_like(den)
    top[...] = jnp.full_like(top, 2 * NEGATIVE)
    factor = LOG2E / math.sqrt(HEAD)

    def body(n, carry):
        rows = pl.ds(pl.multiple_of(list_ref[block, n] * KEY_TILE, KEY_TILE), KEY_TILE)
        bias = jnp.concatenate([bias_ref[rows, :].astype(jnp.float32)] * per_group, axis=1)
        products = [dot_nt(kv_ref[rows, g * HEAD : (g + 1) * HEAD], qs[g]) for g in range(KV_HEADS)]
        for group in range(KV_HEADS):
            values = kv_ref[rows, (KV_HEADS + group) * HEAD : (KV_HEADS + group + 1) * HEAD]
            scores = products[group] * factor + bias
            old = top[group]
            new = jnp.maximum(old, jnp.max(scores, axis=0, keepdims=True))
            probs = jnp.exp2(scores - new)
            shrink = jnp.exp2(old - new)
            den[group] = den[group] * shrink + jnp.sum(probs, axis=0, keepdims=True)
            acc[group] = acc[group] * shrink + dot_tn(values, probs.astype(jnp.bfloat16))
            top[group] = new
        return carry

    lax.fori_loop(0, count_ref[block], body, 0)
    for group in range(KV_HEADS):
        out = acc[group] / den[group]
        lse_ref[0, group] = top[group] + jnp.log(den[group]) * LOG2E
        for h in range(per_group):
            head = group * per_group + h
            o_ref[:, head * HEAD : (head + 1) * HEAD] = out[:, h * HEAD : (h + 1) * HEAD].T.astype(o_ref.dtype)


def attend_fast(block_list, block_count, query, keyval, bias):
    rows, qwidth = query.shape
    slots = keyval.shape[0]
    blocks = rows // QUERY_TILE
    per_group = HEADS // KV_HEADS
    lanes = per_group * QUERY_TILE
    whole = pl.BlockSpec(keyval.shape, lambda i, a, b: (0, 0))
    tile = pl.BlockSpec((QUERY_TILE, qwidth), lambda i, a, b: (i, 0))
    return pl.pallas_call(
        attend_body,
        grid_spec=pltpu.PrefetchScalarGridSpec(
            num_scalar_prefetch=2,
            grid=(blocks,),
            in_specs=[tile, whole, pl.BlockSpec((slots, QUERY_TILE), lambda i, a, b: (0, i))],
            out_specs=[tile, pl.BlockSpec((1, KV_HEADS, 1, lanes), lambda i, a, b: (i, 0, 0, 0))],
            scratch_shapes=[
                pltpu.VMEM((KV_HEADS, lanes, HEAD), jnp.bfloat16),
                pltpu.VMEM((KV_HEADS, HEAD, lanes), jnp.float32),
                pltpu.VMEM((KV_HEADS, 1, lanes), jnp.float32),
                pltpu.VMEM((KV_HEADS, 1, lanes), jnp.float32),
            ],
        ),
        out_shape=[
            jax.ShapeDtypeStruct((rows, qwidth), jnp.bfloat16),
            jax.ShapeDtypeStruct((blocks, KV_HEADS, 1, lanes), jnp.float32),
        ],
        compiler_params=params(48),
        cost_estimate=cost(2 * rows * slots * qwidth * 2, 4 * slots * rows, HEADS * rows * slots // 2),
        name="tree_attention",
    )(block_list, block_count, query, keyval, bias)


def attend_back_body(
    list_ref, count_ref, q_ref, kv_ref, bias_ref, lse_ref, o_ref, do_ref, cos_ref, sin_ref,
    dq_ref, dkv_ref, qs, dos, delta, dqt, dkv,
):
    block = pl.program_id(0)
    per_group = HEADS // KV_HEADS
    scale = 1.0 / math.sqrt(HEAD)
    factor = LOG2E * scale
    lanes = qs.shape[1]

    @pl.when(block == 0)
    def _():
        dkv[...] = jnp.zeros_like(dkv)

    for group in range(KV_HEADS):
        qs[group] = group_rows(q_ref, group, per_group)
        grads = group_rows(do_ref, group, per_group)
        dos[group] = grads
        both = grads.astype(jnp.float32) * group_rows(o_ref, group, per_group).astype(jnp.float32)
        delta[group] = lax.dot_general(
            jnp.ones((8, HEAD), jnp.float32), both, (((1,), (1,)), ((), ())),
            precision=lax.Precision.HIGHEST, preferred_element_type=jnp.float32,
        )[0:1]
    dqt[...] = jnp.zeros_like(dqt)

    def body(n, carry):
        rows = pl.ds(pl.multiple_of(list_ref[block, n] * KEY_TILE, KEY_TILE), KEY_TILE)
        bias = jnp.concatenate([bias_ref[rows, :].astype(jnp.float32)] * per_group, axis=1)
        for group in range(KV_HEADS):
            kcols = slice(group * HEAD, (group + 1) * HEAD)
            vcols = slice((KV_HEADS + group) * HEAD, (KV_HEADS + group + 1) * HEAD)
            keys = kv_ref[rows, kcols]
            values = kv_ref[rows, vcols]
            scores = dot_nt(keys, qs[group]) * factor + bias
            probs = jnp.exp2(scores - lse_ref[0, group])
            grad_probs = dot_nt(values, dos[group])
            grad_scores = (probs * (grad_probs - delta[group])).astype(jnp.bfloat16)
            dkv[rows, vcols] += dot_nn(probs.astype(jnp.bfloat16), dos[group])
            dkv[rows, kcols] += dot_nn(grad_scores, qs[group])
            dqt[group] += dot_tn(keys, grad_scores)
        return carry

    lax.fori_loop(0, count_ref[block], body, 0)
    cosine, sine = cos_ref[...], sin_ref[...]
    for group in range(KV_HEADS):
        for h in range(per_group):
            head = group * per_group + h
            grad = dqt[group, :, h * HEAD : (h + 1) * HEAD].T * scale
            grad = grad * cosine - pltpu.roll(grad, HEAD // 2, 1) * sine
            dq_ref[:, head * HEAD : (head + 1) * HEAD] = grad.astype(dq_ref.dtype)

    @pl.when(block == pl.num_programs(0) - 1)
    def _():
        kwidth = KV_HEADS * HEAD
        dkv_ref[:, :kwidth] = (dkv[:, :kwidth] * scale).astype(dkv_ref.dtype)
        dkv_ref[:, kwidth:] = dkv[:, kwidth:].astype(dkv_ref.dtype)


def attend_back_fast(block_list, block_count, query, keyval, bias, lse, heads_out, grad_heads, cosine, sine):
    rows, qwidth = query.shape
    slots = keyval.shape[0]
    blocks = rows // QUERY_TILE
    per_group = HEADS // KV_HEADS
    lanes = per_group * QUERY_TILE
    whole = pl.BlockSpec(keyval.shape, lambda i, a, b: (0, 0))
    tile = pl.BlockSpec((QUERY_TILE, qwidth), lambda i, a, b: (i, 0))
    turned = pl.BlockSpec((QUERY_TILE, HEAD), lambda i, a, b: (i, 0))
    return pl.pallas_call(
        attend_back_body,
        grid_spec=pltpu.PrefetchScalarGridSpec(
            num_scalar_prefetch=2,
            grid=(blocks,),
            in_specs=[
                tile,
                whole,
                pl.BlockSpec((slots, QUERY_TILE), lambda i, a, b: (0, i)),
                pl.BlockSpec((1, KV_HEADS, 1, lanes), lambda i, a, b: (i, 0, 0, 0)),
                tile,
                tile,
                turned,
                turned,
            ],
            out_specs=[tile, whole],
            scratch_shapes=[
                pltpu.VMEM((KV_HEADS, lanes, HEAD), jnp.bfloat16),
                pltpu.VMEM((KV_HEADS, lanes, HEAD), jnp.bfloat16),
                pltpu.VMEM((KV_HEADS, 1, lanes), jnp.float32),
                pltpu.VMEM((KV_HEADS, HEAD, lanes), jnp.float32),
                pltpu.VMEM(keyval.shape, jnp.float32),
            ],
        ),
        out_shape=[
            jax.ShapeDtypeStruct((rows, qwidth), jnp.bfloat16),
            jax.ShapeDtypeStruct(keyval.shape, jnp.bfloat16),
        ],
        compiler_params=params(56),
        cost_estimate=cost(5 * rows * slots * qwidth * 2, 8 * slots * rows, HEADS * rows * slots // 2),
        name="tree_attention_back",
    )(block_list, block_count, query, keyval, bias, lse, heads_out, grad_heads, cosine, sine)


def project_body(x_ref, gain_ref, w_ref, b_ref, cos_ref, sin_ref, n_ref, q_ref, kv_ref):
    values = x_ref[...].astype(jnp.float32)
    inverse = lax.rsqrt(jnp.mean(values * values, axis=-1, keepdims=True) + EPS)
    normed = (values * inverse * gain_ref[...]).astype(jnp.bfloat16)
    n_ref[...] = normed
    linear = dot_nn(normed, w_ref[...]) + b_ref[...]
    cosine, sine = cos_ref[...], sin_ref[...]
    for head in range(HEADS + KV_HEADS):
        lane = linear[:, head * HEAD : (head + 1) * HEAD]
        lane = (lane * cosine + pltpu.roll(lane, HEAD // 2, 1) * sine).astype(jnp.bfloat16)
        if head < HEADS:
            q_ref[:, head * HEAD : (head + 1) * HEAD] = lane
        else:
            kv_ref[:, (head - HEADS) * HEAD : (head - HEADS + 1) * HEAD] = lane
    kv_ref[:, KV_HEADS * HEAD :] = linear[:, (HEADS + KV_HEADS) * HEAD :].astype(jnp.bfloat16)


def project(inputs, gain, w_qkv, bias, cosine, sine):
    rows, width = inputs.shape
    qwidth, kwidth = HEADS * HEAD, 2 * KV_HEADS * HEAD
    tile = ROW_TILE
    fixed = lambda i: (0, 0)
    moving = lambda i: (i, 0)
    return pl.pallas_call(
        project_body,
        grid=(rows // tile,),
        in_specs=[
            pl.BlockSpec((tile, width), moving),
            pl.BlockSpec((1, width), fixed),
            pl.BlockSpec((width, qwidth + kwidth), fixed),
            pl.BlockSpec((1, qwidth + kwidth), fixed),
            pl.BlockSpec((tile, HEAD), moving),
            pl.BlockSpec((tile, HEAD), moving),
        ],
        out_specs=[
            pl.BlockSpec((tile, width), moving),
            pl.BlockSpec((tile, qwidth), moving),
            pl.BlockSpec((tile, kwidth), moving),
        ],
        out_shape=[
            jax.ShapeDtypeStruct((rows, width), jnp.bfloat16),
            jax.ShapeDtypeStruct((rows, qwidth), jnp.bfloat16),
            jax.ShapeDtypeStruct((rows, kwidth), jnp.bfloat16),
        ],
        compiler_params=params(48),
        cost_estimate=cost(2 * rows * width * (qwidth + kwidth), 2 * width * (qwidth + kwidth) + 8 * rows * width),
        name="project",
    )(inputs, gain, w_qkv, bias, cosine, sine)


def spread_body(*refs):
    owns, rows, whole, rows_x, rows_y, rows_d, sent, landed, kept = refs[:4], *refs[4:]
    me, plane = lax.axis_index("gy"), lax.axis_index("gx")
    peers = peers_of()
    along_x, along_y, across = (peers[bits]["gy"] for bits in OTHERS)
    places = [lax.rem(plane + 4 - k, 4) for k in range(4)]
    greet((CORE, ALONG_X, ALONG_Y))
    copies = []

    def send(source, target, bits):
        copy = pltpu.make_async_remote_copy(
            source,
            target,
            sent.at[len(copies)],
            landed.at[len(copies)],
            device_id=peers[bits],
            device_id_type=pl.DeviceIdType.MESH,
        )
        copies.append(copy)
        copy.start()
        return copy

    from_x, from_y, from_d, from_core, local = [], [], [], [], []
    for k in range(4):
        block = whole.at[places[k], me]
        from_x.append(send(owns[k], block, ALONG_X))
        from_y.append(send(owns[k], block, ALONG_Y))
        from_core.append(send(owns[k], block, CORE))
        local.append(pltpu.make_async_copy(owns[k], block, kept.at[k]))
        local[k].start()
    moved_x, moved_y = send(rows, rows_x, ALONG_X), send(rows, rows_y, ALONG_Y)
    for k in range(4):
        block_x, block_y = whole.at[places[k], along_x], whole.at[places[k], along_y]
        from_x[k].wait_recv()
        if k < 2:
            from_d.append(send(block_x, block_x, ALONG_Y))
        from_core.append(send(block_x, block_x, CORE))
        from_y[k].wait_recv()
        if k >= 2:
            from_d.append(send(block_y, block_y, ALONG_X))
        from_core.append(send(block_y, block_y, CORE))
    for k in range(4):
        block = whole.at[places[k], across]
        from_d[k].wait_recv()
        from_core.append(send(block, block, CORE))
    half = rows.shape[0] // 2
    first, second = pl.ds(0, half), pl.ds(half, half)
    moved_x.wait_recv()
    moved_d = [send(rows_x.at[first], rows_d.at[first], ALONG_Y)]
    moved_y.wait_recv()
    moved_d.append(send(rows_y.at[second], rows_d.at[second], ALONG_X))
    for copy in from_core + moved_d:
        copy.wait_recv()
    for copy in copies:
        copy.wait_send()
    for copy in local:
        copy.wait()


def spread(owns, rows):
    deep, wide = owns[0].shape
    anywhere = pl.BlockSpec(memory_space=pl.ANY)
    whole, *others = pl.pallas_call(
        spread_body,
        in_specs=[anywhere] * 5,
        out_specs=[anywhere] * 4,
        out_shape=[jax.ShapeDtypeStruct((4, 8, deep, wide), rows.dtype)]
        + [jax.ShapeDtypeStruct(rows.shape, rows.dtype)] * 3,
        scratch_shapes=[
            pltpu.SemaphoreType.DMA((32,)),
            pltpu.SemaphoreType.DMA((32,)),
            pltpu.SemaphoreType.DMA((4,)),
        ],
        compiler_params=pltpu.CompilerParams(collective_id=0, has_side_effects=True),
        cost_estimate=cost(0, 300 * 1024 * 1024),
        name="spread",
    )(*owns, rows)
    return whole.reshape(32 * deep, wide), others


def unit_back(grad_normed, values, gain):
    inverse = lax.rsqrt(jnp.mean(values * values, axis=-1, keepdims=True) + EPS)
    unit = values * inverse
    scaled = grad_normed * gain
    back = inverse * (scaled - unit * jnp.mean(scaled * unit, axis=-1, keepdims=True))
    return back, jnp.sum(grad_normed * unit, axis=0, keepdims=True)


def branch_back_body(own_ref, xa_ref, xb_ref, ya_ref, yb_ref, resid_ref, cot_ref, gain_ref, heads_ref, *refs):
    turned, (resid_out, heads_out, gain_out, weight_out, branch) = refs[:-5], refs[-5:]
    step, full = pl.program_id(0), jnp.float32
    tile = own_ref.shape[0]
    from_x = jnp.where(step < BRANCH_CUTS[0], xa_ref[...].astype(full), xb_ref[...].astype(full))
    from_y = jnp.where(step < BRANCH_CUTS[1], ya_ref[...].astype(full), yb_ref[...].astype(full))
    grad_normed = own_ref[...].astype(full) + from_x + from_y
    back, gain_part = unit_back(grad_normed, resid_ref[...], gain_ref[...])
    grad_resid = cot_ref[...].astype(full) + back
    resid_out[...] = grad_resid
    low = grad_resid.astype(jnp.bfloat16)
    branch[pl.ds(pl.multiple_of(step * tile, tile), tile), :] = low
    gain_out[...] = jnp.where(step == 0, 0.0, gain_out[...]) + gain_part
    wide = turned[0].shape[1]
    for index, piece in enumerate(turned):
        heads_out[:, index * wide : (index + 1) * wide] = dot_nn(low, piece[...]).astype(jnp.bfloat16)

    @pl.when(step == pl.num_programs(0) - 1)
    def _():
        weight_out[...] = dot_tn(branch[...], heads_ref[...]).astype(jnp.bfloat16)


def branch_back(own, from_x, from_y, resid, cotan, gain, heads, weights, first_column):
    rows, width = own.shape
    tile, wide = ROW_TILE, 512
    steps = rows // tile
    low, full = jnp.bfloat16, jnp.float32
    moving = pl.BlockSpec((tile, width), lambda i: (i, 0))
    fixed = pl.BlockSpec((1, width), lambda i: (0, 0))
    first, then = [], []
    for count in BRANCH_CUTS:
        first.append(pl.BlockSpec((tile, width), lambda i, n=count: (jnp.minimum(i, n - 1), 0)))
        then.append(pl.BlockSpec((tile, width), lambda i, n=count: (jnp.maximum(i - n, 0), 0)))
    return pl.pallas_call(
        branch_back_body,
        grid=(steps,),
        in_specs=[moving, first[0], then[0], first[1], then[1], moving, moving, fixed]
        + [pl.BlockSpec((rows, width), lambda i: (0, 0))]
        + [pl.BlockSpec((width, wide), lambda i, j=j: (0, first_column // wide + j)) for j in range(width // wide)],
        out_specs=[moving, moving, fixed, pl.BlockSpec((width, width), lambda i: (0, 0))],
        out_shape=[
            jax.ShapeDtypeStruct((rows, width), full),
            jax.ShapeDtypeStruct((rows, width), low),
            jax.ShapeDtypeStruct((1, width), full),
            jax.ShapeDtypeStruct((width, width), low),
        ],
        scratch_shapes=[pltpu.VMEM((rows, width), low)],
        compiler_params=params(56),
        cost_estimate=cost(4 * rows * width * width, 20 * rows * width + 4 * width * width),
        name="branch_back",
    )(own, *from_x, *from_y, resid, cotan, gain, heads, *[weights] * (width // wide))


def project_back_body(q_ref, own_ref, x_ref, y_ref, d_ref, cos_ref, sin_ref, w_ref, in_ref, gain_ref, resid_ref, normed_ref,
                      tokens_out, bias_out, gain_out, weight_out, linear):
    step, full = pl.program_id(0), jnp.float32
    tile, qwidth = q_ref.shape
    total = own_ref[...].astype(full) + x_ref[...].astype(full) + y_ref[...].astype(full) + d_ref[...].astype(full)
    pieces = [q_ref[...]]
    for head in range(2 * KV_HEADS):
        lane = total[:, head * HEAD : (head + 1) * HEAD]
        if head < KV_HEADS:
            lane = lane * cos_ref[...] - pltpu.roll(lane, HEAD // 2, 1) * sin_ref[...]
        pieces.append(lane.astype(jnp.bfloat16))
    lin = jnp.concatenate(pieces, axis=1)
    linear[pl.ds(pl.multiple_of(step * tile, tile), tile), :] = lin
    bias_part = jnp.sum(lin.astype(full), axis=0, keepdims=True)
    bias_out[...] = jnp.where(step == 0, 0.0, bias_out[...]) + bias_part
    back, gain_part = unit_back(dot_nt(lin, w_ref[...]), in_ref[...].astype(full), gain_ref[...])
    gain_out[...] = jnp.where(step == 0, 0.0, gain_out[...]) + gain_part
    tokens_out[...] = (resid_ref[...] + back).astype(jnp.bfloat16)

    @pl.when(step == pl.num_programs(0) - 1)
    def _():
        weight_out[:, : linear.shape[1]] = dot_tn(normed_ref[...], linear[...]).astype(jnp.bfloat16)


def project_back(query_lin, parts, cosine, sine, weights, inputs, gain, grad_resid, normed, collective, sides):
    rows, width = inputs.shape
    qwidth, kwidth = query_lin.shape[1], parts[0].shape[1]
    qwide, tile = qwidth + kwidth, ROW_TILE
    low, full = jnp.bfloat16, jnp.float32

    def moving(columns):
        return pl.BlockSpec((tile, columns), lambda i: (i, 0))

    def fixed(high, columns):
        return pl.BlockSpec((high, columns), lambda i: (0, 0))

    return call_beside(
        project_back_body,
        sides,
        collective,
        (query_lin, *parts, cosine, sine, weights, inputs, gain, grad_resid, normed),
        (rows // tile,),
        [moving(qwidth)]
        + [moving(kwidth)] * 4
        + [moving(HEAD)] * 2
        + [fixed(width, qwide), moving(width), fixed(1, width), moving(width), fixed(rows, width)],
        [moving(width), fixed(1, qwide), fixed(1, width), fixed(width, qwide + HEAD)],
        [
            jax.ShapeDtypeStruct((rows, width), low),
            jax.ShapeDtypeStruct((1, qwide), full),
            jax.ShapeDtypeStruct((1, width), full),
            jax.ShapeDtypeStruct((width, qwide + HEAD), low),
        ],
        [pltpu.VMEM((rows, qwide), low)],
        56,
        cost(4 * rows * width * qwide, 20 * rows * width + 4 * width * qwide),
        "project_back",
    )


def finish_body(wide_ref, out_ref, mine_ref, other_ref, *refs):
    results, scratch = refs[:3], refs[3:]
    kept, got_core, got_first, got_second, got_ring = [scratch[i : i + 2] for i in range(0, 10, 2)]
    units, got_units, units_ring, units_moving, sent, landed, local = scratch[10:]
    me, plane = lax.axis_index("gy"), lax.axis_index("gx")
    core, x, y = lax.rem(me, 2), lax.rem(me // 2, 2), me // 4
    places = [lax.rem(plane + 4 - s, 4) for s in range(4)]
    peers = peers_of()
    full = jnp.float32
    greet((CORE, ALONG_X, ALONG_Y, RING, RING + 1))
    copies, loads = [], []

    def send(source, target, bits):
        copy = pltpu.make_async_remote_copy(
            source,
            target,
            sent.at[len(copies)],
            landed.at[len(copies)],
            device_id=peers[bits],
            device_id_type=pl.DeviceIdType.MESH,
        )
        copies.append(copy)
        copy.start()
        return copy

    def load(source, target):
        copy = pltpu.make_async_copy(source, target, local.at[len(loads)])
        loads.append(copy)
        copy.start()
        return copy

    inputs = (wide_ref, out_ref)
    core_copies = [send(inputs[i].at[:, :, :, 1 - core], got_core[i], CORE) for i in range(2)]
    unit_loads = [load(mine_ref, units), load(other_ref, got_units)]
    held = [load(inputs[i].at[:, :, :, core], kept[i]) for i in range(2)]

    for copy in unit_loads:
        copy.wait()

    @pl.loop(0, 4)
    def _(p):
        units[p] += got_units[p]

    units_copy = send(units.at[places[1]], units_ring.at[0], RING)
    steps = []
    for i in range(2):
        core_copies[i].wait_recv()
        held[i].wait()

        @pl.loop(0, 4)
        def _(p):
            for a in range(2):
                for b in range(2):
                    kept[i][p, a, b] += got_core[i][p, a, b]

        middle = kept[i].shape[-1] // 256 * 128
        first, second = pl.ds(0, middle), pl.ds(middle, kept[i].shape[-1] - middle)
        steps.append((
            send(kept[i].at[:, :, 1 - x, :, first], got_first[i].at[:, :, :, first], ALONG_X),
            send(kept[i].at[:, 1 - y, :, :, second], got_first[i].at[:, :, :, second], ALONG_Y),
            first,
            second,
        ))
    units_copy.wait_recv()
    units_moving[0] = units[places[2]] + units_ring[0]
    units_copy = send(units_moving.at[0], units_ring.at[1], RING)
    nexts = []
    for i in range(2):
        first_copy, second_copy, first, second = steps[i]
        first_copy.wait_recv()

        @pl.loop(0, 4)
        def _(p):
            for a in range(2):
                kept[i][p, a, x, :, first] += got_first[i][p, a, :, first]

        third_copy = send(kept[i].at[:, 1 - y, x, :, first], got_second[i].at[:, :, first], ALONG_Y)
        second_copy.wait_recv()

        @pl.loop(0, 4)
        def _(p):
            for b in range(2):
                kept[i][p, y, b, :, second] += got_first[i][p, b, :, second]

        nexts.append((third_copy, send(kept[i].at[:, y, 1 - x, :, second], got_second[i].at[:, :, second], ALONG_X)))
    units_copy.wait_recv()
    units_moving[1] = units[places[3]] + units_ring[1]
    units_copy = send(units_moving.at[1], units_ring.at[2], RING)
    ring_copies = []
    for i in range(2):
        for copy in nexts[i]:
            copy.wait_recv()

        @pl.loop(0, 4)
        def _(p):
            kept[i][p, y, x] += got_second[i][p]

        for k, bits in ((1, RING), (2, RING + 1), (3, -RING)):
            there = lax.rem(plane + k, 4)
            ring_copies.append(send(kept[i].at[there, y, x], got_ring[i].at[k - 1], bits))
    for i in range(2):
        total = kept[i][plane, y, x].astype(full)
        for k in range(3):
            ring_copies[3 * i + k].wait_recv()
            total = total + got_ring[i][k].astype(full)
        results[i][...] = total
    units_copy.wait_recv()
    results[2][...] = units[places[0]].astype(full) + units_ring[2].astype(full)
    for copy in copies:
        copy.wait_send()


def finish(wide, out, mine, other, collective):
    low, full = jnp.bfloat16, jnp.float32
    deep = wide.shape[0] // 32
    wide, out = (a.reshape(4, 2, 2, 2, deep, a.shape[1]) for a in (wide, out))
    columns = (wide.shape[-1], out.shape[-1])
    block = mine.shape[1:]
    anywhere = pl.BlockSpec(memory_space=pl.ANY)
    inside = pl.BlockSpec(memory_space=pltpu.VMEM)

    def pairs(*lead):
        return [pltpu.VMEM((*lead, deep, c), low) for c in columns]

    return pl.pallas_call(
        finish_body,
        in_specs=[anywhere] * 4,
        out_specs=[inside] * 3,
        out_shape=[jax.ShapeDtypeStruct((deep, c), full) for c in columns] + [jax.ShapeDtypeStruct(block, full)],
        scratch_shapes=[
            *pairs(4, 2, 2),
            *pairs(4, 2, 2),
            *pairs(4, 2),
            *pairs(4),
            *pairs(3),
            pltpu.VMEM((4, *block), low),
            pltpu.VMEM((4, *block), low),
            pltpu.VMEM((3, *block), low),
            pltpu.VMEM((2, *block), low),
            pltpu.SemaphoreType.DMA((19,)),
            pltpu.SemaphoreType.DMA((19,)),
            pltpu.SemaphoreType.DMA((4,)),
        ],
        compiler_params=pltpu.CompilerParams(
            vmem_limit_bytes=56 * 1024 * 1024, collective_id=collective, has_side_effects=True
        ),
        cost_estimate=cost(0, 200 * 1024 * 1024),
        name="finish",
    )(wide, out, mine, other)


def swap(array, bits):
    return lax.ppermute(array, "gy", [(i, i ^ bits) for i in range(8)])


def pick(array, index):
    return lax.dynamic_index_in_dim(array, index, 0, keepdims=False)


def after(array, *earlier):
    return lax.optimization_barrier((array, *earlier))[0]


def pair_rows(pair, core):
    kept, got = pick(pair, core), swap(pick(pair, 1 - core), CORE)
    return jnp.where(core == 0, jnp.concatenate([kept, got]), jnp.concatenate([got, kept]))


def unpair_rows(rows, core):
    half = rows.shape[0] // 2
    kept = lax.dynamic_slice_in_dim(rows, core * half, half, 0)
    got = swap(lax.dynamic_slice_in_dim(rows, (1 - core) * half, half, 0), CORE)
    return jnp.where(core == 0, jnp.stack([kept, got]), jnp.stack([got, kept]))


def plane_order(blocks, chip):
    rows = blocks[0].shape[0]
    whole = jnp.zeros((4 * rows,) + blocks[0].shape[1:], blocks[0].dtype)
    for index, block in enumerate(blocks):
        whole = lax.dynamic_update_slice_in_dim(whole, block, (chip ^ index) * rows, 0)
    return whole


def on_core(
    tokens,
    cotangent,
    segment,
    parent,
    w_qkv,
    qkv_bias,
    w_out,
    gain_attn,
    gain_ffn,
    w_gate,
    w_up,
    w_down,
):
    low, full = jnp.bfloat16, jnp.float32
    me = lax.axis_index("gy")
    plane = lax.axis_index("gx")
    core, chip = me % 2, me // 2
    rows, width = 2 * tokens.shape[1], tokens.shape[2]
    slot_len = segment.shape[1]
    own_units = w_gate.shape[1]
    pad_units = -(-own_units // 384) * 384
    qwidth, kwidth = HEADS * HEAD, KV_HEADS * HEAD
    offset = chip * rows

    nb, ng = qkv_bias.shape[0], gain_attn.shape[0]
    packed = jnp.concatenate([qkv_bias, gain_attn, gain_ffn]).reshape(-1, 1)
    packed = jnp.pad(packed, ((0, 4 * ng - packed.shape[0]), (0, 0))).reshape(4, ng).T
    packed = jnp.pad(packed, ((0, 0), (0, HEAD - 4)))
    attn_own = jnp.concatenate([w_qkv, w_out.T, packed], axis=1)
    attn_slots = [attn_own] + [
        lax.ppermute(attn_own, "gx", [(i, (i + k) % 4) for i in range(4)]) for k in (1, 2, 3)
    ]

    inputs_low = pair_rows(tokens, core)
    grad_low = pair_rows(cotangent, core)

    seg_tree = pick(segment, core)
    valid, upper_one, upper_two, depth_pos = tree_tables(seg_tree, pick(parent, core))
    places = jnp.arange(slot_len, dtype=jnp.int32)

    def take_own(array):
        return lax.dynamic_slice_in_dim(array, offset, rows, 0)

    cosine, sine = rotation(take_own(depth_pos), HEAD)
    sine = sine * jnp.where(jnp.arange(HEAD) < HEAD // 2, -1.0, 1.0)

    more = pad_units - own_units
    shards = [jnp.pad(w, ((0, 0), (0, more))) for w in (w_gate, w_up, w_down.T)]
    weights = [
        lax.all_gather(after(w, *attn_slots, inputs_low, grad_low), "gx", axis=0, tiled=True) for w in shards[:2]
    ]
    weights.append(lax.all_gather(after(shards[2], weights[0]), "gx", axis=0, tiled=True))
    attn_all, cotan_others = spread([after(s, inputs_low, cosine, sine, *shards) for s in attn_slots], grad_low)
    cotan_blocks = [grad_low] + cotan_others
    qwide = qwidth + 2 * kwidth
    small = attn_all[:, qwide + width :].reshape(32, ng, HEAD)[:, :, :4].transpose(0, 2, 1).reshape(32, 4 * ng)
    small = small.astype(full)
    bias_full = small[:, :nb].reshape(1, -1)
    gain_one = small[:, nb : nb + ng].reshape(1, -1)
    gain_two = small[:, nb + ng : nb + 2 * ng].reshape(1, -1)
    out_turned = attn_all[:, qwide : qwide + width]

    normed_one, query, keyval_own = project(inputs_low, gain_one, attn_all, bias_full, cosine, sine)
    mask = allowed(
        after(take_own(seg_tree), keyval_own), take_own(upper_one), take_own(upper_two), take_own(places), seg_tree, valid, places
    )
    qblocks, kblocks = rows // QUERY_TILE, slot_len // KEY_TILE
    active = mask.reshape(qblocks, QUERY_TILE, kblocks, KEY_TILE).any(axis=(1, 3))
    block_count = active.sum(axis=1).astype(jnp.int32)
    rank = jnp.cumsum(active.astype(jnp.int32), axis=1) - 1
    numbers = jnp.arange(kblocks, dtype=jnp.int32)
    hit = active[:, :, None] & (rank[:, :, None] == numbers[None, None, :])
    block_list = jnp.sum(jnp.where(hit, numbers[None, :, None], 0), axis=1).astype(jnp.int32)
    mask_bias = jnp.where(mask.T, 0.0, NEGATIVE).astype(low)

    keyval = plane_order([keyval_own] + [swap(keyval_own, bits) for bits in OTHERS], chip)
    other_weights = [swap(after(w, keyval), CORE) for w in weights[:2]]
    query = after(query, *other_weights)
    heads_out, lse = attend_fast(block_list, block_count, query, keyval, mask_bias)
    inputs = inputs_low.astype(full)
    resid = inputs + lax.dot_general(heads_out, out_turned, (((1,), (1,)), ((), ())), preferred_element_type=full)
    normed_two = norm_parts(resid, gain_two)[2]

    other_weights.append(swap(after(weights[2], heads_out), CORE))
    pieces = weights + other_weights
    half = rows // 2
    first, second = (0, half), (half, half)
    own, (normed_x, normed_y) = ffn_block(
        normed_two, cotan_blocks[0], pieces, 1, [whole_side(normed_two, ALONG_X), whole_side(normed_two, ALONG_Y)]
    )
    passed_on = [(normed_x, first, first, ALONG_Y), (normed_y, second, second, ALONG_X)]
    near_x, (normed_d,) = ffn_block(normed_x, cotan_blocks[1], pieces, 2, [passed_on])
    cut, early = (count * ROW_TILE for count in BRANCH_CUTS)
    rest, few = rows - cut, rows // 10 * 3
    far, (back_x,) = ffn_block(normed_d, cotan_blocks[3], pieces, 3, [rows_side(near_x[4], 0, cut, ALONG_X)])
    near_y, (back_d,) = ffn_block(
        after(normed_y, far[4]), cotan_blocks[2], pieces, 4, [rows_side(far[4], 0, cut, ALONG_X)]
    )
    normed_blocks = [normed_two, normed_x, normed_y, normed_d]
    hidden_b, gate_b, up_b, out_b, back_b = zip(own, near_x, near_y, far)

    def join(mine, passed):
        return (mine.astype(full) + passed.astype(full)).astype(low)

    (down_mine, down_sent), (back_x_end, back_d_end, out_d_end, back_y) = wgrad(
        hidden_b,
        cotan_blocks,
        4,
        5,
        [
            rows_side(back_b[1], cut, rest, ALONG_X),
            rows_side(back_b[3], cut, rest, ALONG_X),
            rows_side(out_b[3], 0, few, ALONG_X),
            rows_side(join(back_b[2][:early], back_d[:early]), 0, early, ALONG_Y),
        ],
    )
    late = join(back_b[2][early:], jnp.concatenate([back_d[early:], back_d_end]))
    (gate_mine, gate_sent), (down_got, out_d, back_y_end) = wgrad(
        gate_b,
        normed_blocks,
        4,
        6,
        [
            whole_side(down_sent, CORE),
            rows_side(out_b[3], few, rows - few, ALONG_X),
            rows_side(late, 0, rows - early, ALONG_Y),
        ],
    )
    gate_got = swap(gate_sent, CORE)
    down_sum = down_mine.astype(full) + down_got.astype(full)
    out_d = jnp.concatenate([out_d_end, out_d])

    grad_resid, grad_heads, grad_gain_two, grad_wout = branch_back(
        back_b[0],
        (back_x, back_x_end),
        (back_y, back_y_end),
        resid,
        grad_low,
        gain_two,
        heads_out,
        attn_all,
        qwide,
    )
    out_got = [swap(after(out_b[1], gate_sent), ALONG_X), swap(join(out_b[2], out_d), ALONG_Y)]
    gate_sum = gate_mine.astype(full) + gate_got.astype(full)
    both = jnp.concatenate([down_sum, gate_sum], axis=1).astype(low)
    grad_heads = after(grad_heads, grad_wout, both)
    both = lax.psum_scatter(both, "gx", scatter_dimension=0, tiled=True)[0].astype(full)
    grad_down, grad_wgate = both[:own_units], both[pad_units : pad_units + own_units].T
    query_lin, keyval_part = attend_back_fast(
        block_list, block_count, query, keyval, mask_bias, lse, heads_out, grad_heads, cosine, sine
    )

    keyval_own = lax.dynamic_slice_in_dim(keyval_part, offset, rows, 0)
    (up_mine, up_sent), others = wgrad(
        up_b, normed_blocks, 4, 7, [chip_side(keyval_part, bits) for bits in OTHERS]
    )

    (grad_rows, grad_bias, grad_gain_one, grad_wqkv), (up_got,) = project_back(
        query_lin,
        (keyval_own, *others),
        cosine,
        sine,
        attn_all,
        inputs_low,
        gain_one,
        grad_resid,
        normed_one,
        9,
        [whole_side(up_sent, CORE)],
    )
    grad_tokens = unpair_rows(grad_rows, core)
    ffn_out = sum(after(b, query_lin).astype(full) for b in [out_b[0]] + out_got)
    layer_out = unpair_rows((resid + ffn_out).astype(low), core)

    packed = jnp.concatenate(
        [grad_bias.reshape(32, nb), grad_gain_one.reshape(32, ng), grad_gain_two.reshape(32, ng)], axis=1
    )
    packed = jnp.pad(packed, ((0, 0), (0, 4 * ng - packed.shape[1]))).reshape(32, 4, ng).transpose(0, 2, 1)
    packed = jnp.pad(packed.reshape(32 * ng, 4), ((0, 0), (0, HEAD - 4))).astype(low)
    wide, grad_wout, grad_wup = finish(
        lax.dynamic_update_slice_in_dim(grad_wqkv, packed, qwide, 1), grad_wout, up_mine, up_got, 8
    )
    grad_wqkv, grad_wout = wide[:, :qwide], grad_wout.T
    small = wide[:, qwide : qwide + 4].T.reshape(-1)
    grad_wup = grad_wup.T[:, :own_units]
    return (
        layer_out,
        grad_tokens,
        grad_wqkv,
        small[:nb],
        grad_wout,
        small[nb : nb + ng],
        small[nb + ng : nb + 2 * ng],
        grad_wgate,
        grad_wup,
        grad_down,
    )


def solution(mesh):
    in_specs = (
        P("gx", "gy", None),
        P("gx", "gy", None),
        P("gx", None),
        P("gx", None),
        P(("gx", "gy"), None),
        P(("gx", "gy")),
        P(None, ("gx", "gy")),
        P(("gx", "gy")),
        P(("gx", "gy")),
        P("gx", "gy"),
        P("gx", "gy"),
        P("gy", "gx"),
    )
    out_specs = (
        P("gx", "gy", None),
        P("gx", "gy", None),
        P(("gx", "gy"), None),
        P(("gx", "gy")),
        P(None, ("gx", "gy")),
        P(("gx", "gy")),
        P(("gx", "gy")),
        P("gx", "gy"),
        P("gx", "gy"),
        P("gy", "gx"),
    )
    return jax.shard_map(
        on_core if tuple(mesh.shape.values()) == (4, 8) else on_device,
        mesh=mesh,
        in_specs=in_specs,
        out_specs=out_specs,
        check_vma=False,
    )
```

```python
from functools import reduce
import math

import jax
import jax.numpy as jnp
from jax import lax
from jax.experimental import pallas as pl
from jax.experimental.pallas import tpu as pltpu
from jax.sharding import PartitionSpec as P

HEADS = 12
KV_HEADS = 2
HEAD = 128

QUERY_TILE = 128
KEY_TILE = 256
ROW_TILE = 128
BRANCH_CUTS = (4, 3)
FFN_CHUNK = 768
FFN_PARTS = 2
WG_TILE = 384
PACE = 1.0
LOG2E = 1.0 / math.log(2.0)

CORE, ALONG_X, ALONG_Y, ACROSS = 1, 2, 4, 6
OTHERS = (ALONG_X, ALONG_Y, ACROSS)
RING = 8


EPS = 1e-06
THETA = 1000000.0
NEGATIVE = -1e30


def tree_tables(segment, parent):
    slot_len = segment.shape[0]
    seg_count = parent.shape[0]
    places = jnp.arange(slot_len, dtype=jnp.int32)
    labels = jnp.arange(seg_count, dtype=jnp.int32)
    member = segment[:, None] == labels[None, :]
    valid = segment >= 0
    first = jnp.min(jnp.where(member, places[:, None], slot_len), axis=0)
    length = jnp.sum(member.astype(jnp.int32), axis=0)
    parent_hit = parent[:, None] == labels[None, :]
    grand = jnp.sum(jnp.where(parent_hit, parent[None, :], 0), axis=1)
    grand_hit = grand[:, None] == labels[None, :]
    parent_len = jnp.sum(jnp.where(parent_hit, length[None, :], 0), axis=1)
    grand_len = jnp.sum(jnp.where(grand_hit, length[None, :], 0), axis=1)
    base = jnp.where(parent != labels, parent_len, 0) + jnp.where(grand != parent, grand_len, 0)

    def lookup(table):
        return jnp.sum(jnp.where(member, table[None, :], 0), axis=1)

    upper_one = jnp.where(valid, lookup(parent), -2)
    upper_two = jnp.where(valid, lookup(grand), -2)
    depth_pos = jnp.where(valid, places - lookup(first) + lookup(base), 0)
    return (valid, upper_one, upper_two, depth_pos)


def allowed(seg_query, upper_one, upper_two, place_query, seg_keys, valid_keys, place_keys):
    related = (seg_keys[None, :] == seg_query[:, None]) | (seg_keys[None, :] == upper_one[:, None])
    related = related | (seg_keys[None, :] == upper_two[:, None])
    earlier = place_keys[None, :] <= place_query[:, None]
    return related & earlier & valid_keys[None, :] | (place_keys[None, :] == place_query[:, None])


def rotation(depth_pos, width):
    half = width // 2
    freqs = jnp.exp(jnp.arange(half, dtype=jnp.float32) * (-2.0 * math.log(THETA) / width))
    angle = depth_pos.astype(jnp.float32)[:, None] * freqs[None, :]
    cosine = jnp.concatenate([jnp.cos(angle), jnp.cos(angle)], axis=1)
    sine = jnp.concatenate([jnp.sin(angle), jnp.sin(angle)], axis=1)
    return (cosine, sine)


def turn(heads, cosine, sine):
    half = heads.shape[-1] // 2
    swapped = jnp.concatenate([-heads[..., half:], heads[..., :half]], axis=-1)
    return heads * cosine[:, None, :] + swapped * sine[:, None, :]


def norm_parts(values, gain):
    inverse = lax.rsqrt(jnp.mean(values * values, axis=-1, keepdims=True) + EPS)
    unit = values * inverse
    return (unit, inverse, (unit * gain).astype(jnp.bfloat16))


def norm_back(grad_normed, unit, inverse, gain):
    scaled = grad_normed * gain
    back = inverse * (scaled - unit * jnp.mean(scaled * unit, axis=-1, keepdims=True))
    return (back, jnp.sum(grad_normed * unit, axis=0))


def masked_scores(group_query, group_keys, mask, scale):
    scores = (
        jnp.einsum("rhd,kd->hrk", group_query, group_keys, preferred_element_type=jnp.float32)
        * scale
    )
    return jnp.where(mask[None], scores, NEGATIVE)


def attend(query_low, keys_all, values_all, mask, scale):
    group = HEADS // KV_HEADS
    pieces = []
    totals = []
    for head_group in range(KV_HEADS):
        group_query = query_low[:, head_group * group : (head_group + 1) * group, :]
        columns = slice(head_group * HEAD, (head_group + 1) * HEAD)
        scores = masked_scores(group_query, keys_all[:, columns], mask, scale)
        top_score = jnp.max(scores, axis=-1, keepdims=True)
        expo = jnp.exp(scores - top_score)
        denom = jnp.sum(expo, axis=-1, keepdims=True)
        probs_low = (expo / denom).astype(jnp.bfloat16)
        pieces.append(
            jnp.einsum(
                "hrk,kd->rhd", probs_low, values_all[:, columns], preferred_element_type=jnp.float32
            )
        )
        totals.append(top_score + jnp.log(denom))
    return (jnp.concatenate(pieces, axis=1), totals)


def attend_back(query_low, keys_all, values_all, mask, totals, grad_heads, scale):
    group = HEADS // KV_HEADS
    grad_query, grad_keys, grad_values = ([], [], [])
    for head_group in range(KV_HEADS):
        heads_sel = slice(head_group * group, (head_group + 1) * group)
        columns = slice(head_group * HEAD, (head_group + 1) * HEAD)
        group_query = query_low[:, heads_sel, :]
        group_keys = keys_all[:, columns]
        group_grad = grad_heads[:, heads_sel, :]
        scores = masked_scores(group_query, group_keys, mask, scale)
        probs = jnp.exp(scores - totals[head_group])
        probs_low = probs.astype(jnp.bfloat16)
        grad_values.append(
            jnp.einsum("hrk,rhd->kd", probs_low, group_grad, preferred_element_type=jnp.float32)
        )
        grad_probs = jnp.einsum(
            "rhd,kd->hrk", group_grad, values_all[:, columns], preferred_element_type=jnp.float32
        )
        grad_scores = (
            probs * (grad_probs - jnp.sum(probs * grad_probs, axis=-1, keepdims=True))
        ).astype(jnp.bfloat16)
        grad_query.append(
            jnp.einsum("hrk,kd->rhd", grad_scores, group_keys, preferred_element_type=jnp.float32)
            * scale
        )
        grad_keys.append(
            jnp.einsum("hrk,rhd->kd", grad_scores, group_query, preferred_element_type=jnp.float32)
            * scale
        )
    return (
        jnp.concatenate(grad_query, axis=1),
        jnp.concatenate(grad_keys, axis=1),
        jnp.concatenate(grad_values, axis=1),
    )


def add_trees(left, right):
    return jax.tree.map(jnp.add, left, right)


def on_device(
    tokens,
    cotangent,
    segment,
    parent,
    w_qkv,
    qkv_bias,
    w_out,
    gain_attn,
    gain_ffn,
    w_gate,
    w_up,
    w_down,
):
    micro = tokens.shape[0]
    row_count = tokens.shape[1]
    slot_len = segment.shape[1]
    qwidth = HEADS * HEAD
    kwidth = KV_HEADS * HEAD
    scale = 1.0 / math.sqrt(HEAD)
    offset = lax.axis_index("gy") * row_count
    place_all = jnp.arange(slot_len, dtype=jnp.int32)
    place_own = offset + jnp.arange(row_count, dtype=jnp.int32)
    outputs, input_grads, attn_list, ffn_list = ([], [], [], [])
    for micro_index in range(micro):
        attn_full = (
            lax.all_gather(w_qkv, ("gx", "gy"), axis=0, tiled=True),
            lax.all_gather(qkv_bias, ("gx", "gy"), axis=0, tiled=True),
            lax.all_gather(w_out, ("gx", "gy"), axis=1, tiled=True),
            lax.all_gather(gain_attn, ("gx", "gy"), axis=0, tiled=True),
            lax.all_gather(gain_ffn, ("gx", "gy"), axis=0, tiled=True),
        )
        ffn_full = (
            lax.all_gather(w_gate, "gx", axis=0, tiled=True),
            lax.all_gather(w_up, "gx", axis=0, tiled=True),
            lax.all_gather(w_down, "gx", axis=1, tiled=True),
        )
        qkv_full, bias_full, out_full, gain_one_full, gain_two_full = attn_full
        gate_full, up_full, down_full = ffn_full
        gain_one = gain_one_full.astype(jnp.float32)
        gain_two = gain_two_full.astype(jnp.float32)
        seg_tree = segment[micro_index]
        valid, upper_one, upper_two, depth_pos = tree_tables(seg_tree, parent[micro_index])

        def take_own(array):
            return lax.dynamic_slice_in_dim(array, offset, row_count, 0)

        mask = allowed(
            take_own(seg_tree),
            take_own(upper_one),
            take_own(upper_two),
            place_own,
            seg_tree,
            valid,
            place_all,
        )
        cosine, sine = rotation(take_own(depth_pos), HEAD)
        inputs = tokens[micro_index].astype(jnp.float32)
        unit_one, inverse_one, normed_one = norm_parts(inputs, gain_one)
        linear = jnp.dot(
            normed_one, qkv_full, preferred_element_type=jnp.float32
        ) + bias_full.astype(jnp.float32)
        query_low = turn(linear[:, :qwidth].reshape(row_count, HEADS, HEAD), cosine, sine).astype(
            jnp.bfloat16
        )
        keys_low = turn(
            linear[:, qwidth : qwidth + kwidth].reshape(row_count, KV_HEADS, HEAD), cosine, sine
        )
        keys_low = keys_low.reshape(row_count, kwidth).astype(jnp.bfloat16)
        values_low = linear[:, qwidth + kwidth :].astype(jnp.bfloat16)
        keys_all, values_all = (
            lax.all_gather(keys_low, "gy", axis=0, tiled=True),
            lax.all_gather(values_low, "gy", axis=0, tiled=True),
        )
        heads_raw, totals = attend(query_low, keys_all, values_all, mask, scale)
        heads_out = heads_raw.reshape(row_count, qwidth).astype(jnp.bfloat16)
        resid = inputs + jnp.dot(heads_out, out_full, preferred_element_type=jnp.float32)
        unit_two, inverse_two, normed_two = norm_parts(resid, gain_two)
        normed_all = lax.all_gather(normed_two, "gy", axis=0, tiled=True)
        gate = jnp.dot(normed_all, gate_full, preferred_element_type=jnp.float32)
        upward = jnp.dot(normed_all, up_full, preferred_element_type=jnp.float32)
        sigma = jax.nn.sigmoid(gate)
        swish = gate * sigma
        hidden = (swish * upward).astype(jnp.bfloat16)
        ffn_own = lax.psum_scatter(
            jnp.dot(hidden, down_full, preferred_element_type=jnp.float32),
            "gy",
            scatter_dimension=0,
            tiled=True,
        )
        outputs.append((resid + ffn_own).astype(jnp.bfloat16))
        grad_low = cotangent[micro_index]
        grad_all = lax.all_gather(grad_low, "gy", axis=0, tiled=True)
        grad_hidden = jnp.dot(grad_all, down_full.T, preferred_element_type=jnp.float32)
        grad_down = jnp.dot(hidden.T, grad_all, preferred_element_type=jnp.float32)
        grad_gate = (grad_hidden * upward * sigma * (1.0 + gate * (1.0 - sigma))).astype(
            jnp.bfloat16
        )
        grad_up = (grad_hidden * swish).astype(jnp.bfloat16)
        grad_wgate = jnp.dot(normed_all.T, grad_gate, preferred_element_type=jnp.float32)
        grad_wup = jnp.dot(normed_all.T, grad_up, preferred_element_type=jnp.float32)
        grad_normed_two = lax.psum_scatter(
            jnp.dot(grad_gate, gate_full.T, preferred_element_type=jnp.float32)
            + jnp.dot(grad_up, up_full.T, preferred_element_type=jnp.float32),
            "gy",
            scatter_dimension=0,
            tiled=True,
        )
        back_two, grad_gain_two = norm_back(grad_normed_two, unit_two, inverse_two, gain_two)
        grad_resid = grad_low.astype(jnp.float32) + back_two
        grad_branch = grad_resid.astype(jnp.bfloat16)
        grad_wout = jnp.dot(heads_out.T, grad_branch, preferred_element_type=jnp.float32)
        grad_heads = jnp.dot(grad_branch, out_full.T, preferred_element_type=jnp.float32).astype(
            jnp.bfloat16
        )
        grad_heads = grad_heads.reshape(row_count, HEADS, HEAD)
        grad_query, keys_part, values_part = attend_back(
            query_low, keys_all, values_all, mask, totals, grad_heads, scale
        )
        grad_keys, grad_values = (
            lax.psum_scatter(keys_part, "gy", scatter_dimension=0, tiled=True),
            lax.psum_scatter(values_part, "gy", scatter_dimension=0, tiled=True),
        )
        query_lin = turn(grad_query, cosine, -sine).reshape(row_count, qwidth)
        keys_lin = turn(grad_keys.reshape(row_count, KV_HEADS, HEAD), cosine, -sine).reshape(
            row_count, kwidth
        )
        grad_linear = jnp.concatenate([query_lin, keys_lin, grad_values], axis=1).astype(
            jnp.bfloat16
        )
        grad_wqkv = jnp.dot(normed_one.T, grad_linear, preferred_element_type=jnp.float32)
        grad_bias = jnp.sum(grad_linear.astype(jnp.float32), axis=0)
        grad_normed_one = jnp.dot(grad_linear, qkv_full.T, preferred_element_type=jnp.float32)
        back_one, grad_gain_one = norm_back(grad_normed_one, unit_one, inverse_one, gain_one)
        input_grads.append((grad_resid + back_one).astype(jnp.bfloat16))
        attn_list.append((grad_wqkv, grad_bias, grad_wout, grad_gain_one, grad_gain_two))
        ffn_list.append((grad_wgate, grad_wup, grad_down))
    attn_total = reduce(add_trees, attn_list)
    ffn_total = reduce(add_trees, ffn_list)
    attn_total = (
        lax.psum_scatter(attn_total[0], ("gx", "gy"), scatter_dimension=0, tiled=True),
        lax.psum_scatter(attn_total[1], ("gx", "gy"), scatter_dimension=0, tiled=True),
        lax.psum_scatter(attn_total[2], ("gx", "gy"), scatter_dimension=1, tiled=True),
        lax.psum_scatter(attn_total[3], ("gx", "gy"), scatter_dimension=0, tiled=True),
        lax.psum_scatter(attn_total[4], ("gx", "gy"), scatter_dimension=0, tiled=True),
    )
    ffn_total = (
        lax.psum_scatter(ffn_total[0], "gx", scatter_dimension=0, tiled=True),
        lax.psum_scatter(ffn_total[1], "gx", scatter_dimension=0, tiled=True),
        lax.psum_scatter(ffn_total[2], "gx", scatter_dimension=1, tiled=True),
    )
    layer_out = jnp.stack(outputs, axis=0)
    grad_tokens = jnp.stack(input_grads, axis=0)
    return (
        layer_out,
        grad_tokens,
        attn_total[0],
        attn_total[1],
        attn_total[2],
        attn_total[3],
        attn_total[4],
        ffn_total[0],
        ffn_total[1],
        ffn_total[2],
    )


def dot_nn(left, right):
    return lax.dot_general(left, right, (((1,), (0,)), ((), ())), preferred_element_type=jnp.float32)


def dot_nt(left, right):
    return lax.dot_general(left, right, (((1,), (1,)), ((), ())), preferred_element_type=jnp.float32)


def dot_tn(left, right):
    return lax.dot_general(left, right, (((0,), (0,)), ((), ())), preferred_element_type=jnp.float32)


def cost(flops, moved, trans=0):
    return pl.CostEstimate(flops=int(flops * PACE), bytes_accessed=int(moved * PACE), transcendentals=int(trans * PACE))


def params(mib):
    return pltpu.CompilerParams(vmem_limit_bytes=mib * 1024 * 1024)


def sigmoid(v):
    return 0.5 * jnp.tanh(0.5 * v) + 0.5


def peers_of():
    me, plane = lax.axis_index("gy"), lax.axis_index("gx")
    along_x = me + 2 - 4 * lax.rem(me // 2, 2)
    return {
        CORE: {"gy": me + 1 - 2 * lax.rem(me, 2)},
        ALONG_X: {"gy": along_x},
        ALONG_Y: {"gy": me + 4 - 8 * (me // 4)},
        ACROSS: {"gy": along_x + 4 - 8 * (along_x // 4)},
        RING: {"gx": lax.rem(plane + 1, 4)},
        RING + 1: {"gx": lax.rem(plane + 2, 4)},
        -RING: {"gx": lax.rem(plane + 3, 4)},
    }


def greet(bits_used):
    peers = peers_of()
    barrier = pltpu.get_barrier_semaphore()
    greeted = [bits for bits in bits_used] + [-RING] * (RING in bits_used)
    for bits in greeted:
        pl.semaphore_signal(barrier, inc=1, device_id=peers[bits], device_id_type=pl.DeviceIdType.MESH)
    pl.semaphore_wait(barrier, len(greeted))


def side_copies(sides, sources, targets, sent, landed):
    peers = peers_of()
    copies = []
    for parts, target in zip(sides, targets):
        for _, take, fill, bits in parts:
            if take is None:
                take = (pl.multiple_of(peers[bits]["gy"] // 2 * fill[1], fill[1]), fill[1])
            copies.append(
                pltpu.make_async_remote_copy(
                    sources[len(copies)].at[pl.ds(*take)],
                    target.at[pl.ds(*fill)],
                    sent.at[len(copies)],
                    landed.at[len(copies)],
                    device_id=peers[bits],
                    device_id_type=pl.DeviceIdType.MESH,
                )
            )
    return copies


def whole_side(array, bits):
    return [(array, (0, array.shape[0]), (0, array.shape[0]), bits)]


def rows_side(array, start, count, bits):
    return [(array, (start, count), (0, count), bits)]


def chip_side(array, bits):
    return [(array, None, (0, array.shape[0] // 4), bits)]


def call_beside(body, sides, collective, operands, grid, in_specs, out_specs, out_shape, scratch_shapes, mib, estimate, name):
    n_in, n_out, n_scratch = len(in_specs), len(out_specs), len(scratch_shapes)
    flat = [part for parts in sides for part in parts]
    bits_used = sorted({part[3] for part in flat})

    def whole_body(*refs):
        ins, refs = refs[:n_in], refs[n_in:]
        sources, refs = refs[: len(flat)], refs[len(flat) :]
        outs, refs = refs[:n_out], refs[n_out:]
        targets, refs = refs[: len(sides)], refs[len(sides) :]
        scratch, refs = refs[:n_scratch], refs[n_scratch:]
        step, last = pl.program_id(0), pl.num_programs(0) - 1
        if flat:

            @pl.when(step == 0)
            def _():
                greet(bits_used)
                for copy in side_copies(sides, sources, targets, *refs):
                    copy.start()

        body(*ins, *outs, *scratch)
        if flat:

            @pl.when(step == last)
            def _():
                for copy in side_copies(sides, sources, targets, *refs):
                    copy.wait()

    anywhere = pl.BlockSpec(memory_space=pl.ANY)
    extra = {"collective_id": collective, "has_side_effects": True} if flat else {}
    results = pl.pallas_call(
        whole_body,
        grid=grid,
        in_specs=list(in_specs) + [anywhere] * len(flat),
        out_specs=list(out_specs) + [anywhere] * len(sides),
        out_shape=list(out_shape)
        + [jax.ShapeDtypeStruct((sum(p[2][1] for p in parts),) + parts[0][0].shape[1:], parts[0][0].dtype) for parts in sides],
        scratch_shapes=list(scratch_shapes) + ([pltpu.SemaphoreType.DMA((len(flat),))] * 2 if flat else []),
        compiler_params=pltpu.CompilerParams(vmem_limit_bytes=mib * 1024 * 1024, **extra),
        cost_estimate=estimate,
        name=name,
    )(*operands, *[part[0] for part in flat])
    return results[:n_out], results[n_out:]


def ffn_copies(chunk, pieces, held, sems):
    units = pieces[0].shape[1]
    tile = FFN_CHUNK // 2
    slot = chunk % 2
    copies = []
    for part in range(2):
        column = chunk * FFN_CHUNK + part * tile
        owner, inside = column // units, column % units
        for kind in range(3):
            copies.append(
                pltpu.make_async_copy(
                    pieces[3 * owner + kind].at[:, pl.ds(inside, tile)],
                    held.at[slot, kind, :, pl.ds(part * tile, tile)],
                    sems.at[slot, part * 3 + kind],
                )
            )
    return copies


def ffn_body(n_ref, c_ref, *refs):
    pieces = refs[:6]
    hid_ref, dg_ref, du_ref, f_ref, dn_ref, f_acc, dn_acc, held, sems = refs[6:]
    step = pl.program_id(0)
    chunks = 2 * pieces[0].shape[1] // FFN_CHUNK

    @pl.when(step == 0)
    def _():
        for copy in ffn_copies(0, pieces, held, sems):
            copy.start()
        f_acc[...] = jnp.zeros_like(f_acc)
        dn_acc[...] = jnp.zeros_like(dn_acc)

    for chunk in range(chunks):

        @pl.when(step == chunk)
        def _():
            if chunk + 1 < chunks:
                for copy in ffn_copies(chunk + 1, pieces, held, sems):
                    copy.start()
            for copy in ffn_copies(chunk, pieces, held, sems):
                copy.wait()

    slot = step % 2
    rows = n_ref.shape[0]
    part = rows // FFN_PARTS
    takes = [pl.ds(index * part, part) for index in range(FFN_PARTS)]

    def products(take):
        return (
            dot_nn(n_ref[take, :], held[slot, 0]),
            dot_nn(n_ref[take, :], held[slot, 1]),
            dot_nn(c_ref[take, :], held[slot, 2]),
        )

    later = products(takes[0])
    for index, take in enumerate(takes):
        gate, upward, grad_hidden = later
        if index + 1 < FFN_PARTS:
            later = products(takes[index + 1])
        sigma = sigmoid(gate)
        swish = gate * sigma
        hidden = (swish * upward).astype(jnp.bfloat16)
        hid_ref[take, :] = hidden
        grad_gate = (grad_hidden * upward * sigma * (1.0 + gate * (1.0 - sigma))).astype(jnp.bfloat16)
        grad_up = (grad_hidden * swish).astype(jnp.bfloat16)
        dg_ref[take, :] = grad_gate
        du_ref[take, :] = grad_up
        f_acc[take, :] += dot_nt(hidden, held[slot, 2])
        dn_acc[take, :] += dot_nt(grad_gate, held[slot, 0]) + dot_nt(grad_up, held[slot, 1])

    @pl.when(step == pl.num_programs(0) - 1)
    def _():
        f_ref[...] = f_acc[...].astype(f_ref.dtype)
        dn_ref[...] = dn_acc[...].astype(dn_ref.dtype)


def ffn_block(normed, cotan, pieces, collective, sides=()):
    rows, width = normed.shape
    units = 2 * pieces[0].shape[1]
    chunk = FFN_CHUNK
    whole = pl.BlockSpec((rows, width), lambda j: (0, 0))
    tall = pl.BlockSpec((rows, chunk), lambda j: (0, j))
    low = jnp.bfloat16
    return call_beside(
        ffn_body,
        sides,
        collective,
        (normed, cotan, *pieces),
        (units // chunk,),
        [whole, whole] + [pl.BlockSpec(memory_space=pl.ANY)] * len(pieces),
        [tall, tall, tall, whole, whole],
        [jax.ShapeDtypeStruct((rows, units), low)] * 3 + [jax.ShapeDtypeStruct((rows, width), low)] * 2,
        [pltpu.VMEM((rows, width), jnp.float32)] * 2
        + [pltpu.VMEM((2, 3, width, chunk), low), pltpu.SemaphoreType.DMA((2, len(pieces)))],
        60,
        cost(12 * rows * width * units, 6 * width * units + 6 * rows * (width + units)),
        "ffn_block",
    )


def wgrad_body(per_half, *refs):
    count = (len(refs) - 2) // 2
    total = dot_tn(refs[0][...], refs[count][...])
    for index in range(1, count):
        total = total + dot_tn(refs[index][...], refs[count + index][...])

    def store(out_ref):
        slots, _, wide = out_ref.shape
        for slot in range(slots):
            out_ref[slot] = total[:, slot * wide : (slot + 1) * wide].astype(out_ref.dtype)

    first = pl.program_id(0) < per_half
    pl.when(first)(lambda: store(refs[-2]))
    pl.when(jnp.logical_not(first))(lambda: store(refs[-1]))


def wgrad(lefts, rights, slots, collective, sides=()):
    rows, units = lefts[0].shape
    width = rights[0].shape[1]
    tile = WG_TILE
    per_half = units // 2 // tile
    wide = width // slots
    count = len(lefts)
    return call_beside(
        lambda *refs: wgrad_body(per_half, *refs),
        sides,
        collective,
        (*lefts, *rights),
        (units // tile,),
        [pl.BlockSpec((rows, tile), lambda j: (0, j))] * count
        + [pl.BlockSpec((rows, width), lambda j: (0, 0))] * count,
        [
            pl.BlockSpec((slots, tile, wide), lambda j: (0, jnp.minimum(j, per_half - 1), 0)),
            pl.BlockSpec((slots, tile, wide), lambda j: (0, jnp.maximum(j - per_half, 0), 0)),
        ],
        [jax.ShapeDtypeStruct((slots, units // 2, wide), jnp.bfloat16)] * 2,
        [],
        60,
        cost(2 * count * rows * width * units, 2 * count * rows * (width + units)),
        "ffn_wgrad",
    )


def group_rows(source_ref, group, per_group):
    return jnp.concatenate(
        [source_ref[:, (group * per_group + h) * HEAD : (group * per_group + h + 1) * HEAD] for h in range(per_group)],
        axis=0,
    )


def attend_body(list_ref, count_ref, q_ref, kv_ref, bias_ref, o_ref, lse_ref, qs, acc, top, den):
    block = pl.program_id(0)
    per_group = HEADS // KV_HEADS
    for group in range(KV_HEADS):
        qs[group] = group_rows(q_ref, group, per_group)
    acc[...] = jnp.zeros_like(acc)
    den[...] = jnp.zeros_like(den)
    top[...] = jnp.full_like(top, 2 * NEGATIVE)
    factor = LOG2E / math.sqrt(HEAD)

    def body(n, carry):
        rows = pl.ds(pl.multiple_of(list_ref[block, n] * KEY_TILE, KEY_TILE), KEY_TILE)
        bias = jnp.concatenate([bias_ref[rows, :].astype(jnp.float32)] * per_group, axis=1)
        products = [dot_nt(kv_ref[rows, g * HEAD : (g + 1) * HEAD], qs[g]) for g in range(KV_HEADS)]
        for group in range(KV_HEADS):
            values = kv_ref[rows, (KV_HEADS + group) * HEAD : (KV_HEADS + group + 1) * HEAD]
            scores = products[group] * factor + bias
            old = top[group]
            new = jnp.maximum(old, jnp.max(scores, axis=0, keepdims=True))
            probs = jnp.exp2(scores - new)
            shrink = jnp.exp2(old - new)
            den[group] = den[group] * shrink + jnp.sum(probs, axis=0, keepdims=True)
            acc[group] = acc[group] * shrink + dot_tn(values, probs.astype(jnp.bfloat16))
            top[group] = new
        return carry

    lax.fori_loop(0, count_ref[block], body, 0)
    for group in range(KV_HEADS):
        out = acc[group] / den[group]
        lse_ref[0, group] = top[group] + jnp.log(den[group]) * LOG2E
        for h in range(per_group):
            head = group * per_group + h
            o_ref[:, head * HEAD : (head + 1) * HEAD] = out[:, h * HEAD : (h + 1) * HEAD].T.astype(o_ref.dtype)


def attend_fast(block_list, block_count, query, keyval, bias):
    rows, qwidth = query.shape
    slots = keyval.shape[0]
    blocks = rows // QUERY_TILE
    per_group = HEADS // KV_HEADS
    lanes = per_group * QUERY_TILE
    whole = pl.BlockSpec(keyval.shape, lambda i, a, b: (0, 0))
    tile = pl.BlockSpec((QUERY_TILE, qwidth), lambda i, a, b: (i, 0))
    return pl.pallas_call(
        attend_body,
        grid_spec=pltpu.PrefetchScalarGridSpec(
            num_scalar_prefetch=2,
            grid=(blocks,),
            in_specs=[tile, whole, pl.BlockSpec((slots, QUERY_TILE), lambda i, a, b: (0, i))],
            out_specs=[tile, pl.BlockSpec((1, KV_HEADS, 1, lanes), lambda i, a, b: (i, 0, 0, 0))],
            scratch_shapes=[
                pltpu.VMEM((KV_HEADS, lanes, HEAD), jnp.bfloat16),
                pltpu.VMEM((KV_HEADS, HEAD, lanes), jnp.float32),
                pltpu.VMEM((KV_HEADS, 1, lanes), jnp.float32),
                pltpu.VMEM((KV_HEADS, 1, lanes), jnp.float32),
            ],
        ),
        out_shape=[
            jax.ShapeDtypeStruct((rows, qwidth), jnp.bfloat16),
            jax.ShapeDtypeStruct((blocks, KV_HEADS, 1, lanes), jnp.float32),
        ],
        compiler_params=params(48),
        cost_estimate=cost(2 * rows * slots * qwidth * 2, 4 * slots * rows, HEADS * rows * slots // 2),
        name="tree_attention",
    )(block_list, block_count, query, keyval, bias)


def attend_back_body(
    list_ref, count_ref, q_ref, kv_ref, bias_ref, lse_ref, o_ref, do_ref, cos_ref, sin_ref,
    dq_ref, dkv_ref, qs, dos, delta, dqt, dkv,
):
    block = pl.program_id(0)
    per_group = HEADS // KV_HEADS
    scale = 1.0 / math.sqrt(HEAD)
    factor = LOG2E * scale
    lanes = qs.shape[1]

    @pl.when(block == 0)
    def _():
        dkv[...] = jnp.zeros_like(dkv)

    for group in range(KV_HEADS):
        qs[group] = group_rows(q_ref, group, per_group)
        grads = group_rows(do_ref, group, per_group)
        dos[group] = grads
        both = grads.astype(jnp.float32) * group_rows(o_ref, group, per_group).astype(jnp.float32)
        delta[group] = lax.dot_general(
            jnp.ones((8, HEAD), jnp.float32), both, (((1,), (1,)), ((), ())),
            precision=lax.Precision.HIGHEST, preferred_element_type=jnp.float32,
        )[0:1]
    dqt[...] = jnp.zeros_like(dqt)

    def body(n, carry):
        rows = pl.ds(pl.multiple_of(list_ref[block, n] * KEY_TILE, KEY_TILE), KEY_TILE)
        bias = jnp.concatenate([bias_ref[rows, :].astype(jnp.float32)] * per_group, axis=1)
        for group in range(KV_HEADS):
            kcols = slice(group * HEAD, (group + 1) * HEAD)
            vcols = slice((KV_HEADS + group) * HEAD, (KV_HEADS + group + 1) * HEAD)
            keys = kv_ref[rows, kcols]
            values = kv_ref[rows, vcols]
            scores = dot_nt(keys, qs[group]) * factor + bias
            probs = jnp.exp2(scores - lse_ref[0, group])
            grad_probs = dot_nt(values, dos[group])
            grad_scores = (probs * (grad_probs - delta[group])).astype(jnp.bfloat16)
            dkv[rows, vcols] += dot_nn(probs.astype(jnp.bfloat16), dos[group])
            dkv[rows, kcols] += dot_nn(grad_scores, qs[group])
            dqt[group] += dot_tn(keys, grad_scores)
        return carry

    lax.fori_loop(0, count_ref[block], body, 0)
    cosine, sine = cos_ref[...], sin_ref[...]
    for group in range(KV_HEADS):
        for h in range(per_group):
            head = group * per_group + h
            grad = dqt[group, :, h * HEAD : (h + 1) * HEAD].T * scale
            grad = grad * cosine - pltpu.roll(grad, HEAD // 2, 1) * sine
            dq_ref[:, head * HEAD : (head + 1) * HEAD] = grad.astype(dq_ref.dtype)

    @pl.when(block == pl.num_programs(0) - 1)
    def _():
        kwidth = KV_HEADS * HEAD
        dkv_ref[:, :kwidth] = (dkv[:, :kwidth] * scale).astype(dkv_ref.dtype)
        dkv_ref[:, kwidth:] = dkv[:, kwidth:].astype(dkv_ref.dtype)


def attend_back_fast(block_list, block_count, query, keyval, bias, lse, heads_out, grad_heads, cosine, sine):
    rows, qwidth = query.shape
    slots = keyval.shape[0]
    blocks = rows // QUERY_TILE
    per_group = HEADS // KV_HEADS
    lanes = per_group * QUERY_TILE
    whole = pl.BlockSpec(keyval.shape, lambda i, a, b: (0, 0))
    tile = pl.BlockSpec((QUERY_TILE, qwidth), lambda i, a, b: (i, 0))
    turned = pl.BlockSpec((QUERY_TILE, HEAD), lambda i, a, b: (i, 0))
    return pl.pallas_call(
        attend_back_body,
        grid_spec=pltpu.PrefetchScalarGridSpec(
            num_scalar_prefetch=2,
            grid=(blocks,),
            in_specs=[
                tile,
                whole,
                pl.BlockSpec((slots, QUERY_TILE), lambda i, a, b: (0, i)),
                pl.BlockSpec((1, KV_HEADS, 1, lanes), lambda i, a, b: (i, 0, 0, 0)),
                tile,
                tile,
                turned,
                turned,
            ],
            out_specs=[tile, whole],
            scratch_shapes=[
                pltpu.VMEM((KV_HEADS, lanes, HEAD), jnp.bfloat16),
                pltpu.VMEM((KV_HEADS, lanes, HEAD), jnp.bfloat16),
                pltpu.VMEM((KV_HEADS, 1, lanes), jnp.float32),
                pltpu.VMEM((KV_HEADS, HEAD, lanes), jnp.float32),
                pltpu.VMEM(keyval.shape, jnp.float32),
            ],
        ),
        out_shape=[
            jax.ShapeDtypeStruct((rows, qwidth), jnp.bfloat16),
            jax.ShapeDtypeStruct(keyval.shape, jnp.bfloat16),
        ],
        compiler_params=params(56),
        cost_estimate=cost(5 * rows * slots * qwidth * 2, 8 * slots * rows, HEADS * rows * slots // 2),
        name="tree_attention_back",
    )(block_list, block_count, query, keyval, bias, lse, heads_out, grad_heads, cosine, sine)


def project_body(x_ref, gain_ref, w_ref, b_ref, cos_ref, sin_ref, n_ref, q_ref, kv_ref):
    values = x_ref[...].astype(jnp.float32)
    inverse = lax.rsqrt(jnp.mean(values * values, axis=-1, keepdims=True) + EPS)
    normed = (values * inverse * gain_ref[...]).astype(jnp.bfloat16)
    n_ref[...] = normed
    linear = dot_nn(normed, w_ref[...]) + b_ref[...]
    cosine, sine = cos_ref[...], sin_ref[...]
    for head in range(HEADS + KV_HEADS):
        lane = linear[:, head * HEAD : (head + 1) * HEAD]
        lane = (lane * cosine + pltpu.roll(lane, HEAD // 2, 1) * sine).astype(jnp.bfloat16)
        if head < HEADS:
            q_ref[:, head * HEAD : (head + 1) * HEAD] = lane
        else:
            kv_ref[:, (head - HEADS) * HEAD : (head - HEADS + 1) * HEAD] = lane
    kv_ref[:, KV_HEADS * HEAD :] = linear[:, (HEADS + KV_HEADS) * HEAD :].astype(jnp.bfloat16)


def project(inputs, gain, w_qkv, bias, cosine, sine):
    rows, width = inputs.shape
    qwidth, kwidth = HEADS * HEAD, 2 * KV_HEADS * HEAD
    tile = ROW_TILE
    fixed = lambda i: (0, 0)
    moving = lambda i: (i, 0)
    return pl.pallas_call(
        project_body,
        grid=(rows // tile,),
        in_specs=[
            pl.BlockSpec((tile, width), moving),
            pl.BlockSpec((1, width), fixed),
            pl.BlockSpec((width, qwidth + kwidth), fixed),
            pl.BlockSpec((1, qwidth + kwidth), fixed),
            pl.BlockSpec((tile, HEAD), moving),
            pl.BlockSpec((tile, HEAD), moving),
        ],
        out_specs=[
            pl.BlockSpec((tile, width), moving),
            pl.BlockSpec((tile, qwidth), moving),
            pl.BlockSpec((tile, kwidth), moving),
        ],
        out_shape=[
            jax.ShapeDtypeStruct((rows, width), jnp.bfloat16),
            jax.ShapeDtypeStruct((rows, qwidth), jnp.bfloat16),
            jax.ShapeDtypeStruct((rows, kwidth), jnp.bfloat16),
        ],
        compiler_params=params(48),
        cost_estimate=cost(2 * rows * width * (qwidth + kwidth), 2 * width * (qwidth + kwidth) + 8 * rows * width),
        name="project",
    )(inputs, gain, w_qkv, bias, cosine, sine)


def spread_body(*refs):
    owns, rows, whole, rows_x, rows_y, rows_d, sent, landed, kept = refs[:4], *refs[4:]
    me, plane = lax.axis_index("gy"), lax.axis_index("gx")
    peers = peers_of()
    along_x, along_y, across = (peers[bits]["gy"] for bits in OTHERS)
    places = [lax.rem(plane + 4 - k, 4) for k in range(4)]
    greet((CORE, ALONG_X, ALONG_Y))
    copies = []

    def send(source, target, bits):
        copy = pltpu.make_async_remote_copy(
            source,
            target,
            sent.at[len(copies)],
            landed.at[len(copies)],
            device_id=peers[bits],
            device_id_type=pl.DeviceIdType.MESH,
        )
        copies.append(copy)
        copy.start()
        return copy

    from_x, from_y, from_d, from_core, local = [], [], [], [], []
    for k in range(4):
        block = whole.at[places[k], me]
        from_x.append(send(owns[k], block, ALONG_X))
        from_y.append(send(owns[k], block, ALONG_Y))
        from_core.append(send(owns[k], block, CORE))
        local.append(pltpu.make_async_copy(owns[k], block, kept.at[k]))
        local[k].start()
    moved_x, moved_y = send(rows, rows_x, ALONG_X), send(rows, rows_y, ALONG_Y)
    for k in range(4):
        block_x, block_y = whole.at[places[k], along_x], whole.at[places[k], along_y]
        from_x[k].wait_recv()
        if k < 2:
            from_d.append(send(block_x, block_x, ALONG_Y))
        from_core.append(send(block_x, block_x, CORE))
        from_y[k].wait_recv()
        if k >= 2:
            from_d.append(send(block_y, block_y, ALONG_X))
        from_core.append(send(block_y, block_y, CORE))
    for k in range(4):
        block = whole.at[places[k], across]
        from_d[k].wait_recv()
        from_core.append(send(block, block, CORE))
    half = rows.shape[0] // 2
    first, second = pl.ds(0, half), pl.ds(half, half)
    moved_x.wait_recv()
    moved_d = [send(rows_x.at[first], rows_d.at[first], ALONG_Y)]
    moved_y.wait_recv()
    moved_d.append(send(rows_y.at[second], rows_d.at[second], ALONG_X))
    for copy in from_core + moved_d:
        copy.wait_recv()
    for copy in copies:
        copy.wait_send()
    for copy in local:
        copy.wait()


def spread(owns, rows):
    deep, wide = owns[0].shape
    anywhere = pl.BlockSpec(memory_space=pl.ANY)
    whole, *others = pl.pallas_call(
        spread_body,
        in_specs=[anywhere] * 5,
        out_specs=[anywhere] * 4,
        out_shape=[jax.ShapeDtypeStruct((4, 8, deep, wide), rows.dtype)]
        + [jax.ShapeDtypeStruct(rows.shape, rows.dtype)] * 3,
        scratch_shapes=[
            pltpu.SemaphoreType.DMA((32,)),
            pltpu.SemaphoreType.DMA((32,)),
            pltpu.SemaphoreType.DMA((4,)),
        ],
        compiler_params=pltpu.CompilerParams(collective_id=0, has_side_effects=True),
        cost_estimate=cost(0, 300 * 1024 * 1024),
        name="spread",
    )(*owns, rows)
    return whole.reshape(32 * deep, wide), others


def unit_back(grad_normed, values, gain):
    inverse = lax.rsqrt(jnp.mean(values * values, axis=-1, keepdims=True) + EPS)
    unit = values * inverse
    scaled = grad_normed * gain
    back = inverse * (scaled - unit * jnp.mean(scaled * unit, axis=-1, keepdims=True))
    return back, jnp.sum(grad_normed * unit, axis=0, keepdims=True)


def branch_back_body(own_ref, xa_ref, xb_ref, ya_ref, yb_ref, resid_ref, cot_ref, gain_ref, heads_ref, *refs):
    turned, (resid_out, heads_out, gain_out, weight_out, branch) = refs[:-5], refs[-5:]
    step, full = pl.program_id(0), jnp.float32
    tile = own_ref.shape[0]
    from_x = jnp.where(step < BRANCH_CUTS[0], xa_ref[...].astype(full), xb_ref[...].astype(full))
    from_y = jnp.where(step < BRANCH_CUTS[1], ya_ref[...].astype(full), yb_ref[...].astype(full))
    grad_normed = own_ref[...].astype(full) + from_x + from_y
    back, gain_part = unit_back(grad_normed, resid_ref[...], gain_ref[...])
    grad_resid = cot_ref[...].astype(full) + back
    resid_out[...] = grad_resid
    low = grad_resid.astype(jnp.bfloat16)
    branch[pl.ds(pl.multiple_of(step * tile, tile), tile), :] = low
    gain_out[...] = jnp.where(step == 0, 0.0, gain_out[...]) + gain_part
    wide = turned[0].shape[1]
    for index, piece in enumerate(turned):
        heads_out[:, index * wide : (index + 1) * wide] = dot_nn(low, piece[...]).astype(jnp.bfloat16)

    @pl.when(step == pl.num_programs(0) - 1)
    def _():
        weight_out[...] = dot_tn(branch[...], heads_ref[...]).astype(jnp.bfloat16)


def branch_back(own, from_x, from_y, resid, cotan, gain, heads, weights, first_column):
    rows, width = own.shape
    tile, wide = ROW_TILE, 512
    steps = rows // tile
    low, full = jnp.bfloat16, jnp.float32
    moving = pl.BlockSpec((tile, width), lambda i: (i, 0))
    fixed = pl.BlockSpec((1, width), lambda i: (0, 0))
    first, then = [], []
    for count in BRANCH_CUTS:
        first.append(pl.BlockSpec((tile, width), lambda i, n=count: (jnp.minimum(i, n - 1), 0)))
        then.append(pl.BlockSpec((tile, width), lambda i, n=count: (jnp.maximum(i - n, 0), 0)))
    return pl.pallas_call(
        branch_back_body,
        grid=(steps,),
        in_specs=[moving, first[0], then[0], first[1], then[1], moving, moving, fixed]
        + [pl.BlockSpec((rows, width), lambda i: (0, 0))]
        + [pl.BlockSpec((width, wide), lambda i, j=j: (0, first_column // wide + j)) for j in range(width // wide)],
        out_specs=[moving, moving, fixed, pl.BlockSpec((width, width), lambda i: (0, 0))],
        out_shape=[
            jax.ShapeDtypeStruct((rows, width), full),
            jax.ShapeDtypeStruct((rows, width), low),
            jax.ShapeDtypeStruct((1, width), full),
            jax.ShapeDtypeStruct((width, width), low),
        ],
        scratch_shapes=[pltpu.VMEM((rows, width), low)],
        compiler_params=params(56),
        cost_estimate=cost(4 * rows * width * width, 20 * rows * width + 4 * width * width),
        name="branch_back",
    )(own, *from_x, *from_y, resid, cotan, gain, heads, *[weights] * (width // wide))


def project_back_body(q_ref, own_ref, x_ref, y_ref, d_ref, cos_ref, sin_ref, w_ref, in_ref, gain_ref, resid_ref, normed_ref,
                      tokens_out, bias_out, gain_out, weight_out, linear):
    step, full = pl.program_id(0), jnp.float32
    tile, qwidth = q_ref.shape
    total = own_ref[...].astype(full) + x_ref[...].astype(full) + y_ref[...].astype(full) + d_ref[...].astype(full)
    pieces = [q_ref[...]]
    for head in range(2 * KV_HEADS):
        lane = total[:, head * HEAD : (head + 1) * HEAD]
        if head < KV_HEADS:
            lane = lane * cos_ref[...] - pltpu.roll(lane, HEAD // 2, 1) * sin_ref[...]
        pieces.append(lane.astype(jnp.bfloat16))
    lin = jnp.concatenate(pieces, axis=1)
    linear[pl.ds(pl.multiple_of(step * tile, tile), tile), :] = lin
    bias_part = jnp.sum(lin.astype(full), axis=0, keepdims=True)
    bias_out[...] = jnp.where(step == 0, 0.0, bias_out[...]) + bias_part
    back, gain_part = unit_back(dot_nt(lin, w_ref[...]), in_ref[...].astype(full), gain_ref[...])
    gain_out[...] = jnp.where(step == 0, 0.0, gain_out[...]) + gain_part
    tokens_out[...] = (resid_ref[...] + back).astype(jnp.bfloat16)

    @pl.when(step == pl.num_programs(0) - 1)
    def _():
        weight_out[:, : linear.shape[1]] = dot_tn(normed_ref[...], linear[...]).astype(jnp.bfloat16)


def project_back(query_lin, parts, cosine, sine, weights, inputs, gain, grad_resid, normed, collective, sides):
    rows, width = inputs.shape
    qwidth, kwidth = query_lin.shape[1], parts[0].shape[1]
    qwide, tile = qwidth + kwidth, ROW_TILE
    low, full = jnp.bfloat16, jnp.float32

    def moving(columns):
        return pl.BlockSpec((tile, columns), lambda i: (i, 0))

    def fixed(high, columns):
        return pl.BlockSpec((high, columns), lambda i: (0, 0))

    return call_beside(
        project_back_body,
        sides,
        collective,
        (query_lin, *parts, cosine, sine, weights, inputs, gain, grad_resid, normed),
        (rows // tile,),
        [moving(qwidth)]
        + [moving(kwidth)] * 4
        + [moving(HEAD)] * 2
        + [fixed(width, qwide), moving(width), fixed(1, width), moving(width), fixed(rows, width)],
        [moving(width), fixed(1, qwide), fixed(1, width), fixed(width, qwide + HEAD)],
        [
            jax.ShapeDtypeStruct((rows, width), low),
            jax.ShapeDtypeStruct((1, qwide), full),
            jax.ShapeDtypeStruct((1, width), full),
            jax.ShapeDtypeStruct((width, qwide + HEAD), low),
        ],
        [pltpu.VMEM((rows, qwide), low)],
        56,
        cost(4 * rows * width * qwide, 20 * rows * width + 4 * width * qwide),
        "project_back",
    )


def finish_body(wide_ref, out_ref, mine_ref, other_ref, both_ref, layer_ref, tokens_ref, *refs):
    results, rows_out, scratch = refs[:5], refs[5:7], refs[7:]
    kept, got_core, got_first, got_second, got_ring = [scratch[i : i + 2] for i in range(0, 10, 2)]
    units, got_units, units_ring, units_moving, both, sent, landed, local = scratch[10:]
    me, plane = lax.axis_index("gy"), lax.axis_index("gx")
    core, x, y = lax.rem(me, 2), lax.rem(me // 2, 2), me // 4
    places = [lax.rem(plane + 4 - s, 4) for s in range(4)]
    peers = peers_of()
    full = jnp.float32
    greet((CORE, ALONG_X, ALONG_Y, RING, RING + 1))
    copies, loads = [], []

    def send(source, target, bits):
        copy = pltpu.make_async_remote_copy(
            source,
            target,
            sent.at[len(copies)],
            landed.at[len(copies)],
            device_id=peers[bits],
            device_id_type=pl.DeviceIdType.MESH,
        )
        copies.append(copy)
        copy.start()
        return copy

    def load(source, target):
        copy = pltpu.make_async_copy(source, target, local.at[len(loads)])
        loads.append(copy)
        copy.start()
        return copy

    inputs = (wide_ref, out_ref)
    core_copies = [send(inputs[i].at[:, :, :, 1 - core], got_core[i], CORE) for i in range(2)]
    unit_loads = [load(mine_ref, units), load(other_ref, got_units)]
    both_load = load(both_ref, both)
    held = [load(inputs[i].at[:, :, :, core], kept[i]) for i in range(2)]

    for copy in unit_loads:
        copy.wait()

    @pl.loop(0, 4)
    def _(p):
        units[p] += got_units[p]

    units_copy = send(units.at[places[1]], units_ring.at[0], RING)
    steps = []
    for i in range(2):
        core_copies[i].wait_recv()
        held[i].wait()

        @pl.loop(0, 4)
        def _(p):
            for a in range(2):
                for b in range(2):
                    kept[i][p, a, b] += got_core[i][p, a, b]

        middle = kept[i].shape[-1] // 256 * 128
        first, second = pl.ds(0, middle), pl.ds(middle, kept[i].shape[-1] - middle)
        steps.append((
            send(kept[i].at[:, :, 1 - x, :, first], got_first[i].at[:, :, :, first], ALONG_X),
            send(kept[i].at[:, 1 - y, :, :, second], got_first[i].at[:, :, :, second], ALONG_Y),
            first,
            second,
        ))
    units_copy.wait_recv()
    units_moving[0] = units[places[2]] + units_ring[0]
    units_copy = send(units_moving.at[0], units_ring.at[1], RING)
    half = layer_ref.shape[0] // 2
    row_copies = []
    for source, target in ((layer_ref, rows_out[0]), (tokens_ref, rows_out[1])):
        row_copies.append(send(source.at[pl.ds((1 - core) * half, half)], target.at[core], CORE))
        held.append(load(source.at[pl.ds(core * half, half)], target.at[core]))
    both_load.wait()
    high, own = both.shape[0] // 2, results[3].shape[0]
    results[3][...] = both[0:own, :].astype(full)
    results[4][...] = both[high : high + own, :].astype(full)
    nexts = []
    for i in range(2):
        first_copy, second_copy, first, second = steps[i]
        first_copy.wait_recv()

        @pl.loop(0, 4)
        def _(p):
            for a in range(2):
                kept[i][p, a, x, :, first] += got_first[i][p, a, :, first]

        third_copy = send(kept[i].at[:, 1 - y, x, :, first], got_second[i].at[:, :, first], ALONG_Y)
        second_copy.wait_recv()

        @pl.loop(0, 4)
        def _(p):
            for b in range(2):
                kept[i][p, y, b, :, second] += got_first[i][p, b, :, second]

        nexts.append((third_copy, send(kept[i].at[:, y, 1 - x, :, second], got_second[i].at[:, :, second], ALONG_X)))
    units_copy.wait_recv()
    units_moving[1] = units[places[3]] + units_ring[1]
    units_copy = send(units_moving.at[1], units_ring.at[2], RING)
    ring_copies = []
    for i in range(2):
        for copy in nexts[i]:
            copy.wait_recv()

        @pl.loop(0, 4)
        def _(p):
            kept[i][p, y, x] += got_second[i][p]

        for k, bits in ((1, RING), (2, RING + 1), (3, -RING)):
            there = lax.rem(plane + k, 4)
            ring_copies.append(send(kept[i].at[there, y, x], got_ring[i].at[k - 1], bits))
    units_copy.wait_recv()
    results[2][...] = units[places[0], 0:own, :].astype(full) + units_ring[2, 0:own, :].astype(full)
    for i in range(2):
        total = kept[i][plane, y, x].astype(full)
        for k in range(3):
            ring_copies[3 * i + k].wait_recv()
            total = total + got_ring[i][k].astype(full)
        results[i][...] = total
    for copy in row_copies:
        copy.wait_recv()
    for copy in held[2:]:
        copy.wait()
    for copy in copies:
        copy.wait_send()


def finish(wide, out, mine, other, both, layer, tokens, own_units, collective):
    low, full = jnp.bfloat16, jnp.float32
    deep = wide.shape[0] // 32
    wide, out = (a.reshape(4, 2, 2, 2, deep, a.shape[1]) for a in (wide, out))
    columns = (wide.shape[-1], out.shape[-1])
    block = mine.shape[1:]
    anywhere = pl.BlockSpec(memory_space=pl.ANY)
    inside = pl.BlockSpec(memory_space=pltpu.VMEM)

    def pairs(*lead):
        return [pltpu.VMEM((*lead, deep, c), low) for c in columns]

    return pl.pallas_call(
        finish_body,
        in_specs=[anywhere] * 7,
        out_specs=[inside] * 5 + [anywhere] * 2,
        out_shape=[jax.ShapeDtypeStruct((deep, c), full) for c in columns]
        + [jax.ShapeDtypeStruct((own_units, block[1]), full)] * 3
        + [jax.ShapeDtypeStruct((2, rows.shape[0] // 2, rows.shape[1]), low) for rows in (layer, tokens)],
        scratch_shapes=[
            *pairs(4, 2, 2),
            *pairs(4, 2, 2),
            *pairs(4, 2),
            *pairs(4),
            *pairs(3),
            pltpu.VMEM((4, *block), low),
            pltpu.VMEM((4, *block), low),
            pltpu.VMEM((3, *block), low),
            pltpu.VMEM((2, *block), low),
            pltpu.VMEM(both.shape, low),
            pltpu.SemaphoreType.DMA((21,)),
            pltpu.SemaphoreType.DMA((21,)),
            pltpu.SemaphoreType.DMA((7,)),
        ],
        compiler_params=pltpu.CompilerParams(
            vmem_limit_bytes=56 * 1024 * 1024, collective_id=collective, has_side_effects=True
        ),
        cost_estimate=cost(0, 200 * 1024 * 1024),
        name="finish",
    )(wide, out, mine, other, both, layer, tokens)


def swap(array, bits):
    return lax.ppermute(array, "gy", [(i, i ^ bits) for i in range(8)])


def pick(array, index):
    return lax.dynamic_index_in_dim(array, index, 0, keepdims=False)


def after(array, *earlier):
    return lax.optimization_barrier((array, *earlier))[0]


def pair_rows(pair, core):
    kept, got = pick(pair, core), swap(pick(pair, 1 - core), CORE)
    return jnp.where(core == 0, jnp.concatenate([kept, got]), jnp.concatenate([got, kept]))


def plane_order(blocks, chip):
    rows = blocks[0].shape[0]
    whole = jnp.zeros((4 * rows,) + blocks[0].shape[1:], blocks[0].dtype)
    for index, block in enumerate(blocks):
        whole = lax.dynamic_update_slice_in_dim(whole, block, (chip ^ index) * rows, 0)
    return whole


def on_core(
    tokens,
    cotangent,
    segment,
    parent,
    w_qkv,
    qkv_bias,
    w_out,
    gain_attn,
    gain_ffn,
    w_gate,
    w_up,
    w_down,
):
    low, full = jnp.bfloat16, jnp.float32
    me = lax.axis_index("gy")
    plane = lax.axis_index("gx")
    core, chip = me % 2, me // 2
    rows, width = 2 * tokens.shape[1], tokens.shape[2]
    slot_len = segment.shape[1]
    own_units = w_gate.shape[1]
    pad_units = -(-own_units // 384) * 384
    qwidth, kwidth = HEADS * HEAD, KV_HEADS * HEAD
    offset = chip * rows

    nb, ng = qkv_bias.shape[0], gain_attn.shape[0]
    packed = jnp.concatenate([qkv_bias, gain_attn, gain_ffn]).reshape(-1, 1)
    packed = jnp.pad(packed, ((0, 4 * ng - packed.shape[0]), (0, 0))).reshape(4, ng).T
    packed = jnp.pad(packed, ((0, 0), (0, HEAD - 4)))
    attn_own = jnp.concatenate([w_qkv, w_out.T, packed], axis=1)
    attn_slots = [attn_own] + [
        lax.ppermute(attn_own, "gx", [(i, (i + k) % 4) for i in range(4)]) for k in (1, 2, 3)
    ]

    inputs_low = pair_rows(tokens, core)
    grad_low = pair_rows(cotangent, core)

    seg_tree = pick(segment, core)
    valid, upper_one, upper_two, depth_pos = tree_tables(seg_tree, pick(parent, core))
    places = jnp.arange(slot_len, dtype=jnp.int32)

    def take_own(array):
        return lax.dynamic_slice_in_dim(array, offset, rows, 0)

    cosine, sine = rotation(take_own(depth_pos), HEAD)
    sine = sine * jnp.where(jnp.arange(HEAD) < HEAD // 2, -1.0, 1.0)

    more = pad_units - own_units
    shards = [jnp.pad(w, ((0, 0), (0, more))) for w in (w_gate, w_up, w_down.T)]
    weights = [
        lax.all_gather(after(w, *attn_slots, inputs_low, grad_low), "gx", axis=0, tiled=True) for w in shards[:2]
    ]
    weights.append(lax.all_gather(after(shards[2], weights[0]), "gx", axis=0, tiled=True))
    attn_all, cotan_others = spread([after(s, inputs_low, cosine, sine, *shards) for s in attn_slots], grad_low)
    cotan_blocks = [grad_low] + cotan_others
    qwide = qwidth + 2 * kwidth
    small = attn_all[:, qwide + width :].reshape(32, ng, HEAD)[:, :, :4].transpose(0, 2, 1).reshape(32, 4 * ng)
    small = small.astype(full)
    bias_full = small[:, :nb].reshape(1, -1)
    gain_one = small[:, nb : nb + ng].reshape(1, -1)
    gain_two = small[:, nb + ng : nb + 2 * ng].reshape(1, -1)
    out_turned = attn_all[:, qwide : qwide + width]

    normed_one, query, keyval_own = project(inputs_low, gain_one, attn_all, bias_full, cosine, sine)
    mask = allowed(
        after(take_own(seg_tree), keyval_own), take_own(upper_one), take_own(upper_two), take_own(places), seg_tree, valid, places
    )
    qblocks, kblocks = rows // QUERY_TILE, slot_len // KEY_TILE
    active = mask.reshape(qblocks, QUERY_TILE, kblocks, KEY_TILE).any(axis=(1, 3))
    block_count = active.sum(axis=1).astype(jnp.int32)
    rank = jnp.cumsum(active.astype(jnp.int32), axis=1) - 1
    numbers = jnp.arange(kblocks, dtype=jnp.int32)
    hit = active[:, :, None] & (rank[:, :, None] == numbers[None, None, :])
    block_list = jnp.sum(jnp.where(hit, numbers[None, :, None], 0), axis=1).astype(jnp.int32)
    mask_bias = jnp.where(mask.T, 0.0, NEGATIVE).astype(low)

    keyval = plane_order([keyval_own] + [swap(keyval_own, bits) for bits in OTHERS], chip)
    other_weights = [swap(after(w, keyval), CORE) for w in weights[:2]]
    query = after(query, *other_weights)
    heads_out, lse = attend_fast(block_list, block_count, query, keyval, mask_bias)
    inputs = inputs_low.astype(full)
    resid = inputs + lax.dot_general(heads_out, out_turned, (((1,), (1,)), ((), ())), preferred_element_type=full)
    normed_two = norm_parts(resid, gain_two)[2]

    other_weights.append(swap(after(weights[2], heads_out), CORE))
    pieces = weights + other_weights
    half = rows // 2
    first, second = (0, half), (half, half)
    own, (normed_x, normed_y) = ffn_block(
        normed_two, cotan_blocks[0], pieces, 1, [whole_side(normed_two, ALONG_X), whole_side(normed_two, ALONG_Y)]
    )
    passed_on = [(normed_x, first, first, ALONG_Y), (normed_y, second, second, ALONG_X)]
    near_x, (normed_d,) = ffn_block(normed_x, cotan_blocks[1], pieces, 2, [passed_on])
    cut, early = (count * ROW_TILE for count in BRANCH_CUTS)
    rest, few = rows - cut, rows // 10 * 3
    far, (back_x,) = ffn_block(normed_d, cotan_blocks[3], pieces, 3, [rows_side(near_x[4], 0, cut, ALONG_X)])
    near_y, (back_d,) = ffn_block(
        after(normed_y, far[4]), cotan_blocks[2], pieces, 4, [rows_side(far[4], 0, cut, ALONG_X)]
    )
    normed_blocks = [normed_two, normed_x, normed_y, normed_d]
    hidden_b, gate_b, up_b, out_b, back_b = zip(own, near_x, near_y, far)

    def join(mine, passed):
        return (mine.astype(full) + passed.astype(full)).astype(low)

    (down_mine, down_sent), (back_x_end, back_d_end, out_d_end, back_y) = wgrad(
        hidden_b,
        cotan_blocks,
        4,
        5,
        [
            rows_side(back_b[1], cut, rest, ALONG_X),
            rows_side(back_b[3], cut, rest, ALONG_X),
            rows_side(out_b[3], 0, few, ALONG_X),
            rows_side(join(back_b[2][:early], back_d[:early]), 0, early, ALONG_Y),
        ],
    )
    late = join(back_b[2][early:], jnp.concatenate([back_d[early:], back_d_end]))
    (gate_mine, gate_sent), (down_got, out_d, back_y_end) = wgrad(
        gate_b,
        normed_blocks,
        4,
        6,
        [
            whole_side(down_sent, CORE),
            rows_side(out_b[3], few, rows - few, ALONG_X),
            rows_side(late, 0, rows - early, ALONG_Y),
        ],
    )
    gate_got = swap(gate_sent, CORE)
    down_sum = down_mine.astype(full) + down_got.astype(full)
    out_d = jnp.concatenate([out_d_end, out_d])

    grad_resid, grad_heads, grad_gain_two, grad_wout = branch_back(
        back_b[0],
        (back_x, back_x_end),
        (back_y, back_y_end),
        resid,
        grad_low,
        gain_two,
        heads_out,
        attn_all,
        qwide,
    )
    out_got = [swap(after(out_b[1], gate_sent), ALONG_X), swap(join(out_b[2], out_d), ALONG_Y)]
    gate_sum = gate_mine.astype(full) + gate_got.astype(full)
    both = jnp.concatenate([down_sum, gate_sum], axis=1).astype(low)
    grad_heads = after(grad_heads, grad_wout, both)
    both = lax.psum_scatter(both, "gx", scatter_dimension=0, tiled=True)[0]
    query_lin, keyval_part = attend_back_fast(
        block_list, block_count, query, keyval, mask_bias, lse, heads_out, grad_heads, cosine, sine
    )

    keyval_own = lax.dynamic_slice_in_dim(keyval_part, offset, rows, 0)
    (up_mine, up_sent), others = wgrad(
        up_b, normed_blocks, 4, 7, [chip_side(keyval_part, bits) for bits in OTHERS]
    )

    (grad_rows, grad_bias, grad_gain_one, grad_wqkv), (up_got,) = project_back(
        query_lin,
        (keyval_own, *others),
        cosine,
        sine,
        attn_all,
        inputs_low,
        gain_one,
        grad_resid,
        normed_one,
        9,
        [whole_side(up_sent, CORE)],
    )
    ffn_out = sum(after(b, query_lin).astype(full) for b in [out_b[0]] + out_got)
    layer_rows = (resid + ffn_out).astype(low)

    packed = jnp.concatenate(
        [grad_bias.reshape(32, nb), grad_gain_one.reshape(32, ng), grad_gain_two.reshape(32, ng)], axis=1
    )
    packed = jnp.pad(packed, ((0, 0), (0, 4 * ng - packed.shape[1]))).reshape(32, 4, ng).transpose(0, 2, 1)
    packed = jnp.pad(packed.reshape(32 * ng, 4), ((0, 0), (0, HEAD - 4))).astype(low)
    wide, grad_wout, grad_wup, grad_down, grad_wgate, layer_out, grad_tokens = finish(
        lax.dynamic_update_slice_in_dim(grad_wqkv, packed, qwide, 1),
        grad_wout,
        up_mine,
        up_got,
        both,
        layer_rows,
        grad_rows,
        own_units,
        8,
    )
    grad_wqkv, grad_wout = wide[:, :qwide], grad_wout.T
    small = wide[:, qwide : qwide + 4].T.reshape(-1)
    grad_wgate, grad_wup = grad_wgate.T, grad_wup.T
    return (
        layer_out,
        grad_tokens,
        grad_wqkv,
        small[:nb],
        grad_wout,
        small[nb : nb + ng],
        small[nb + ng : nb + 2 * ng],
        grad_wgate,
        grad_wup,
        grad_down,
    )


def solution(mesh):
    in_specs = (
        P("gx", "gy", None),
        P("gx", "gy", None),
        P("gx", None),
        P("gx", None),
        P(("gx", "gy"), None),
        P(("gx", "gy")),
        P(None, ("gx", "gy")),
        P(("gx", "gy")),
        P(("gx", "gy")),
        P("gx", "gy"),
        P("gx", "gy"),
        P("gy", "gx"),
    )
    out_specs = (
        P("gx", "gy", None),
        P("gx", "gy", None),
        P(("gx", "gy"), None),
        P(("gx", "gy")),
        P(None, ("gx", "gy")),
        P(("gx", "gy")),
        P(("gx", "gy")),
        P("gx", "gy"),
        P("gx", "gy"),
        P("gy", "gx"),
    )
    return jax.shard_map(
        on_core if tuple(mesh.shape.values()) == (4, 8) else on_device,
        mesh=mesh,
        in_specs=in_specs,
        out_specs=out_specs,
        check_vma=False,
    )
```

```python
from functools import reduce
import math

import jax
import jax.numpy as jnp
from jax import lax
from jax.experimental import pallas as pl
from jax.experimental.pallas import tpu as pltpu
from jax.sharding import PartitionSpec as P

HEADS = 12
KV_HEADS = 2
HEAD = 128

QUERY_TILE = 128
KEY_TILE = 256
ROW_TILE = 128
BRANCH_CUTS = (4, 3)
FFN_CHUNK = 768
FFN_PARTS = 2
WG_TILE = 384
PACE = 1.0
LOG2E = 1.0 / math.log(2.0)

CORE, ALONG_X, ALONG_Y, ACROSS = 1, 2, 4, 6
OTHERS = (ALONG_X, ALONG_Y, ACROSS)
RING = 8


EPS = 1e-06
THETA = 1000000.0
NEGATIVE = -1e30


def tree_tables(segment, parent):
    slot_len = segment.shape[0]
    seg_count = parent.shape[0]
    places = jnp.arange(slot_len, dtype=jnp.int32)
    labels = jnp.arange(seg_count, dtype=jnp.int32)
    member = segment[:, None] == labels[None, :]
    valid = segment >= 0
    first = jnp.min(jnp.where(member, places[:, None], slot_len), axis=0)
    length = jnp.sum(member.astype(jnp.int32), axis=0)
    parent_hit = parent[:, None] == labels[None, :]
    grand = jnp.sum(jnp.where(parent_hit, parent[None, :], 0), axis=1)
    grand_hit = grand[:, None] == labels[None, :]
    parent_len = jnp.sum(jnp.where(parent_hit, length[None, :], 0), axis=1)
    grand_len = jnp.sum(jnp.where(grand_hit, length[None, :], 0), axis=1)
    base = jnp.where(parent != labels, parent_len, 0) + jnp.where(grand != parent, grand_len, 0)

    def lookup(table):
        return jnp.sum(jnp.where(member, table[None, :], 0), axis=1)

    upper_one = jnp.where(valid, lookup(parent), -2)
    upper_two = jnp.where(valid, lookup(grand), -2)
    depth_pos = jnp.where(valid, places - lookup(first) + lookup(base), 0)
    return (valid, upper_one, upper_two, depth_pos)


def allowed(seg_query, upper_one, upper_two, place_query, seg_keys, valid_keys, place_keys):
    related = (seg_keys[None, :] == seg_query[:, None]) | (seg_keys[None, :] == upper_one[:, None])
    related = related | (seg_keys[None, :] == upper_two[:, None])
    earlier = place_keys[None, :] <= place_query[:, None]
    return related & earlier & valid_keys[None, :] | (place_keys[None, :] == place_query[:, None])


def rotation(depth_pos, width):
    half = width // 2
    freqs = jnp.exp(jnp.arange(half, dtype=jnp.float32) * (-2.0 * math.log(THETA) / width))
    angle = depth_pos.astype(jnp.float32)[:, None] * freqs[None, :]
    cosine = jnp.concatenate([jnp.cos(angle), jnp.cos(angle)], axis=1)
    sine = jnp.concatenate([jnp.sin(angle), jnp.sin(angle)], axis=1)
    return (cosine, sine)


def turn(heads, cosine, sine):
    half = heads.shape[-1] // 2
    swapped = jnp.concatenate([-heads[..., half:], heads[..., :half]], axis=-1)
    return heads * cosine[:, None, :] + swapped * sine[:, None, :]


def norm_parts(values, gain):
    inverse = lax.rsqrt(jnp.mean(values * values, axis=-1, keepdims=True) + EPS)
    unit = values * inverse
    return (unit, inverse, (unit * gain).astype(jnp.bfloat16))


def norm_back(grad_normed, unit, inverse, gain):
    scaled = grad_normed * gain
    back = inverse * (scaled - unit * jnp.mean(scaled * unit, axis=-1, keepdims=True))
    return (back, jnp.sum(grad_normed * unit, axis=0))


def masked_scores(group_query, group_keys, mask, scale):
    scores = (
        jnp.einsum("rhd,kd->hrk", group_query, group_keys, preferred_element_type=jnp.float32)
        * scale
    )
    return jnp.where(mask[None], scores, NEGATIVE)


def attend(query_low, keys_all, values_all, mask, scale):
    group = HEADS // KV_HEADS
    pieces = []
    totals = []
    for head_group in range(KV_HEADS):
        group_query = query_low[:, head_group * group : (head_group + 1) * group, :]
        columns = slice(head_group * HEAD, (head_group + 1) * HEAD)
        scores = masked_scores(group_query, keys_all[:, columns], mask, scale)
        top_score = jnp.max(scores, axis=-1, keepdims=True)
        expo = jnp.exp(scores - top_score)
        denom = jnp.sum(expo, axis=-1, keepdims=True)
        probs_low = (expo / denom).astype(jnp.bfloat16)
        pieces.append(
            jnp.einsum(
                "hrk,kd->rhd", probs_low, values_all[:, columns], preferred_element_type=jnp.float32
            )
        )
        totals.append(top_score + jnp.log(denom))
    return (jnp.concatenate(pieces, axis=1), totals)


def attend_back(query_low, keys_all, values_all, mask, totals, grad_heads, scale):
    group = HEADS // KV_HEADS
    grad_query, grad_keys, grad_values = ([], [], [])
    for head_group in range(KV_HEADS):
        heads_sel = slice(head_group * group, (head_group + 1) * group)
        columns = slice(head_group * HEAD, (head_group + 1) * HEAD)
        group_query = query_low[:, heads_sel, :]
        group_keys = keys_all[:, columns]
        group_grad = grad_heads[:, heads_sel, :]
        scores = masked_scores(group_query, group_keys, mask, scale)
        probs = jnp.exp(scores - totals[head_group])
        probs_low = probs.astype(jnp.bfloat16)
        grad_values.append(
            jnp.einsum("hrk,rhd->kd", probs_low, group_grad, preferred_element_type=jnp.float32)
        )
        grad_probs = jnp.einsum(
            "rhd,kd->hrk", group_grad, values_all[:, columns], preferred_element_type=jnp.float32
        )
        grad_scores = (
            probs * (grad_probs - jnp.sum(probs * grad_probs, axis=-1, keepdims=True))
        ).astype(jnp.bfloat16)
        grad_query.append(
            jnp.einsum("hrk,kd->rhd", grad_scores, group_keys, preferred_element_type=jnp.float32)
            * scale
        )
        grad_keys.append(
            jnp.einsum("hrk,rhd->kd", grad_scores, group_query, preferred_element_type=jnp.float32)
            * scale
        )
    return (
        jnp.concatenate(grad_query, axis=1),
        jnp.concatenate(grad_keys, axis=1),
        jnp.concatenate(grad_values, axis=1),
    )


def add_trees(left, right):
    return jax.tree.map(jnp.add, left, right)


def on_device(
    tokens,
    cotangent,
    segment,
    parent,
    w_qkv,
    qkv_bias,
    w_out,
    gain_attn,
    gain_ffn,
    w_gate,
    w_up,
    w_down,
):
    micro = tokens.shape[0]
    row_count = tokens.shape[1]
    slot_len = segment.shape[1]
    qwidth = HEADS * HEAD
    kwidth = KV_HEADS * HEAD
    scale = 1.0 / math.sqrt(HEAD)
    offset = lax.axis_index("gy") * row_count
    place_all = jnp.arange(slot_len, dtype=jnp.int32)
    place_own = offset + jnp.arange(row_count, dtype=jnp.int32)
    outputs, input_grads, attn_list, ffn_list = ([], [], [], [])
    for micro_index in range(micro):
        attn_full = (
            lax.all_gather(w_qkv, ("gx", "gy"), axis=0, tiled=True),
            lax.all_gather(qkv_bias, ("gx", "gy"), axis=0, tiled=True),
            lax.all_gather(w_out, ("gx", "gy"), axis=1, tiled=True),
            lax.all_gather(gain_attn, ("gx", "gy"), axis=0, tiled=True),
            lax.all_gather(gain_ffn, ("gx", "gy"), axis=0, tiled=True),
        )
        ffn_full = (
            lax.all_gather(w_gate, "gx", axis=0, tiled=True),
            lax.all_gather(w_up, "gx", axis=0, tiled=True),
            lax.all_gather(w_down, "gx", axis=1, tiled=True),
        )
        qkv_full, bias_full, out_full, gain_one_full, gain_two_full = attn_full
        gate_full, up_full, down_full = ffn_full
        gain_one = gain_one_full.astype(jnp.float32)
        gain_two = gain_two_full.astype(jnp.float32)
        seg_tree = segment[micro_index]
        valid, upper_one, upper_two, depth_pos = tree_tables(seg_tree, parent[micro_index])

        def take_own(array):
            return lax.dynamic_slice_in_dim(array, offset, row_count, 0)

        mask = allowed(
            take_own(seg_tree),
            take_own(upper_one),
            take_own(upper_two),
            place_own,
            seg_tree,
            valid,
            place_all,
        )
        cosine, sine = rotation(take_own(depth_pos), HEAD)
        inputs = tokens[micro_index].astype(jnp.float32)
        unit_one, inverse_one, normed_one = norm_parts(inputs, gain_one)
        linear = jnp.dot(
            normed_one, qkv_full, preferred_element_type=jnp.float32
        ) + bias_full.astype(jnp.float32)
        query_low = turn(linear[:, :qwidth].reshape(row_count, HEADS, HEAD), cosine, sine).astype(
            jnp.bfloat16
        )
        keys_low = turn(
            linear[:, qwidth : qwidth + kwidth].reshape(row_count, KV_HEADS, HEAD), cosine, sine
        )
        keys_low = keys_low.reshape(row_count, kwidth).astype(jnp.bfloat16)
        values_low = linear[:, qwidth + kwidth :].astype(jnp.bfloat16)
        keys_all, values_all = (
            lax.all_gather(keys_low, "gy", axis=0, tiled=True),
            lax.all_gather(values_low, "gy", axis=0, tiled=True),
        )
        heads_raw, totals = attend(query_low, keys_all, values_all, mask, scale)
        heads_out = heads_raw.reshape(row_count, qwidth).astype(jnp.bfloat16)
        resid = inputs + jnp.dot(heads_out, out_full, preferred_element_type=jnp.float32)
        unit_two, inverse_two, normed_two = norm_parts(resid, gain_two)
        normed_all = lax.all_gather(normed_two, "gy", axis=0, tiled=True)
        gate = jnp.dot(normed_all, gate_full, preferred_element_type=jnp.float32)
        upward = jnp.dot(normed_all, up_full, preferred_element_type=jnp.float32)
        sigma = jax.nn.sigmoid(gate)
        swish = gate * sigma
        hidden = (swish * upward).astype(jnp.bfloat16)
        ffn_own = lax.psum_scatter(
            jnp.dot(hidden, down_full, preferred_element_type=jnp.float32),
            "gy",
            scatter_dimension=0,
            tiled=True,
        )
        outputs.append((resid + ffn_own).astype(jnp.bfloat16))
        grad_low = cotangent[micro_index]
        grad_all = lax.all_gather(grad_low, "gy", axis=0, tiled=True)
        grad_hidden = jnp.dot(grad_all, down_full.T, preferred_element_type=jnp.float32)
        grad_down = jnp.dot(hidden.T, grad_all, preferred_element_type=jnp.float32)
        grad_gate = (grad_hidden * upward * sigma * (1.0 + gate * (1.0 - sigma))).astype(
            jnp.bfloat16
        )
        grad_up = (grad_hidden * swish).astype(jnp.bfloat16)
        grad_wgate = jnp.dot(normed_all.T, grad_gate, preferred_element_type=jnp.float32)
        grad_wup = jnp.dot(normed_all.T, grad_up, preferred_element_type=jnp.float32)
        grad_normed_two = lax.psum_scatter(
            jnp.dot(grad_gate, gate_full.T, preferred_element_type=jnp.float32)
            + jnp.dot(grad_up, up_full.T, preferred_element_type=jnp.float32),
            "gy",
            scatter_dimension=0,
            tiled=True,
        )
        back_two, grad_gain_two = norm_back(grad_normed_two, unit_two, inverse_two, gain_two)
        grad_resid = grad_low.astype(jnp.float32) + back_two
        grad_branch = grad_resid.astype(jnp.bfloat16)
        grad_wout = jnp.dot(heads_out.T, grad_branch, preferred_element_type=jnp.float32)
        grad_heads = jnp.dot(grad_branch, out_full.T, preferred_element_type=jnp.float32).astype(
            jnp.bfloat16
        )
        grad_heads = grad_heads.reshape(row_count, HEADS, HEAD)
        grad_query, keys_part, values_part = attend_back(
            query_low, keys_all, values_all, mask, totals, grad_heads, scale
        )
        grad_keys, grad_values = (
            lax.psum_scatter(keys_part, "gy", scatter_dimension=0, tiled=True),
            lax.psum_scatter(values_part, "gy", scatter_dimension=0, tiled=True),
        )
        query_lin = turn(grad_query, cosine, -sine).reshape(row_count, qwidth)
        keys_lin = turn(grad_keys.reshape(row_count, KV_HEADS, HEAD), cosine, -sine).reshape(
            row_count, kwidth
        )
        grad_linear = jnp.concatenate([query_lin, keys_lin, grad_values], axis=1).astype(
            jnp.bfloat16
        )
        grad_wqkv = jnp.dot(normed_one.T, grad_linear, preferred_element_type=jnp.float32)
        grad_bias = jnp.sum(grad_linear.astype(jnp.float32), axis=0)
        grad_normed_one = jnp.dot(grad_linear, qkv_full.T, preferred_element_type=jnp.float32)
        back_one, grad_gain_one = norm_back(grad_normed_one, unit_one, inverse_one, gain_one)
        input_grads.append((grad_resid + back_one).astype(jnp.bfloat16))
        attn_list.append((grad_wqkv, grad_bias, grad_wout, grad_gain_one, grad_gain_two))
        ffn_list.append((grad_wgate, grad_wup, grad_down))
    attn_total = reduce(add_trees, attn_list)
    ffn_total = reduce(add_trees, ffn_list)
    attn_total = (
        lax.psum_scatter(attn_total[0], ("gx", "gy"), scatter_dimension=0, tiled=True),
        lax.psum_scatter(attn_total[1], ("gx", "gy"), scatter_dimension=0, tiled=True),
        lax.psum_scatter(attn_total[2], ("gx", "gy"), scatter_dimension=1, tiled=True),
        lax.psum_scatter(attn_total[3], ("gx", "gy"), scatter_dimension=0, tiled=True),
        lax.psum_scatter(attn_total[4], ("gx", "gy"), scatter_dimension=0, tiled=True),
    )
    ffn_total = (
        lax.psum_scatter(ffn_total[0], "gx", scatter_dimension=0, tiled=True),
        lax.psum_scatter(ffn_total[1], "gx", scatter_dimension=0, tiled=True),
        lax.psum_scatter(ffn_total[2], "gx", scatter_dimension=1, tiled=True),
    )
    layer_out = jnp.stack(outputs, axis=0)
    grad_tokens = jnp.stack(input_grads, axis=0)
    return (
        layer_out,
        grad_tokens,
        attn_total[0],
        attn_total[1],
        attn_total[2],
        attn_total[3],
        attn_total[4],
        ffn_total[0],
        ffn_total[1],
        ffn_total[2],
    )


def dot_nn(left, right):
    return lax.dot_general(left, right, (((1,), (0,)), ((), ())), preferred_element_type=jnp.float32)


def dot_nt(left, right):
    return lax.dot_general(left, right, (((1,), (1,)), ((), ())), preferred_element_type=jnp.float32)


def dot_tn(left, right):
    return lax.dot_general(left, right, (((0,), (0,)), ((), ())), preferred_element_type=jnp.float32)


def cost(flops, moved, trans=0):
    return pl.CostEstimate(flops=int(flops * PACE), bytes_accessed=int(moved * PACE), transcendentals=int(trans * PACE))


def params(mib):
    return pltpu.CompilerParams(vmem_limit_bytes=mib * 1024 * 1024)


def sigmoid(v):
    return 0.5 * jnp.tanh(0.5 * v) + 0.5


def peers_of():
    me, plane = lax.axis_index("gy"), lax.axis_index("gx")
    along_x = me + 2 - 4 * lax.rem(me // 2, 2)
    return {
        CORE: {"gy": me + 1 - 2 * lax.rem(me, 2)},
        ALONG_X: {"gy": along_x},
        ALONG_Y: {"gy": me + 4 - 8 * (me // 4)},
        ACROSS: {"gy": along_x + 4 - 8 * (along_x // 4)},
        RING: {"gx": lax.rem(plane + 1, 4)},
        RING + 1: {"gx": lax.rem(plane + 2, 4)},
        -RING: {"gx": lax.rem(plane + 3, 4)},
    }


def greet(bits_used):
    peers = peers_of()
    barrier = pltpu.get_barrier_semaphore()
    greeted = [bits for bits in bits_used] + [-RING] * (RING in bits_used)
    for bits in greeted:
        pl.semaphore_signal(barrier, inc=1, device_id=peers[bits], device_id_type=pl.DeviceIdType.MESH)
    pl.semaphore_wait(barrier, len(greeted))


def side_copies(sides, sources, targets, sent, landed):
    peers = peers_of()
    copies = []
    for parts, target in zip(sides, targets):
        for _, take, fill, bits in parts:
            if take is None:
                take = (pl.multiple_of(peers[bits]["gy"] // 2 * fill[1], fill[1]), fill[1])
            copies.append(
                pltpu.make_async_remote_copy(
                    sources[len(copies)].at[pl.ds(*take)],
                    target.at[pl.ds(*fill)],
                    sent.at[len(copies)],
                    landed.at[len(copies)],
                    device_id=peers[bits],
                    device_id_type=pl.DeviceIdType.MESH,
                )
            )
    return copies


def whole_side(array, bits):
    return [(array, (0, array.shape[0]), (0, array.shape[0]), bits)]


def rows_side(array, start, count, bits):
    return [(array, (start, count), (0, count), bits)]


def chip_side(array, bits):
    return [(array, None, (0, array.shape[0] // 4), bits)]


def call_beside(body, sides, collective, operands, grid, in_specs, out_specs, out_shape, scratch_shapes, mib, estimate, name):
    n_in, n_out, n_scratch = len(in_specs), len(out_specs), len(scratch_shapes)
    flat = [part for parts in sides for part in parts]
    bits_used = sorted({part[3] for part in flat})

    def whole_body(*refs):
        ins, refs = refs[:n_in], refs[n_in:]
        sources, refs = refs[: len(flat)], refs[len(flat) :]
        outs, refs = refs[:n_out], refs[n_out:]
        targets, refs = refs[: len(sides)], refs[len(sides) :]
        scratch, refs = refs[:n_scratch], refs[n_scratch:]
        step, last = pl.program_id(0), pl.num_programs(0) - 1
        if flat:

            @pl.when(step == 0)
            def _():
                greet(bits_used)
                for copy in side_copies(sides, sources, targets, *refs):
                    copy.start()

        body(*ins, *outs, *scratch)
        if flat:

            @pl.when(step == last)
            def _():
                for copy in side_copies(sides, sources, targets, *refs):
                    copy.wait()

    anywhere = pl.BlockSpec(memory_space=pl.ANY)
    extra = {"collective_id": collective, "has_side_effects": True} if flat else {}
    results = pl.pallas_call(
        whole_body,
        grid=grid,
        in_specs=list(in_specs) + [anywhere] * len(flat),
        out_specs=list(out_specs) + [anywhere] * len(sides),
        out_shape=list(out_shape)
        + [jax.ShapeDtypeStruct((sum(p[2][1] for p in parts),) + parts[0][0].shape[1:], parts[0][0].dtype) for parts in sides],
        scratch_shapes=list(scratch_shapes) + ([pltpu.SemaphoreType.DMA((len(flat),))] * 2 if flat else []),
        compiler_params=pltpu.CompilerParams(vmem_limit_bytes=mib * 1024 * 1024, **extra),
        cost_estimate=estimate,
        name=name,
    )(*operands, *[part[0] for part in flat])
    return results[:n_out], results[n_out:]


def ffn_copies(chunk, pieces, held, sems):
    units = pieces[0].shape[1]
    tile = FFN_CHUNK // 2
    slot = chunk % 2
    copies = []
    for part in range(2):
        column = chunk * FFN_CHUNK + part * tile
        owner, inside = column // units, column % units
        for kind in range(3):
            copies.append(
                pltpu.make_async_copy(
                    pieces[3 * owner + kind].at[:, pl.ds(inside, tile)],
                    held.at[slot, kind, :, pl.ds(part * tile, tile)],
                    sems.at[slot, part * 3 + kind],
                )
            )
    return copies


def ffn_body(n_ref, c_ref, *refs):
    pieces = refs[:6]
    hid_ref, dg_ref, du_ref, f_ref, dn_ref, f_acc, dn_acc, held, sems = refs[6:]
    step = pl.program_id(0)
    chunks = 2 * pieces[0].shape[1] // FFN_CHUNK

    @pl.when(step == 0)
    def _():
        for copy in ffn_copies(0, pieces, held, sems):
            copy.start()
        f_acc[...] = jnp.zeros_like(f_acc)
        dn_acc[...] = jnp.zeros_like(dn_acc)

    for chunk in range(chunks):

        @pl.when(step == chunk)
        def _():
            if chunk + 1 < chunks:
                for copy in ffn_copies(chunk + 1, pieces, held, sems):
                    copy.start()
            for copy in ffn_copies(chunk, pieces, held, sems):
                copy.wait()

    slot = step % 2
    rows = n_ref.shape[0]
    part = rows // FFN_PARTS
    takes = [pl.ds(index * part, part) for index in range(FFN_PARTS)]

    def products(take):
        return (
            dot_nn(n_ref[take, :], held[slot, 0]),
            dot_nn(n_ref[take, :], held[slot, 1]),
            dot_nn(c_ref[take, :], held[slot, 2]),
        )

    later = products(takes[0])
    for index, take in enumerate(takes):
        gate, upward, grad_hidden = later
        if index + 1 < FFN_PARTS:
            later = products(takes[index + 1])
        sigma = sigmoid(gate)
        swish = gate * sigma
        hidden = (swish * upward).astype(jnp.bfloat16)
        hid_ref[take, :] = hidden
        grad_gate = (grad_hidden * upward * sigma * (1.0 + gate * (1.0 - sigma))).astype(jnp.bfloat16)
        grad_up = (grad_hidden * swish).astype(jnp.bfloat16)
        dg_ref[take, :] = grad_gate
        du_ref[take, :] = grad_up
        f_acc[take, :] += dot_nt(hidden, held[slot, 2])
        dn_acc[take, :] += dot_nt(grad_gate, held[slot, 0]) + dot_nt(grad_up, held[slot, 1])

    @pl.when(step == pl.num_programs(0) - 1)
    def _():
        f_ref[...] = f_acc[...].astype(f_ref.dtype)
        dn_ref[...] = dn_acc[...].astype(dn_ref.dtype)


def ffn_block(normed, cotan, pieces, collective, sides=()):
    rows, width = normed.shape
    units = 2 * pieces[0].shape[1]
    chunk = FFN_CHUNK
    whole = pl.BlockSpec((rows, width), lambda j: (0, 0))
    tall = pl.BlockSpec((rows, chunk), lambda j: (0, j))
    low = jnp.bfloat16
    return call_beside(
        ffn_body,
        sides,
        collective,
        (normed, cotan, *pieces),
        (units // chunk,),
        [whole, whole] + [pl.BlockSpec(memory_space=pl.ANY)] * len(pieces),
        [tall, tall, tall, whole, whole],
        [jax.ShapeDtypeStruct((rows, units), low)] * 3 + [jax.ShapeDtypeStruct((rows, width), low)] * 2,
        [pltpu.VMEM((rows, width), jnp.float32)] * 2
        + [pltpu.VMEM((2, 3, width, chunk), low), pltpu.SemaphoreType.DMA((2, len(pieces)))],
        60,
        cost(12 * rows * width * units, 6 * width * units + 6 * rows * (width + units)),
        "ffn_block",
    )


def wgrad_body(per_half, *refs):
    count = (len(refs) - 2) // 2
    total = dot_tn(refs[0][...], refs[count][...])
    for index in range(1, count):
        total = total + dot_tn(refs[index][...], refs[count + index][...])

    def store(out_ref):
        slots, _, wide = out_ref.shape
        for slot in range(slots):
            out_ref[slot] = total[:, slot * wide : (slot + 1) * wide].astype(out_ref.dtype)

    first = pl.program_id(0) < per_half
    pl.when(first)(lambda: store(refs[-2]))
    pl.when(jnp.logical_not(first))(lambda: store(refs[-1]))


def wgrad(lefts, rights, slots, collective, sides=()):
    rows, units = lefts[0].shape
    width = rights[0].shape[1]
    tile = WG_TILE
    per_half = units // 2 // tile
    wide = width // slots
    count = len(lefts)
    return call_beside(
        lambda *refs: wgrad_body(per_half, *refs),
        sides,
        collective,
        (*lefts, *rights),
        (units // tile,),
        [pl.BlockSpec((rows, tile), lambda j: (0, j))] * count
        + [pl.BlockSpec((rows, width), lambda j: (0, 0))] * count,
        [
            pl.BlockSpec((slots, tile, wide), lambda j: (0, jnp.minimum(j, per_half - 1), 0)),
            pl.BlockSpec((slots, tile, wide), lambda j: (0, jnp.maximum(j - per_half, 0), 0)),
        ],
        [jax.ShapeDtypeStruct((slots, units // 2, wide), jnp.bfloat16)] * 2,
        [],
        60,
        cost(2 * count * rows * width * units, 2 * count * rows * (width + units)),
        "ffn_wgrad",
    )


def group_rows(source_ref, group, per_group):
    return jnp.concatenate(
        [source_ref[:, (group * per_group + h) * HEAD : (group * per_group + h + 1) * HEAD] for h in range(per_group)],
        axis=0,
    )


def attend_body(list_ref, count_ref, q_ref, kv_ref, bias_ref, o_ref, lse_ref, qs, acc, top, den):
    block = pl.program_id(0)
    per_group = HEADS // KV_HEADS
    for group in range(KV_HEADS):
        qs[group] = group_rows(q_ref, group, per_group)
    acc[...] = jnp.zeros_like(acc)
    den[...] = jnp.zeros_like(den)
    top[...] = jnp.full_like(top, 2 * NEGATIVE)
    factor = LOG2E / math.sqrt(HEAD)

    def body(n, carry):
        rows = pl.ds(pl.multiple_of(list_ref[block, n] * KEY_TILE, KEY_TILE), KEY_TILE)
        bias = jnp.concatenate([bias_ref[rows, :].astype(jnp.float32)] * per_group, axis=1)
        products = [dot_nt(kv_ref[rows, g * HEAD : (g + 1) * HEAD], qs[g]) for g in range(KV_HEADS)]
        for group in range(KV_HEADS):
            values = kv_ref[rows, (KV_HEADS + group) * HEAD : (KV_HEADS + group + 1) * HEAD]
            scores = products[group] * factor + bias
            old = top[group]
            new = jnp.maximum(old, jnp.max(scores, axis=0, keepdims=True))
            probs = jnp.exp2(scores - new)
            shrink = jnp.exp2(old - new)
            den[group] = den[group] * shrink + jnp.sum(probs, axis=0, keepdims=True)
            acc[group] = acc[group] * shrink + dot_tn(values, probs.astype(jnp.bfloat16))
            top[group] = new
        return carry

    lax.fori_loop(0, count_ref[block], body, 0)
    for group in range(KV_HEADS):
        out = acc[group] / den[group]
        lse_ref[0, group] = top[group] + jnp.log(den[group]) * LOG2E
        for h in range(per_group):
            head = group * per_group + h
            o_ref[:, head * HEAD : (head + 1) * HEAD] = out[:, h * HEAD : (h + 1) * HEAD].T.astype(o_ref.dtype)


def attend_fast(block_list, block_count, query, keyval, bias):
    rows, qwidth = query.shape
    slots = keyval.shape[0]
    blocks = rows // QUERY_TILE
    per_group = HEADS // KV_HEADS
    lanes = per_group * QUERY_TILE
    whole = pl.BlockSpec(keyval.shape, lambda i, a, b: (0, 0))
    tile = pl.BlockSpec((QUERY_TILE, qwidth), lambda i, a, b: (i, 0))
    return pl.pallas_call(
        attend_body,
        grid_spec=pltpu.PrefetchScalarGridSpec(
            num_scalar_prefetch=2,
            grid=(blocks,),
            in_specs=[tile, whole, pl.BlockSpec((slots, QUERY_TILE), lambda i, a, b: (0, i))],
            out_specs=[tile, pl.BlockSpec((1, KV_HEADS, 1, lanes), lambda i, a, b: (i, 0, 0, 0))],
            scratch_shapes=[
                pltpu.VMEM((KV_HEADS, lanes, HEAD), jnp.bfloat16),
                pltpu.VMEM((KV_HEADS, HEAD, lanes), jnp.float32),
                pltpu.VMEM((KV_HEADS, 1, lanes), jnp.float32),
                pltpu.VMEM((KV_HEADS, 1, lanes), jnp.float32),
            ],
        ),
        out_shape=[
            jax.ShapeDtypeStruct((rows, qwidth), jnp.bfloat16),
            jax.ShapeDtypeStruct((blocks, KV_HEADS, 1, lanes), jnp.float32),
        ],
        compiler_params=params(48),
        cost_estimate=cost(2 * rows * slots * qwidth * 2, 4 * slots * rows, HEADS * rows * slots // 2),
        name="tree_attention",
    )(block_list, block_count, query, keyval, bias)


def attend_back_body(
    list_ref, count_ref, q_ref, kv_ref, bias_ref, lse_ref, o_ref, do_ref, cos_ref, sin_ref,
    dq_ref, dkv_ref, qs, dos, delta, dqt, dkv,
):
    block = pl.program_id(0)
    per_group = HEADS // KV_HEADS
    scale = 1.0 / math.sqrt(HEAD)
    factor = LOG2E * scale
    lanes = qs.shape[1]

    @pl.when(block == 0)
    def _():
        dkv[...] = jnp.zeros_like(dkv)

    for group in range(KV_HEADS):
        qs[group] = group_rows(q_ref, group, per_group)
        grads = group_rows(do_ref, group, per_group)
        dos[group] = grads
        both = grads.astype(jnp.float32) * group_rows(o_ref, group, per_group).astype(jnp.float32)
        delta[group] = lax.dot_general(
            jnp.ones((8, HEAD), jnp.float32), both, (((1,), (1,)), ((), ())),
            precision=lax.Precision.HIGHEST, preferred_element_type=jnp.float32,
        )[0:1]
    dqt[...] = jnp.zeros_like(dqt)

    def body(n, carry):
        rows = pl.ds(pl.multiple_of(list_ref[block, n] * KEY_TILE, KEY_TILE), KEY_TILE)
        bias = jnp.concatenate([bias_ref[rows, :].astype(jnp.float32)] * per_group, axis=1)
        for group in range(KV_HEADS):
            kcols = slice(group * HEAD, (group + 1) * HEAD)
            vcols = slice((KV_HEADS + group) * HEAD, (KV_HEADS + group + 1) * HEAD)
            keys = kv_ref[rows, kcols]
            values = kv_ref[rows, vcols]
            scores = dot_nt(keys, qs[group]) * factor + bias
            probs = jnp.exp2(scores - lse_ref[0, group])
            grad_probs = dot_nt(values, dos[group])
            grad_scores = (probs * (grad_probs - delta[group])).astype(jnp.bfloat16)
            dkv[rows, vcols] += dot_nn(probs.astype(jnp.bfloat16), dos[group])
            dkv[rows, kcols] += dot_nn(grad_scores, qs[group])
            dqt[group] += dot_tn(keys, grad_scores)
        return carry

    lax.fori_loop(0, count_ref[block], body, 0)
    cosine, sine = cos_ref[...], sin_ref[...]
    for group in range(KV_HEADS):
        for h in range(per_group):
            head = group * per_group + h
            grad = dqt[group, :, h * HEAD : (h + 1) * HEAD].T * scale
            grad = grad * cosine - pltpu.roll(grad, HEAD // 2, 1) * sine
            dq_ref[:, head * HEAD : (head + 1) * HEAD] = grad.astype(dq_ref.dtype)

    @pl.when(block == pl.num_programs(0) - 1)
    def _():
        kwidth = KV_HEADS * HEAD
        dkv_ref[:, :kwidth] = (dkv[:, :kwidth] * scale).astype(dkv_ref.dtype)
        dkv_ref[:, kwidth:] = dkv[:, kwidth:].astype(dkv_ref.dtype)


def attend_back_fast(block_list, block_count, query, keyval, bias, lse, heads_out, grad_heads, cosine, sine):
    rows, qwidth = query.shape
    slots = keyval.shape[0]
    blocks = rows // QUERY_TILE
    per_group = HEADS // KV_HEADS
    lanes = per_group * QUERY_TILE
    whole = pl.BlockSpec(keyval.shape, lambda i, a, b: (0, 0))
    tile = pl.BlockSpec((QUERY_TILE, qwidth), lambda i, a, b: (i, 0))
    turned = pl.BlockSpec((QUERY_TILE, HEAD), lambda i, a, b: (i, 0))
    return pl.pallas_call(
        attend_back_body,
        grid_spec=pltpu.PrefetchScalarGridSpec(
            num_scalar_prefetch=2,
            grid=(blocks,),
            in_specs=[
                tile,
                whole,
                pl.BlockSpec((slots, QUERY_TILE), lambda i, a, b: (0, i)),
                pl.BlockSpec((1, KV_HEADS, 1, lanes), lambda i, a, b: (i, 0, 0, 0)),
                tile,
                tile,
                turned,
                turned,
            ],
            out_specs=[tile, whole],
            scratch_shapes=[
                pltpu.VMEM((KV_HEADS, lanes, HEAD), jnp.bfloat16),
                pltpu.VMEM((KV_HEADS, lanes, HEAD), jnp.bfloat16),
                pltpu.VMEM((KV_HEADS, 1, lanes), jnp.float32),
                pltpu.VMEM((KV_HEADS, HEAD, lanes), jnp.float32),
                pltpu.VMEM(keyval.shape, jnp.float32),
            ],
        ),
        out_shape=[
            jax.ShapeDtypeStruct((rows, qwidth), jnp.bfloat16),
            jax.ShapeDtypeStruct(keyval.shape, jnp.bfloat16),
        ],
        compiler_params=params(56),
        cost_estimate=cost(5 * rows * slots * qwidth * 2, 8 * slots * rows, HEADS * rows * slots // 2),
        name="tree_attention_back",
    )(block_list, block_count, query, keyval, bias, lse, heads_out, grad_heads, cosine, sine)


def project_body(x_ref, gain_ref, w_ref, b_ref, cos_ref, sin_ref, n_ref, q_ref, kv_ref):
    values = x_ref[...].astype(jnp.float32)
    inverse = lax.rsqrt(jnp.mean(values * values, axis=-1, keepdims=True) + EPS)
    normed = (values * inverse * gain_ref[...]).astype(jnp.bfloat16)
    n_ref[...] = normed
    linear = dot_nn(normed, w_ref[...]) + b_ref[...]
    cosine, sine = cos_ref[...], sin_ref[...]
    for head in range(HEADS + KV_HEADS):
        lane = linear[:, head * HEAD : (head + 1) * HEAD]
        lane = (lane * cosine + pltpu.roll(lane, HEAD // 2, 1) * sine).astype(jnp.bfloat16)
        if head < HEADS:
            q_ref[:, head * HEAD : (head + 1) * HEAD] = lane
        else:
            kv_ref[:, (head - HEADS) * HEAD : (head - HEADS + 1) * HEAD] = lane
    kv_ref[:, KV_HEADS * HEAD :] = linear[:, (HEADS + KV_HEADS) * HEAD :].astype(jnp.bfloat16)


def project(inputs, gain, w_qkv, bias, cosine, sine):
    rows, width = inputs.shape
    qwidth, kwidth = HEADS * HEAD, 2 * KV_HEADS * HEAD
    tile = ROW_TILE
    fixed = lambda i: (0, 0)
    moving = lambda i: (i, 0)
    return pl.pallas_call(
        project_body,
        grid=(rows // tile,),
        in_specs=[
            pl.BlockSpec((tile, width), moving),
            pl.BlockSpec((1, width), fixed),
            pl.BlockSpec((width, qwidth + kwidth), fixed),
            pl.BlockSpec((1, qwidth + kwidth), fixed),
            pl.BlockSpec((tile, HEAD), moving),
            pl.BlockSpec((tile, HEAD), moving),
        ],
        out_specs=[
            pl.BlockSpec((tile, width), moving),
            pl.BlockSpec((tile, qwidth), moving),
            pl.BlockSpec((tile, kwidth), moving),
        ],
        out_shape=[
            jax.ShapeDtypeStruct((rows, width), jnp.bfloat16),
            jax.ShapeDtypeStruct((rows, qwidth), jnp.bfloat16),
            jax.ShapeDtypeStruct((rows, kwidth), jnp.bfloat16),
        ],
        compiler_params=params(48),
        cost_estimate=cost(2 * rows * width * (qwidth + kwidth), 2 * width * (qwidth + kwidth) + 8 * rows * width),
        name="project",
    )(inputs, gain, w_qkv, bias, cosine, sine)


def spread_body(*refs):
    owns, rows, whole, rows_x, rows_y, rows_d, sent, landed, kept = refs[:4], *refs[4:]
    me, plane = lax.axis_index("gy"), lax.axis_index("gx")
    peers = peers_of()
    along_x, along_y, across = (peers[bits]["gy"] for bits in OTHERS)
    places = [lax.rem(plane + 4 - k, 4) for k in range(4)]
    greet((CORE, ALONG_X, ALONG_Y))
    copies = []

    def send(source, target, bits):
        copy = pltpu.make_async_remote_copy(
            source,
            target,
            sent.at[len(copies)],
            landed.at[len(copies)],
            device_id=peers[bits],
            device_id_type=pl.DeviceIdType.MESH,
        )
        copies.append(copy)
        copy.start()
        return copy

    from_x, from_y, from_d, from_core, local = [], [], [], [], []
    for k in range(4):
        block = whole.at[places[k], me]
        from_x.append(send(owns[k], block, ALONG_X))
        from_y.append(send(owns[k], block, ALONG_Y))
        from_core.append(send(owns[k], block, CORE))
        local.append(pltpu.make_async_copy(owns[k], block, kept.at[k]))
        local[k].start()
    moved_x, moved_y = send(rows, rows_x, ALONG_X), send(rows, rows_y, ALONG_Y)
    for k in range(4):
        block_x, block_y = whole.at[places[k], along_x], whole.at[places[k], along_y]
        from_x[k].wait_recv()
        if k < 2:
            from_d.append(send(block_x, block_x, ALONG_Y))
        from_core.append(send(block_x, block_x, CORE))
        from_y[k].wait_recv()
        if k >= 2:
            from_d.append(send(block_y, block_y, ALONG_X))
        from_core.append(send(block_y, block_y, CORE))
    for k in range(4):
        block = whole.at[places[k], across]
        from_d[k].wait_recv()
        from_core.append(send(block, block, CORE))
    half = rows.shape[0] // 2
    first, second = pl.ds(0, half), pl.ds(half, half)
    moved_x.wait_recv()
    moved_d = [send(rows_x.at[first], rows_d.at[first], ALONG_Y)]
    moved_y.wait_recv()
    moved_d.append(send(rows_y.at[second], rows_d.at[second], ALONG_X))
    for copy in from_core + moved_d:
        copy.wait_recv()
    for copy in copies:
        copy.wait_send()
    for copy in local:
        copy.wait()


def spread(owns, rows):
    deep, wide = owns[0].shape
    anywhere = pl.BlockSpec(memory_space=pl.ANY)
    whole, *others = pl.pallas_call(
        spread_body,
        in_specs=[anywhere] * 5,
        out_specs=[anywhere] * 4,
        out_shape=[jax.ShapeDtypeStruct((4, 8, deep, wide), rows.dtype)]
        + [jax.ShapeDtypeStruct(rows.shape, rows.dtype)] * 3,
        scratch_shapes=[
            pltpu.SemaphoreType.DMA((32,)),
            pltpu.SemaphoreType.DMA((32,)),
            pltpu.SemaphoreType.DMA((4,)),
        ],
        compiler_params=pltpu.CompilerParams(collective_id=0, has_side_effects=True),
        cost_estimate=cost(0, 300 * 1024 * 1024),
        name="spread",
    )(*owns, rows)
    return whole.reshape(32 * deep, wide), others


def unit_back(grad_normed, values, gain):
    inverse = lax.rsqrt(jnp.mean(values * values, axis=-1, keepdims=True) + EPS)
    unit = values * inverse
    scaled = grad_normed * gain
    back = inverse * (scaled - unit * jnp.mean(scaled * unit, axis=-1, keepdims=True))
    return back, jnp.sum(grad_normed * unit, axis=0, keepdims=True)


def branch_back_body(own_ref, xa_ref, xb_ref, ya_ref, yb_ref, resid_ref, cot_ref, gain_ref, heads_ref, *refs):
    turned, (resid_out, heads_out, gain_out, weight_out, branch) = refs[:-5], refs[-5:]
    step, full = pl.program_id(0), jnp.float32
    tile = own_ref.shape[0]
    from_x = jnp.where(step < BRANCH_CUTS[0], xa_ref[...].astype(full), xb_ref[...].astype(full))
    from_y = jnp.where(step < BRANCH_CUTS[1], ya_ref[...].astype(full), yb_ref[...].astype(full))
    grad_normed = own_ref[...].astype(full) + from_x + from_y
    back, gain_part = unit_back(grad_normed, resid_ref[...], gain_ref[...])
    grad_resid = cot_ref[...].astype(full) + back
    resid_out[...] = grad_resid
    low = grad_resid.astype(jnp.bfloat16)
    branch[pl.ds(pl.multiple_of(step * tile, tile), tile), :] = low
    gain_out[...] = jnp.where(step == 0, 0.0, gain_out[...]) + gain_part
    wide = turned[0].shape[1]
    for index, piece in enumerate(turned):
        heads_out[:, index * wide : (index + 1) * wide] = dot_nn(low, piece[...]).astype(jnp.bfloat16)

    @pl.when(step == pl.num_programs(0) - 1)
    def _():
        weight_out[...] = dot_tn(branch[...], heads_ref[...]).astype(jnp.bfloat16)


def branch_back(own, from_x, from_y, resid, cotan, gain, heads, weights, first_column):
    rows, width = own.shape
    tile, wide = ROW_TILE, 512
    steps = rows // tile
    low, full = jnp.bfloat16, jnp.float32
    moving = pl.BlockSpec((tile, width), lambda i: (i, 0))
    fixed = pl.BlockSpec((1, width), lambda i: (0, 0))
    first, then = [], []
    for count in BRANCH_CUTS:
        first.append(pl.BlockSpec((tile, width), lambda i, n=count: (jnp.minimum(i, n - 1), 0)))
        then.append(pl.BlockSpec((tile, width), lambda i, n=count: (jnp.maximum(i - n, 0), 0)))
    return pl.pallas_call(
        branch_back_body,
        grid=(steps,),
        in_specs=[moving, first[0], then[0], first[1], then[1], moving, moving, fixed]
        + [pl.BlockSpec((rows, width), lambda i: (0, 0))]
        + [pl.BlockSpec((width, wide), lambda i, j=j: (0, first_column // wide + j)) for j in range(width // wide)],
        out_specs=[moving, moving, fixed, pl.BlockSpec((width, width), lambda i: (0, 0))],
        out_shape=[
            jax.ShapeDtypeStruct((rows, width), full),
            jax.ShapeDtypeStruct((rows, width), low),
            jax.ShapeDtypeStruct((1, width), full),
            jax.ShapeDtypeStruct((width, width), low),
        ],
        scratch_shapes=[pltpu.VMEM((rows, width), low)],
        compiler_params=params(56),
        cost_estimate=cost(4 * rows * width * width, 20 * rows * width + 4 * width * width),
        name="branch_back",
    )(own, *from_x, *from_y, resid, cotan, gain, heads, *[weights] * (width // wide))


def project_back_body(q_ref, own_ref, x_ref, y_ref, d_ref, cos_ref, sin_ref, w_ref, in_ref, gain_ref, resid_ref, normed_ref,
                      tokens_out, bias_out, gain_out, weight_out, linear):
    step, full = pl.program_id(0), jnp.float32
    tile, qwidth = q_ref.shape
    total = own_ref[...].astype(full) + x_ref[...].astype(full) + y_ref[...].astype(full) + d_ref[...].astype(full)
    pieces = [q_ref[...]]
    for head in range(2 * KV_HEADS):
        lane = total[:, head * HEAD : (head + 1) * HEAD]
        if head < KV_HEADS:
            lane = lane * cos_ref[...] - pltpu.roll(lane, HEAD // 2, 1) * sin_ref[...]
        pieces.append(lane.astype(jnp.bfloat16))
    lin = jnp.concatenate(pieces, axis=1)
    linear[pl.ds(pl.multiple_of(step * tile, tile), tile), :] = lin
    bias_part = jnp.sum(lin.astype(full), axis=0, keepdims=True)
    bias_out[...] = jnp.where(step == 0, 0.0, bias_out[...]) + bias_part
    back, gain_part = unit_back(dot_nt(lin, w_ref[...]), in_ref[...].astype(full), gain_ref[...])
    gain_out[...] = jnp.where(step == 0, 0.0, gain_out[...]) + gain_part
    tokens_out[...] = (resid_ref[...] + back).astype(jnp.bfloat16)

    @pl.when(step == pl.num_programs(0) - 1)
    def _():
        weight_out[:, : linear.shape[1]] = dot_tn(normed_ref[...], linear[...]).astype(jnp.bfloat16)


def project_back(query_lin, parts, cosine, sine, weights, inputs, gain, grad_resid, normed, collective, sides):
    rows, width = inputs.shape
    qwidth, kwidth = query_lin.shape[1], parts[0].shape[1]
    qwide, tile = qwidth + kwidth, ROW_TILE
    low, full = jnp.bfloat16, jnp.float32

    def moving(columns):
        return pl.BlockSpec((tile, columns), lambda i: (i, 0))

    def fixed(high, columns):
        return pl.BlockSpec((high, columns), lambda i: (0, 0))

    return call_beside(
        project_back_body,
        sides,
        collective,
        (query_lin, *parts, cosine, sine, weights, inputs, gain, grad_resid, normed),
        (rows // tile,),
        [moving(qwidth)]
        + [moving(kwidth)] * 4
        + [moving(HEAD)] * 2
        + [fixed(width, qwide), moving(width), fixed(1, width), moving(width), fixed(rows, width)],
        [moving(width), fixed(1, qwide), fixed(1, width), fixed(width, qwide + HEAD)],
        [
            jax.ShapeDtypeStruct((rows, width), low),
            jax.ShapeDtypeStruct((1, qwide), full),
            jax.ShapeDtypeStruct((1, width), full),
            jax.ShapeDtypeStruct((width, qwide + HEAD), low),
        ],
        [pltpu.VMEM((rows, qwide), low)],
        56,
        cost(4 * rows * width * qwide, 20 * rows * width + 4 * width * qwide),
        "project_back",
    )


def both_body(first_mine, first_other, second_mine, second_other, out_ref):
    deep = first_mine.shape[1]
    out_ref[0, :deep] = (first_mine[0].astype(jnp.float32) + first_other[0].astype(jnp.float32)).astype(out_ref.dtype)
    out_ref[0, deep:] = (second_mine[0].astype(jnp.float32) + second_other[0].astype(jnp.float32)).astype(out_ref.dtype)


def both_sums(*arrays):
    planes, deep, wide = arrays[0].shape
    return pl.pallas_call(
        both_body,
        grid=(planes,),
        in_specs=[pl.BlockSpec((1, deep, wide), lambda i: (i, 0, 0))] * 4,
        out_specs=pl.BlockSpec((1, 2 * deep, wide), lambda i: (i, 0, 0)),
        out_shape=jax.ShapeDtypeStruct((planes, 2 * deep, wide), arrays[0].dtype),
        compiler_params=params(48),
        cost_estimate=cost(0, 12 * planes * deep * wide),
        name="both_back",
    )(*arrays)


def finish_body(wide_ref, out_ref, mine_ref, other_ref, both_ref, tokens_ref, resid_ref, *refs):
    layer_refs, results, rows_out, scratch = refs[:3], refs[3:8], refs[8:10], refs[10:]
    kept, got_core, got_first, got_second, got_ring = [scratch[i : i + 2] for i in range(0, 10, 2)]
    units, got_units, units_ring, units_moving, both, layer, resid, *layer_parts, sent, landed, local = scratch[10:]
    me, plane = lax.axis_index("gy"), lax.axis_index("gx")
    core, x, y = lax.rem(me, 2), lax.rem(me // 2, 2), me // 4
    places = [lax.rem(plane + 4 - s, 4) for s in range(4)]
    peers = peers_of()
    full = jnp.float32
    greet((CORE, ALONG_X, ALONG_Y, RING, RING + 1))
    copies, loads = [], []

    def send(source, target, bits):
        copy = pltpu.make_async_remote_copy(
            source,
            target,
            sent.at[len(copies)],
            landed.at[len(copies)],
            device_id=peers[bits],
            device_id_type=pl.DeviceIdType.MESH,
        )
        copies.append(copy)
        copy.start()
        return copy

    def load(source, target):
        copy = pltpu.make_async_copy(source, target, local.at[len(loads)])
        loads.append(copy)
        copy.start()
        return copy

    inputs = (wide_ref, out_ref)
    core_copies = [send(inputs[i].at[:, :, :, 1 - core], got_core[i], CORE) for i in range(2)]
    unit_loads = [load(mine_ref, units), load(other_ref, got_units)]
    both_load = load(both_ref, both)
    layer_loads = [load(a, b) for a, b in zip((resid_ref, *layer_refs), (resid, *layer_parts))]
    held = [load(inputs[i].at[:, :, :, core], kept[i]) for i in range(2)]

    for copy in unit_loads:
        copy.wait()

    @pl.loop(0, 4)
    def _(p):
        units[p] += got_units[p]

    units_copy = send(units.at[places[1]], units_ring.at[0], RING)
    steps = []
    for i in range(2):
        core_copies[i].wait_recv()
        held[i].wait()

        @pl.loop(0, 4)
        def _(p):
            for a in range(2):
                for b in range(2):
                    kept[i][p, a, b] += got_core[i][p, a, b]

        middle = kept[i].shape[-1] // 256 * 128
        first, second = pl.ds(0, middle), pl.ds(middle, kept[i].shape[-1] - middle)
        steps.append((
            send(kept[i].at[:, :, 1 - x, :, first], got_first[i].at[:, :, :, first], ALONG_X),
            send(kept[i].at[:, 1 - y, :, :, second], got_first[i].at[:, :, :, second], ALONG_Y),
            first,
            second,
        ))
    units_copy.wait_recv()
    units_moving[0] = units[places[2]] + units_ring[0]
    units_copy = send(units_moving.at[0], units_ring.at[1], RING)
    for copy in layer_loads:
        copy.wait()

    @pl.loop(0, resid.shape[0] // ROW_TILE)
    def _(p):
        take = pl.ds(pl.multiple_of(p * ROW_TILE, ROW_TILE), ROW_TILE)
        total = layer_parts[0][take, :].astype(full) + layer_parts[1][take, :].astype(full)
        layer[take, :] = (resid[take, :] + (total + layer_parts[2][take, :].astype(full))).astype(jnp.bfloat16)

    half = resid.shape[0] // 2
    row_copies = []
    for source, target in ((layer, rows_out[0]), (tokens_ref, rows_out[1])):
        row_copies.append(send(source.at[pl.ds((1 - core) * half, half)], target.at[core], CORE))
        held.append(load(source.at[pl.ds(core * half, half)], target.at[core]))
    both_load.wait()
    high, own = both.shape[0] // 2, results[3].shape[0]
    results[3][...] = both[0:own, :].astype(full)
    results[4][...] = both[high : high + own, :].astype(full)
    nexts = []
    for i in range(2):
        first_copy, second_copy, first, second = steps[i]
        first_copy.wait_recv()

        @pl.loop(0, 4)
        def _(p):
            for a in range(2):
                kept[i][p, a, x, :, first] += got_first[i][p, a, :, first]

        third_copy = send(kept[i].at[:, 1 - y, x, :, first], got_second[i].at[:, :, first], ALONG_Y)
        second_copy.wait_recv()

        @pl.loop(0, 4)
        def _(p):
            for b in range(2):
                kept[i][p, y, b, :, second] += got_first[i][p, b, :, second]

        nexts.append((third_copy, send(kept[i].at[:, y, 1 - x, :, second], got_second[i].at[:, :, second], ALONG_X)))
    units_copy.wait_recv()
    units_moving[1] = units[places[3]] + units_ring[1]
    units_copy = send(units_moving.at[1], units_ring.at[2], RING)
    ring_copies = []
    for i in range(2):
        for copy in nexts[i]:
            copy.wait_recv()

        @pl.loop(0, 4)
        def _(p):
            kept[i][p, y, x] += got_second[i][p]

        for k, bits in ((1, RING), (2, RING + 1), (3, -RING)):
            there = lax.rem(plane + k, 4)
            ring_copies.append(send(kept[i].at[there, y, x], got_ring[i].at[k - 1], bits))
    units_copy.wait_recv()
    results[2][...] = units[places[0], 0:own, :].astype(full) + units_ring[2, 0:own, :].astype(full)
    for i in range(2):
        total = kept[i][plane, y, x].astype(full)
        for k in range(3):
            ring_copies[3 * i + k].wait_recv()
            total = total + got_ring[i][k].astype(full)
        results[i][...] = total
    for copy in row_copies:
        copy.wait_recv()
    for copy in held[2:]:
        copy.wait()
    for copy in copies:
        copy.wait_send()


def finish(wide, out, mine, other, both, tokens, resid, layer_parts, own_units, collective):
    low, full = jnp.bfloat16, jnp.float32
    deep = wide.shape[0] // 32
    wide, out = (a.reshape(4, 2, 2, 2, deep, a.shape[1]) for a in (wide, out))
    columns = (wide.shape[-1], out.shape[-1])
    block = mine.shape[1:]
    anywhere = pl.BlockSpec(memory_space=pl.ANY)
    inside = pl.BlockSpec(memory_space=pltpu.VMEM)

    def pairs(*lead):
        return [pltpu.VMEM((*lead, deep, c), low) for c in columns]

    return pl.pallas_call(
        finish_body,
        in_specs=[anywhere] * 10,
        out_specs=[inside] * 5 + [anywhere] * 2,
        out_shape=[jax.ShapeDtypeStruct((deep, c), full) for c in columns]
        + [jax.ShapeDtypeStruct((own_units, block[1]), full)] * 3
        + [jax.ShapeDtypeStruct((2, tokens.shape[0] // 2, tokens.shape[1]), low)] * 2,
        scratch_shapes=[
            *pairs(4, 2, 2),
            *pairs(4, 2, 2),
            *pairs(4, 2),
            *pairs(4),
            *pairs(3),
            pltpu.VMEM((4, *block), low),
            pltpu.VMEM((4, *block), low),
            pltpu.VMEM((3, *block), low),
            pltpu.VMEM((2, *block), low),
            pltpu.VMEM(both.shape, low),
            pltpu.VMEM(tokens.shape, low),
            pltpu.VMEM(resid.shape, full),
            *[pltpu.VMEM(tokens.shape, low)] * 3,
            pltpu.SemaphoreType.DMA((21,)),
            pltpu.SemaphoreType.DMA((21,)),
            pltpu.SemaphoreType.DMA((11,)),
        ],
        compiler_params=pltpu.CompilerParams(
            vmem_limit_bytes=60 * 1024 * 1024, collective_id=collective, has_side_effects=True
        ),
        cost_estimate=cost(0, 200 * 1024 * 1024),
        name="finish",
    )(wide, out, mine, other, both, tokens, resid, *layer_parts)


def swap(array, bits):
    return lax.ppermute(array, "gy", [(i, i ^ bits) for i in range(8)])


def pick(array, index):
    return lax.dynamic_index_in_dim(array, index, 0, keepdims=False)


def after(array, *earlier):
    return lax.optimization_barrier((array, *earlier))[0]


def pair_rows(pair, core):
    kept, got = pick(pair, core), swap(pick(pair, 1 - core), CORE)
    return jnp.where(core == 0, jnp.concatenate([kept, got]), jnp.concatenate([got, kept]))


def plane_order(blocks, chip):
    rows = blocks[0].shape[0]
    whole = jnp.zeros((4 * rows,) + blocks[0].shape[1:], blocks[0].dtype)
    for index, block in enumerate(blocks):
        whole = lax.dynamic_update_slice_in_dim(whole, block, (chip ^ index) * rows, 0)
    return whole


def on_core(
    tokens,
    cotangent,
    segment,
    parent,
    w_qkv,
    qkv_bias,
    w_out,
    gain_attn,
    gain_ffn,
    w_gate,
    w_up,
    w_down,
):
    low, full = jnp.bfloat16, jnp.float32
    me = lax.axis_index("gy")
    plane = lax.axis_index("gx")
    core, chip = me % 2, me // 2
    rows, width = 2 * tokens.shape[1], tokens.shape[2]
    slot_len = segment.shape[1]
    own_units = w_gate.shape[1]
    pad_units = -(-own_units // 384) * 384
    qwidth, kwidth = HEADS * HEAD, KV_HEADS * HEAD
    offset = chip * rows

    nb, ng = qkv_bias.shape[0], gain_attn.shape[0]
    packed = jnp.concatenate([qkv_bias, gain_attn, gain_ffn]).reshape(-1, 1)
    packed = jnp.pad(packed, ((0, 4 * ng - packed.shape[0]), (0, 0))).reshape(4, ng).T
    packed = jnp.pad(packed, ((0, 0), (0, HEAD - 4)))
    attn_own = jnp.concatenate([w_qkv, w_out.T, packed], axis=1)
    attn_slots = [attn_own] + [
        lax.ppermute(attn_own, "gx", [(i, (i + k) % 4) for i in range(4)]) for k in (1, 2, 3)
    ]

    inputs_low = pair_rows(tokens, core)
    grad_low = pair_rows(cotangent, core)

    seg_tree = pick(segment, core)
    valid, upper_one, upper_two, depth_pos = tree_tables(seg_tree, pick(parent, core))
    places = jnp.arange(slot_len, dtype=jnp.int32)

    def take_own(array):
        return lax.dynamic_slice_in_dim(array, offset, rows, 0)

    cosine, sine = rotation(take_own(depth_pos), HEAD)
    sine = sine * jnp.where(jnp.arange(HEAD) < HEAD // 2, -1.0, 1.0)

    more = pad_units - own_units
    shards = [jnp.pad(w, ((0, 0), (0, more))) for w in (w_gate, w_up, w_down.T)]
    weights = [
        lax.all_gather(after(w, *attn_slots, inputs_low, grad_low), "gx", axis=0, tiled=True) for w in shards[:2]
    ]
    weights.append(lax.all_gather(after(shards[2], weights[0]), "gx", axis=0, tiled=True))
    attn_all, cotan_others = spread([after(s, inputs_low, cosine, sine, *shards) for s in attn_slots], grad_low)
    cotan_blocks = [grad_low] + cotan_others
    qwide = qwidth + 2 * kwidth
    small = attn_all[:, qwide + width :].reshape(32, ng, HEAD)[:, :, :4].transpose(0, 2, 1).reshape(32, 4 * ng)
    small = small.astype(full)
    bias_full = small[:, :nb].reshape(1, -1)
    gain_one = small[:, nb : nb + ng].reshape(1, -1)
    gain_two = small[:, nb + ng : nb + 2 * ng].reshape(1, -1)
    out_turned = attn_all[:, qwide : qwide + width]

    normed_one, query, keyval_own = project(inputs_low, gain_one, attn_all, bias_full, cosine, sine)
    mask = allowed(
        after(take_own(seg_tree), keyval_own), take_own(upper_one), take_own(upper_two), take_own(places), seg_tree, valid, places
    )
    qblocks, kblocks = rows // QUERY_TILE, slot_len // KEY_TILE
    active = mask.reshape(qblocks, QUERY_TILE, kblocks, KEY_TILE).any(axis=(1, 3))
    block_count = active.sum(axis=1).astype(jnp.int32)
    rank = jnp.cumsum(active.astype(jnp.int32), axis=1) - 1
    numbers = jnp.arange(kblocks, dtype=jnp.int32)
    hit = active[:, :, None] & (rank[:, :, None] == numbers[None, None, :])
    block_list = jnp.sum(jnp.where(hit, numbers[None, :, None], 0), axis=1).astype(jnp.int32)
    mask_bias = jnp.where(mask.T, 0.0, NEGATIVE).astype(low)

    keyval = plane_order([keyval_own] + [swap(keyval_own, bits) for bits in OTHERS], chip)
    other_weights = [swap(after(w, keyval), CORE) for w in weights[:2]]
    query = after(query, *other_weights)
    heads_out, lse = attend_fast(block_list, block_count, query, keyval, mask_bias)
    inputs = inputs_low.astype(full)
    resid = inputs + lax.dot_general(heads_out, out_turned, (((1,), (1,)), ((), ())), preferred_element_type=full)
    normed_two = norm_parts(resid, gain_two)[2]

    other_weights.append(swap(after(weights[2], heads_out), CORE))
    pieces = weights + other_weights
    half = rows // 2
    first, second = (0, half), (half, half)
    own, (normed_x, normed_y) = ffn_block(
        normed_two, cotan_blocks[0], pieces, 1, [whole_side(normed_two, ALONG_X), whole_side(normed_two, ALONG_Y)]
    )
    passed_on = [(normed_x, first, first, ALONG_Y), (normed_y, second, second, ALONG_X)]
    near_x, (normed_d,) = ffn_block(normed_x, cotan_blocks[1], pieces, 2, [passed_on])
    cut, early = (count * ROW_TILE for count in BRANCH_CUTS)
    rest, few = rows - cut, rows // 10 * 3
    far, (back_x,) = ffn_block(normed_d, cotan_blocks[3], pieces, 3, [rows_side(near_x[4], 0, cut, ALONG_X)])
    near_y, (back_d,) = ffn_block(
        after(normed_y, far[4]), cotan_blocks[2], pieces, 4, [rows_side(far[4], 0, cut, ALONG_X)]
    )
    normed_blocks = [normed_two, normed_x, normed_y, normed_d]
    hidden_b, gate_b, up_b, out_b, back_b = zip(own, near_x, near_y, far)

    def join(mine, passed):
        return (mine.astype(full) + passed.astype(full)).astype(low)

    (down_mine, down_sent), (back_x_end, back_d_end, out_d_end, back_y) = wgrad(
        hidden_b,
        cotan_blocks,
        4,
        5,
        [
            rows_side(back_b[1], cut, rest, ALONG_X),
            rows_side(back_b[3], cut, rest, ALONG_X),
            rows_side(out_b[3], 0, few, ALONG_X),
            rows_side(join(back_b[2][:early], back_d[:early]), 0, early, ALONG_Y),
        ],
    )
    late = join(back_b[2][early:], jnp.concatenate([back_d[early:], back_d_end]))
    (gate_mine, gate_sent), (down_got, out_d, back_y_end) = wgrad(
        gate_b,
        normed_blocks,
        4,
        6,
        [
            whole_side(down_sent, CORE),
            rows_side(out_b[3], few, rows - few, ALONG_X),
            rows_side(late, 0, rows - early, ALONG_Y),
        ],
    )
    gate_got = swap(gate_sent, CORE)
    out_d = jnp.concatenate([out_d_end, out_d])

    grad_resid, grad_heads, grad_gain_two, grad_wout = branch_back(
        back_b[0],
        (back_x, back_x_end),
        (back_y, back_y_end),
        resid,
        grad_low,
        gain_two,
        heads_out,
        attn_all,
        qwide,
    )
    out_got = [swap(after(out_b[1], gate_sent), ALONG_X), swap(join(out_b[2], out_d), ALONG_Y)]
    both = both_sums(down_mine, down_got, gate_mine, gate_got)
    grad_heads = after(grad_heads, grad_wout, both)
    both = lax.psum_scatter(both, "gx", scatter_dimension=0, tiled=True)[0]
    query_lin, keyval_part = attend_back_fast(
        block_list, block_count, query, keyval, mask_bias, lse, heads_out, grad_heads, cosine, sine
    )

    keyval_own = lax.dynamic_slice_in_dim(keyval_part, offset, rows, 0)
    (up_mine, up_sent), others = wgrad(
        up_b, normed_blocks, 4, 7, [chip_side(keyval_part, bits) for bits in OTHERS]
    )

    (grad_rows, grad_bias, grad_gain_one, grad_wqkv), (up_got,) = project_back(
        query_lin,
        (keyval_own, *others),
        cosine,
        sine,
        attn_all,
        inputs_low,
        gain_one,
        grad_resid,
        normed_one,
        9,
        [whole_side(up_sent, CORE)],
    )
    packed = jnp.concatenate(
        [grad_bias.reshape(32, nb), grad_gain_one.reshape(32, ng), grad_gain_two.reshape(32, ng)], axis=1
    )
    packed = jnp.pad(packed, ((0, 0), (0, 4 * ng - packed.shape[1]))).reshape(32, 4, ng).transpose(0, 2, 1)
    packed = jnp.pad(packed.reshape(32 * ng, 4), ((0, 0), (0, HEAD - 4))).astype(low)
    wide, grad_wout, grad_wup, grad_down, grad_wgate, layer_out, grad_tokens = finish(
        lax.dynamic_update_slice_in_dim(grad_wqkv, packed, qwide, 1),
        grad_wout,
        up_mine,
        up_got,
        both,
        grad_rows,
        resid,
        (out_b[0], *out_got),
        own_units,
        8,
    )
    grad_wqkv, grad_wout = wide[:, :qwide], grad_wout.T
    small = wide[:, qwide : qwide + 4].T.reshape(-1)
    grad_wgate, grad_wup = grad_wgate.T, grad_wup.T
    return (
        layer_out,
        grad_tokens,
        grad_wqkv,
        small[:nb],
        grad_wout,
        small[nb : nb + ng],
        small[nb + ng : nb + 2 * ng],
        grad_wgate,
        grad_wup,
        grad_down,
    )


def solution(mesh):
    in_specs = (
        P("gx", "gy", None),
        P("gx", "gy", None),
        P("gx", None),
        P("gx", None),
        P(("gx", "gy"), None),
        P(("gx", "gy")),
        P(None, ("gx", "gy")),
        P(("gx", "gy")),
        P(("gx", "gy")),
        P("gx", "gy"),
        P("gx", "gy"),
        P("gy", "gx"),
    )
    out_specs = (
        P("gx", "gy", None),
        P("gx", "gy", None),
        P(("gx", "gy"), None),
        P(("gx", "gy")),
        P(None, ("gx", "gy")),
        P(("gx", "gy")),
        P(("gx", "gy")),
        P("gx", "gy"),
        P("gx", "gy"),
        P("gy", "gx"),
    )
    return jax.shard_map(
        on_core if tuple(mesh.shape.values()) == (4, 8) else on_device,
        mesh=mesh,
        in_specs=in_specs,
        out_specs=out_specs,
        check_vma=False,
    )
```

```python
from functools import reduce
import math

import jax
import jax.numpy as jnp
from jax import lax
from jax.experimental import pallas as pl
from jax.experimental.pallas import tpu as pltpu
from jax.sharding import PartitionSpec as P

HEADS = 12
KV_HEADS = 2
HEAD = 128

QUERY_TILE = 128
KEY_TILE = 256
ROW_TILE = 128
BRANCH_CUTS = (4, 3)
FFN_CHUNK = 768
FFN_PARTS = 2
WG_TILE = 384
PACE = 1.0
LOG2E = 1.0 / math.log(2.0)

CORE, ALONG_X, ALONG_Y, ACROSS = 1, 2, 4, 6
OTHERS = (ALONG_X, ALONG_Y, ACROSS)
RING = 8


EPS = 1e-06
THETA = 1000000.0
NEGATIVE = -1e30


def tree_tables(segment, parent):
    slot_len = segment.shape[0]
    seg_count = parent.shape[0]
    places = jnp.arange(slot_len, dtype=jnp.int32)
    labels = jnp.arange(seg_count, dtype=jnp.int32)
    member = segment[:, None] == labels[None, :]
    valid = segment >= 0
    first = jnp.min(jnp.where(member, places[:, None], slot_len), axis=0)
    length = jnp.sum(member.astype(jnp.int32), axis=0)
    parent_hit = parent[:, None] == labels[None, :]
    grand = jnp.sum(jnp.where(parent_hit, parent[None, :], 0), axis=1)
    grand_hit = grand[:, None] == labels[None, :]
    parent_len = jnp.sum(jnp.where(parent_hit, length[None, :], 0), axis=1)
    grand_len = jnp.sum(jnp.where(grand_hit, length[None, :], 0), axis=1)
    base = jnp.where(parent != labels, parent_len, 0) + jnp.where(grand != parent, grand_len, 0)

    def lookup(table):
        return jnp.sum(jnp.where(member, table[None, :], 0), axis=1)

    upper_one = jnp.where(valid, lookup(parent), -2)
    upper_two = jnp.where(valid, lookup(grand), -2)
    depth_pos = jnp.where(valid, places - lookup(first) + lookup(base), 0)
    return (valid, upper_one, upper_two, depth_pos)


def allowed(seg_query, upper_one, upper_two, place_query, seg_keys, valid_keys, place_keys):
    related = (seg_keys[None, :] == seg_query[:, None]) | (seg_keys[None, :] == upper_one[:, None])
    related = related | (seg_keys[None, :] == upper_two[:, None])
    earlier = place_keys[None, :] <= place_query[:, None]
    return related & earlier & valid_keys[None, :] | (place_keys[None, :] == place_query[:, None])


def rotation(depth_pos, width):
    half = width // 2
    freqs = jnp.exp(jnp.arange(half, dtype=jnp.float32) * (-2.0 * math.log(THETA) / width))
    angle = depth_pos.astype(jnp.float32)[:, None] * freqs[None, :]
    cosine = jnp.concatenate([jnp.cos(angle), jnp.cos(angle)], axis=1)
    sine = jnp.concatenate([jnp.sin(angle), jnp.sin(angle)], axis=1)
    return (cosine, sine)


def turn(heads, cosine, sine):
    half = heads.shape[-1] // 2
    swapped = jnp.concatenate([-heads[..., half:], heads[..., :half]], axis=-1)
    return heads * cosine[:, None, :] + swapped * sine[:, None, :]


def norm_parts(values, gain):
    inverse = lax.rsqrt(jnp.mean(values * values, axis=-1, keepdims=True) + EPS)
    unit = values * inverse
    return (unit, inverse, (unit * gain).astype(jnp.bfloat16))


def norm_back(grad_normed, unit, inverse, gain):
    scaled = grad_normed * gain
    back = inverse * (scaled - unit * jnp.mean(scaled * unit, axis=-1, keepdims=True))
    return (back, jnp.sum(grad_normed * unit, axis=0))


def masked_scores(group_query, group_keys, mask, scale):
    scores = (
        jnp.einsum("rhd,kd->hrk", group_query, group_keys, preferred_element_type=jnp.float32)
        * scale
    )
    return jnp.where(mask[None], scores, NEGATIVE)


def attend(query_low, keys_all, values_all, mask, scale):
    group = HEADS // KV_HEADS
    pieces = []
    totals = []
    for head_group in range(KV_HEADS):
        group_query = query_low[:, head_group * group : (head_group + 1) * group, :]
        columns = slice(head_group * HEAD, (head_group + 1) * HEAD)
        scores = masked_scores(group_query, keys_all[:, columns], mask, scale)
        top_score = jnp.max(scores, axis=-1, keepdims=True)
        expo = jnp.exp(scores - top_score)
        denom = jnp.sum(expo, axis=-1, keepdims=True)
        probs_low = (expo / denom).astype(jnp.bfloat16)
        pieces.append(
            jnp.einsum(
                "hrk,kd->rhd", probs_low, values_all[:, columns], preferred_element_type=jnp.float32
            )
        )
        totals.append(top_score + jnp.log(denom))
    return (jnp.concatenate(pieces, axis=1), totals)


def attend_back(query_low, keys_all, values_all, mask, totals, grad_heads, scale):
    group = HEADS // KV_HEADS
    grad_query, grad_keys, grad_values = ([], [], [])
    for head_group in range(KV_HEADS):
        heads_sel = slice(head_group * group, (head_group + 1) * group)
        columns = slice(head_group * HEAD, (head_group + 1) * HEAD)
        group_query = query_low[:, heads_sel, :]
        group_keys = keys_all[:, columns]
        group_grad = grad_heads[:, heads_sel, :]
        scores = masked_scores(group_query, group_keys, mask, scale)
        probs = jnp.exp(scores - totals[head_group])
        probs_low = probs.astype(jnp.bfloat16)
        grad_values.append(
            jnp.einsum("hrk,rhd->kd", probs_low, group_grad, preferred_element_type=jnp.float32)
        )
        grad_probs = jnp.einsum(
            "rhd,kd->hrk", group_grad, values_all[:, columns], preferred_element_type=jnp.float32
        )
        grad_scores = (
            probs * (grad_probs - jnp.sum(probs * grad_probs, axis=-1, keepdims=True))
        ).astype(jnp.bfloat16)
        grad_query.append(
            jnp.einsum("hrk,kd->rhd", grad_scores, group_keys, preferred_element_type=jnp.float32)
            * scale
        )
        grad_keys.append(
            jnp.einsum("hrk,rhd->kd", grad_scores, group_query, preferred_element_type=jnp.float32)
            * scale
        )
    return (
        jnp.concatenate(grad_query, axis=1),
        jnp.concatenate(grad_keys, axis=1),
        jnp.concatenate(grad_values, axis=1),
    )


def add_trees(left, right):
    return jax.tree.map(jnp.add, left, right)


def on_device(
    tokens,
    cotangent,
    segment,
    parent,
    w_qkv,
    qkv_bias,
    w_out,
    gain_attn,
    gain_ffn,
    w_gate,
    w_up,
    w_down,
):
    micro = tokens.shape[0]
    row_count = tokens.shape[1]
    slot_len = segment.shape[1]
    qwidth = HEADS * HEAD
    kwidth = KV_HEADS * HEAD
    scale = 1.0 / math.sqrt(HEAD)
    offset = lax.axis_index("gy") * row_count
    place_all = jnp.arange(slot_len, dtype=jnp.int32)
    place_own = offset + jnp.arange(row_count, dtype=jnp.int32)
    outputs, input_grads, attn_list, ffn_list = ([], [], [], [])
    for micro_index in range(micro):
        attn_full = (
            lax.all_gather(w_qkv, ("gx", "gy"), axis=0, tiled=True),
            lax.all_gather(qkv_bias, ("gx", "gy"), axis=0, tiled=True),
            lax.all_gather(w_out, ("gx", "gy"), axis=1, tiled=True),
            lax.all_gather(gain_attn, ("gx", "gy"), axis=0, tiled=True),
            lax.all_gather(gain_ffn, ("gx", "gy"), axis=0, tiled=True),
        )
        ffn_full = (
            lax.all_gather(w_gate, "gx", axis=0, tiled=True),
            lax.all_gather(w_up, "gx", axis=0, tiled=True),
            lax.all_gather(w_down, "gx", axis=1, tiled=True),
        )
        qkv_full, bias_full, out_full, gain_one_full, gain_two_full = attn_full
        gate_full, up_full, down_full = ffn_full
        gain_one = gain_one_full.astype(jnp.float32)
        gain_two = gain_two_full.astype(jnp.float32)
        seg_tree = segment[micro_index]
        valid, upper_one, upper_two, depth_pos = tree_tables(seg_tree, parent[micro_index])

        def take_own(array):
            return lax.dynamic_slice_in_dim(array, offset, row_count, 0)

        mask = allowed(
            take_own(seg_tree),
            take_own(upper_one),
            take_own(upper_two),
            place_own,
            seg_tree,
            valid,
            place_all,
        )
        cosine, sine = rotation(take_own(depth_pos), HEAD)
        inputs = tokens[micro_index].astype(jnp.float32)
        unit_one, inverse_one, normed_one = norm_parts(inputs, gain_one)
        linear = jnp.dot(
            normed_one, qkv_full, preferred_element_type=jnp.float32
        ) + bias_full.astype(jnp.float32)
        query_low = turn(linear[:, :qwidth].reshape(row_count, HEADS, HEAD), cosine, sine).astype(
            jnp.bfloat16
        )
        keys_low = turn(
            linear[:, qwidth : qwidth + kwidth].reshape(row_count, KV_HEADS, HEAD), cosine, sine
        )
        keys_low = keys_low.reshape(row_count, kwidth).astype(jnp.bfloat16)
        values_low = linear[:, qwidth + kwidth :].astype(jnp.bfloat16)
        keys_all, values_all = (
            lax.all_gather(keys_low, "gy", axis=0, tiled=True),
            lax.all_gather(values_low, "gy", axis=0, tiled=True),
        )
        heads_raw, totals = attend(query_low, keys_all, values_all, mask, scale)
        heads_out = heads_raw.reshape(row_count, qwidth).astype(jnp.bfloat16)
        resid = inputs + jnp.dot(heads_out, out_full, preferred_element_type=jnp.float32)
        unit_two, inverse_two, normed_two = norm_parts(resid, gain_two)
        normed_all = lax.all_gather(normed_two, "gy", axis=0, tiled=True)
        gate = jnp.dot(normed_all, gate_full, preferred_element_type=jnp.float32)
        upward = jnp.dot(normed_all, up_full, preferred_element_type=jnp.float32)
        sigma = jax.nn.sigmoid(gate)
        swish = gate * sigma
        hidden = (swish * upward).astype(jnp.bfloat16)
        ffn_own = lax.psum_scatter(
            jnp.dot(hidden, down_full, preferred_element_type=jnp.float32),
            "gy",
            scatter_dimension=0,
            tiled=True,
        )
        outputs.append((resid + ffn_own).astype(jnp.bfloat16))
        grad_low = cotangent[micro_index]
        grad_all = lax.all_gather(grad_low, "gy", axis=0, tiled=True)
        grad_hidden = jnp.dot(grad_all, down_full.T, preferred_element_type=jnp.float32)
        grad_down = jnp.dot(hidden.T, grad_all, preferred_element_type=jnp.float32)
        grad_gate = (grad_hidden * upward * sigma * (1.0 + gate * (1.0 - sigma))).astype(
            jnp.bfloat16
        )
        grad_up = (grad_hidden * swish).astype(jnp.bfloat16)
        grad_wgate = jnp.dot(normed_all.T, grad_gate, preferred_element_type=jnp.float32)
        grad_wup = jnp.dot(normed_all.T, grad_up, preferred_element_type=jnp.float32)
        grad_normed_two = lax.psum_scatter(
            jnp.dot(grad_gate, gate_full.T, preferred_element_type=jnp.float32)
            + jnp.dot(grad_up, up_full.T, preferred_element_type=jnp.float32),
            "gy",
            scatter_dimension=0,
            tiled=True,
        )
        back_two, grad_gain_two = norm_back(grad_normed_two, unit_two, inverse_two, gain_two)
        grad_resid = grad_low.astype(jnp.float32) + back_two
        grad_branch = grad_resid.astype(jnp.bfloat16)
        grad_wout = jnp.dot(heads_out.T, grad_branch, preferred_element_type=jnp.float32)
        grad_heads = jnp.dot(grad_branch, out_full.T, preferred_element_type=jnp.float32).astype(
            jnp.bfloat16
        )
        grad_heads = grad_heads.reshape(row_count, HEADS, HEAD)
        grad_query, keys_part, values_part = attend_back(
            query_low, keys_all, values_all, mask, totals, grad_heads, scale
        )
        grad_keys, grad_values = (
            lax.psum_scatter(keys_part, "gy", scatter_dimension=0, tiled=True),
            lax.psum_scatter(values_part, "gy", scatter_dimension=0, tiled=True),
        )
        query_lin = turn(grad_query, cosine, -sine).reshape(row_count, qwidth)
        keys_lin = turn(grad_keys.reshape(row_count, KV_HEADS, HEAD), cosine, -sine).reshape(
            row_count, kwidth
        )
        grad_linear = jnp.concatenate([query_lin, keys_lin, grad_values], axis=1).astype(
            jnp.bfloat16
        )
        grad_wqkv = jnp.dot(normed_one.T, grad_linear, preferred_element_type=jnp.float32)
        grad_bias = jnp.sum(grad_linear.astype(jnp.float32), axis=0)
        grad_normed_one = jnp.dot(grad_linear, qkv_full.T, preferred_element_type=jnp.float32)
        back_one, grad_gain_one = norm_back(grad_normed_one, unit_one, inverse_one, gain_one)
        input_grads.append((grad_resid + back_one).astype(jnp.bfloat16))
        attn_list.append((grad_wqkv, grad_bias, grad_wout, grad_gain_one, grad_gain_two))
        ffn_list.append((grad_wgate, grad_wup, grad_down))
    attn_total = reduce(add_trees, attn_list)
    ffn_total = reduce(add_trees, ffn_list)
    attn_total = (
        lax.psum_scatter(attn_total[0], ("gx", "gy"), scatter_dimension=0, tiled=True),
        lax.psum_scatter(attn_total[1], ("gx", "gy"), scatter_dimension=0, tiled=True),
        lax.psum_scatter(attn_total[2], ("gx", "gy"), scatter_dimension=1, tiled=True),
        lax.psum_scatter(attn_total[3], ("gx", "gy"), scatter_dimension=0, tiled=True),
        lax.psum_scatter(attn_total[4], ("gx", "gy"), scatter_dimension=0, tiled=True),
    )
    ffn_total = (
        lax.psum_scatter(ffn_total[0], "gx", scatter_dimension=0, tiled=True),
        lax.psum_scatter(ffn_total[1], "gx", scatter_dimension=0, tiled=True),
        lax.psum_scatter(ffn_total[2], "gx", scatter_dimension=1, tiled=True),
    )
    layer_out = jnp.stack(outputs, axis=0)
    grad_tokens = jnp.stack(input_grads, axis=0)
    return (
        layer_out,
        grad_tokens,
        attn_total[0],
        attn_total[1],
        attn_total[2],
        attn_total[3],
        attn_total[4],
        ffn_total[0],
        ffn_total[1],
        ffn_total[2],
    )


def dot_nn(left, right):
    return lax.dot_general(left, right, (((1,), (0,)), ((), ())), preferred_element_type=jnp.float32)


def dot_nt(left, right):
    return lax.dot_general(left, right, (((1,), (1,)), ((), ())), preferred_element_type=jnp.float32)


def dot_tn(left, right):
    return lax.dot_general(left, right, (((0,), (0,)), ((), ())), preferred_element_type=jnp.float32)


def cost(flops, moved, trans=0):
    return pl.CostEstimate(flops=int(flops * PACE), bytes_accessed=int(moved * PACE), transcendentals=int(trans * PACE))


def params(mib):
    return pltpu.CompilerParams(vmem_limit_bytes=mib * 1024 * 1024)


def sigmoid(v):
    return 0.5 * jnp.tanh(0.5 * v) + 0.5


def peers_of():
    me, plane = lax.axis_index("gy"), lax.axis_index("gx")
    along_x = me + 2 - 4 * lax.rem(me // 2, 2)
    return {
        CORE: {"gy": me + 1 - 2 * lax.rem(me, 2)},
        ALONG_X: {"gy": along_x},
        ALONG_Y: {"gy": me + 4 - 8 * (me // 4)},
        ACROSS: {"gy": along_x + 4 - 8 * (along_x // 4)},
        RING: {"gx": lax.rem(plane + 1, 4)},
        RING + 1: {"gx": lax.rem(plane + 2, 4)},
        -RING: {"gx": lax.rem(plane + 3, 4)},
    }


def greet(bits_used):
    peers = peers_of()
    barrier = pltpu.get_barrier_semaphore()
    greeted = [bits for bits in bits_used] + [-RING] * (RING in bits_used)
    for bits in greeted:
        pl.semaphore_signal(barrier, inc=1, device_id=peers[bits], device_id_type=pl.DeviceIdType.MESH)
    pl.semaphore_wait(barrier, len(greeted))


def side_copies(sides, sources, targets, sent, landed):
    peers = peers_of()
    copies = []
    for parts, target in zip(sides, targets):
        for _, take, fill, bits in parts:
            if take is None:
                take = (pl.multiple_of(peers[bits]["gy"] // 2 * fill[1], fill[1]), fill[1])
            copies.append(
                pltpu.make_async_remote_copy(
                    sources[len(copies)].at[pl.ds(*take)],
                    target.at[pl.ds(*fill)],
                    sent.at[len(copies)],
                    landed.at[len(copies)],
                    device_id=peers[bits],
                    device_id_type=pl.DeviceIdType.MESH,
                )
            )
    return copies


def whole_side(array, bits):
    return [(array, (0, array.shape[0]), (0, array.shape[0]), bits)]


def rows_side(array, start, count, bits):
    return [(array, (start, count), (0, count), bits)]


def chip_side(array, bits):
    return [(array, None, (0, array.shape[0] // 4), bits)]


def call_beside(body, sides, collective, operands, grid, in_specs, out_specs, out_shape, scratch_shapes, mib, estimate, name):
    n_in, n_out, n_scratch = len(in_specs), len(out_specs), len(scratch_shapes)
    flat = [part for parts in sides for part in parts]
    bits_used = sorted({part[3] for part in flat})

    def whole_body(*refs):
        ins, refs = refs[:n_in], refs[n_in:]
        sources, refs = refs[: len(flat)], refs[len(flat) :]
        outs, refs = refs[:n_out], refs[n_out:]
        targets, refs = refs[: len(sides)], refs[len(sides) :]
        scratch, refs = refs[:n_scratch], refs[n_scratch:]
        step, last = pl.program_id(0), pl.num_programs(0) - 1
        if flat:

            @pl.when(step == 0)
            def _():
                greet(bits_used)
                for copy in side_copies(sides, sources, targets, *refs):
                    copy.start()

        body(*ins, *outs, *scratch)
        if flat:

            @pl.when(step == last)
            def _():
                for copy in side_copies(sides, sources, targets, *refs):
                    copy.wait()

    anywhere = pl.BlockSpec(memory_space=pl.ANY)
    extra = {"collective_id": collective, "has_side_effects": True} if flat else {}
    results = pl.pallas_call(
        whole_body,
        grid=grid,
        in_specs=list(in_specs) + [anywhere] * len(flat),
        out_specs=list(out_specs) + [anywhere] * len(sides),
        out_shape=list(out_shape)
        + [jax.ShapeDtypeStruct((sum(p[2][1] for p in parts),) + parts[0][0].shape[1:], parts[0][0].dtype) for parts in sides],
        scratch_shapes=list(scratch_shapes) + ([pltpu.SemaphoreType.DMA((len(flat),))] * 2 if flat else []),
        compiler_params=pltpu.CompilerParams(vmem_limit_bytes=mib * 1024 * 1024, **extra),
        cost_estimate=estimate,
        name=name,
    )(*operands, *[part[0] for part in flat])
    return results[:n_out], results[n_out:]


def ffn_copies(chunk, pieces, held, sems):
    units = pieces[0].shape[1]
    tile = FFN_CHUNK // 2
    slot = chunk % 2
    copies = []
    for part in range(2):
        column = chunk * FFN_CHUNK + part * tile
        owner, inside = column // units, column % units
        for kind in range(3):
            copies.append(
                pltpu.make_async_copy(
                    pieces[3 * owner + kind].at[:, pl.ds(inside, tile)],
                    held.at[slot, kind, :, pl.ds(part * tile, tile)],
                    sems.at[slot, part * 3 + kind],
                )
            )
    return copies


def ffn_body(n_ref, c_ref, *refs):
    pieces = refs[:6]
    hid_ref, dg_ref, du_ref, f_ref, dn_ref, f_acc, dn_acc, held, sems = refs[6:]
    step = pl.program_id(0)
    chunks = 2 * pieces[0].shape[1] // FFN_CHUNK

    @pl.when(step == 0)
    def _():
        for copy in ffn_copies(0, pieces, held, sems):
            copy.start()
        f_acc[...] = jnp.zeros_like(f_acc)
        dn_acc[...] = jnp.zeros_like(dn_acc)

    for chunk in range(chunks):

        @pl.when(step == chunk)
        def _():
            if chunk + 1 < chunks:
                for copy in ffn_copies(chunk + 1, pieces, held, sems):
                    copy.start()
            for copy in ffn_copies(chunk, pieces, held, sems):
                copy.wait()

    slot = step % 2
    rows = n_ref.shape[0]
    part = rows // FFN_PARTS
    takes = [pl.ds(index * part, part) for index in range(FFN_PARTS)]

    def products(take):
        return (
            dot_nn(n_ref[take, :], held[slot, 0]),
            dot_nn(n_ref[take, :], held[slot, 1]),
            dot_nn(c_ref[take, :], held[slot, 2]),
        )

    later = products(takes[0])
    for index, take in enumerate(takes):
        gate, upward, grad_hidden = later
        if index + 1 < FFN_PARTS:
            later = products(takes[index + 1])
        sigma = sigmoid(gate)
        swish = gate * sigma
        hidden = (swish * upward).astype(jnp.bfloat16)
        hid_ref[take, :] = hidden
        grad_gate = (grad_hidden * upward * sigma * (1.0 + gate * (1.0 - sigma))).astype(jnp.bfloat16)
        grad_up = (grad_hidden * swish).astype(jnp.bfloat16)
        dg_ref[take, :] = grad_gate
        du_ref[take, :] = grad_up
        f_acc[take, :] += dot_nt(hidden, held[slot, 2])
        dn_acc[take, :] += dot_nt(grad_gate, held[slot, 0]) + dot_nt(grad_up, held[slot, 1])

    @pl.when(step == pl.num_programs(0) - 1)
    def _():
        f_ref[...] = f_acc[...].astype(f_ref.dtype)
        dn_ref[...] = dn_acc[...].astype(dn_ref.dtype)


def ffn_block(normed, cotan, pieces, collective, sides=()):
    rows, width = normed.shape
    units = 2 * pieces[0].shape[1]
    chunk = FFN_CHUNK
    whole = pl.BlockSpec((rows, width), lambda j: (0, 0))
    tall = pl.BlockSpec((rows, chunk), lambda j: (0, j))
    low = jnp.bfloat16
    return call_beside(
        ffn_body,
        sides,
        collective,
        (normed, cotan, *pieces),
        (units // chunk,),
        [whole, whole] + [pl.BlockSpec(memory_space=pl.ANY)] * len(pieces),
        [tall, tall, tall, whole, whole],
        [jax.ShapeDtypeStruct((rows, units), low)] * 3 + [jax.ShapeDtypeStruct((rows, width), low)] * 2,
        [pltpu.VMEM((rows, width), jnp.float32)] * 2
        + [pltpu.VMEM((2, 3, width, chunk), low), pltpu.SemaphoreType.DMA((2, len(pieces)))],
        60,
        cost(12 * rows * width * units, 6 * width * units + 6 * rows * (width + units)),
        "ffn_block",
    )


def wgrad_body(per_half, *refs):
    count = (len(refs) - 2) // 2
    total = dot_tn(refs[0][...], refs[count][...])
    for index in range(1, count):
        total = total + dot_tn(refs[index][...], refs[count + index][...])

    def store(out_ref):
        slots, _, wide = out_ref.shape
        for slot in range(slots):
            out_ref[slot] = total[:, slot * wide : (slot + 1) * wide].astype(out_ref.dtype)

    first = pl.program_id(0) < per_half
    pl.when(first)(lambda: store(refs[-2]))
    pl.when(jnp.logical_not(first))(lambda: store(refs[-1]))


def wgrad(lefts, rights, slots, collective, sides=()):
    rows, units = lefts[0].shape
    width = rights[0].shape[1]
    tile = WG_TILE
    per_half = units // 2 // tile
    wide = width // slots
    count = len(lefts)
    return call_beside(
        lambda *refs: wgrad_body(per_half, *refs),
        sides,
        collective,
        (*lefts, *rights),
        (units // tile,),
        [pl.BlockSpec((rows, tile), lambda j: (0, j))] * count
        + [pl.BlockSpec((rows, width), lambda j: (0, 0))] * count,
        [
            pl.BlockSpec((slots, tile, wide), lambda j: (0, jnp.minimum(j, per_half - 1), 0)),
            pl.BlockSpec((slots, tile, wide), lambda j: (0, jnp.maximum(j - per_half, 0), 0)),
        ],
        [jax.ShapeDtypeStruct((slots, units // 2, wide), jnp.bfloat16)] * 2,
        [],
        60,
        cost(2 * count * rows * width * units, 2 * count * rows * (width + units)),
        "ffn_wgrad",
    )


def group_rows(source_ref, group, per_group):
    return jnp.concatenate(
        [source_ref[:, (group * per_group + h) * HEAD : (group * per_group + h + 1) * HEAD] for h in range(per_group)],
        axis=0,
    )


def attend_body(list_ref, count_ref, q_ref, kv_ref, bias_ref, o_ref, lse_ref, qs, acc, top, den):
    block = pl.program_id(0)
    per_group = HEADS // KV_HEADS
    for group in range(KV_HEADS):
        qs[group] = group_rows(q_ref, group, per_group)
    acc[...] = jnp.zeros_like(acc)
    den[...] = jnp.zeros_like(den)
    top[...] = jnp.full_like(top, 2 * NEGATIVE)
    factor = LOG2E / math.sqrt(HEAD)

    def body(n, carry):
        rows = pl.ds(pl.multiple_of(list_ref[block, n] * KEY_TILE, KEY_TILE), KEY_TILE)
        bias = jnp.concatenate([bias_ref[rows, :].astype(jnp.float32)] * per_group, axis=1)
        products = [dot_nt(kv_ref[rows, g * HEAD : (g + 1) * HEAD], qs[g]) for g in range(KV_HEADS)]
        for group in range(KV_HEADS):
            values = kv_ref[rows, (KV_HEADS + group) * HEAD : (KV_HEADS + group + 1) * HEAD]
            scores = products[group] * factor + bias
            old = top[group]
            new = jnp.maximum(old, jnp.max(scores, axis=0, keepdims=True))
            probs = jnp.exp2(scores - new)
            shrink = jnp.exp2(old - new)
            den[group] = den[group] * shrink + jnp.sum(probs, axis=0, keepdims=True)
            acc[group] = acc[group] * shrink + dot_tn(values, probs.astype(jnp.bfloat16))
            top[group] = new
        return carry

    lax.fori_loop(0, count_ref[block], body, 0)
    for group in range(KV_HEADS):
        out = acc[group] / den[group]
        lse_ref[0, group] = top[group] + jnp.log(den[group]) * LOG2E
        for h in range(per_group):
            head = group * per_group + h
            o_ref[:, head * HEAD : (head + 1) * HEAD] = out[:, h * HEAD : (h + 1) * HEAD].T.astype(o_ref.dtype)


def attend_fast(block_list, block_count, query, keyval, bias):
    rows, qwidth = query.shape
    slots = keyval.shape[0]
    blocks = rows // QUERY_TILE
    per_group = HEADS // KV_HEADS
    lanes = per_group * QUERY_TILE
    whole = pl.BlockSpec(keyval.shape, lambda i, a, b: (0, 0))
    tile = pl.BlockSpec((QUERY_TILE, qwidth), lambda i, a, b: (i, 0))
    return pl.pallas_call(
        attend_body,
        grid_spec=pltpu.PrefetchScalarGridSpec(
            num_scalar_prefetch=2,
            grid=(blocks,),
            in_specs=[tile, whole, pl.BlockSpec((slots, QUERY_TILE), lambda i, a, b: (0, i))],
            out_specs=[tile, pl.BlockSpec((1, KV_HEADS, 1, lanes), lambda i, a, b: (i, 0, 0, 0))],
            scratch_shapes=[
                pltpu.VMEM((KV_HEADS, lanes, HEAD), jnp.bfloat16),
                pltpu.VMEM((KV_HEADS, HEAD, lanes), jnp.float32),
                pltpu.VMEM((KV_HEADS, 1, lanes), jnp.float32),
                pltpu.VMEM((KV_HEADS, 1, lanes), jnp.float32),
            ],
        ),
        out_shape=[
            jax.ShapeDtypeStruct((rows, qwidth), jnp.bfloat16),
            jax.ShapeDtypeStruct((blocks, KV_HEADS, 1, lanes), jnp.float32),
        ],
        compiler_params=params(48),
        cost_estimate=cost(2 * rows * slots * qwidth * 2, 4 * slots * rows, HEADS * rows * slots // 2),
        name="tree_attention",
    )(block_list, block_count, query, keyval, bias)


def attend_back_body(
    list_ref, count_ref, q_ref, kv_ref, bias_ref, lse_ref, o_ref, do_ref, cos_ref, sin_ref,
    dq_ref, dkv_ref, qs, dos, delta, dqt, dkv,
):
    block = pl.program_id(0)
    per_group = HEADS // KV_HEADS
    scale = 1.0 / math.sqrt(HEAD)
    factor = LOG2E * scale
    lanes = qs.shape[1]

    @pl.when(block == 0)
    def _():
        dkv[...] = jnp.zeros_like(dkv)

    for group in range(KV_HEADS):
        qs[group] = group_rows(q_ref, group, per_group)
        grads = group_rows(do_ref, group, per_group)
        dos[group] = grads
        both = grads.astype(jnp.float32) * group_rows(o_ref, group, per_group).astype(jnp.float32)
        delta[group] = lax.dot_general(
            jnp.ones((8, HEAD), jnp.float32), both, (((1,), (1,)), ((), ())),
            precision=lax.Precision.HIGHEST, preferred_element_type=jnp.float32,
        )[0:1]
    dqt[...] = jnp.zeros_like(dqt)

    def body(n, carry):
        rows = pl.ds(pl.multiple_of(list_ref[block, n] * KEY_TILE, KEY_TILE), KEY_TILE)
        bias = jnp.concatenate([bias_ref[rows, :].astype(jnp.float32)] * per_group, axis=1)
        for group in range(KV_HEADS):
            kcols = slice(group * HEAD, (group + 1) * HEAD)
            vcols = slice((KV_HEADS + group) * HEAD, (KV_HEADS + group + 1) * HEAD)
            keys = kv_ref[rows, kcols]
            values = kv_ref[rows, vcols]
            scores = dot_nt(keys, qs[group]) * factor + bias
            probs = jnp.exp2(scores - lse_ref[0, group])
            grad_probs = dot_nt(values, dos[group])
            grad_scores = (probs * (grad_probs - delta[group])).astype(jnp.bfloat16)
            dkv[rows, vcols] += dot_nn(probs.astype(jnp.bfloat16), dos[group])
            dkv[rows, kcols] += dot_nn(grad_scores, qs[group])
            dqt[group] += dot_tn(keys, grad_scores)
        return carry

    lax.fori_loop(0, count_ref[block], body, 0)
    cosine, sine = cos_ref[...], sin_ref[...]
    for group in range(KV_HEADS):
        for h in range(per_group):
            head = group * per_group + h
            grad = dqt[group, :, h * HEAD : (h + 1) * HEAD].T * scale
            grad = grad * cosine - pltpu.roll(grad, HEAD // 2, 1) * sine
            dq_ref[:, head * HEAD : (head + 1) * HEAD] = grad.astype(dq_ref.dtype)

    @pl.when(block == pl.num_programs(0) - 1)
    def _():
        kwidth = KV_HEADS * HEAD
        dkv_ref[:, :kwidth] = (dkv[:, :kwidth] * scale).astype(dkv_ref.dtype)
        dkv_ref[:, kwidth:] = dkv[:, kwidth:].astype(dkv_ref.dtype)


def attend_back_fast(block_list, block_count, query, keyval, bias, lse, heads_out, grad_heads, cosine, sine):
    rows, qwidth = query.shape
    slots = keyval.shape[0]
    blocks = rows // QUERY_TILE
    per_group = HEADS // KV_HEADS
    lanes = per_group * QUERY_TILE
    whole = pl.BlockSpec(keyval.shape, lambda i, a, b: (0, 0))
    tile = pl.BlockSpec((QUERY_TILE, qwidth), lambda i, a, b: (i, 0))
    turned = pl.BlockSpec((QUERY_TILE, HEAD), lambda i, a, b: (i, 0))
    return pl.pallas_call(
        attend_back_body,
        grid_spec=pltpu.PrefetchScalarGridSpec(
            num_scalar_prefetch=2,
            grid=(blocks,),
            in_specs=[
                tile,
                whole,
                pl.BlockSpec((slots, QUERY_TILE), lambda i, a, b: (0, i)),
                pl.BlockSpec((1, KV_HEADS, 1, lanes), lambda i, a, b: (i, 0, 0, 0)),
                tile,
                tile,
                turned,
                turned,
            ],
            out_specs=[tile, whole],
            scratch_shapes=[
                pltpu.VMEM((KV_HEADS, lanes, HEAD), jnp.bfloat16),
                pltpu.VMEM((KV_HEADS, lanes, HEAD), jnp.bfloat16),
                pltpu.VMEM((KV_HEADS, 1, lanes), jnp.float32),
                pltpu.VMEM((KV_HEADS, HEAD, lanes), jnp.float32),
                pltpu.VMEM(keyval.shape, jnp.float32),
            ],
        ),
        out_shape=[
            jax.ShapeDtypeStruct((rows, qwidth), jnp.bfloat16),
            jax.ShapeDtypeStruct(keyval.shape, jnp.bfloat16),
        ],
        compiler_params=params(56),
        cost_estimate=cost(5 * rows * slots * qwidth * 2, 8 * slots * rows, HEADS * rows * slots // 2),
        name="tree_attention_back",
    )(block_list, block_count, query, keyval, bias, lse, heads_out, grad_heads, cosine, sine)


def project_body(x_ref, gain_ref, w_ref, b_ref, cos_ref, sin_ref, n_ref, q_ref, kv_ref):
    values = x_ref[...].astype(jnp.float32)
    inverse = lax.rsqrt(jnp.mean(values * values, axis=-1, keepdims=True) + EPS)
    normed = (values * inverse * gain_ref[...]).astype(jnp.bfloat16)
    n_ref[...] = normed
    linear = dot_nn(normed, w_ref[...]) + b_ref[...]
    cosine, sine = cos_ref[...], sin_ref[...]
    for head in range(HEADS + KV_HEADS):
        lane = linear[:, head * HEAD : (head + 1) * HEAD]
        lane = (lane * cosine + pltpu.roll(lane, HEAD // 2, 1) * sine).astype(jnp.bfloat16)
        if head < HEADS:
            q_ref[:, head * HEAD : (head + 1) * HEAD] = lane
        else:
            kv_ref[:, (head - HEADS) * HEAD : (head - HEADS + 1) * HEAD] = lane
    kv_ref[:, KV_HEADS * HEAD :] = linear[:, (HEADS + KV_HEADS) * HEAD :].astype(jnp.bfloat16)


def project(inputs, gain, w_qkv, bias, cosine, sine):
    rows, width = inputs.shape
    qwidth, kwidth = HEADS * HEAD, 2 * KV_HEADS * HEAD
    tile = ROW_TILE
    fixed = lambda i: (0, 0)
    moving = lambda i: (i, 0)
    return pl.pallas_call(
        project_body,
        grid=(rows // tile,),
        in_specs=[
            pl.BlockSpec((tile, width), moving),
            pl.BlockSpec((1, width), fixed),
            pl.BlockSpec((width, qwidth + kwidth), fixed),
            pl.BlockSpec((1, qwidth + kwidth), fixed),
            pl.BlockSpec((tile, HEAD), moving),
            pl.BlockSpec((tile, HEAD), moving),
        ],
        out_specs=[
            pl.BlockSpec((tile, width), moving),
            pl.BlockSpec((tile, qwidth), moving),
            pl.BlockSpec((tile, kwidth), moving),
        ],
        out_shape=[
            jax.ShapeDtypeStruct((rows, width), jnp.bfloat16),
            jax.ShapeDtypeStruct((rows, qwidth), jnp.bfloat16),
            jax.ShapeDtypeStruct((rows, kwidth), jnp.bfloat16),
        ],
        compiler_params=params(48),
        cost_estimate=cost(2 * rows * width * (qwidth + kwidth), 2 * width * (qwidth + kwidth) + 8 * rows * width),
        name="project",
    )(inputs, gain, w_qkv, bias, cosine, sine)


def spread_body(*refs):
    owns, rows, whole, rows_x, rows_y, rows_d, sent, landed, kept = refs[:4], *refs[4:]
    me, plane = lax.axis_index("gy"), lax.axis_index("gx")
    peers = peers_of()
    along_x, along_y, across = (peers[bits]["gy"] for bits in OTHERS)
    places = [lax.rem(plane + 4 - k, 4) for k in range(4)]
    greet((CORE, ALONG_X, ALONG_Y))
    copies = []

    def send(source, target, bits):
        copy = pltpu.make_async_remote_copy(
            source,
            target,
            sent.at[len(copies)],
            landed.at[len(copies)],
            device_id=peers[bits],
            device_id_type=pl.DeviceIdType.MESH,
        )
        copies.append(copy)
        copy.start()
        return copy

    from_x, from_y, from_d, from_core, local = [], [], [], [], []
    for k in range(4):
        block = whole.at[places[k], me]
        from_x.append(send(owns[k], block, ALONG_X))
        from_y.append(send(owns[k], block, ALONG_Y))
        from_core.append(send(owns[k], block, CORE))
        local.append(pltpu.make_async_copy(owns[k], block, kept.at[k]))
        local[k].start()
    moved_x, moved_y = send(rows, rows_x, ALONG_X), send(rows, rows_y, ALONG_Y)
    for k in range(4):
        block_x, block_y = whole.at[places[k], along_x], whole.at[places[k], along_y]
        from_x[k].wait_recv()
        if k < 2:
            from_d.append(send(block_x, block_x, ALONG_Y))
        from_core.append(send(block_x, block_x, CORE))
        from_y[k].wait_recv()
        if k >= 2:
            from_d.append(send(block_y, block_y, ALONG_X))
        from_core.append(send(block_y, block_y, CORE))
    for k in range(4):
        block = whole.at[places[k], across]
        from_d[k].wait_recv()
        from_core.append(send(block, block, CORE))
    half = rows.shape[0] // 2
    first, second = pl.ds(0, half), pl.ds(half, half)
    moved_x.wait_recv()
    moved_d = [send(rows_x.at[first], rows_d.at[first], ALONG_Y)]
    moved_y.wait_recv()
    moved_d.append(send(rows_y.at[second], rows_d.at[second], ALONG_X))
    for copy in from_core + moved_d:
        copy.wait_recv()
    for copy in copies:
        copy.wait_send()
    for copy in local:
        copy.wait()


def spread(owns, rows):
    deep, wide = owns[0].shape
    anywhere = pl.BlockSpec(memory_space=pl.ANY)
    whole, *others = pl.pallas_call(
        spread_body,
        in_specs=[anywhere] * 5,
        out_specs=[anywhere] * 4,
        out_shape=[jax.ShapeDtypeStruct((4, 8, deep, wide), rows.dtype)]
        + [jax.ShapeDtypeStruct(rows.shape, rows.dtype)] * 3,
        scratch_shapes=[
            pltpu.SemaphoreType.DMA((32,)),
            pltpu.SemaphoreType.DMA((32,)),
            pltpu.SemaphoreType.DMA((4,)),
        ],
        compiler_params=pltpu.CompilerParams(collective_id=0, has_side_effects=True),
        cost_estimate=cost(0, 300 * 1024 * 1024),
        name="spread",
    )(*owns, rows)
    return whole.reshape(32 * deep, wide), others


def unit_back(grad_normed, values, gain):
    inverse = lax.rsqrt(jnp.mean(values * values, axis=-1, keepdims=True) + EPS)
    unit = values * inverse
    scaled = grad_normed * gain
    back = inverse * (scaled - unit * jnp.mean(scaled * unit, axis=-1, keepdims=True))
    return back, jnp.sum(grad_normed * unit, axis=0, keepdims=True)


def branch_back_body(own_ref, xa_ref, xb_ref, ya_ref, yb_ref, resid_ref, cot_ref, gain_ref, heads_ref, *refs):
    turned, (resid_out, heads_out, gain_out, weight_out, branch) = refs[:-5], refs[-5:]
    step, full = pl.program_id(0), jnp.float32
    tile = own_ref.shape[0]
    from_x = jnp.where(step < BRANCH_CUTS[0], xa_ref[...].astype(full), xb_ref[...].astype(full))
    from_y = jnp.where(step < BRANCH_CUTS[1], ya_ref[...].astype(full), yb_ref[...].astype(full))
    grad_normed = own_ref[...].astype(full) + from_x + from_y
    back, gain_part = unit_back(grad_normed, resid_ref[...], gain_ref[...])
    grad_resid = cot_ref[...].astype(full) + back
    resid_out[...] = grad_resid
    low = grad_resid.astype(jnp.bfloat16)
    branch[pl.ds(pl.multiple_of(step * tile, tile), tile), :] = low
    gain_out[...] = jnp.where(step == 0, 0.0, gain_out[...]) + gain_part
    wide = turned[0].shape[1]
    for index, piece in enumerate(turned):
        heads_out[:, index * wide : (index + 1) * wide] = dot_nn(low, piece[...]).astype(jnp.bfloat16)

    @pl.when(step == pl.num_programs(0) - 1)
    def _():
        weight_out[...] = dot_tn(branch[...], heads_ref[...]).astype(jnp.bfloat16)


def branch_back(own, from_x, from_y, resid, cotan, gain, heads, weights, first_column):
    rows, width = own.shape
    tile, wide = ROW_TILE, 512
    steps = rows // tile
    low, full = jnp.bfloat16, jnp.float32
    moving = pl.BlockSpec((tile, width), lambda i: (i, 0))
    fixed = pl.BlockSpec((1, width), lambda i: (0, 0))
    first, then = [], []
    for count in BRANCH_CUTS:
        first.append(pl.BlockSpec((tile, width), lambda i, n=count: (jnp.minimum(i, n - 1), 0)))
        then.append(pl.BlockSpec((tile, width), lambda i, n=count: (jnp.maximum(i - n, 0), 0)))
    return pl.pallas_call(
        branch_back_body,
        grid=(steps,),
        in_specs=[moving, first[0], then[0], first[1], then[1], moving, moving, fixed]
        + [pl.BlockSpec((rows, width), lambda i: (0, 0))]
        + [pl.BlockSpec((width, wide), lambda i, j=j: (0, first_column // wide + j)) for j in range(width // wide)],
        out_specs=[moving, moving, fixed, pl.BlockSpec((width, width), lambda i: (0, 0))],
        out_shape=[
            jax.ShapeDtypeStruct((rows, width), full),
            jax.ShapeDtypeStruct((rows, width), low),
            jax.ShapeDtypeStruct((1, width), full),
            jax.ShapeDtypeStruct((width, width), low),
        ],
        scratch_shapes=[pltpu.VMEM((rows, width), low)],
        compiler_params=params(56),
        cost_estimate=cost(4 * rows * width * width, 20 * rows * width + 4 * width * width),
        name="branch_back",
    )(own, *from_x, *from_y, resid, cotan, gain, heads, *[weights] * (width // wide))


def project_back_body(q_ref, own_ref, x_ref, y_ref, d_ref, cos_ref, sin_ref, w_ref, in_ref, gain_ref, resid_ref, normed_ref,
                      tokens_out, bias_out, gain_out, weight_out, linear):
    step, full = pl.program_id(0), jnp.float32
    tile, qwidth = q_ref.shape
    total = own_ref[...].astype(full) + x_ref[...].astype(full) + y_ref[...].astype(full) + d_ref[...].astype(full)
    pieces = [q_ref[...]]
    for head in range(2 * KV_HEADS):
        lane = total[:, head * HEAD : (head + 1) * HEAD]
        if head < KV_HEADS:
            lane = lane * cos_ref[...] - pltpu.roll(lane, HEAD // 2, 1) * sin_ref[...]
        pieces.append(lane.astype(jnp.bfloat16))
    lin = jnp.concatenate(pieces, axis=1)
    linear[pl.ds(pl.multiple_of(step * tile, tile), tile), :] = lin
    bias_part = jnp.sum(lin.astype(full), axis=0, keepdims=True)
    bias_out[...] = jnp.where(step == 0, 0.0, bias_out[...]) + bias_part
    back, gain_part = unit_back(dot_nt(lin, w_ref[...]), in_ref[...].astype(full), gain_ref[...])
    gain_out[...] = jnp.where(step == 0, 0.0, gain_out[...]) + gain_part
    tokens_out[...] = (resid_ref[...] + back).astype(jnp.bfloat16)

    @pl.when(step == pl.num_programs(0) - 1)
    def _():
        weight_out[:, : linear.shape[1]] = dot_tn(normed_ref[...], linear[...]).astype(jnp.bfloat16)


def project_back(query_lin, parts, cosine, sine, weights, inputs, gain, grad_resid, normed, collective, sides):
    rows, width = inputs.shape
    qwidth, kwidth = query_lin.shape[1], parts[0].shape[1]
    qwide, tile = qwidth + kwidth, ROW_TILE
    low, full = jnp.bfloat16, jnp.float32

    def moving(columns):
        return pl.BlockSpec((tile, columns), lambda i: (i, 0))

    def fixed(high, columns):
        return pl.BlockSpec((high, columns), lambda i: (0, 0))

    return call_beside(
        project_back_body,
        sides,
        collective,
        (query_lin, *parts, cosine, sine, weights, inputs, gain, grad_resid, normed),
        (rows // tile,),
        [moving(qwidth)]
        + [moving(kwidth)] * 4
        + [moving(HEAD)] * 2
        + [fixed(width, qwide), moving(width), fixed(1, width), moving(width), fixed(rows, width)],
        [moving(width), fixed(1, qwide), fixed(1, width), fixed(width, qwide + HEAD)],
        [
            jax.ShapeDtypeStruct((rows, width), low),
            jax.ShapeDtypeStruct((1, qwide), full),
            jax.ShapeDtypeStruct((1, width), full),
            jax.ShapeDtypeStruct((width, qwide + HEAD), low),
        ],
        [pltpu.VMEM((rows, qwide), low)],
        56,
        cost(4 * rows * width * qwide, 20 * rows * width + 4 * width * qwide),
        "project_back",
    )


def both_body(first_mine, first_other, second_mine, second_other, out_ref):
    deep = first_mine.shape[1]
    out_ref[0, :deep] = (first_mine[0].astype(jnp.float32) + first_other[0].astype(jnp.float32)).astype(out_ref.dtype)
    out_ref[0, deep:] = (second_mine[0].astype(jnp.float32) + second_other[0].astype(jnp.float32)).astype(out_ref.dtype)


def both_sums(*arrays):
    planes, deep, wide = arrays[0].shape
    return pl.pallas_call(
        both_body,
        grid=(planes,),
        in_specs=[pl.BlockSpec((1, deep, wide), lambda i: (i, 0, 0))] * 4,
        out_specs=pl.BlockSpec((1, 2 * deep, wide), lambda i: (i, 0, 0)),
        out_shape=jax.ShapeDtypeStruct((planes, 2 * deep, wide), arrays[0].dtype),
        compiler_params=params(48),
        cost_estimate=cost(0, 12 * planes * deep * wide),
        name="both_back",
    )(*arrays)


def finish_body(wide_ref, out_ref, mine_ref, other_ref, both_ref, tokens_ref, resid_ref, *refs):
    layer_refs, results, rows_out, scratch = refs[:3], refs[3:8], refs[8:10], refs[10:]
    kept, got_core, got_first, got_second, got_ring = [scratch[i : i + 2] for i in range(0, 10, 2)]
    units, got_units, units_ring, units_moving, both, layer, resid, *layer_parts, sent, landed, local = scratch[10:]
    me, plane = lax.axis_index("gy"), lax.axis_index("gx")
    core, x, y = lax.rem(me, 2), lax.rem(me // 2, 2), me // 4
    places = [lax.rem(plane + 4 - s, 4) for s in range(4)]
    peers = peers_of()
    full = jnp.float32
    greet((CORE, ALONG_X, ALONG_Y, RING, RING + 1))
    copies, loads = [], []

    def send(source, target, bits):
        copy = pltpu.make_async_remote_copy(
            source,
            target,
            sent.at[len(copies)],
            landed.at[len(copies)],
            device_id=peers[bits],
            device_id_type=pl.DeviceIdType.MESH,
        )
        copies.append(copy)
        copy.start()
        return copy

    def load(source, target):
        copy = pltpu.make_async_copy(source, target, local.at[len(loads)])
        loads.append(copy)
        copy.start()
        return copy

    inputs = (wide_ref, out_ref)
    core_copies = [send(inputs[i].at[:, :, :, 1 - core], got_core[i], CORE) for i in range(2)]
    unit_loads = [load(mine_ref, units), load(other_ref, got_units)]
    both_load = load(both_ref, both)
    layer_loads = [load(a, b) for a, b in zip((resid_ref, *layer_refs), (resid, *layer_parts))]
    held = [load(inputs[i].at[:, :, :, core], kept[i]) for i in range(2)]

    for copy in unit_loads:
        copy.wait()

    @pl.loop(0, 4)
    def _(p):
        units[p] += got_units[p]

    units_copy = send(units.at[places[1]], units_ring.at[0], RING)
    steps = []
    for i in range(2):
        core_copies[i].wait_recv()
        held[i].wait()

        @pl.loop(0, 4)
        def _(p):
            for a in range(2):
                for b in range(2):
                    kept[i][p, a, b] += got_core[i][p, a, b]

        middle = kept[i].shape[-1] // 256 * 128
        first, second = pl.ds(0, middle), pl.ds(middle, kept[i].shape[-1] - middle)
        steps.append((
            send(kept[i].at[:, :, 1 - x, :, first], got_first[i].at[:, :, :, first], ALONG_X),
            send(kept[i].at[:, 1 - y, :, :, second], got_first[i].at[:, :, :, second], ALONG_Y),
            first,
            second,
        ))
    units_copy.wait_recv()
    units_moving[0] = units[places[2]] + units_ring[0]
    units_copy = send(units_moving.at[0], units_ring.at[1], RING)
    for copy in layer_loads:
        copy.wait()

    @pl.loop(0, resid.shape[0] // ROW_TILE)
    def _(p):
        take = pl.ds(pl.multiple_of(p * ROW_TILE, ROW_TILE), ROW_TILE)
        total = layer_parts[0][take, :].astype(full) + layer_parts[1][take, :].astype(full)
        layer[take, :] = (resid[take, :] + (total + layer_parts[2][take, :].astype(full))).astype(jnp.bfloat16)

    half = resid.shape[0] // 2
    row_copies = []
    for source, target in ((layer, rows_out[0]), (tokens_ref, rows_out[1])):
        row_copies.append(send(source.at[pl.ds((1 - core) * half, half)], target.at[core], CORE))
        held.append(load(source.at[pl.ds(core * half, half)], target.at[core]))
    both_load.wait()
    high, own = both.shape[0] // 2, results[3].shape[0]
    results[3][...] = both[0:own, :].astype(full)
    results[4][...] = both[high : high + own, :].astype(full)
    nexts = []
    for i in range(2):
        first_copy, second_copy, first, second = steps[i]
        first_copy.wait_recv()

        @pl.loop(0, 4)
        def _(p):
            for a in range(2):
                kept[i][p, a, x, :, first] += got_first[i][p, a, :, first]

        third_copy = send(kept[i].at[:, 1 - y, x, :, first], got_second[i].at[:, :, first], ALONG_Y)
        second_copy.wait_recv()

        @pl.loop(0, 4)
        def _(p):
            for b in range(2):
                kept[i][p, y, b, :, second] += got_first[i][p, b, :, second]

        nexts.append((third_copy, send(kept[i].at[:, y, 1 - x, :, second], got_second[i].at[:, :, second], ALONG_X)))
    units_copy.wait_recv()
    units_moving[1] = units[places[3]] + units_ring[1]
    units_copy = send(units_moving.at[1], units_ring.at[2], RING)
    ring_copies = []
    for i in range(2):
        for copy in nexts[i]:
            copy.wait_recv()

        @pl.loop(0, 4)
        def _(p):
            kept[i][p, y, x] += got_second[i][p]

        for k, bits in ((1, RING), (2, RING + 1), (3, -RING)):
            there = lax.rem(plane + k, 4)
            ring_copies.append(send(kept[i].at[there, y, x], got_ring[i].at[k - 1], bits))
    units_copy.wait_recv()
    results[2][...] = units[places[0], 0:own, :].astype(full) + units_ring[2, 0:own, :].astype(full)
    for i in range(2):
        total = kept[i][plane, y, x].astype(full)
        for k in range(3):
            ring_copies[3 * i + k].wait_recv()
            total = total + got_ring[i][k].astype(full)
        results[i][...] = total
    for copy in row_copies:
        copy.wait_recv()
    for copy in held[2:]:
        copy.wait()
    for copy in copies:
        copy.wait_send()


def finish(wide, out, mine, other, both, tokens, resid, layer_parts, own_units, collective):
    low, full = jnp.bfloat16, jnp.float32
    deep = wide.shape[0] // 32
    wide, out = (a.reshape(4, 2, 2, 2, deep, a.shape[1]) for a in (wide, out))
    columns = (wide.shape[-1], out.shape[-1])
    block = mine.shape[1:]
    anywhere = pl.BlockSpec(memory_space=pl.ANY)
    inside = pl.BlockSpec(memory_space=pltpu.VMEM)

    def pairs(*lead):
        return [pltpu.VMEM((*lead, deep, c), low) for c in columns]

    return pl.pallas_call(
        finish_body,
        in_specs=[anywhere] * 10,
        out_specs=[inside] * 5 + [anywhere] * 2,
        out_shape=[jax.ShapeDtypeStruct((deep, c), full) for c in columns]
        + [jax.ShapeDtypeStruct((own_units, block[1]), full)] * 3
        + [jax.ShapeDtypeStruct((2, tokens.shape[0] // 2, tokens.shape[1]), low)] * 2,
        scratch_shapes=[
            *pairs(4, 2, 2),
            *pairs(4, 2, 2),
            *pairs(4, 2),
            *pairs(4),
            *pairs(3),
            pltpu.VMEM((4, *block), low),
            pltpu.VMEM((4, *block), low),
            pltpu.VMEM((3, *block), low),
            pltpu.VMEM((2, *block), low),
            pltpu.VMEM(both.shape, low),
            pltpu.VMEM(tokens.shape, low),
            pltpu.VMEM(resid.shape, full),
            *[pltpu.VMEM(tokens.shape, low)] * 3,
            pltpu.SemaphoreType.DMA((21,)),
            pltpu.SemaphoreType.DMA((21,)),
            pltpu.SemaphoreType.DMA((11,)),
        ],
        compiler_params=pltpu.CompilerParams(
            vmem_limit_bytes=60 * 1024 * 1024, collective_id=collective, has_side_effects=True
        ),
        cost_estimate=cost(0, 200 * 1024 * 1024),
        name="finish",
    )(wide, out, mine, other, both, tokens, resid, *layer_parts)


def swap(array, bits):
    return lax.ppermute(array, "gy", [(i, i ^ bits) for i in range(8)])


def pick(array, index):
    return lax.dynamic_index_in_dim(array, index, 0, keepdims=False)


def after(array, *earlier):
    return lax.optimization_barrier((array, *earlier))[0]


def pair_rows(pair, core):
    kept, got = pick(pair, core), swap(pick(pair, 1 - core), CORE)
    return jnp.where(core == 0, jnp.concatenate([kept, got]), jnp.concatenate([got, kept]))


def plane_order(blocks, chip):
    rows = blocks[0].shape[0]
    whole = jnp.zeros((4 * rows,) + blocks[0].shape[1:], blocks[0].dtype)
    for index, block in enumerate(blocks):
        whole = lax.dynamic_update_slice_in_dim(whole, block, (chip ^ index) * rows, 0)
    return whole


def on_core(
    tokens,
    cotangent,
    segment,
    parent,
    w_qkv,
    qkv_bias,
    w_out,
    gain_attn,
    gain_ffn,
    w_gate,
    w_up,
    w_down,
):
    low, full = jnp.bfloat16, jnp.float32
    me = lax.axis_index("gy")
    plane = lax.axis_index("gx")
    core, chip = me % 2, me // 2
    rows, width = 2 * tokens.shape[1], tokens.shape[2]
    slot_len = segment.shape[1]
    own_units = w_gate.shape[1]
    pad_units = -(-own_units // 384) * 384
    qwidth, kwidth = HEADS * HEAD, KV_HEADS * HEAD
    offset = chip * rows

    nb, ng = qkv_bias.shape[0], gain_attn.shape[0]
    packed = jnp.concatenate([qkv_bias, gain_attn, gain_ffn]).reshape(-1, 1)
    packed = jnp.pad(packed, ((0, 4 * ng - packed.shape[0]), (0, 0))).reshape(4, ng).T
    packed = jnp.pad(packed, ((0, 0), (0, HEAD - 4)))
    attn_own = jnp.concatenate([w_qkv, w_out.T, packed], axis=1)
    attn_slots = [attn_own] + [
        lax.ppermute(attn_own, "gx", [(i, (i + k) % 4) for i in range(4)]) for k in (1, 2, 3)
    ]

    inputs_low = pair_rows(tokens, core)
    grad_low = pair_rows(cotangent, core)

    seg_tree = pick(segment, core)
    valid, upper_one, upper_two, depth_pos = tree_tables(seg_tree, pick(parent, core))
    places = jnp.arange(slot_len, dtype=jnp.int32)

    def take_own(array):
        return lax.dynamic_slice_in_dim(array, offset, rows, 0)

    cosine, sine = rotation(take_own(depth_pos), HEAD)
    sine = sine * jnp.where(jnp.arange(HEAD) < HEAD // 2, -1.0, 1.0)

    more = pad_units - own_units
    shards = [jnp.pad(w, ((0, 0), (0, more))) for w in (w_gate, w_up, w_down.T)]
    weights = [
        lax.all_gather(after(w, *attn_slots, inputs_low, grad_low), "gx", axis=0, tiled=True) for w in shards[:2]
    ]
    weights.append(lax.all_gather(after(shards[2], weights[0]), "gx", axis=0, tiled=True))
    attn_all, cotan_others = spread([after(s, inputs_low, cosine, sine, *shards) for s in attn_slots], grad_low)
    cotan_blocks = [grad_low] + cotan_others
    qwide = qwidth + 2 * kwidth
    small = attn_all[:, qwide + width :].reshape(32, ng, HEAD)[:, :, :4].transpose(0, 2, 1).reshape(32, 4 * ng)
    small = small.astype(full)
    bias_full = small[:, :nb].reshape(1, -1)
    gain_one = small[:, nb : nb + ng].reshape(1, -1)
    gain_two = small[:, nb + ng : nb + 2 * ng].reshape(1, -1)
    out_turned = attn_all[:, qwide : qwide + width]

    normed_one, query, keyval_own = project(inputs_low, gain_one, attn_all, bias_full, cosine, sine)
    mask = allowed(
        after(take_own(seg_tree), keyval_own), take_own(upper_one), take_own(upper_two), take_own(places), seg_tree, valid, places
    )
    qblocks, kblocks = rows // QUERY_TILE, slot_len // KEY_TILE
    active = mask.reshape(qblocks, QUERY_TILE, kblocks, KEY_TILE).any(axis=(1, 3))
    block_count = active.sum(axis=1).astype(jnp.int32)
    rank = jnp.cumsum(active.astype(jnp.int32), axis=1) - 1
    numbers = jnp.arange(kblocks, dtype=jnp.int32)
    hit = active[:, :, None] & (rank[:, :, None] == numbers[None, None, :])
    block_list = jnp.sum(jnp.where(hit, numbers[None, :, None], 0), axis=1).astype(jnp.int32)
    mask_bias = jnp.where(mask.T, 0.0, NEGATIVE).astype(low)

    keyval = plane_order([keyval_own] + [swap(keyval_own, bits) for bits in OTHERS], chip)
    other_weights = [swap(after(w, keyval), CORE) for w in weights[:2]]
    query = after(query, *other_weights)
    heads_out, lse = attend_fast(block_list, block_count, query, keyval, mask_bias)
    inputs = inputs_low.astype(full)
    resid = inputs + lax.dot_general(heads_out, out_turned, (((1,), (1,)), ((), ())), preferred_element_type=full)
    normed_two = norm_parts(resid, gain_two)[2]

    other_weights.append(swap(after(weights[2], heads_out), CORE))
    pieces = weights + other_weights
    half = rows // 2
    first, second = (0, half), (half, half)
    own, (normed_x, normed_y) = ffn_block(
        normed_two, cotan_blocks[0], pieces, 1, [whole_side(normed_two, ALONG_X), whole_side(normed_two, ALONG_Y)]
    )
    passed_on = [(normed_x, first, first, ALONG_Y), (normed_y, second, second, ALONG_X)]
    near_x, (normed_d,) = ffn_block(normed_x, cotan_blocks[1], pieces, 2, [passed_on])
    cut, early = (count * ROW_TILE for count in BRANCH_CUTS)
    rest, few = rows - cut, rows // 10 * 3
    far, (back_x,) = ffn_block(normed_d, cotan_blocks[3], pieces, 3, [rows_side(near_x[4], 0, cut, ALONG_X)])
    near_y, (back_d,) = ffn_block(
        after(normed_y, far[4]), cotan_blocks[2], pieces, 4, [rows_side(far[4], 0, cut, ALONG_X)]
    )
    normed_blocks = [normed_two, normed_x, normed_y, normed_d]
    hidden_b, gate_b, up_b, out_b, back_b = zip(own, near_x, near_y, far)

    def join(mine, passed):
        return (mine.astype(full) + passed.astype(full)).astype(low)

    (down_mine, down_sent), (back_x_end, back_d_end, out_d_end, back_y) = wgrad(
        hidden_b,
        cotan_blocks,
        4,
        5,
        [
            rows_side(back_b[1], cut, rest, ALONG_X),
            rows_side(back_b[3], cut, rest, ALONG_X),
            rows_side(out_b[3], 0, few, ALONG_X),
            rows_side(join(back_b[2][:early], back_d[:early]), 0, early, ALONG_Y),
        ],
    )
    late = join(back_b[2][early:], jnp.concatenate([back_d[early:], back_d_end]))
    (gate_mine, gate_sent), (down_got, out_d, back_y_end) = wgrad(
        gate_b,
        normed_blocks,
        4,
        6,
        [
            whole_side(down_sent, CORE),
            rows_side(out_b[3], few, rows - few, ALONG_X),
            rows_side(late, 0, rows - early, ALONG_Y),
        ],
    )
    gate_got = swap(gate_sent, CORE)
    out_d = jnp.concatenate([out_d_end, out_d])

    grad_resid, grad_heads, grad_gain_two, grad_wout = branch_back(
        back_b[0],
        (back_x, back_x_end),
        (back_y, back_y_end),
        resid,
        grad_low,
        gain_two,
        heads_out,
        attn_all,
        qwide,
    )
    out_got = [swap(after(out_b[1], gate_sent), ALONG_X), swap(join(out_b[2], out_d), ALONG_Y)]
    both = both_sums(down_mine, down_got, after(gate_mine, grad_heads), gate_got)
    grad_heads = after(grad_heads, grad_wout, both)
    both = lax.psum_scatter(both, "gx", scatter_dimension=0, tiled=True)[0]
    query_lin, keyval_part = attend_back_fast(
        block_list, block_count, query, keyval, mask_bias, lse, heads_out, grad_heads, cosine, sine
    )

    keyval_own = lax.dynamic_slice_in_dim(keyval_part, offset, rows, 0)
    (up_mine, up_sent), others = wgrad(
        up_b, normed_blocks, 4, 7, [chip_side(keyval_part, bits) for bits in OTHERS]
    )

    (grad_rows, grad_bias, grad_gain_one, grad_wqkv), (up_got,) = project_back(
        query_lin,
        (keyval_own, *others),
        cosine,
        sine,
        attn_all,
        inputs_low,
        gain_one,
        grad_resid,
        normed_one,
        9,
        [whole_side(up_sent, CORE)],
    )
    packed = jnp.concatenate(
        [grad_bias.reshape(32, nb), grad_gain_one.reshape(32, ng), grad_gain_two.reshape(32, ng)], axis=1
    )
    packed = jnp.pad(packed, ((0, 0), (0, 4 * ng - packed.shape[1]))).reshape(32, 4, ng).transpose(0, 2, 1)
    packed = jnp.pad(packed.reshape(32 * ng, 4), ((0, 0), (0, HEAD - 4))).astype(low)
    wide, grad_wout, grad_wup, grad_down, grad_wgate, layer_out, grad_tokens = finish(
        lax.dynamic_update_slice_in_dim(grad_wqkv, packed, qwide, 1),
        grad_wout,
        up_mine,
        up_got,
        both,
        grad_rows,
        resid,
        (out_b[0], *out_got),
        own_units,
        8,
    )
    grad_wqkv, grad_wout = wide[:, :qwide], grad_wout.T
    small = wide[:, qwide : qwide + 4].T.reshape(-1)
    grad_wgate, grad_wup = grad_wgate.T, grad_wup.T
    return (
        layer_out,
        grad_tokens,
        grad_wqkv,
        small[:nb],
        grad_wout,
        small[nb : nb + ng],
        small[nb + ng : nb + 2 * ng],
        grad_wgate,
        grad_wup,
        grad_down,
    )


def solution(mesh):
    in_specs = (
        P("gx", "gy", None),
        P("gx", "gy", None),
        P("gx", None),
        P("gx", None),
        P(("gx", "gy"), None),
        P(("gx", "gy")),
        P(None, ("gx", "gy")),
        P(("gx", "gy")),
        P(("gx", "gy")),
        P("gx", "gy"),
        P("gx", "gy"),
        P("gy", "gx"),
    )
    out_specs = (
        P("gx", "gy", None),
        P("gx", "gy", None),
        P(("gx", "gy"), None),
        P(("gx", "gy")),
        P(None, ("gx", "gy")),
        P(("gx", "gy")),
        P(("gx", "gy")),
        P("gx", "gy"),
        P("gx", "gy"),
        P("gy", "gx"),
    )
    return jax.shard_map(
        on_core if tuple(mesh.shape.values()) == (4, 8) else on_device,
        mesh=mesh,
        in_specs=in_specs,
        out_specs=out_specs,
        check_vma=False,
    )
```

```python
from functools import reduce
import math

import jax
import jax.numpy as jnp
from jax import lax
from jax.experimental import pallas as pl
from jax.experimental.pallas import tpu as pltpu
from jax.sharding import PartitionSpec as P

HEADS = 12
KV_HEADS = 2
HEAD = 128

QUERY_TILE = 128
KEY_TILE = 256
ROW_TILE = 128
BRANCH_CUTS = (4, 3)
FFN_CHUNK = 256
FFN_PARTS = 2
WG_TILE = 384
PACE = 1.0
LOG2E = 1.0 / math.log(2.0)

CORE, ALONG_X, ALONG_Y, ACROSS = 1, 2, 4, 6
OTHERS = (ALONG_X, ALONG_Y, ACROSS)
RING = 8


EPS = 1e-06
THETA = 1000000.0
NEGATIVE = -1e30


def tree_tables(segment, parent):
    slot_len = segment.shape[0]
    seg_count = parent.shape[0]
    places = jnp.arange(slot_len, dtype=jnp.int32)
    labels = jnp.arange(seg_count, dtype=jnp.int32)
    member = segment[:, None] == labels[None, :]
    valid = segment >= 0
    first = jnp.min(jnp.where(member, places[:, None], slot_len), axis=0)
    length = jnp.sum(member.astype(jnp.int32), axis=0)
    parent_hit = parent[:, None] == labels[None, :]
    grand = jnp.sum(jnp.where(parent_hit, parent[None, :], 0), axis=1)
    grand_hit = grand[:, None] == labels[None, :]
    parent_len = jnp.sum(jnp.where(parent_hit, length[None, :], 0), axis=1)
    grand_len = jnp.sum(jnp.where(grand_hit, length[None, :], 0), axis=1)
    base = jnp.where(parent != labels, parent_len, 0) + jnp.where(grand != parent, grand_len, 0)

    def lookup(table):
        return jnp.sum(jnp.where(member, table[None, :], 0), axis=1)

    upper_one = jnp.where(valid, lookup(parent), -2)
    upper_two = jnp.where(valid, lookup(grand), -2)
    depth_pos = jnp.where(valid, places - lookup(first) + lookup(base), 0)
    return (valid, upper_one, upper_two, depth_pos)


def allowed(seg_query, upper_one, upper_two, place_query, seg_keys, valid_keys, place_keys):
    related = (seg_keys[None, :] == seg_query[:, None]) | (seg_keys[None, :] == upper_one[:, None])
    related = related | (seg_keys[None, :] == upper_two[:, None])
    earlier = place_keys[None, :] <= place_query[:, None]
    return related & earlier & valid_keys[None, :] | (place_keys[None, :] == place_query[:, None])


def rotation(depth_pos, width):
    half = width // 2
    freqs = jnp.exp(jnp.arange(half, dtype=jnp.float32) * (-2.0 * math.log(THETA) / width))
    angle = depth_pos.astype(jnp.float32)[:, None] * freqs[None, :]
    cosine = jnp.concatenate([jnp.cos(angle), jnp.cos(angle)], axis=1)
    sine = jnp.concatenate([jnp.sin(angle), jnp.sin(angle)], axis=1)
    return (cosine, sine)


def turn(heads, cosine, sine):
    half = heads.shape[-1] // 2
    swapped = jnp.concatenate([-heads[..., half:], heads[..., :half]], axis=-1)
    return heads * cosine[:, None, :] + swapped * sine[:, None, :]


def norm_parts(values, gain):
    inverse = lax.rsqrt(jnp.mean(values * values, axis=-1, keepdims=True) + EPS)
    unit = values * inverse
    return (unit, inverse, (unit * gain).astype(jnp.bfloat16))


def norm_back(grad_normed, unit, inverse, gain):
    scaled = grad_normed * gain
    back = inverse * (scaled - unit * jnp.mean(scaled * unit, axis=-1, keepdims=True))
    return (back, jnp.sum(grad_normed * unit, axis=0))


def masked_scores(group_query, group_keys, mask, scale):
    scores = (
        jnp.einsum("rhd,kd->hrk", group_query, group_keys, preferred_element_type=jnp.float32)
        * scale
    )
    return jnp.where(mask[None], scores, NEGATIVE)


def attend(query_low, keys_all, values_all, mask, scale):
    group = HEADS // KV_HEADS
    pieces = []
    totals = []
    for head_group in range(KV_HEADS):
        group_query = query_low[:, head_group * group : (head_group + 1) * group, :]
        columns = slice(head_group * HEAD, (head_group + 1) * HEAD)
        scores = masked_scores(group_query, keys_all[:, columns], mask, scale)
        top_score = jnp.max(scores, axis=-1, keepdims=True)
        expo = jnp.exp(scores - top_score)
        denom = jnp.sum(expo, axis=-1, keepdims=True)
        probs_low = (expo / denom).astype(jnp.bfloat16)
        pieces.append(
            jnp.einsum(
                "hrk,kd->rhd", probs_low, values_all[:, columns], preferred_element_type=jnp.float32
            )
        )
        totals.append(top_score + jnp.log(denom))
    return (jnp.concatenate(pieces, axis=1), totals)


def attend_back(query_low, keys_all, values_all, mask, totals, grad_heads, scale):
    group = HEADS // KV_HEADS
    grad_query, grad_keys, grad_values = ([], [], [])
    for head_group in range(KV_HEADS):
        heads_sel = slice(head_group * group, (head_group + 1) * group)
        columns = slice(head_group * HEAD, (head_group + 1) * HEAD)
        group_query = query_low[:, heads_sel, :]
        group_keys = keys_all[:, columns]
        group_grad = grad_heads[:, heads_sel, :]
        scores = masked_scores(group_query, group_keys, mask, scale)
        probs = jnp.exp(scores - totals[head_group])
        probs_low = probs.astype(jnp.bfloat16)
        grad_values.append(
            jnp.einsum("hrk,rhd->kd", probs_low, group_grad, preferred_element_type=jnp.float32)
        )
        grad_probs = jnp.einsum(
            "rhd,kd->hrk", group_grad, values_all[:, columns], preferred_element_type=jnp.float32
        )
        grad_scores = (
            probs * (grad_probs - jnp.sum(probs * grad_probs, axis=-1, keepdims=True))
        ).astype(jnp.bfloat16)
        grad_query.append(
            jnp.einsum("hrk,kd->rhd", grad_scores, group_keys, preferred_element_type=jnp.float32)
            * scale
        )
        grad_keys.append(
            jnp.einsum("hrk,rhd->kd", grad_scores, group_query, preferred_element_type=jnp.float32)
            * scale
        )
    return (
        jnp.concatenate(grad_query, axis=1),
        jnp.concatenate(grad_keys, axis=1),
        jnp.concatenate(grad_values, axis=1),
    )


def add_trees(left, right):
    return jax.tree.map(jnp.add, left, right)


def on_device(
    tokens,
    cotangent,
    segment,
    parent,
    w_qkv,
    qkv_bias,
    w_out,
    gain_attn,
    gain_ffn,
    w_gate,
    w_up,
    w_down,
):
    micro = tokens.shape[0]
    row_count = tokens.shape[1]
    slot_len = segment.shape[1]
    qwidth = HEADS * HEAD
    kwidth = KV_HEADS * HEAD
    scale = 1.0 / math.sqrt(HEAD)
    offset = lax.axis_index("gy") * row_count
    place_all = jnp.arange(slot_len, dtype=jnp.int32)
    place_own = offset + jnp.arange(row_count, dtype=jnp.int32)
    outputs, input_grads, attn_list, ffn_list = ([], [], [], [])
    for micro_index in range(micro):
        attn_full = (
            lax.all_gather(w_qkv, ("gx", "gy"), axis=0, tiled=True),
            lax.all_gather(qkv_bias, ("gx", "gy"), axis=0, tiled=True),
            lax.all_gather(w_out, ("gx", "gy"), axis=1, tiled=True),
            lax.all_gather(gain_attn, ("gx", "gy"), axis=0, tiled=True),
            lax.all_gather(gain_ffn, ("gx", "gy"), axis=0, tiled=True),
        )
        ffn_full = (
            lax.all_gather(w_gate, "gx", axis=0, tiled=True),
            lax.all_gather(w_up, "gx", axis=0, tiled=True),
            lax.all_gather(w_down, "gx", axis=1, tiled=True),
        )
        qkv_full, bias_full, out_full, gain_one_full, gain_two_full = attn_full
        gate_full, up_full, down_full = ffn_full
        gain_one = gain_one_full.astype(jnp.float32)
        gain_two = gain_two_full.astype(jnp.float32)
        seg_tree = segment[micro_index]
        valid, upper_one, upper_two, depth_pos = tree_tables(seg_tree, parent[micro_index])

        def take_own(array):
            return lax.dynamic_slice_in_dim(array, offset, row_count, 0)

        mask = allowed(
            take_own(seg_tree),
            take_own(upper_one),
            take_own(upper_two),
            place_own,
            seg_tree,
            valid,
            place_all,
        )
        cosine, sine = rotation(take_own(depth_pos), HEAD)
        inputs = tokens[micro_index].astype(jnp.float32)
        unit_one, inverse_one, normed_one = norm_parts(inputs, gain_one)
        linear = jnp.dot(
            normed_one, qkv_full, preferred_element_type=jnp.float32
        ) + bias_full.astype(jnp.float32)
        query_low = turn(linear[:, :qwidth].reshape(row_count, HEADS, HEAD), cosine, sine).astype(
            jnp.bfloat16
        )
        keys_low = turn(
            linear[:, qwidth : qwidth + kwidth].reshape(row_count, KV_HEADS, HEAD), cosine, sine
        )
        keys_low = keys_low.reshape(row_count, kwidth).astype(jnp.bfloat16)
        values_low = linear[:, qwidth + kwidth :].astype(jnp.bfloat16)
        keys_all, values_all = (
            lax.all_gather(keys_low, "gy", axis=0, tiled=True),
            lax.all_gather(values_low, "gy", axis=0, tiled=True),
        )
        heads_raw, totals = attend(query_low, keys_all, values_all, mask, scale)
        heads_out = heads_raw.reshape(row_count, qwidth).astype(jnp.bfloat16)
        resid = inputs + jnp.dot(heads_out, out_full, preferred_element_type=jnp.float32)
        unit_two, inverse_two, normed_two = norm_parts(resid, gain_two)
        normed_all = lax.all_gather(normed_two, "gy", axis=0, tiled=True)
        gate = jnp.dot(normed_all, gate_full, preferred_element_type=jnp.float32)
        upward = jnp.dot(normed_all, up_full, preferred_element_type=jnp.float32)
        sigma = jax.nn.sigmoid(gate)
        swish = gate * sigma
        hidden = (swish * upward).astype(jnp.bfloat16)
        ffn_own = lax.psum_scatter(
            jnp.dot(hidden, down_full, preferred_element_type=jnp.float32),
            "gy",
            scatter_dimension=0,
            tiled=True,
        )
        outputs.append((resid + ffn_own).astype(jnp.bfloat16))
        grad_low = cotangent[micro_index]
        grad_all = lax.all_gather(grad_low, "gy", axis=0, tiled=True)
        grad_hidden = jnp.dot(grad_all, down_full.T, preferred_element_type=jnp.float32)
        grad_down = jnp.dot(hidden.T, grad_all, preferred_element_type=jnp.float32)
        grad_gate = (grad_hidden * upward * sigma * (1.0 + gate * (1.0 - sigma))).astype(
            jnp.bfloat16
        )
        grad_up = (grad_hidden * swish).astype(jnp.bfloat16)
        grad_wgate = jnp.dot(normed_all.T, grad_gate, preferred_element_type=jnp.float32)
        grad_wup = jnp.dot(normed_all.T, grad_up, preferred_element_type=jnp.float32)
        grad_normed_two = lax.psum_scatter(
            jnp.dot(grad_gate, gate_full.T, preferred_element_type=jnp.float32)
            + jnp.dot(grad_up, up_full.T, preferred_element_type=jnp.float32),
            "gy",
            scatter_dimension=0,
            tiled=True,
        )
        back_two, grad_gain_two = norm_back(grad_normed_two, unit_two, inverse_two, gain_two)
        grad_resid = grad_low.astype(jnp.float32) + back_two
        grad_branch = grad_resid.astype(jnp.bfloat16)
        grad_wout = jnp.dot(heads_out.T, grad_branch, preferred_element_type=jnp.float32)
        grad_heads = jnp.dot(grad_branch, out_full.T, preferred_element_type=jnp.float32).astype(
            jnp.bfloat16
        )
        grad_heads = grad_heads.reshape(row_count, HEADS, HEAD)
        grad_query, keys_part, values_part = attend_back(
            query_low, keys_all, values_all, mask, totals, grad_heads, scale
        )
        grad_keys, grad_values = (
            lax.psum_scatter(keys_part, "gy", scatter_dimension=0, tiled=True),
            lax.psum_scatter(values_part, "gy", scatter_dimension=0, tiled=True),
        )
        query_lin = turn(grad_query, cosine, -sine).reshape(row_count, qwidth)
        keys_lin = turn(grad_keys.reshape(row_count, KV_HEADS, HEAD), cosine, -sine).reshape(
            row_count, kwidth
        )
        grad_linear = jnp.concatenate([query_lin, keys_lin, grad_values], axis=1).astype(
            jnp.bfloat16
        )
        grad_wqkv = jnp.dot(normed_one.T, grad_linear, preferred_element_type=jnp.float32)
        grad_bias = jnp.sum(grad_linear.astype(jnp.float32), axis=0)
        grad_normed_one = jnp.dot(grad_linear, qkv_full.T, preferred_element_type=jnp.float32)
        back_one, grad_gain_one = norm_back(grad_normed_one, unit_one, inverse_one, gain_one)
        input_grads.append((grad_resid + back_one).astype(jnp.bfloat16))
        attn_list.append((grad_wqkv, grad_bias, grad_wout, grad_gain_one, grad_gain_two))
        ffn_list.append((grad_wgate, grad_wup, grad_down))
    attn_total = reduce(add_trees, attn_list)
    ffn_total = reduce(add_trees, ffn_list)
    attn_total = (
        lax.psum_scatter(attn_total[0], ("gx", "gy"), scatter_dimension=0, tiled=True),
        lax.psum_scatter(attn_total[1], ("gx", "gy"), scatter_dimension=0, tiled=True),
        lax.psum_scatter(attn_total[2], ("gx", "gy"), scatter_dimension=1, tiled=True),
        lax.psum_scatter(attn_total[3], ("gx", "gy"), scatter_dimension=0, tiled=True),
        lax.psum_scatter(attn_total[4], ("gx", "gy"), scatter_dimension=0, tiled=True),
    )
    ffn_total = (
        lax.psum_scatter(ffn_total[0], "gx", scatter_dimension=0, tiled=True),
        lax.psum_scatter(ffn_total[1], "gx", scatter_dimension=0, tiled=True),
        lax.psum_scatter(ffn_total[2], "gx", scatter_dimension=1, tiled=True),
    )
    layer_out = jnp.stack(outputs, axis=0)
    grad_tokens = jnp.stack(input_grads, axis=0)
    return (
        layer_out,
        grad_tokens,
        attn_total[0],
        attn_total[1],
        attn_total[2],
        attn_total[3],
        attn_total[4],
        ffn_total[0],
        ffn_total[1],
        ffn_total[2],
    )


def dot_nn(left, right):
    return lax.dot_general(left, right, (((1,), (0,)), ((), ())), preferred_element_type=jnp.float32)


def dot_nt(left, right):
    return lax.dot_general(left, right, (((1,), (1,)), ((), ())), preferred_element_type=jnp.float32)


def dot_tn(left, right):
    return lax.dot_general(left, right, (((0,), (0,)), ((), ())), preferred_element_type=jnp.float32)


def cost(flops, moved, trans=0):
    return pl.CostEstimate(flops=int(flops * PACE), bytes_accessed=int(moved * PACE), transcendentals=int(trans * PACE))


def params(mib):
    return pltpu.CompilerParams(vmem_limit_bytes=mib * 1024 * 1024)


def sigmoid(v):
    return 0.5 * jnp.tanh(0.5 * v) + 0.5


def peers_of():
    me, plane = lax.axis_index("gy"), lax.axis_index("gx")
    along_x = me + 2 - 4 * lax.rem(me // 2, 2)
    return {
        CORE: {"gy": me + 1 - 2 * lax.rem(me, 2)},
        ALONG_X: {"gy": along_x},
        ALONG_Y: {"gy": me + 4 - 8 * (me // 4)},
        ACROSS: {"gy": along_x + 4 - 8 * (along_x // 4)},
        RING: {"gx": lax.rem(plane + 1, 4)},
        RING + 1: {"gx": lax.rem(plane + 2, 4)},
        -RING: {"gx": lax.rem(plane + 3, 4)},
    }


def greet(bits_used):
    peers = peers_of()
    barrier = pltpu.get_barrier_semaphore()
    greeted = [bits for bits in bits_used] + [-RING] * (RING in bits_used)
    for bits in greeted:
        pl.semaphore_signal(barrier, inc=1, device_id=peers[bits], device_id_type=pl.DeviceIdType.MESH)
    pl.semaphore_wait(barrier, len(greeted))


def side_copies(sides, sources, targets, sent, landed):
    peers = peers_of()
    copies = []
    for parts, target in zip(sides, targets):
        for _, take, fill, bits in parts:
            if take is None:
                take = (pl.multiple_of(peers[bits]["gy"] // 2 * fill[1], fill[1]), fill[1])
            copies.append(
                pltpu.make_async_remote_copy(
                    sources[len(copies)].at[pl.ds(*take)],
                    target.at[pl.ds(*fill)],
                    sent.at[len(copies)],
                    landed.at[len(copies)],
                    device_id=peers[bits],
                    device_id_type=pl.DeviceIdType.MESH,
                )
            )
    return copies


def whole_side(array, bits):
    return [(array, (0, array.shape[0]), (0, array.shape[0]), bits)]


def rows_side(array, start, count, bits):
    return [(array, (start, count), (0, count), bits)]


def chip_side(array, bits):
    return [(array, None, (0, array.shape[0] // 4), bits)]


def call_beside(body, sides, collective, operands, grid, in_specs, out_specs, out_shape, scratch_shapes, mib, estimate, name):
    n_in, n_out, n_scratch = len(in_specs), len(out_specs), len(scratch_shapes)
    flat = [part for parts in sides for part in parts]
    bits_used = sorted({part[3] for part in flat})

    def whole_body(*refs):
        ins, refs = refs[:n_in], refs[n_in:]
        sources, refs = refs[: len(flat)], refs[len(flat) :]
        outs, refs = refs[:n_out], refs[n_out:]
        targets, refs = refs[: len(sides)], refs[len(sides) :]
        scratch, refs = refs[:n_scratch], refs[n_scratch:]
        step, last = pl.program_id(0), pl.num_programs(0) - 1
        if flat:

            @pl.when(step == 0)
            def _():
                greet(bits_used)
                for copy in side_copies(sides, sources, targets, *refs):
                    copy.start()

        body(*ins, *outs, *scratch)
        if flat:

            @pl.when(step == last)
            def _():
                for copy in side_copies(sides, sources, targets, *refs):
                    copy.wait()

    anywhere = pl.BlockSpec(memory_space=pl.ANY)
    extra = {"collective_id": collective, "has_side_effects": True} if flat else {}
    results = pl.pallas_call(
        whole_body,
        grid=grid,
        in_specs=list(in_specs) + [anywhere] * len(flat),
        out_specs=list(out_specs) + [anywhere] * len(sides),
        out_shape=list(out_shape)
        + [jax.ShapeDtypeStruct((sum(p[2][1] for p in parts),) + parts[0][0].shape[1:], parts[0][0].dtype) for parts in sides],
        scratch_shapes=list(scratch_shapes) + ([pltpu.SemaphoreType.DMA((len(flat),))] * 2 if flat else []),
        compiler_params=pltpu.CompilerParams(vmem_limit_bytes=mib * 1024 * 1024, **extra),
        cost_estimate=estimate,
        name=name,
    )(*operands, *[part[0] for part in flat])
    return results[:n_out], results[n_out:]


def ffn_copies(chunk, pieces, held, sems):
    units = pieces[0].shape[1]
    tile = FFN_CHUNK // 2
    slot = chunk % 2
    copies = []
    for part in range(2):
        column = chunk * FFN_CHUNK + part * tile
        owner, inside = column // units, column % units
        for kind in range(3):
            copies.append(
                pltpu.make_async_copy(
                    pieces[3 * owner + kind].at[:, pl.ds(inside, tile)],
                    held.at[slot, kind, :, pl.ds(part * tile, tile)],
                    sems.at[slot, part * 3 + kind],
                )
            )
    return copies


def ffn_body(n_ref, c_ref, *refs):
    pieces = refs[:6]
    hid_ref, dg_ref, du_ref, f_ref, dn_ref, f_acc, dn_acc, held, sems = refs[6:]
    step = pl.program_id(0)
    chunks = 2 * pieces[0].shape[1] // FFN_CHUNK

    @pl.when(step == 0)
    def _():
        for copy in ffn_copies(0, pieces, held, sems):
            copy.start()
        f_acc[...] = jnp.zeros_like(f_acc)
        dn_acc[...] = jnp.zeros_like(dn_acc)

    for chunk in range(chunks):

        @pl.when(step == chunk)
        def _():
            if chunk + 1 < chunks:
                for copy in ffn_copies(chunk + 1, pieces, held, sems):
                    copy.start()
            for copy in ffn_copies(chunk, pieces, held, sems):
                copy.wait()

    slot = step % 2
    rows = n_ref.shape[0]
    part = rows // FFN_PARTS
    takes = [pl.ds(index * part, part) for index in range(FFN_PARTS)]

    def products(take):
        return (
            dot_nn(n_ref[take, :], held[slot, 0]),
            dot_nn(n_ref[take, :], held[slot, 1]),
            dot_nn(c_ref[take, :], held[slot, 2]),
        )

    later = products(takes[0])
    for index, take in enumerate(takes):
        gate, upward, grad_hidden = later
        if index + 1 < FFN_PARTS:
            later = products(takes[index + 1])
        sigma = sigmoid(gate)
        swish = gate * sigma
        hidden = (swish * upward).astype(jnp.bfloat16)
        hid_ref[take, :] = hidden
        grad_gate = (grad_hidden * upward * sigma * (1.0 + gate * (1.0 - sigma))).astype(jnp.bfloat16)
        grad_up = (grad_hidden * swish).astype(jnp.bfloat16)
        dg_ref[take, :] = grad_gate
        du_ref[take, :] = grad_up
        f_acc[take, :] += dot_nt(hidden, held[slot, 2])
        dn_acc[take, :] += dot_nt(grad_gate, held[slot, 0]) + dot_nt(grad_up, held[slot, 1])

    @pl.when(step == pl.num_programs(0) - 1)
    def _():
        f_ref[...] = f_acc[...].astype(f_ref.dtype)
        dn_ref[...] = dn_acc[...].astype(dn_ref.dtype)


def ffn_block(normed, cotan, pieces, collective, sides=()):
    rows, width = normed.shape
    units = 2 * pieces[0].shape[1]
    chunk = FFN_CHUNK
    whole = pl.BlockSpec((rows, width), lambda j: (0, 0))
    tall = pl.BlockSpec((rows, chunk), lambda j: (0, j))
    low = jnp.bfloat16
    return call_beside(
        ffn_body,
        sides,
        collective,
        (normed, cotan, *pieces),
        (units // chunk,),
        [whole, whole] + [pl.BlockSpec(memory_space=pl.ANY)] * len(pieces),
        [tall, tall, tall, whole, whole],
        [jax.ShapeDtypeStruct((rows, units), low)] * 3 + [jax.ShapeDtypeStruct((rows, width), low)] * 2,
        [pltpu.VMEM((rows, width), jnp.float32)] * 2
        + [pltpu.VMEM((2, 3, width, chunk), low), pltpu.SemaphoreType.DMA((2, len(pieces)))],
        60,
        cost(12 * rows * width * units, 6 * width * units + 6 * rows * (width + units)),
        "ffn_block",
    )


def wgrad_body(per_half, *refs):
    count = (len(refs) - 2) // 2
    total = dot_tn(refs[0][...], refs[count][...])
    for index in range(1, count):
        total = total + dot_tn(refs[index][...], refs[count + index][...])

    def store(out_ref):
        slots, _, wide = out_ref.shape
        for slot in range(slots):
            out_ref[slot] = total[:, slot * wide : (slot + 1) * wide].astype(out_ref.dtype)

    first = pl.program_id(0) < per_half
    pl.when(first)(lambda: store(refs[-2]))
    pl.when(jnp.logical_not(first))(lambda: store(refs[-1]))


def wgrad(lefts, rights, slots, collective, sides=()):
    rows, units = lefts[0].shape
    width = rights[0].shape[1]
    tile = WG_TILE
    per_half = units // 2 // tile
    wide = width // slots
    count = len(lefts)
    return call_beside(
        lambda *refs: wgrad_body(per_half, *refs),
        sides,
        collective,
        (*lefts, *rights),
        (units // tile,),
        [pl.BlockSpec((rows, tile), lambda j: (0, j))] * count
        + [pl.BlockSpec((rows, width), lambda j: (0, 0))] * count,
        [
            pl.BlockSpec((slots, tile, wide), lambda j: (0, jnp.minimum(j, per_half - 1), 0)),
            pl.BlockSpec((slots, tile, wide), lambda j: (0, jnp.maximum(j - per_half, 0), 0)),
        ],
        [jax.ShapeDtypeStruct((slots, units // 2, wide), jnp.bfloat16)] * 2,
        [],
        60,
        cost(2 * count * rows * width * units, 2 * count * rows * (width + units)),
        "ffn_wgrad",
    )


def group_rows(source_ref, group, per_group):
    return jnp.concatenate(
        [source_ref[:, (group * per_group + h) * HEAD : (group * per_group + h + 1) * HEAD] for h in range(per_group)],
        axis=0,
    )


def attend_body(list_ref, count_ref, q_ref, kv_ref, bias_ref, o_ref, lse_ref, qs, acc, top, den):
    block = pl.program_id(0)
    per_group = HEADS // KV_HEADS
    for group in range(KV_HEADS):
        qs[group] = group_rows(q_ref, group, per_group)
    acc[...] = jnp.zeros_like(acc)
    den[...] = jnp.zeros_like(den)
    top[...] = jnp.full_like(top, 2 * NEGATIVE)
    factor = LOG2E / math.sqrt(HEAD)

    def body(n, carry):
        rows = pl.ds(pl.multiple_of(list_ref[block, n] * KEY_TILE, KEY_TILE), KEY_TILE)
        bias = jnp.concatenate([bias_ref[rows, :].astype(jnp.float32)] * per_group, axis=1)
        products = [dot_nt(kv_ref[rows, g * HEAD : (g + 1) * HEAD], qs[g]) for g in range(KV_HEADS)]
        for group in range(KV_HEADS):
            values = kv_ref[rows, (KV_HEADS + group) * HEAD : (KV_HEADS + group + 1) * HEAD]
            scores = products[group] * factor + bias
            old = top[group]
            new = jnp.maximum(old, jnp.max(scores, axis=0, keepdims=True))
            probs = jnp.exp2(scores - new)
            shrink = jnp.exp2(old - new)
            den[group] = den[group] * shrink + jnp.sum(probs, axis=0, keepdims=True)
            acc[group] = acc[group] * shrink + dot_tn(values, probs.astype(jnp.bfloat16))
            top[group] = new
        return carry

    lax.fori_loop(0, count_ref[block], body, 0)
    for group in range(KV_HEADS):
        out = acc[group] / den[group]
        lse_ref[0, group] = top[group] + jnp.log(den[group]) * LOG2E
        for h in range(per_group):
            head = group * per_group + h
            o_ref[:, head * HEAD : (head + 1) * HEAD] = out[:, h * HEAD : (h + 1) * HEAD].T.astype(o_ref.dtype)


def attend_fast(block_list, block_count, query, keyval, bias):
    rows, qwidth = query.shape
    slots = keyval.shape[0]
    blocks = rows // QUERY_TILE
    per_group = HEADS // KV_HEADS
    lanes = per_group * QUERY_TILE
    whole = pl.BlockSpec(keyval.shape, lambda i, a, b: (0, 0))
    tile = pl.BlockSpec((QUERY_TILE, qwidth), lambda i, a, b: (i, 0))
    return pl.pallas_call(
        attend_body,
        grid_spec=pltpu.PrefetchScalarGridSpec(
            num_scalar_prefetch=2,
            grid=(blocks,),
            in_specs=[tile, whole, pl.BlockSpec((slots, QUERY_TILE), lambda i, a, b: (0, i))],
            out_specs=[tile, pl.BlockSpec((1, KV_HEADS, 1, lanes), lambda i, a, b: (i, 0, 0, 0))],
            scratch_shapes=[
                pltpu.VMEM((KV_HEADS, lanes, HEAD), jnp.bfloat16),
                pltpu.VMEM((KV_HEADS, HEAD, lanes), jnp.float32),
                pltpu.VMEM((KV_HEADS, 1, lanes), jnp.float32),
                pltpu.VMEM((KV_HEADS, 1, lanes), jnp.float32),
            ],
        ),
        out_shape=[
            jax.ShapeDtypeStruct((rows, qwidth), jnp.bfloat16),
            jax.ShapeDtypeStruct((blocks, KV_HEADS, 1, lanes), jnp.float32),
        ],
        compiler_params=params(48),
        cost_estimate=cost(2 * rows * slots * qwidth * 2, 4 * slots * rows, HEADS * rows * slots // 2),
        name="tree_attention",
    )(block_list, block_count, query, keyval, bias)


def attend_back_body(
    list_ref, count_ref, q_ref, kv_ref, bias_ref, lse_ref, o_ref, do_ref, cos_ref, sin_ref,
    dq_ref, dkv_ref, qs, dos, delta, dqt, dkv,
):
    block = pl.program_id(0)
    per_group = HEADS // KV_HEADS
    scale = 1.0 / math.sqrt(HEAD)
    factor = LOG2E * scale
    lanes = qs.shape[1]

    @pl.when(block == 0)
    def _():
        dkv[...] = jnp.zeros_like(dkv)

    for group in range(KV_HEADS):
        qs[group] = group_rows(q_ref, group, per_group)
        grads = group_rows(do_ref, group, per_group)
        dos[group] = grads
        both = grads.astype(jnp.float32) * group_rows(o_ref, group, per_group).astype(jnp.float32)
        delta[group] = lax.dot_general(
            jnp.ones((8, HEAD), jnp.float32), both, (((1,), (1,)), ((), ())),
            precision=lax.Precision.HIGHEST, preferred_element_type=jnp.float32,
        )[0:1]
    dqt[...] = jnp.zeros_like(dqt)

    def body(n, carry):
        rows = pl.ds(pl.multiple_of(list_ref[block, n] * KEY_TILE, KEY_TILE), KEY_TILE)
        bias = jnp.concatenate([bias_ref[rows, :].astype(jnp.float32)] * per_group, axis=1)
        for group in range(KV_HEADS):
            kcols = slice(group * HEAD, (group + 1) * HEAD)
            vcols = slice((KV_HEADS + group) * HEAD, (KV_HEADS + group + 1) * HEAD)
            keys = kv_ref[rows, kcols]
            values = kv_ref[rows, vcols]
            scores = dot_nt(keys, qs[group]) * factor + bias
            probs = jnp.exp2(scores - lse_ref[0, group])
            grad_probs = dot_nt(values, dos[group])
            grad_scores = (probs * (grad_probs - delta[group])).astype(jnp.bfloat16)
            dkv[rows, vcols] += dot_nn(probs.astype(jnp.bfloat16), dos[group])
            dkv[rows, kcols] += dot_nn(grad_scores, qs[group])
            dqt[group] += dot_tn(keys, grad_scores)
        return carry

    lax.fori_loop(0, count_ref[block], body, 0)
    cosine, sine = cos_ref[...], sin_ref[...]
    for group in range(KV_HEADS):
        for h in range(per_group):
            head = group * per_group + h
            grad = dqt[group, :, h * HEAD : (h + 1) * HEAD].T * scale
            grad = grad * cosine - pltpu.roll(grad, HEAD // 2, 1) * sine
            dq_ref[:, head * HEAD : (head + 1) * HEAD] = grad.astype(dq_ref.dtype)

    @pl.when(block == pl.num_programs(0) - 1)
    def _():
        kwidth = KV_HEADS * HEAD
        dkv_ref[:, :kwidth] = (dkv[:, :kwidth] * scale).astype(dkv_ref.dtype)
        dkv_ref[:, kwidth:] = dkv[:, kwidth:].astype(dkv_ref.dtype)


def attend_back_fast(block_list, block_count, query, keyval, bias, lse, heads_out, grad_heads, cosine, sine):
    rows, qwidth = query.shape
    slots = keyval.shape[0]
    blocks = rows // QUERY_TILE
    per_group = HEADS // KV_HEADS
    lanes = per_group * QUERY_TILE
    whole = pl.BlockSpec(keyval.shape, lambda i, a, b: (0, 0))
    tile = pl.BlockSpec((QUERY_TILE, qwidth), lambda i, a, b: (i, 0))
    turned = pl.BlockSpec((QUERY_TILE, HEAD), lambda i, a, b: (i, 0))
    return pl.pallas_call(
        attend_back_body,
        grid_spec=pltpu.PrefetchScalarGridSpec(
            num_scalar_prefetch=2,
            grid=(blocks,),
            in_specs=[
                tile,
                whole,
                pl.BlockSpec((slots, QUERY_TILE), lambda i, a, b: (0, i)),
                pl.BlockSpec((1, KV_HEADS, 1, lanes), lambda i, a, b: (i, 0, 0, 0)),
                tile,
                tile,
                turned,
                turned,
            ],
            out_specs=[tile, whole],
            scratch_shapes=[
                pltpu.VMEM((KV_HEADS, lanes, HEAD), jnp.bfloat16),
                pltpu.VMEM((KV_HEADS, lanes, HEAD), jnp.bfloat16),
                pltpu.VMEM((KV_HEADS, 1, lanes), jnp.float32),
                pltpu.VMEM((KV_HEADS, HEAD, lanes), jnp.float32),
                pltpu.VMEM(keyval.shape, jnp.float32),
            ],
        ),
        out_shape=[
            jax.ShapeDtypeStruct((rows, qwidth), jnp.bfloat16),
            jax.ShapeDtypeStruct(keyval.shape, jnp.bfloat16),
        ],
        compiler_params=params(56),
        cost_estimate=cost(5 * rows * slots * qwidth * 2, 8 * slots * rows, HEADS * rows * slots // 2),
        name="tree_attention_back",
    )(block_list, block_count, query, keyval, bias, lse, heads_out, grad_heads, cosine, sine)


def project_body(x_ref, gain_ref, w_ref, b_ref, cos_ref, sin_ref, n_ref, q_ref, kv_ref):
    values = x_ref[...].astype(jnp.float32)
    inverse = lax.rsqrt(jnp.mean(values * values, axis=-1, keepdims=True) + EPS)
    normed = (values * inverse * gain_ref[...]).astype(jnp.bfloat16)
    n_ref[...] = normed
    linear = dot_nn(normed, w_ref[...]) + b_ref[...]
    cosine, sine = cos_ref[...], sin_ref[...]
    for head in range(HEADS + KV_HEADS):
        lane = linear[:, head * HEAD : (head + 1) * HEAD]
        lane = (lane * cosine + pltpu.roll(lane, HEAD // 2, 1) * sine).astype(jnp.bfloat16)
        if head < HEADS:
            q_ref[:, head * HEAD : (head + 1) * HEAD] = lane
        else:
            kv_ref[:, (head - HEADS) * HEAD : (head - HEADS + 1) * HEAD] = lane
    kv_ref[:, KV_HEADS * HEAD :] = linear[:, (HEADS + KV_HEADS) * HEAD :].astype(jnp.bfloat16)


def project(inputs, gain, w_qkv, bias, cosine, sine):
    rows, width = inputs.shape
    qwidth, kwidth = HEADS * HEAD, 2 * KV_HEADS * HEAD
    tile = ROW_TILE
    fixed = lambda i: (0, 0)
    moving = lambda i: (i, 0)
    return pl.pallas_call(
        project_body,
        grid=(rows // tile,),
        in_specs=[
            pl.BlockSpec((tile, width), moving),
            pl.BlockSpec((1, width), fixed),
            pl.BlockSpec((width, qwidth + kwidth), fixed),
            pl.BlockSpec((1, qwidth + kwidth), fixed),
            pl.BlockSpec((tile, HEAD), moving),
            pl.BlockSpec((tile, HEAD), moving),
        ],
        out_specs=[
            pl.BlockSpec((tile, width), moving),
            pl.BlockSpec((tile, qwidth), moving),
            pl.BlockSpec((tile, kwidth), moving),
        ],
        out_shape=[
            jax.ShapeDtypeStruct((rows, width), jnp.bfloat16),
            jax.ShapeDtypeStruct((rows, qwidth), jnp.bfloat16),
            jax.ShapeDtypeStruct((rows, kwidth), jnp.bfloat16),
        ],
        compiler_params=params(48),
        cost_estimate=cost(2 * rows * width * (qwidth + kwidth), 2 * width * (qwidth + kwidth) + 8 * rows * width),
        name="project",
    )(inputs, gain, w_qkv, bias, cosine, sine)


def spread_body(*refs):
    owns, rows, whole, rows_x, rows_y, rows_d, sent, landed, kept = refs[:4], *refs[4:]
    me, plane = lax.axis_index("gy"), lax.axis_index("gx")
    peers = peers_of()
    along_x, along_y, across = (peers[bits]["gy"] for bits in OTHERS)
    places = [lax.rem(plane + 4 - k, 4) for k in range(4)]
    greet((CORE, ALONG_X, ALONG_Y))
    copies = []

    def send(source, target, bits):
        copy = pltpu.make_async_remote_copy(
            source,
            target,
            sent.at[len(copies)],
            landed.at[len(copies)],
            device_id=peers[bits],
            device_id_type=pl.DeviceIdType.MESH,
        )
        copies.append(copy)
        copy.start()
        return copy

    from_x, from_y, from_d, from_core, local = [], [], [], [], []
    for k in range(4):
        block = whole.at[places[k], me]
        from_x.append(send(owns[k], block, ALONG_X))
        from_y.append(send(owns[k], block, ALONG_Y))
        from_core.append(send(owns[k], block, CORE))
        local.append(pltpu.make_async_copy(owns[k], block, kept.at[k]))
        local[k].start()
    moved_x, moved_y = send(rows, rows_x, ALONG_X), send(rows, rows_y, ALONG_Y)
    for k in range(4):
        block_x, block_y = whole.at[places[k], along_x], whole.at[places[k], along_y]
        from_x[k].wait_recv()
        if k < 2:
            from_d.append(send(block_x, block_x, ALONG_Y))
        from_core.append(send(block_x, block_x, CORE))
        from_y[k].wait_recv()
        if k >= 2:
            from_d.append(send(block_y, block_y, ALONG_X))
        from_core.append(send(block_y, block_y, CORE))
    for k in range(4):
        block = whole.at[places[k], across]
        from_d[k].wait_recv()
        from_core.append(send(block, block, CORE))
    half = rows.shape[0] // 2
    first, second = pl.ds(0, half), pl.ds(half, half)
    moved_x.wait_recv()
    moved_d = [send(rows_x.at[first], rows_d.at[first], ALONG_Y)]
    moved_y.wait_recv()
    moved_d.append(send(rows_y.at[second], rows_d.at[second], ALONG_X))
    for copy in from_core + moved_d:
        copy.wait_recv()
    for copy in copies:
        copy.wait_send()
    for copy in local:
        copy.wait()


def spread(owns, rows):
    deep, wide = owns[0].shape
    anywhere = pl.BlockSpec(memory_space=pl.ANY)
    whole, *others = pl.pallas_call(
        spread_body,
        in_specs=[anywhere] * 5,
        out_specs=[anywhere] * 4,
        out_shape=[jax.ShapeDtypeStruct((4, 8, deep, wide), rows.dtype)]
        + [jax.ShapeDtypeStruct(rows.shape, rows.dtype)] * 3,
        scratch_shapes=[
            pltpu.SemaphoreType.DMA((32,)),
            pltpu.SemaphoreType.DMA((32,)),
            pltpu.SemaphoreType.DMA((4,)),
        ],
        compiler_params=pltpu.CompilerParams(collective_id=0, has_side_effects=True),
        cost_estimate=cost(0, 300 * 1024 * 1024),
        name="spread",
    )(*owns, rows)
    return whole.reshape(32 * deep, wide), others


def unit_back(grad_normed, values, gain):
    inverse = lax.rsqrt(jnp.mean(values * values, axis=-1, keepdims=True) + EPS)
    unit = values * inverse
    scaled = grad_normed * gain
    back = inverse * (scaled - unit * jnp.mean(scaled * unit, axis=-1, keepdims=True))
    return back, jnp.sum(grad_normed * unit, axis=0, keepdims=True)


def branch_back_body(own_ref, xa_ref, xb_ref, ya_ref, yb_ref, resid_ref, cot_ref, gain_ref, heads_ref, *refs):
    turned, (resid_out, heads_out, gain_out, weight_out, branch) = refs[:-5], refs[-5:]
    step, full = pl.program_id(0), jnp.float32
    tile = own_ref.shape[0]
    from_x = jnp.where(step < BRANCH_CUTS[0], xa_ref[...].astype(full), xb_ref[...].astype(full))
    from_y = jnp.where(step < BRANCH_CUTS[1], ya_ref[...].astype(full), yb_ref[...].astype(full))
    grad_normed = own_ref[...].astype(full) + from_x + from_y
    back, gain_part = unit_back(grad_normed, resid_ref[...], gain_ref[...])
    grad_resid = cot_ref[...].astype(full) + back
    resid_out[...] = grad_resid
    low = grad_resid.astype(jnp.bfloat16)
    branch[pl.ds(pl.multiple_of(step * tile, tile), tile), :] = low
    gain_out[...] = jnp.where(step == 0, 0.0, gain_out[...]) + gain_part
    wide = turned[0].shape[1]
    for index, piece in enumerate(turned):
        heads_out[:, index * wide : (index + 1) * wide] = dot_nn(low, piece[...]).astype(jnp.bfloat16)

    @pl.when(step == pl.num_programs(0) - 1)
    def _():
        weight_out[...] = dot_tn(branch[...], heads_ref[...]).astype(jnp.bfloat16)


def branch_back(own, from_x, from_y, resid, cotan, gain, heads, weights, first_column):
    rows, width = own.shape
    tile, wide = ROW_TILE, 512
    steps = rows // tile
    low, full = jnp.bfloat16, jnp.float32
    moving = pl.BlockSpec((tile, width), lambda i: (i, 0))
    fixed = pl.BlockSpec((1, width), lambda i: (0, 0))
    first, then = [], []
    for count in BRANCH_CUTS:
        first.append(pl.BlockSpec((tile, width), lambda i, n=count: (jnp.minimum(i, n - 1), 0)))
        then.append(pl.BlockSpec((tile, width), lambda i, n=count: (jnp.maximum(i - n, 0), 0)))
    return pl.pallas_call(
        branch_back_body,
        grid=(steps,),
        in_specs=[moving, first[0], then[0], first[1], then[1], moving, moving, fixed]
        + [pl.BlockSpec((rows, width), lambda i: (0, 0))]
        + [pl.BlockSpec((width, wide), lambda i, j=j: (0, first_column // wide + j)) for j in range(width // wide)],
        out_specs=[moving, moving, fixed, pl.BlockSpec((width, width), lambda i: (0, 0))],
        out_shape=[
            jax.ShapeDtypeStruct((rows, width), full),
            jax.ShapeDtypeStruct((rows, width), low),
            jax.ShapeDtypeStruct((1, width), full),
            jax.ShapeDtypeStruct((width, width), low),
        ],
        scratch_shapes=[pltpu.VMEM((rows, width), low)],
        compiler_params=params(56),
        cost_estimate=cost(4 * rows * width * width, 20 * rows * width + 4 * width * width),
        name="branch_back",
    )(own, *from_x, *from_y, resid, cotan, gain, heads, *[weights] * (width // wide))


def project_back_body(q_ref, own_ref, x_ref, y_ref, d_ref, cos_ref, sin_ref, w_ref, in_ref, gain_ref, resid_ref, normed_ref,
                      tokens_out, bias_out, gain_out, weight_out, linear):
    step, full = pl.program_id(0), jnp.float32
    tile, qwidth = q_ref.shape
    total = own_ref[...].astype(full) + x_ref[...].astype(full) + y_ref[...].astype(full) + d_ref[...].astype(full)
    pieces = [q_ref[...]]
    for head in range(2 * KV_HEADS):
        lane = total[:, head * HEAD : (head + 1) * HEAD]
        if head < KV_HEADS:
            lane = lane * cos_ref[...] - pltpu.roll(lane, HEAD // 2, 1) * sin_ref[...]
        pieces.append(lane.astype(jnp.bfloat16))
    lin = jnp.concatenate(pieces, axis=1)
    linear[pl.ds(pl.multiple_of(step * tile, tile), tile), :] = lin
    bias_part = jnp.sum(lin.astype(full), axis=0, keepdims=True)
    bias_out[...] = jnp.where(step == 0, 0.0, bias_out[...]) + bias_part
    back, gain_part = unit_back(dot_nt(lin, w_ref[...]), in_ref[...].astype(full), gain_ref[...])
    gain_out[...] = jnp.where(step == 0, 0.0, gain_out[...]) + gain_part
    tokens_out[...] = (resid_ref[...] + back).astype(jnp.bfloat16)

    @pl.when(step == pl.num_programs(0) - 1)
    def _():
        weight_out[:, : linear.shape[1]] = dot_tn(normed_ref[...], linear[...]).astype(jnp.bfloat16)


def project_back(query_lin, parts, cosine, sine, weights, inputs, gain, grad_resid, normed, collective, sides):
    rows, width = inputs.shape
    qwidth, kwidth = query_lin.shape[1], parts[0].shape[1]
    qwide, tile = qwidth + kwidth, ROW_TILE
    low, full = jnp.bfloat16, jnp.float32

    def moving(columns):
        return pl.BlockSpec((tile, columns), lambda i: (i, 0))

    def fixed(high, columns):
        return pl.BlockSpec((high, columns), lambda i: (0, 0))

    return call_beside(
        project_back_body,
        sides,
        collective,
        (query_lin, *parts, cosine, sine, weights, inputs, gain, grad_resid, normed),
        (rows // tile,),
        [moving(qwidth)]
        + [moving(kwidth)] * 4
        + [moving(HEAD)] * 2
        + [fixed(width, qwide), moving(width), fixed(1, width), moving(width), fixed(rows, width)],
        [moving(width), fixed(1, qwide), fixed(1, width), fixed(width, qwide + HEAD)],
        [
            jax.ShapeDtypeStruct((rows, width), low),
            jax.ShapeDtypeStruct((1, qwide), full),
            jax.ShapeDtypeStruct((1, width), full),
            jax.ShapeDtypeStruct((width, qwide + HEAD), low),
        ],
        [pltpu.VMEM((rows, qwide), low)],
        56,
        cost(4 * rows * width * qwide, 20 * rows * width + 4 * width * qwide),
        "project_back",
    )


def both_body(first_mine, first_other, second_mine, second_other, out_ref):
    deep = first_mine.shape[1]
    out_ref[0, :deep] = (first_mine[0].astype(jnp.float32) + first_other[0].astype(jnp.float32)).astype(out_ref.dtype)
    out_ref[0, deep:] = (second_mine[0].astype(jnp.float32) + second_other[0].astype(jnp.float32)).astype(out_ref.dtype)


def both_sums(*arrays):
    planes, deep, wide = arrays[0].shape
    return pl.pallas_call(
        both_body,
        grid=(planes,),
        in_specs=[pl.BlockSpec((1, deep, wide), lambda i: (i, 0, 0))] * 4,
        out_specs=pl.BlockSpec((1, 2 * deep, wide), lambda i: (i, 0, 0)),
        out_shape=jax.ShapeDtypeStruct((planes, 2 * deep, wide), arrays[0].dtype),
        compiler_params=params(48),
        cost_estimate=cost(0, 12 * planes * deep * wide),
        name="both_back",
    )(*arrays)


def finish_body(wide_ref, out_ref, mine_ref, other_ref, both_ref, tokens_ref, resid_ref, *refs):
    layer_refs, results, rows_out, scratch = refs[:3], refs[3:8], refs[8:10], refs[10:]
    kept, got_core, got_first, got_second, got_ring = [scratch[i : i + 2] for i in range(0, 10, 2)]
    units, got_units, units_ring, units_moving, both, layer, resid, *layer_parts, sent, landed, local = scratch[10:]
    me, plane = lax.axis_index("gy"), lax.axis_index("gx")
    core, x, y = lax.rem(me, 2), lax.rem(me // 2, 2), me // 4
    places = [lax.rem(plane + 4 - s, 4) for s in range(4)]
    peers = peers_of()
    full = jnp.float32
    greet((CORE, ALONG_X, ALONG_Y, RING, RING + 1))
    copies, loads = [], []

    def send(source, target, bits):
        copy = pltpu.make_async_remote_copy(
            source,
            target,
            sent.at[len(copies)],
            landed.at[len(copies)],
            device_id=peers[bits],
            device_id_type=pl.DeviceIdType.MESH,
        )
        copies.append(copy)
        copy.start()
        return copy

    def load(source, target):
        copy = pltpu.make_async_copy(source, target, local.at[len(loads)])
        loads.append(copy)
        copy.start()
        return copy

    inputs = (wide_ref, out_ref)
    core_copies = [send(inputs[i].at[:, :, :, 1 - core], got_core[i], CORE) for i in range(2)]
    unit_loads = [load(mine_ref, units), load(other_ref, got_units)]
    both_load = load(both_ref, both)
    layer_loads = [load(a, b) for a, b in zip((resid_ref, *layer_refs), (resid, *layer_parts))]
    held = [load(inputs[i].at[:, :, :, core], kept[i]) for i in range(2)]

    for copy in unit_loads:
        copy.wait()

    @pl.loop(0, 4)
    def _(p):
        units[p] += got_units[p]

    units_copy = send(units.at[places[1]], units_ring.at[0], RING)
    steps = []
    for i in range(2):
        core_copies[i].wait_recv()
        held[i].wait()

        @pl.loop(0, 4)
        def _(p):
            for a in range(2):
                for b in range(2):
                    kept[i][p, a, b] += got_core[i][p, a, b]

        middle = kept[i].shape[-1] // 256 * 128
        first, second = pl.ds(0, middle), pl.ds(middle, kept[i].shape[-1] - middle)
        steps.append((
            send(kept[i].at[:, :, 1 - x, :, first], got_first[i].at[:, :, :, first], ALONG_X),
            send(kept[i].at[:, 1 - y, :, :, second], got_first[i].at[:, :, :, second], ALONG_Y),
            first,
            second,
        ))
    units_copy.wait_recv()
    units_moving[0] = units[places[2]] + units_ring[0]
    units_copy = send(units_moving.at[0], units_ring.at[1], RING)
    for copy in layer_loads:
        copy.wait()

    @pl.loop(0, resid.shape[0] // ROW_TILE)
    def _(p):
        take = pl.ds(pl.multiple_of(p * ROW_TILE, ROW_TILE), ROW_TILE)
        total = layer_parts[0][take, :].astype(full) + layer_parts[1][take, :].astype(full)
        layer[take, :] = (resid[take, :] + (total + layer_parts[2][take, :].astype(full))).astype(jnp.bfloat16)

    half = resid.shape[0] // 2
    row_copies = []
    for source, target in ((layer, rows_out[0]), (tokens_ref, rows_out[1])):
        row_copies.append(send(source.at[pl.ds((1 - core) * half, half)], target.at[core], CORE))
        held.append(load(source.at[pl.ds(core * half, half)], target.at[core]))
    both_load.wait()
    high, own = both.shape[0] // 2, results[3].shape[0]
    results[3][...] = both[0:own, :].astype(full)
    results[4][...] = both[high : high + own, :].astype(full)
    nexts = []
    for i in range(2):
        first_copy, second_copy, first, second = steps[i]
        first_copy.wait_recv()

        @pl.loop(0, 4)
        def _(p):
            for a in range(2):
                kept[i][p, a, x, :, first] += got_first[i][p, a, :, first]

        third_copy = send(kept[i].at[:, 1 - y, x, :, first], got_second[i].at[:, :, first], ALONG_Y)
        second_copy.wait_recv()

        @pl.loop(0, 4)
        def _(p):
            for b in range(2):
                kept[i][p, y, b, :, second] += got_first[i][p, b, :, second]

        nexts.append((third_copy, send(kept[i].at[:, y, 1 - x, :, second], got_second[i].at[:, :, second], ALONG_X)))
    units_copy.wait_recv()
    units_moving[1] = units[places[3]] + units_ring[1]
    units_copy = send(units_moving.at[1], units_ring.at[2], RING)
    ring_copies = []
    for i in range(2):
        for copy in nexts[i]:
            copy.wait_recv()

        @pl.loop(0, 4)
        def _(p):
            kept[i][p, y, x] += got_second[i][p]

        for k, bits in ((1, RING), (2, RING + 1), (3, -RING)):
            there = lax.rem(plane + k, 4)
            ring_copies.append(send(kept[i].at[there, y, x], got_ring[i].at[k - 1], bits))
    units_copy.wait_recv()
    results[2][...] = units[places[0], 0:own, :].astype(full) + units_ring[2, 0:own, :].astype(full)
    for i in range(2):
        total = kept[i][plane, y, x].astype(full)
        for k in range(3):
            ring_copies[3 * i + k].wait_recv()
            total = total + got_ring[i][k].astype(full)
        results[i][...] = total
    for copy in row_copies:
        copy.wait_recv()
    for copy in held[2:]:
        copy.wait()
    for copy in copies:
        copy.wait_send()


def finish(wide, out, mine, other, both, tokens, resid, layer_parts, own_units, collective):
    low, full = jnp.bfloat16, jnp.float32
    deep = wide.shape[0] // 32
    wide, out = (a.reshape(4, 2, 2, 2, deep, a.shape[1]) for a in (wide, out))
    columns = (wide.shape[-1], out.shape[-1])
    block = mine.shape[1:]
    anywhere = pl.BlockSpec(memory_space=pl.ANY)
    inside = pl.BlockSpec(memory_space=pltpu.VMEM)

    def pairs(*lead):
        return [pltpu.VMEM((*lead, deep, c), low) for c in columns]

    return pl.pallas_call(
        finish_body,
        in_specs=[anywhere] * 10,
        out_specs=[inside] * 5 + [anywhere] * 2,
        out_shape=[jax.ShapeDtypeStruct((deep, c), full) for c in columns]
        + [jax.ShapeDtypeStruct((own_units, block[1]), full)] * 3
        + [jax.ShapeDtypeStruct((2, tokens.shape[0] // 2, tokens.shape[1]), low)] * 2,
        scratch_shapes=[
            *pairs(4, 2, 2),
            *pairs(4, 2, 2),
            *pairs(4, 2),
            *pairs(4),
            *pairs(3),
            pltpu.VMEM((4, *block), low),
            pltpu.VMEM((4, *block), low),
            pltpu.VMEM((3, *block), low),
            pltpu.VMEM((2, *block), low),
            pltpu.VMEM(both.shape, low),
            pltpu.VMEM(tokens.shape, low),
            pltpu.VMEM(resid.shape, full),
            *[pltpu.VMEM(tokens.shape, low)] * 3,
            pltpu.SemaphoreType.DMA((21,)),
            pltpu.SemaphoreType.DMA((21,)),
            pltpu.SemaphoreType.DMA((11,)),
        ],
        compiler_params=pltpu.CompilerParams(
            vmem_limit_bytes=60 * 1024 * 1024, collective_id=collective, has_side_effects=True
        ),
        cost_estimate=cost(0, 200 * 1024 * 1024),
        name="finish",
    )(wide, out, mine, other, both, tokens, resid, *layer_parts)


def swap(array, bits):
    return lax.ppermute(array, "gy", [(i, i ^ bits) for i in range(8)])


def pick(array, index):
    return lax.dynamic_index_in_dim(array, index, 0, keepdims=False)


def after(array, *earlier):
    return lax.optimization_barrier((array, *earlier))[0]


def pair_rows(pair, core):
    kept, got = pick(pair, core), swap(pick(pair, 1 - core), CORE)
    return jnp.where(core == 0, jnp.concatenate([kept, got]), jnp.concatenate([got, kept]))


def plane_order(blocks, chip):
    rows = blocks[0].shape[0]
    whole = jnp.zeros((4 * rows,) + blocks[0].shape[1:], blocks[0].dtype)
    for index, block in enumerate(blocks):
        whole = lax.dynamic_update_slice_in_dim(whole, block, (chip ^ index) * rows, 0)
    return whole


def on_core(
    tokens,
    cotangent,
    segment,
    parent,
    w_qkv,
    qkv_bias,
    w_out,
    gain_attn,
    gain_ffn,
    w_gate,
    w_up,
    w_down,
):
    low, full = jnp.bfloat16, jnp.float32
    me = lax.axis_index("gy")
    plane = lax.axis_index("gx")
    core, chip = me % 2, me // 2
    rows, width = 2 * tokens.shape[1], tokens.shape[2]
    slot_len = segment.shape[1]
    own_units = w_gate.shape[1]
    pad_units = -(-own_units // 384) * 384
    qwidth, kwidth = HEADS * HEAD, KV_HEADS * HEAD
    offset = chip * rows

    nb, ng = qkv_bias.shape[0], gain_attn.shape[0]
    packed = jnp.concatenate([qkv_bias, gain_attn, gain_ffn]).reshape(-1, 1)
    packed = jnp.pad(packed, ((0, 4 * ng - packed.shape[0]), (0, 0))).reshape(4, ng).T
    packed = jnp.pad(packed, ((0, 0), (0, HEAD - 4)))
    attn_own = jnp.concatenate([w_qkv, w_out.T, packed], axis=1)
    attn_slots = [attn_own] + [
        lax.ppermute(attn_own, "gx", [(i, (i + k) % 4) for i in range(4)]) for k in (1, 2, 3)
    ]

    inputs_low = pair_rows(tokens, core)
    grad_low = pair_rows(cotangent, core)

    seg_tree = pick(segment, core)
    valid, upper_one, upper_two, depth_pos = tree_tables(seg_tree, pick(parent, core))
    places = jnp.arange(slot_len, dtype=jnp.int32)

    def take_own(array):
        return lax.dynamic_slice_in_dim(array, offset, rows, 0)

    cosine, sine = rotation(take_own(depth_pos), HEAD)
    sine = sine * jnp.where(jnp.arange(HEAD) < HEAD // 2, -1.0, 1.0)

    more = pad_units - own_units
    shards = [jnp.pad(w, ((0, 0), (0, more))) for w in (w_gate, w_up, w_down.T)]
    weights = [
        lax.all_gather(after(w, *attn_slots, inputs_low, grad_low), "gx", axis=0, tiled=True) for w in shards[:2]
    ]
    weights.append(lax.all_gather(after(shards[2], weights[0]), "gx", axis=0, tiled=True))
    attn_all, cotan_others = spread([after(s, inputs_low, cosine, sine, *shards) for s in attn_slots], grad_low)
    cotan_blocks = [grad_low] + cotan_others
    qwide = qwidth + 2 * kwidth
    small = attn_all[:, qwide + width :].reshape(32, ng, HEAD)[:, :, :4].transpose(0, 2, 1).reshape(32, 4 * ng)
    small = small.astype(full)
    bias_full = small[:, :nb].reshape(1, -1)
    gain_one = small[:, nb : nb + ng].reshape(1, -1)
    gain_two = small[:, nb + ng : nb + 2 * ng].reshape(1, -1)
    out_turned = attn_all[:, qwide : qwide + width]

    normed_one, query, keyval_own = project(inputs_low, gain_one, attn_all, bias_full, cosine, sine)
    mask = allowed(
        after(take_own(seg_tree), keyval_own), take_own(upper_one), take_own(upper_two), take_own(places), seg_tree, valid, places
    )
    qblocks, kblocks = rows // QUERY_TILE, slot_len // KEY_TILE
    active = mask.reshape(qblocks, QUERY_TILE, kblocks, KEY_TILE).any(axis=(1, 3))
    block_count = active.sum(axis=1).astype(jnp.int32)
    rank = jnp.cumsum(active.astype(jnp.int32), axis=1) - 1
    numbers = jnp.arange(kblocks, dtype=jnp.int32)
    hit = active[:, :, None] & (rank[:, :, None] == numbers[None, None, :])
    block_list = jnp.sum(jnp.where(hit, numbers[None, :, None], 0), axis=1).astype(jnp.int32)
    mask_bias = jnp.where(mask.T, 0.0, NEGATIVE).astype(low)

    keyval = plane_order([keyval_own] + [swap(keyval_own, bits) for bits in OTHERS], chip)
    other_weights = [swap(after(w, keyval), CORE) for w in weights[:2]]
    query = after(query, *other_weights)
    heads_out, lse = attend_fast(block_list, block_count, query, keyval, mask_bias)
    inputs = inputs_low.astype(full)
    resid = inputs + lax.dot_general(heads_out, out_turned, (((1,), (1,)), ((), ())), preferred_element_type=full)
    normed_two = norm_parts(resid, gain_two)[2]

    other_weights.append(swap(after(weights[2], heads_out), CORE))
    pieces = weights + other_weights
    half = rows // 2
    first, second = (0, half), (half, half)
    own, (normed_x, normed_y) = ffn_block(
        normed_two, cotan_blocks[0], pieces, 1, [whole_side(normed_two, ALONG_X), whole_side(normed_two, ALONG_Y)]
    )
    passed_on = [(normed_x, first, first, ALONG_Y), (normed_y, second, second, ALONG_X)]
    near_x, (normed_d,) = ffn_block(normed_x, cotan_blocks[1], pieces, 2, [passed_on])
    cut, early = (count * ROW_TILE for count in BRANCH_CUTS)
    rest, few = rows - cut, rows // 10 * 3
    far, (back_x,) = ffn_block(normed_d, cotan_blocks[3], pieces, 3, [rows_side(near_x[4], 0, cut, ALONG_X)])
    near_y, (back_d,) = ffn_block(
        after(normed_y, far[4]), cotan_blocks[2], pieces, 4, [rows_side(far[4], 0, cut, ALONG_X)]
    )
    normed_blocks = [normed_two, normed_x, normed_y, normed_d]
    hidden_b, gate_b, up_b, out_b, back_b = zip(own, near_x, near_y, far)

    def join(mine, passed):
        return (mine.astype(full) + passed.astype(full)).astype(low)

    (down_mine, down_sent), (back_x_end, back_d_end, out_d_end, back_y) = wgrad(
        hidden_b,
        cotan_blocks,
        4,
        5,
        [
            rows_side(back_b[1], cut, rest, ALONG_X),
            rows_side(back_b[3], cut, rest, ALONG_X),
            rows_side(out_b[3], 0, few, ALONG_X),
            rows_side(join(back_b[2][:early], back_d[:early]), 0, early, ALONG_Y),
        ],
    )
    late = join(back_b[2][early:], jnp.concatenate([back_d[early:], back_d_end]))
    (gate_mine, gate_sent), (down_got, out_d, back_y_end) = wgrad(
        gate_b,
        normed_blocks,
        4,
        6,
        [
            whole_side(down_sent, CORE),
            rows_side(out_b[3], few, rows - few, ALONG_X),
            rows_side(late, 0, rows - early, ALONG_Y),
        ],
    )
    gate_got = swap(gate_sent, CORE)
    out_d = jnp.concatenate([out_d_end, out_d])

    grad_resid, grad_heads, grad_gain_two, grad_wout = branch_back(
        back_b[0],
        (back_x, back_x_end),
        (back_y, back_y_end),
        resid,
        grad_low,
        gain_two,
        heads_out,
        attn_all,
        qwide,
    )
    out_got = [swap(after(out_b[1], gate_sent), ALONG_X), swap(join(out_b[2], out_d), ALONG_Y)]
    both = both_sums(down_mine, down_got, after(gate_mine, grad_heads), gate_got)
    grad_heads = after(grad_heads, grad_wout, both)
    both = lax.psum_scatter(both, "gx", scatter_dimension=0, tiled=True)[0]
    query_lin, keyval_part = attend_back_fast(
        block_list, block_count, query, keyval, mask_bias, lse, heads_out, grad_heads, cosine, sine
    )

    keyval_own = lax.dynamic_slice_in_dim(keyval_part, offset, rows, 0)
    (up_mine, up_sent), others = wgrad(
        up_b, normed_blocks, 4, 7, [chip_side(keyval_part, bits) for bits in OTHERS]
    )

    (grad_rows, grad_bias, grad_gain_one, grad_wqkv), (up_got,) = project_back(
        query_lin,
        (keyval_own, *others),
        cosine,
        sine,
        attn_all,
        inputs_low,
        gain_one,
        grad_resid,
        normed_one,
        9,
        [whole_side(up_sent, CORE)],
    )
    packed = jnp.concatenate(
        [grad_bias.reshape(32, nb), grad_gain_one.reshape(32, ng), grad_gain_two.reshape(32, ng)], axis=1
    )
    packed = jnp.pad(packed, ((0, 0), (0, 4 * ng - packed.shape[1]))).reshape(32, 4, ng).transpose(0, 2, 1)
    packed = jnp.pad(packed.reshape(32 * ng, 4), ((0, 0), (0, HEAD - 4))).astype(low)
    wide, grad_wout, grad_wup, grad_down, grad_wgate, layer_out, grad_tokens = finish(
        lax.dynamic_update_slice_in_dim(grad_wqkv, packed, qwide, 1),
        grad_wout,
        up_mine,
        up_got,
        both,
        grad_rows,
        resid,
        (out_b[0], *out_got),
        own_units,
        8,
    )
    grad_wqkv, grad_wout = wide[:, :qwide], grad_wout.T
    small = wide[:, qwide : qwide + 4].T.reshape(-1)
    grad_wgate, grad_wup = grad_wgate.T, grad_wup.T
    return (
        layer_out,
        grad_tokens,
        grad_wqkv,
        small[:nb],
        grad_wout,
        small[nb : nb + ng],
        small[nb + ng : nb + 2 * ng],
        grad_wgate,
        grad_wup,
        grad_down,
    )


def solution(mesh):
    in_specs = (
        P("gx", "gy", None),
        P("gx", "gy", None),
        P("gx", None),
        P("gx", None),
        P(("gx", "gy"), None),
        P(("gx", "gy")),
        P(None, ("gx", "gy")),
        P(("gx", "gy")),
        P(("gx", "gy")),
        P("gx", "gy"),
        P("gx", "gy"),
        P("gy", "gx"),
    )
    out_specs = (
        P("gx", "gy", None),
        P("gx", "gy", None),
        P(("gx", "gy"), None),
        P(("gx", "gy")),
        P(None, ("gx", "gy")),
        P(("gx", "gy")),
        P(("gx", "gy")),
        P("gx", "gy"),
        P("gx", "gy"),
        P("gy", "gx"),
    )
    return jax.shard_map(
        on_core if tuple(mesh.shape.values()) == (4, 8) else on_device,
        mesh=mesh,
        in_specs=in_specs,
        out_specs=out_specs,
        check_vma=False,
    )
```
